32 devices in a mesh: dp: 8 (over z, core), tensor: 4 (over y, x).
Axes of the slice: x: 2, y: 2, z: 4, core: 2. Of those that a mesh axis runs over, the one named last changes fastest.
Arguments:
- residual_in: bfloat16 [2048, 1536], P(('dp', 'tensor')), may hold values from -6 to 6
- norm_gain: bfloat16 [2, 1536], P(None, 'dp'), may hold values from 0.5 to 1.5
- w_zx: bfloat16 [2, 1536, 2, 3072], P(None, 'dp', None, 'tensor'), may hold values from -0.15625 to 0.15625
- w_bc: bfloat16 [2, 1536, 256], P(None, 'dp'), may hold values from -0.15625 to 0.15625
- w_dt: bfloat16 [2, 1536, 48], P(None, 'dp', 'tensor'), may hold values from -0.078125 to 0.078125
- conv_x: float32 [2, 5, 3072], P(None, None, 'tensor'), may hold values from -3 to 3
- conv_bc: bfloat16 [2, 5, 256], P(None, None, 'dp'), may hold values from -3 to 3
- dt_bias: float32 [2, 48], P(None, 'tensor'), may hold values from -8 to -2
- a_log: float32 [2, 48], P(None, 'tensor'), may hold values from 0 to 2.77
- d_skip: float32 [2, 48], P(None, 'tensor'), may hold values from 0.5 to 1.5
- gate_gain: float32 [2, 3072], P(None, 'tensor'), may hold values from 0.5 to 1.5
- w_out: bfloat16 [2, 3072, 1536], P(None, 'tensor', 'dp'), may hold values from -0.109375 to 0.109375
- lengths: int32 [8], P('dp'), may hold values from 128 to 256, as said below
- cotangent: bfloat16 [2048, 1536], P(('dp', 'tensor')), may hold values from -6 to 6
Outputs:
- output: float32 [2048, 1536], P(('dp', 'tensor'))
- grad_residual: float32 [2048, 1536], P(('dp', 'tensor'))
- grad_norm_gain: float32 [2, 1536], P(None, 'dp')
- grad_w_zx: float32 [2, 1536, 2, 3072], P(None, 'dp', None, 'tensor')
- grad_w_bc: float32 [2, 1536, 256], P(None, 'dp')
- grad_w_dt: float32 [2, 1536, 48], P(None, 'dp', 'tensor')
- grad_conv_x: float32 [2, 5, 3072], P(None, None, 'tensor')
- grad_conv_bc: float32 [2, 5, 256], P(None, None, 'dp')
- grad_dt_bias: float32 [2, 48], P(None, 'tensor')
- grad_a_log: float32 [2, 48], P(None, 'tensor')
- grad_d_skip: float32 [2, 48], P(None, 'tensor')
- grad_gate_gain: float32 [2, 3072], P(None, 'tensor')
- grad_w_out: float32 [2, 3072, 1536], P(None, 'tensor', 'dp')
The draws below stay inside these ranges and needn't reach their ends.
Inputs may be any that keep to these rules, and one draw needn't show every extreme that they name: lengths[g] counts the live positions of group g's sequence, which begins at the group's first row; in every draw some group is full (256 positions).
All inputs are finite; a program needn't handle non-finite values.
Results may differ from the reference program's by a relative error of at most 0.025.
Values may be sent and summed in bfloat16 or wider, within the bound.
No kernel may reach another device: no remote copies, remote signals or barrier semaphores. Data moves between devices by JAX's collectives and lax.ppermute only.
A program may use at most 128 MiB of HBM per device.

```python
import jax
import jax.numpy as jnp
from jax import lax

D = 1536
HEADS = 48
STATE = 128
INNER = 3072
SPAN = 256
LAYERS = 2
CAP = 256
TOKENS = 2048
N_DP = 8


def draw_lengths(key, part):
    key = jax.random.fold_in(key, 7)
    first_key, second_key = jax.random.split(key)
    drawn = jax.random.randint(first_key, (N_DP,), CAP // 2, CAP + 1)
    full_group = jax.random.randint(second_key, (), 0, N_DP)
    return jnp.where(jnp.arange(N_DP) == full_group, CAP, drawn).astype(jnp.int32)


def block_scale(rng, dims, shards, smallest, top_value):
    loudness, own = 1.0, jax.random.fold_in(rng, 6)
    for axis_at, parts in shards:
        heights = jnp.exp(jax.random.uniform(jax.random.fold_in(own, axis_at), (parts,), jnp.float32, smallest / len(shards), top_value / len(shards)))
        loudness = loudness * jnp.repeat(heights, dims[axis_at] // parts).reshape([-1 if axis == axis_at else 1 for axis in range(len(dims))])
    return loudness


def normal_values(stream_key, extent, spread, limit, shards=(), held_as=jnp.bfloat16):
    loudness = block_scale(stream_key, extent, shards, -0.22, 0.18) if shards else 1.0
    array = jax.random.normal(stream_key, extent, jnp.float32) * spread * loudness
    return jnp.minimum(jnp.maximum(array, -limit), limit).astype(held_as)


def setup_inputs(seed: int = 0) -> dict:
    key_of = jax.random.split(jax.random.key(seed), 15)
    return {
        "residual_in": normal_values(key_of[0], (TOKENS, D), 1.0, 6.0, ((0, 32),)),
        "norm_gain": jnp.clip(1.0 + 0.1 * jax.random.normal(key_of[1], (LAYERS, D), jnp.float32), 0.5, 1.5).astype(jnp.bfloat16),
        "w_zx": normal_values(key_of[2], (LAYERS, D, 2, INNER), D ** -0.5, 0.15625, ((1, 8), (3, 4))),
        "w_bc": normal_values(key_of[3], (LAYERS, D, 2 * STATE), D ** -0.5, 0.15625, ((1, 8),)),
        "w_dt": normal_values(key_of[4], (LAYERS, D, HEADS), (4 * D) ** -0.5, 0.078125, ((1, 8), (2, 4))),
        "conv_x": normal_values(key_of[5], (LAYERS, 5, INNER), 0.5, 3.0, ((2, 4),), jnp.float32),
        "conv_bc": normal_values(key_of[6], (LAYERS, 5, 2 * STATE), 0.5, 3.0, ((2, 8),)),
        "dt_bias": jnp.clip(-8.0 + 6.0 * jax.random.uniform(key_of[7], (LAYERS, HEADS), jnp.float32) ** block_scale(key_of[7], (LAYERS, HEADS), ((1, 4),), -0.2, 0.2), -8.0, -2.0),
        "a_log": jnp.clip(2.77 * jax.random.uniform(key_of[8], (LAYERS, HEADS), jnp.float32) ** block_scale(key_of[8], (LAYERS, HEADS), ((1, 4),), -0.2, 0.2), 0.0, 2.77),
        "d_skip": jnp.clip(0.5 + 1.0 * jax.random.uniform(key_of[9], (LAYERS, HEADS), jnp.float32) ** block_scale(key_of[9], (LAYERS, HEADS), ((1, 4),), -0.2, 0.2), 0.5, 1.5),
        "gate_gain": jnp.clip(1.0 + 0.1 * jax.random.normal(key_of[10], (LAYERS, INNER), jnp.float32), 0.5, 1.5),
        "w_out": normal_values(key_of[11], (LAYERS, INNER, D), INNER ** -0.5, 0.109375, ((1, 4), (2, 8))),
        "lengths": draw_lengths(jax.random.fold_in(key_of[14], 71), 0),
        "cotangent": normal_values(key_of[13], (TOKENS, D), 1.0, 6.0, ((0, 32),)),
    }


top_precision = lax.Precision.HIGHEST

@jax.custom_vjp
def low(v):
    return lax.optimization_barrier(v.astype(jnp.bfloat16)).astype(jnp.float32)

@jax.custom_vjp
def low_back(v):
    return v

def low_keep(v):
    return (low(v), None)

def low_pass(kept, grad):
    return (grad,)

def back_keep(v):
    return (v, None)

def back_low(kept, grad):
    return (low(grad),)
low.defvjp(low_keep, low_pass)
low_back.defvjp(back_keep, back_low)

def rms_scale(values, gain_row):
    return values * lax.rsqrt(lax.optimization_barrier(jnp.mean(values * values, axis=1, keepdims=True)) + 1e-05) * gain_row

def causal_conv(values, conv_taps):
    row_total = values.shape[0]
    padded = jnp.concatenate([jnp.zeros((3, values.shape[1]), values.dtype), values], axis=0)
    result = conv_taps[4] + conv_taps[3] * values
    for offset in range(3):
        result = result + conv_taps[offset] * padded[offset:offset + row_total]
    return result

def state_space(inputs, step_sizes, rates, b_rows, c_rows, skips, span_size):
    row_total, head_count, head_width = inputs.shape
    blocks = row_total // span_size
    state_width = b_rows.shape[1]
    inputs_b = inputs.reshape(blocks, span_size, head_count, head_width)
    steps_b = step_sizes.reshape(blocks, span_size, head_count)
    b_blocks = b_rows.reshape(blocks, span_size, state_width)
    c_blocks = c_rows.reshape(blocks, span_size, state_width)
    causal = jnp.arange(span_size)[:, None] >= jnp.arange(span_size)[None, :]

    def advance(carried, block_item):
        x_block, dt_block, b_block, c_block = block_item
        running = jnp.cumsum(dt_block * rates[None, :], axis=0)
        by_head = running.T
        gap_matrix = by_head[:, :, None] - by_head[:, None, :]
        decays = jnp.exp(jnp.where(causal[None], gap_matrix, -1e+30))
        scores = jnp.dot(c_block, b_block.T, precision=top_precision)
        mixing = decays * scores[None] * dt_block.T[:, None, :]
        within = jnp.einsum('hij,jhp->ihp', mixing, x_block, precision=top_precision)
        carried_out = jnp.einsum('in,hpn->ihp', c_block, carried, precision=top_precision) * jnp.exp(running)[:, :, None]
        to_end = jnp.exp(running[-1][None, :] - running) * dt_block
        updated = carried * jnp.exp(running[-1])[:, None, None] + jnp.einsum('jh,jhp,jn->hpn', to_end, x_block, b_block, precision=top_precision)
        return (updated, within + carried_out + skips[None, :, None] * x_block)
    initial = jnp.zeros((head_count, head_width, state_width), jnp.float32)
    _, outputs = lax.scan(jax.checkpoint(advance), initial, (inputs_b, steps_b, b_blocks, c_blocks))
    return outputs.reshape(row_total, head_count, head_width)

def mixer_core(gate_in, x_in, bc_in, dt_in, conv_x, conv_bc, dt_bias, a_log, d_skip):
    head_count = dt_in.shape[1]
    state_width = bc_in.shape[1] // 2
    conv_out = jax.nn.silu(causal_conv(x_in, conv_x))
    bc_out = jax.nn.silu(causal_conv(bc_in, conv_bc))
    step_sizes = jax.nn.softplus(dt_in + dt_bias[None, :])
    rates = -jnp.exp(a_log)
    mixed = state_space(conv_out.reshape(conv_out.shape[0], head_count, -1), step_sizes, rates, bc_out[:, :state_width], bc_out[:, state_width:], d_skip, SPAN)
    return mixed.reshape(conv_out.shape) * jax.nn.silu(gate_in)

def layer_forward(group_rows, weights, live_mask):
    norm_gain, w_zx, w_bc, w_dt, conv_x, conv_bc, dt_bias, a_log, d_skip, gate_gain, w_out = weights
    normed = low(rms_scale(group_rows, norm_gain))

    def project(matrix):
        return low_back(jnp.dot(normed, matrix, precision=top_precision))
    gated_out = mixer_core(project(w_zx[:, 0, :]), project(w_zx[:, 1, :]), project(w_bc), project(w_dt), conv_x, conv_bc, dt_bias, a_log, d_skip)
    hidden = low(rms_scale(gated_out, gate_gain) * live_mask)
    return group_rows + low_back(jnp.dot(hidden, w_out, precision=top_precision))

def reference(residual_in, norm_gain, w_zx, w_bc, w_dt, conv_x, conv_bc, dt_bias, a_log, d_skip, gate_gain, w_out, lengths, cotangent):
    weights = tuple((weight.astype(jnp.float32) for weight in (norm_gain, w_zx, w_bc, w_dt, conv_x, conv_bc, dt_bias, a_log, d_skip, gate_gain, w_out)))

    def one_group(totals, group_item):
        group_rows, seed_grad, length = group_item
        live_mask = (jnp.arange(CAP).astype(jnp.int32) < length).astype(jnp.float32)[:, None]

        def forward(start_rows, params):
            current = start_rows
            for layer_index in range(LAYERS):
                current = layer_forward(current, tuple((param[layer_index] for param in params)), live_mask)
            return current
        result, pull_back = jax.vjp(forward, group_rows.astype(jnp.float32), weights)
        grad_rows, grad_weights = pull_back(seed_grad.astype(jnp.float32))
        return (jax.tree.map(jnp.add, totals, grad_weights), (result, grad_rows))
    zero_grads = tuple((jnp.zeros_like(weight) for weight in weights))
    grad_totals, (results, grad_rows) = lax.scan(one_group, zero_grads, (residual_in.reshape(N_DP, CAP, D), cotangent.reshape(N_DP, CAP, D), lengths))
    return (results.reshape(TOKENS, D), grad_rows.reshape(TOKENS, D), grad_totals[0], grad_totals[1], grad_totals[2], grad_totals[3], grad_totals[4], grad_totals[5], grad_totals[6], grad_totals[7], grad_totals[8], grad_totals[9], grad_totals[10])
```

```python
import functools

import jax
import jax.numpy as jnp
from jax import lax
from jax.experimental import pallas as pl
from jax.experimental.pallas import tpu as pltpu
from jax.sharding import PartitionSpec as P

LAYERS = 2
EPSILON = 1e-05
LANES = 128
HALF = 64
F32 = jnp.float32
BF16 = jnp.bfloat16
EXACT = lax.Precision.HIGHEST


def dot(left, right, left_dim=1, right_dim=0, precision=None):
    return lax.dot_general(
        left,
        right,
        (((left_dim,), (right_dim,)), ((), ())),
        precision=precision,
        preferred_element_type=F32,
    )


def iota(shape, dim):
    return lax.broadcasted_iota(jnp.int32, shape, dim)


def sigmoid(values):
    return 1.0 / (1.0 + jnp.exp(-values))


def softplus(values):
    return jnp.maximum(values, 0.0) + jnp.log1p(jnp.exp(-jnp.abs(values)))


def rows_later(values, steps):
    return jnp.where(iota(values.shape, 0) >= steps, pltpu.roll(values, steps, 0), 0.0)


def rows_earlier(values, steps):
    total = values.shape[0]
    return jnp.where(
        iota(values.shape, 0) < total - steps, pltpu.roll(values, total - steps, 0), 0.0
    )


def conv(values, taps):
    result = taps[4:5, :] + taps[3:4, :] * values
    for offset in range(3):
        result = result + taps[offset : offset + 1, :] * rows_later(values, 3 - offset)
    return result


def conv_back(values, taps, grad):
    back = taps[3:4, :] * grad
    for offset in range(3):
        back = back + taps[offset : offset + 1, :] * rows_earlier(grad, 3 - offset)
    sums = [
        jnp.sum(grad * rows_later(values, 3 - offset), axis=0, keepdims=True)
        for offset in range(3)
    ]
    sums.append(jnp.sum(grad * values, axis=0, keepdims=True))
    sums.append(jnp.sum(grad, axis=0, keepdims=True))
    return back, sums


def pair_of_parts(column):
    high = column.astype(BF16).astype(F32)
    wide = jnp.broadcast_to(high, (column.shape[0], LANES))
    rest = jnp.broadcast_to(column - high, (column.shape[0], LANES))
    return jnp.where(iota(wide.shape, 1) < HALF, wide, rest).astype(BF16)


def joined_parts(message, width):
    return message[:, width : width + 1].astype(F32) + message[
        :, width + HALF : width + HALF + 1
    ].astype(F32)


def split_sum(values, spread):
    high = values.astype(BF16)
    rest = values - high.astype(F32)
    middle = rest.astype(BF16)
    low = (rest - middle.astype(F32)).astype(BF16)
    return dot(high, spread) + dot(middle, spread) + dot(low, spread)


def head_spread(inner, head_width):
    shape = (LANES, inner)
    return (iota(shape, 1) // head_width == iota(shape, 0)).astype(BF16)


def head_gather(inner, head_width):
    shape = (inner, LANES)
    return (iota(shape, 0) // head_width == iota(shape, 1)).astype(BF16)


def step_state(q_rows, dt_bias, a_log):
    rows = q_rows.shape[0]
    shifted = q_rows + dt_bias
    steps = softplus(shifted)
    rates = -jnp.exp(a_log)
    below = (iota((rows, rows), 0) >= iota((rows, rows), 1)).astype(F32)
    running = dot(below, steps * rates, precision=EXACT)
    return shifted, steps, rates, running


def mixer_forward(u_rows, bc_rows, q_rows, conv_x, conv_bc, dt_bias, a_log, skips, width):
    rows, inner = u_rows.shape
    states = bc_rows.shape[1] // 2
    mixed_in = conv(u_rows, conv_x)
    mixed_in = mixed_in * sigmoid(mixed_in)
    maps = conv(bc_rows, conv_bc)
    maps = maps * sigmoid(maps)
    _, steps, _, running = step_state(q_rows, dt_bias, a_log)
    turned = running.T
    scores = dot(maps[:, states:], maps[:, :states], 1, 1, EXACT)
    scaled = (mixed_in * split_sum(steps, head_spread(inner, width))).astype(BF16)
    causal = iota((rows, rows), 0) >= iota((rows, rows), 1)
    lane = iota((rows, LANES), 1)
    parts = []
    per_block = LANES // width
    for block in range(inner // LANES):
        block_in = scaled[:, block * LANES : (block + 1) * LANES]
        total = None
        for slot in range(per_block):
            head = block * per_block + slot
            gap = running[:, head : head + 1] - turned[head : head + 1, :]
            decay = jnp.exp(jnp.where(causal, gap, -1e30))
            part = dot((decay * scores).astype(BF16), block_in)
            total = part if slot == 0 else jnp.where(lane < slot * width, total, part)
        parts.append(total)
    return jnp.concatenate(parts, axis=1) + skips * mixed_in


def gather_rows(target, index, blocks, width):
    rows = blocks[0].shape[0]
    for order, block in enumerate(blocks):
        place = pl.multiple_of((index ^ order) * rows, rows)
        target[pl.ds(place, rows), :] = block[:, :width]


def unpack_kernel(heads, *refs):
    index = refs[0][0]
    outs = refs[-3 * LAYERS :]
    blocks = refs[1 : -3 * LAYERS]
    slab = blocks[0].shape[1]
    depth, wide = outs[LAYERS].shape[1], outs[2 * LAYERS].shape[1]
    piece = wide // len(blocks)

    def placed(start, stop, held, total):
        result = None
        for order, block in enumerate(blocks):
            shape = (held, total)
            ones = iota(shape, 1) - (index ^ order) * held == iota(shape, 0)
            part = dot(block[...][start:stop, :held], ones.astype(BF16))
            result = part if result is None else result + part
        return result

    norm_at = LAYERS * heads
    taps_at = norm_at + LAYERS
    rows = placed(0, taps_at, slab, depth)
    taps = placed(taps_at, taps_at + 5 * LAYERS, piece, wide)
    for layer in range(LAYERS):
        steps = rows[layer * heads : (layer + 1) * heads, :]
        padding = jnp.zeros((LANES - heads, depth), F32)
        outs[layer][...] = jnp.concatenate([steps, padding], axis=0).astype(BF16)
        outs[LAYERS + layer][...] = rows[norm_at + layer : norm_at + layer + 1, :]
        outs[2 * LAYERS + layer][...] = taps[5 * layer : 5 * layer + 5, :]


def first_kernel(fresh, shards, width, *refs):
    index = refs[0][0]
    blocks = refs[1 : 1 + shards]
    gain, w_in, w_dt, conv_x, conv_bc, dt_bias, a_log, skips = refs[1 + shards : 9 + shards]
    outs = refs[9 + shards :]
    normed, u_out, bc_out, q_out, y_out = outs[:5]
    depth = normed.shape[1]
    inner = u_out.shape[1]
    rows = blocks[0].shape[0]
    if fresh:
        for order, block in enumerate(blocks):
            values = block[...].astype(F32)
            scale = lax.rsqrt(jnp.mean(values * values, axis=1, keepdims=True) + EPSILON)
            place = pl.multiple_of((index ^ order) * rows, rows)
            normed[pl.ds(place, rows), :] = (values * scale * gain[...]).astype(BF16)
    else:
        gather_rows(normed, index, blocks, depth)
        for order, block in enumerate(blocks):
            place = pl.multiple_of((index ^ order) * rows, rows)
            outs[5][pl.ds(place, rows), :] = jnp.broadcast_to(
                joined_parts(block, depth), (rows, LANES)
            )
    rows_in = normed[...]
    u_rows = dot(rows_in, w_in[:, :inner])
    bc_rows = dot(rows_in, w_in[:, inner:])
    q_rows = dot(rows_in, w_dt[...], 1, 1)
    u_out[...] = u_rows
    bc_out[...] = bc_rows
    q_out[...] = q_rows
    y_out[...] = mixer_forward(
        u_rows,
        bc_rows,
        q_rows,
        conv_x[...],
        conv_bc[...],
        dt_bias[...],
        a_log[...],
        skips[...],
        width,
    )


def live_column(length, rows):
    return (iota((rows, 1), 0) < length).astype(F32)


def second_kernel(last, shards, *refs):
    index = refs[0][0]
    length = refs[1][0]
    normed, w_gate_out, y_rows, gate_gain = refs[2:6]
    refs = refs[6:]
    if last:
        blocks, refs = refs[:shards], refs[shards:]
    z_out = refs[0]
    messages = refs[1 : 1 + shards]
    rest = refs[1 + shards :]
    scratch = rest[-1]
    rows, inner = y_rows.shape
    depth = normed.shape[1]
    part = messages[0].shape[0]
    gate = dot(normed[...], w_gate_out[:, :inner])
    z_out[...] = gate
    gated = y_rows[...] * (gate * sigmoid(gate))
    squares = jnp.sum(gated * gated, axis=1, keepdims=True)
    live = live_column(length, rows)
    weighted = gated * gate_gain[...] * live
    hidden = weighted.astype(BF16)
    w_out = w_gate_out[:, inner:]
    scratch[:, :depth] = dot(hidden, w_out, 1, 1).astype(BF16)
    scratch[:, depth:] = pair_of_parts(squares)
    for order, message in enumerate(messages):
        place = pl.multiple_of((index ^ order) * part, part)
        message[...] = scratch[pl.ds(place, part), :]
    if last:
        grad_all, grad_hidden_out, sums_out = rest[:3]
        gather_rows(grad_all, index, blocks, depth)
        grad_hidden = dot(grad_all[...], w_out)
        grad_hidden_out[...] = grad_hidden
        products = jnp.sum(grad_hidden * weighted, axis=1, keepdims=True)
        lane = iota((rows, LANES), 1)
        table = jnp.where(lane == 0, squares, jnp.where(lane == 1, products, 0.0))
        sums_out[...] = table.T[:8, :]


def gate_back(length, scale, product, inner_all, y_rows, gate, grad_hidden, gate_gain):
    live = live_column(length, y_rows.shape[0])
    turn = sigmoid(gate)
    opened = gate * turn
    gated = y_rows * opened
    grad_live = grad_hidden * live
    grad_gain = jnp.sum(grad_live * gated * scale, axis=0, keepdims=True)
    grad_gated = scale * grad_live * gate_gain - gated * (
        scale * scale * scale * (product / inner_all)
    )
    hidden = (gated * scale * gate_gain * live).astype(BF16)
    grad_y = grad_gated * opened
    grad_gate = grad_gated * y_rows * (turn * (1.0 + gate * (1.0 - turn)))
    return hidden, grad_y, grad_gate.astype(BF16), grad_gain


def last_gate_kernel(shards, inner_all, *refs):
    length = refs[0][0]
    sums = refs[1 : 1 + shards]
    y_rows, gate, grad_hidden, gate_gain = refs[1 + shards : 5 + shards]
    hidden_out, grad_y_out, grad_gate_out, gain_out = refs[5 + shards :]
    rows = y_rows.shape[0]
    total = sums[0][...]
    for other in sums[1:]:
        total = total + other[...]
    table = jnp.concatenate([total, jnp.zeros((LANES - 8, rows), F32)], axis=0).T
    scale = lax.rsqrt(table[:, 0:1] / inner_all + EPSILON)
    hidden, grad_y, grad_gate, grad_gain = gate_back(
        length,
        scale,
        table[:, 1:2],
        inner_all,
        y_rows[...],
        gate[...],
        grad_hidden[...],
        gate_gain[...],
    )
    hidden_out[...] = hidden
    grad_y_out[...] = grad_y
    grad_gate_out[...] = grad_gate
    gain_out[...] = jnp.broadcast_to(grad_gain, gain_out.shape)


def gate_kernel(shards, inner_all, *refs):
    index = refs[0][0]
    length = refs[1][0]
    blocks = refs[2 : 2 + shards]
    scales, w_gate_out, y_rows, gate, gate_gain = refs[2 + shards : 7 + shards]
    grad_all, hidden_out, grad_y_out, grad_gate_out, gain_out, products = refs[7 + shards :]
    depth = grad_all.shape[1]
    inner = y_rows.shape[1]
    part = blocks[0].shape[0]
    gather_rows(grad_all, index, blocks, depth)
    for order, block in enumerate(blocks):
        place = pl.multiple_of((index ^ order) * part, part)
        products[pl.ds(place, part), :] = jnp.broadcast_to(
            joined_parts(block, depth), (part, LANES)
        )
    hidden, grad_y, grad_gate, grad_gain = gate_back(
        length,
        scales[:, 0:1],
        products[:, 0:1],
        inner_all,
        y_rows[...],
        gate[...],
        dot(grad_all[...], w_gate_out[:, inner:]),
        gate_gain[...],
    )
    hidden_out[...] = hidden
    grad_y_out[...] = grad_y
    grad_gate_out[...] = grad_gate
    gain_out[...] = jnp.broadcast_to(grad_gain, gain_out.shape)


def scan_back_kernel(width, *refs):
    (u_ref, bc_ref, q_ref, y_ref, grad_ref, conv_x, conv_bc, dt_bias, a_log, skips) = refs[:10]
    du_out, dbc_out, dq_out, sums_x, sums_bc = refs[10:]
    u_rows, bc_rows, q_rows = u_ref[...], bc_ref[...], q_ref[...]
    grad_y = grad_ref[...]
    rows, inner = u_rows.shape
    states = bc_rows.shape[1] // 2
    taps_x, taps_bc = conv_x[...], conv_bc[...]
    pre_x = conv(u_rows, taps_x)
    turn_x = sigmoid(pre_x)
    mixed_in = pre_x * turn_x
    pre_bc = conv(bc_rows, taps_bc)
    turn_bc = sigmoid(pre_bc)
    maps = pre_bc * turn_bc
    shifted, steps, rates, running = step_state(q_rows, dt_bias[...], a_log[...])
    turned = running.T
    b_rows, c_rows = maps[:, :states], maps[:, states:]
    scores = dot(b_rows, c_rows, 1, 1, EXACT)
    spread = head_spread(inner, width)
    steps_wide = split_sum(steps, spread)
    scaled = (mixed_in * steps_wide).astype(BF16)
    grad_low = grad_y.astype(BF16)
    causal = iota((rows, rows), 0) <= iota((rows, rows), 1)
    lane = iota((rows, LANES), 1)
    per_block = LANES // width
    grad_scores = jnp.zeros((rows, rows), F32)
    parts = []
    for block in range(inner // LANES):
        cut = slice(block * LANES, (block + 1) * LANES)
        block_in, block_grad = scaled[:, cut], grad_low[:, cut]
        total = None
        for slot in range(per_block):
            head = block * per_block + slot
            gap = turned[head : head + 1, :] - running[:, head : head + 1]
            decay = jnp.exp(jnp.where(causal, gap, -1e30))
            part = dot((decay * scores).astype(BF16), block_grad)
            total = part if slot == 0 else jnp.where(lane < slot * width, total, part)
            own = jnp.where(
                (lane >= slot * width) & (lane < (slot + 1) * width), block_in, jnp.zeros_like(block_in)
            )
            grad_scores = grad_scores + dot(own, block_grad, 1, 1) * decay
        parts.append(total)
    grad_scaled = jnp.concatenate(parts, axis=1)
    grad_b = dot(grad_scores, c_rows, precision=EXACT)
    grad_c = dot(grad_scores, b_rows, 0, 0, EXACT)
    gather = head_gather(inner, width)
    within = y_ref[...] - skips[...] * mixed_in
    grad_running = split_sum(
        grad_low.astype(F32) * within - scaled.astype(F32) * grad_scaled, gather
    )
    grad_steps = split_sum(mixed_in * grad_scaled, gather)
    above = (iota((rows, rows), 0) <= iota((rows, rows), 1)).astype(F32)
    grad_decay = dot(above, grad_running, precision=EXACT)
    grad_steps = grad_steps + grad_decay * rates
    grad_q = grad_steps * sigmoid(shifted)
    dq_out[...] = grad_q.astype(BF16)
    bias_sum = jnp.sum(grad_q, axis=0, keepdims=True)
    rate_sum = jnp.sum(grad_decay * steps, axis=0, keepdims=True) * rates
    skip_sum = split_sum(
        jnp.broadcast_to(jnp.sum(grad_y * mixed_in, axis=0, keepdims=True), (8, inner)), gather
    )[:1, :]
    grad_x = steps_wide * grad_scaled + skips[...] * grad_y
    grad_x = grad_x * (turn_x * (1.0 + pre_x * (1.0 - turn_x)))
    du, tap_sums = conv_back(u_rows, taps_x, grad_x)
    du_out[...] = du.astype(BF16)
    for order, row in enumerate(tap_sums):
        sums_x[order : order + 1, :] = row
    sums_x[5:8, :] = jnp.zeros((3, inner), F32)
    sums_x[6:7, :LANES] = bias_sum
    sums_x[6:7, LANES : 2 * LANES] = rate_sum
    sums_x[6:7, 2 * LANES : 3 * LANES] = skip_sum
    grad_bc = jnp.concatenate([grad_b, grad_c], axis=1)
    grad_bc = grad_bc * (turn_bc * (1.0 + pre_bc * (1.0 - turn_bc)))
    dbc, tap_sums = conv_back(bc_rows, taps_bc, grad_bc)
    dbc_out[...] = dbc.astype(BF16)
    sums_bc[...] = jnp.zeros(sums_bc.shape, F32)
    for order, row in enumerate(tap_sums):
        sums_bc[order : order + 1, :] = row


def early_grads_kernel(normed, grad_gate, grad_all, hidden, out):
    inner = hidden.shape[1]
    out[:, :inner] = dot(normed[...], grad_gate[...], 0, 0).astype(BF16)
    out[:, inner:] = dot(grad_all[...], hidden[...], 0, 0).astype(BF16)


def late_grads_kernel(normed, du, dbc, dq, out):
    inner, wide = du.shape[1], dbc.shape[1]
    rows_in = normed[...]
    out[:, :inner] = dot(rows_in, du[...], 0, 0).astype(BF16)
    out[:, inner : inner + wide] = dot(rows_in, dbc[...], 0, 0).astype(BF16)
    out[:, inner + wide :] = dot(rows_in, dq[...], 0, 0).astype(BF16)


def input_grad_kernel(shards, *refs):
    index = refs[0][0]
    grad_gate, du, dbc, dq, w_in, w_gate_out, w_dt = refs[1:8]
    outs = refs[8 : 8 + shards]
    scratch = refs[8 + shards]
    inner = du.shape[1]
    part = outs[0].shape[0]
    scratch[...] = (
        dot(grad_gate[...], w_gate_out[:, :inner], 1, 1)
        + dot(du[...], w_in[:, :inner], 1, 1)
        + dot(dbc[...], w_in[:, inner:], 1, 1)
        + dot(dq[...], w_dt[...])
    ).astype(BF16)
    for order, out in enumerate(outs):
        place = pl.multiple_of((index ^ order) * part, part)
        out[...] = scratch[pl.ds(place, part), :]


def branch_total(messages, depth, inner_all):
    total = messages[0][:, :depth].astype(F32)
    squares = joined_parts(messages[0], depth)
    for other in messages[1:]:
        total = total + other[:, :depth].astype(F32)
        squares = squares + joined_parts(other, depth)
    return total, lax.rsqrt(squares / inner_all + EPSILON)


def residual_kernel(shards, inner_all, *refs):
    messages = refs[:shards]
    start, gain, current_out, branch_out, message_out = refs[shards:]
    depth = start.shape[1]
    branch, scale = branch_total(messages, depth, inner_all)
    current = start[...].astype(F32) + scale * branch
    current_out[...] = current
    branch_out[...] = branch
    norm = lax.rsqrt(jnp.mean(current * current, axis=1, keepdims=True) + EPSILON)
    message_out[:, :depth] = (current * norm * gain[...]).astype(BF16)
    message_out[:, depth:] = pair_of_parts(scale)


def output_kernel(shards, inner_all, *refs):
    messages = refs[:shards]
    start, out = refs[shards:]
    branch, scale = branch_total(messages, start.shape[1], inner_all)
    out[...] = start[...] + scale * branch


def norm_back_kernel(shards, last, *refs):
    blocks = refs[:shards]
    refs = refs[shards:]
    rows_in, gain, grad_in = refs[:3]
    current = rows_in[...].astype(F32)
    depth = current.shape[1]
    grad_normed = blocks[0][...].astype(F32)
    for other in blocks[1:]:
        grad_normed = grad_normed + other[...].astype(F32)
    norm = lax.rsqrt(jnp.mean(current * current, axis=1, keepdims=True) + EPSILON)
    weighted = grad_normed * gain[...]
    inner_product = jnp.mean(weighted * current, axis=1, keepdims=True)
    grad = grad_in[...].astype(F32) + norm * weighted - current * (norm * norm * norm * inner_product)
    gain_row = jnp.sum(grad_normed * current * norm, axis=0, keepdims=True)
    if last:
        branch, grad_out, gain_out, message_out = refs[3:]
        low = grad.astype(BF16)
        message_out[:, :depth] = low
        message_out[:, depth:] = pair_of_parts(
            jnp.sum(low.astype(F32) * branch[...], axis=1, keepdims=True)
        )
    else:
        grad_out, gain_out = refs[3:]
    grad_out[...] = grad
    gain_out[...] = jnp.broadcast_to(gain_row, gain_out.shape)


def call(kernel, name, scalars, arrays, outs, flops=0, scratch=()):
    held = sum(a.size * a.dtype.itemsize for a in arrays)
    held += sum(int(jnp.dtype(d).itemsize) * functools.reduce(lambda a, b: a * b, s) for s, d in outs)
    return pl.pallas_call(
        kernel,
        out_shape=tuple(jax.ShapeDtypeStruct(s, d) for s, d in outs),
        in_specs=[pl.BlockSpec(memory_space=pltpu.SMEM)] * len(scalars)
        + [pl.BlockSpec(memory_space=pltpu.VMEM)] * len(arrays),
        out_specs=tuple(pl.BlockSpec(memory_space=pltpu.VMEM) for _ in outs),
        scratch_shapes=list(scratch),
        compiler_params=pltpu.CompilerParams(vmem_limit_bytes=48 * 1024 * 1024),
        cost_estimate=pl.CostEstimate(flops=int(flops), bytes_accessed=int(held), transcendentals=0),
        name=name,
    )(*scalars, *arrays)


def exchange(blocks, axis):
    count = lax.axis_size(axis)
    return [blocks[0]] + [
        lax.ppermute(blocks[k], axis, [(i, i ^ k) for i in range(count)]) for k in range(1, count)
    ]


def spread_out(block, axis):
    return exchange([block] * lax.axis_size(axis), axis)


def sum_over_dp(values):
    count = lax.axis_size("dp")
    values = values + lax.ppermute(values, "dp", [(i, i ^ 1) for i in range(count)])
    others = [
        lax.ppermute(values, "dp", [(i, i ^ k) for i in range(count)]) for k in range(2, count, 2)
    ]
    for other in others:
        values = values + other
    return values


def body(
    residual_in,
    norm_gain,
    w_zx,
    w_bc,
    w_dt,
    conv_x,
    conv_bc,
    dt_bias,
    a_log,
    d_skip,
    gate_gain,
    w_out,
    lengths,
    cotangent,
):
    shards = lax.axis_size("tensor")
    dp_count = lax.axis_size("dp")
    rows, depth = residual_in.shape
    inner = gate_gain.shape[1]
    heads = dt_bias.shape[1]
    width = inner // heads
    wide = w_bc.shape[2]
    total_rows = rows * shards
    inner_all = inner * shards
    slab = norm_gain.shape[1]
    index = lax.axis_index("tensor").reshape(1).astype(jnp.int32)
    message = (rows, depth + LANES)

    residual_blocks = spread_out(residual_in, "tensor")
    late_blocks = spread_out(cotangent, "tensor")
    w_first, w_second = [], []
    for layer in range(LAYERS):
        packed = jnp.concatenate([w_zx[layer, :, 1, :], w_bc[layer]], axis=1)
        w_first.append(lax.all_gather(packed, "dp", axis=0, tiled=True))
        packed = jnp.concatenate([w_zx[layer, :, 0, :], w_out[layer].T], axis=1)
        w_second.append(lax.all_gather(packed, "dp", axis=0, tiled=True))
    few = jnp.concatenate(
        [
            w_dt.transpose(0, 2, 1).reshape(LAYERS * heads, slab),
            norm_gain,
            jnp.pad(conv_bc.reshape(LAYERS * 5, -1), ((0, 0), (0, slab - wide // dp_count))),
        ],
        axis=0,
    )
    few = jnp.pad(few, ((0, -few.shape[0] % 16), (0, 0)))
    few = call(
        functools.partial(unpack_kernel, heads),
        "unpack",
        [lax.axis_index("dp").reshape(1).astype(jnp.int32)],
        spread_out(few, "dp"),
        [((LANES, depth), BF16)] * LAYERS + [((1, depth), F32)] * LAYERS + [((5, wide), F32)] * LAYERS,
    )
    w_steps, gains, taps_bc = few[:LAYERS], few[LAYERS : 2 * LAYERS], few[2 * LAYERS :]
    bias = jnp.pad(dt_bias, ((0, 0), (0, LANES - heads)))[:, None, :]
    rates = jnp.pad(a_log, ((0, 0), (0, LANES - heads)))[:, None, :]
    skips = jnp.repeat(d_skip, width, axis=1)[:, None, :]

    flops = 2 * total_rows * depth * inner
    kept = []
    blocks = residual_blocks
    scales = None
    current = residual_in
    for layer in range(LAYERS):
        last = layer == LAYERS - 1
        outs = [
            ((total_rows, depth), BF16),
            ((total_rows, inner), F32),
            ((total_rows, wide), F32),
            ((total_rows, LANES), F32),
            ((total_rows, inner), F32),
        ]
        if layer:
            outs.append(((total_rows, LANES), F32))
        first = call(
            functools.partial(first_kernel, layer == 0, shards, width),
            f"mix_{layer}",
            [index],
            [*blocks, gains[layer], w_first[layer], w_steps[layer], conv_x[layer], taps_bc[layer], bias[layer], rates[layer], skips[layer]],
            outs,
            flops * 3,
        )
        normed, u_rows, bc_rows, q_rows, y_rows = first[:5]
        if layer:
            scales = first[5]
        outs = [((total_rows, inner), F32)] + [(message, BF16)] * shards
        arrays = [normed, w_second[layer], y_rows, gate_gain[layer][None]]
        if last:
            arrays += late_blocks
            outs += [((total_rows, depth), BF16), ((total_rows, inner), F32), ((8, total_rows), F32)]
        second = call(
            functools.partial(second_kernel, last, shards),
            f"gate_{layer}",
            [index, lengths],
            arrays,
            outs,
            flops * (3 if last else 2),
            [pltpu.VMEM((total_rows, depth + LANES), BF16)],
        )
        gate = second[0]
        sent = exchange(second[1 : 1 + shards], "tensor")
        kept.append([normed, u_rows, bc_rows, q_rows, y_rows, gate, current])
        if last:
            sums = spread_out(second[3 + shards], "tensor")
            grad_all, grad_hidden = second[1 + shards : 3 + shards]
            (output,) = call(
                functools.partial(output_kernel, shards, inner_all),
                "output",
                [],
                [*sent, current],
                [((rows, depth), F32)],
            )
        else:
            current, branch, packed = call(
                functools.partial(residual_kernel, shards, inner_all),
                f"residual_{layer}",
                [],
                [*sent, current, gains[layer + 1]],
                [((rows, depth), F32), ((rows, depth), F32), (message, BF16)],
            )
            blocks = spread_out(packed, "tensor")

    grad_now = cotangent
    early, late, few_x, few_bc, few_gain = {}, {}, {}, {}, {}
    for layer in reversed(range(LAYERS)):
        last = layer == LAYERS - 1
        normed, u_rows, bc_rows, q_rows, y_rows, gate, rows_in = kept[layer]
        outs = [
            ((total_rows, inner), BF16),
            ((total_rows, inner), F32),
            ((total_rows, inner), BF16),
            ((8, inner), F32),
        ]
        if last:
            hidden, grad_y, grad_gate, gain_sum = call(
                functools.partial(last_gate_kernel, shards, inner_all),
                f"gate_back_{layer}",
                [lengths],
                [*sums, y_rows, gate, grad_hidden, gate_gain[layer][None]],
                outs,
            )
        else:
            grad_all, hidden, grad_y, grad_gate, gain_sum = call(
                functools.partial(gate_kernel, shards, inner_all),
                f"gate_back_{layer}",
                [index, lengths],
                [*blocks, scales, w_second[layer], y_rows, gate, gate_gain[layer][None]],
                [((total_rows, depth), BF16)] + outs,
                flops,
                [pltpu.VMEM((total_rows, LANES), F32)],
            )
        (grads,) = call(
            early_grads_kernel,
            f"early_{layer}",
            [],
            [normed, grad_gate, grad_all, hidden],
            [((depth, 2 * inner), BF16)],
            flops * 2,
        )
        grads, grad_y = lax.optimization_barrier((grads, grad_y))
        early[layer] = lax.psum_scatter(grads, "dp", scatter_dimension=0, tiled=True)
        du, dbc, dq, sums_x, sums_bc = call(
            functools.partial(scan_back_kernel, width),
            f"mix_back_{layer}",
            [],
            [u_rows, bc_rows, q_rows, y_rows, grad_y, conv_x[layer], taps_bc[layer], bias[layer], rates[layer], skips[layer]],
            [
                ((total_rows, inner), BF16),
                ((total_rows, wide), BF16),
                ((total_rows, LANES), BF16),
                ((8, inner), F32),
                ((8, wide), F32),
            ],
            flops * 2,
        )
        few_x[layer] = sums_x.at[5].set(gain_sum[0])
        few_bc[layer] = sums_bc
        pieces = call(
            functools.partial(input_grad_kernel, shards),
            f"input_grad_{layer}",
            [index],
            [grad_gate, du, dbc, dq, w_first[layer], w_second[layer], w_steps[layer]],
            [((rows, depth), BF16)] * shards,
            flops * 2,
            [pltpu.VMEM((total_rows, depth), BF16)],
        )
        pieces = exchange(pieces, "tensor")
        (grads,) = call(
            late_grads_kernel,
            f"late_{layer}",
            [],
            [normed, du, dbc, dq],
            [((depth, inner + wide + LANES), BF16)],
            flops * 2,
        )
        late[layer] = lax.psum_scatter(grads, "dp", scatter_dimension=0, tiled=True)
        arrays = [*pieces, rows_in, gains[layer], grad_now]
        outs = [((rows, depth), F32), ((8, depth), F32)]
        if layer:
            arrays.append(branch)
            outs.append((message, BF16))
        back = call(
            functools.partial(norm_back_kernel, shards, bool(layer)),
            f"norm_back_{layer}",
            [],
            arrays,
            outs,
        )
        grad_now, few_gain[layer] = back[:2]
        if layer:
            blocks = spread_out(back[2], "tensor")

    order = range(LAYERS)
    shared = jnp.stack(
        [
            jnp.concatenate([few_gain[layer][0], few_bc[layer][:5].reshape(-1)])
            for layer in order
        ]
    )
    shared = functools.reduce(jnp.add, spread_out(shared, "tensor"))
    own = jnp.stack([few_x[layer] for layer in order]).reshape(-1, LANES)
    few = jnp.concatenate([own, shared.reshape(-1, LANES)], axis=0)
    few = sum_over_dp(few)
    own = few[: own.shape[0]].reshape(LAYERS, 8, inner)
    shared = few[own.size // LANES :].reshape(LAYERS, -1)
    place = lax.axis_index("dp")
    grad_gain = lax.dynamic_slice_in_dim(shared[:, :depth], place * slab, slab, 1)
    grad_conv_bc = lax.dynamic_slice_in_dim(
        shared[:, depth:].reshape(LAYERS, 5, wide), place * (wide // dp_count), wide // dp_count, 2
    )
    grad_bc = jnp.stack([late[layer][:, inner : inner + wide] for layer in order])
    grad_bc = functools.reduce(
        jnp.add, [part.astype(F32) for part in spread_out(grad_bc, "tensor")]
    )
    grad_zx = jnp.stack(
        [jnp.stack([early[layer][:, :inner], late[layer][:, :inner]], axis=1) for layer in order]
    ).astype(F32)
    grad_dt = jnp.stack(
        [late[layer][:, inner + wide : inner + wide + heads] for layer in order]
    ).astype(F32)
    grad_out = jnp.stack([early[layer][:, inner:].T for layer in order]).astype(F32)
    return (
        output,
        grad_now,
        grad_gain,
        grad_zx,
        grad_bc,
        grad_dt,
        own[:, :5],
        grad_conv_bc,
        own[:, 6, :heads],
        own[:, 6, LANES : LANES + heads],
        own[:, 6, 2 * LANES : 2 * LANES + heads],
        own[:, 5],
        grad_out,
    )


def solution(mesh):
    return jax.shard_map(
        body,
        mesh=mesh,
        in_specs=(
            P(("dp", "tensor"), None),
            P(None, "dp"),
            P(None, "dp", None, "tensor"),
            P(None, "dp", None),
            P(None, "dp", "tensor"),
            P(None, None, "tensor"),
            P(None, None, "dp"),
            P(None, "tensor"),
            P(None, "tensor"),
            P(None, "tensor"),
            P(None, "tensor"),
            P(None, "tensor", "dp"),
            P("dp"),
            P(("dp", "tensor"), None),
        ),
        out_specs=(
            P(("dp", "tensor"), None),
            P(("dp", "tensor"), None),
            P(None, "dp"),
            P(None, "dp", None, "tensor"),
            P(None, "dp", None),
            P(None, "dp", "tensor"),
            P(None, None, "tensor"),
            P(None, None, "dp"),
            P(None, "tensor"),
            P(None, "tensor"),
            P(None, "tensor"),
            P(None, "tensor"),
            P(None, "tensor", "dp"),
        ),
        check_vma=False,
    )
```

```python
import functools
import math

import jax
import jax.numpy as jnp
from jax import lax
from jax.experimental import pallas as pl
from jax.experimental.pallas import tpu as pltpu
from jax.sharding import PartitionSpec as P

LAYERS = 2
EPSILON = 1e-05
LANES = 128
HALF = 64
F32 = jnp.float32
BF16 = jnp.bfloat16
EXACT = lax.Precision.HIGHEST


def dot(left, right, left_dim=1, right_dim=0, precision=None):
    return lax.dot_general(
        left,
        right,
        (((left_dim,), (right_dim,)), ((), ())),
        precision=precision,
        preferred_element_type=F32,
    )


def iota(shape, dim):
    return lax.broadcasted_iota(jnp.int32, shape, dim)


def sigmoid(values):
    return 1.0 / (1.0 + jnp.exp(-values))


def softplus(values):
    return jnp.maximum(values, 0.0) + jnp.log1p(jnp.exp(-jnp.abs(values)))


def rows_later(values, steps):
    return jnp.where(iota(values.shape, 0) >= steps, pltpu.roll(values, steps, 0), 0.0)


def rows_earlier(values, steps):
    total = values.shape[0]
    return jnp.where(
        iota(values.shape, 0) < total - steps, pltpu.roll(values, total - steps, 0), 0.0
    )


def conv(values, taps):
    result = taps[4:5, :] + taps[3:4, :] * values
    for offset in range(3):
        result = result + taps[offset : offset + 1, :] * rows_later(values, 3 - offset)
    return result


def conv_back(values, taps, grad):
    back = taps[3:4, :] * grad
    for offset in range(3):
        back = back + taps[offset : offset + 1, :] * rows_earlier(grad, 3 - offset)
    sums = [
        jnp.sum(grad * rows_later(values, 3 - offset), axis=0, keepdims=True)
        for offset in range(3)
    ]
    sums.append(jnp.sum(grad * values, axis=0, keepdims=True))
    sums.append(jnp.sum(grad, axis=0, keepdims=True))
    return back, sums


def pair_of_parts(column):
    high = column.astype(BF16).astype(F32)
    wide = jnp.broadcast_to(high, (column.shape[0], LANES))
    rest = jnp.broadcast_to(column - high, (column.shape[0], LANES))
    return jnp.where(iota(wide.shape, 1) < HALF, wide, rest).astype(BF16)


def joined_parts(message, width):
    return message[:, width : width + 1].astype(F32) + message[
        :, width + HALF : width + HALF + 1
    ].astype(F32)


def split_sum(values, spread):
    high = values.astype(BF16)
    rest = values - high.astype(F32)
    middle = rest.astype(BF16)
    low = (rest - middle.astype(F32)).astype(BF16)
    return dot(high, spread) + dot(middle, spread) + dot(low, spread)


def head_spread(inner, head_width):
    shape = (LANES, inner)
    return (iota(shape, 1) // head_width == iota(shape, 0)).astype(BF16)


def head_gather(inner, head_width):
    shape = (inner, LANES)
    return (iota(shape, 0) // head_width == iota(shape, 1)).astype(BF16)


def step_state(q_rows, dt_bias, a_log):
    rows = q_rows.shape[0]
    shifted = q_rows + dt_bias
    steps = softplus(shifted)
    rates = -jnp.exp(a_log)
    below = (iota((rows, rows), 0) >= iota((rows, rows), 1)).astype(F32)
    running = dot(below, steps * rates, precision=EXACT)
    return shifted, steps, rates, running


def mixer_forward(u_rows, bc_rows, q_rows, conv_x, conv_bc, dt_bias, a_log, skips, width):
    rows, inner = u_rows.shape
    states = bc_rows.shape[1] // 2
    mixed_in = conv(u_rows, conv_x)
    mixed_in = mixed_in * sigmoid(mixed_in)
    maps = conv(bc_rows, conv_bc)
    maps = maps * sigmoid(maps)
    _, steps, _, running = step_state(q_rows, dt_bias, a_log)
    turned = running.T
    scores = dot(maps[:, states:], maps[:, :states], 1, 1, EXACT)
    scaled = (mixed_in * split_sum(steps, head_spread(inner, width))).astype(BF16)
    causal = iota((rows, rows), 0) >= iota((rows, rows), 1)
    lane = iota((rows, LANES), 1)
    parts = []
    per_block = LANES // width
    for block in range(inner // LANES):
        block_in = scaled[:, block * LANES : (block + 1) * LANES]
        total = None
        for slot in range(per_block):
            head = block * per_block + slot
            gap = running[:, head : head + 1] - turned[head : head + 1, :]
            decay = jnp.exp(jnp.where(causal, gap, -1e30))
            part = dot((decay * scores).astype(BF16), block_in)
            total = part if slot == 0 else jnp.where(lane < slot * width, total, part)
        parts.append(total)
    return jnp.concatenate(parts, axis=1) + skips * mixed_in


def gather_rows(target, index, blocks, width):
    rows = blocks[0].shape[0]
    for order, block in enumerate(blocks):
        place = pl.multiple_of((index ^ order) * rows, rows)
        target[pl.ds(place, rows), :] = block[:, :width]


def unpack_kernel(heads, *refs):
    index = refs[0][0]
    outs = refs[-3 * LAYERS :]
    blocks = refs[1 : -3 * LAYERS]
    slab = blocks[0].shape[1]
    depth, wide = outs[LAYERS].shape[1], outs[2 * LAYERS].shape[1]
    piece = wide // len(blocks)

    def placed(start, stop, held, total):
        result = None
        for order, block in enumerate(blocks):
            shape = (held, total)
            ones = iota(shape, 1) - (index ^ order) * held == iota(shape, 0)
            part = dot(block[...][start:stop, :held], ones.astype(BF16))
            result = part if result is None else result + part
        return result

    norm_at = LAYERS * heads
    taps_at = norm_at + LAYERS
    rows = placed(0, taps_at, slab, depth)
    taps = placed(taps_at, taps_at + 5 * LAYERS, piece, wide)
    for layer in range(LAYERS):
        steps = rows[layer * heads : (layer + 1) * heads, :]
        padding = jnp.zeros((LANES - heads, depth), F32)
        outs[layer][...] = jnp.concatenate([steps, padding], axis=0).astype(BF16)
        outs[LAYERS + layer][...] = rows[norm_at + layer : norm_at + layer + 1, :]
        outs[2 * LAYERS + layer][...] = taps[5 * layer : 5 * layer + 5, :]


def pack_kernel(index, *refs):
    blocks, (out,) = refs[:-1], refs[-1:]
    gather_rows(out, index[0], blocks, out.shape[1])


def unpack_maps_kernel(index, *refs):
    blocks, outs = refs[:-LAYERS], refs[-LAYERS:]
    piece = blocks[0].shape[1] // LAYERS
    for layer, out in enumerate(outs):
        total = None
        for order, block in enumerate(blocks):
            shape = (LAYERS * piece, out.shape[1])
            row = iota(shape, 0) - layer * piece
            ones = (row == iota(shape, 1) - (index[0] ^ order) * piece) & (row >= 0) & (row < piece)
            part = dot(block[...], ones.astype(BF16))
            total = part if total is None else total + part
        out[...] = total.astype(BF16)


def first_kernel(layer, shards, width, *refs):
    index = refs[0][0]
    blocks, refs = refs[1 : 1 + shards], refs[1 + shards :]
    w_in, w_bc, gain, w_dt, conv_x, conv_bc, dt_bias, a_log, skips = refs[:9]
    outs = refs[9:]
    normed, u_out, bc_out, q_out, y_out = outs[:5]
    depth = normed.shape[1]
    inner = u_out.shape[1]
    rows = blocks[0].shape[0]
    if layer == 0:
        for order, block in enumerate(blocks):
            values = block[...].astype(F32)
            scale = lax.rsqrt(jnp.mean(values * values, axis=1, keepdims=True) + EPSILON)
            place = pl.multiple_of((index ^ order) * rows, rows)
            normed[pl.ds(place, rows), :] = (values * scale * gain[...]).astype(BF16)
    else:
        gather_rows(normed, index, blocks, depth)
        for order, block in enumerate(blocks):
            place = pl.multiple_of((index ^ order) * rows, rows)
            outs[5][pl.ds(place, rows), :] = jnp.broadcast_to(
                joined_parts(block, depth), (rows, LANES)
            )
    rows_in = normed[...]
    u_rows = dot(rows_in, w_in[...])
    bc_rows = dot(rows_in, w_bc[...])
    q_rows = dot(rows_in, w_dt[...], 1, 1)
    u_out[...] = u_rows
    bc_out[...] = bc_rows
    q_out[...] = q_rows
    y_out[...] = mixer_forward(
        u_rows,
        bc_rows,
        q_rows,
        conv_x[...],
        conv_bc[...],
        dt_bias[...],
        a_log[...],
        skips[...],
        width,
    )


def live_column(length, rows):
    return (iota((rows, 1), 0) < length).astype(F32)


def second_kernel(shards, *refs):
    index = refs[0][0]
    length = refs[1][0]
    normed, w_gate, w_out, y_rows, gate_gain, z_out = refs[2:8]
    messages, scratch = refs[8 : 8 + shards], refs[8 + shards]
    depth = normed.shape[1]
    part = messages[0].shape[0]
    gate = dot(normed[...], w_gate[...])
    z_out[...] = gate
    gated = y_rows[...] * (gate * sigmoid(gate))
    live = live_column(length, y_rows.shape[0])
    hidden = (gated * gate_gain[...] * live).astype(BF16)
    scratch[:, :depth] = dot(hidden, w_out[...], 1, 1).astype(BF16)
    scratch[:, depth:] = pair_of_parts(jnp.sum(gated * gated, axis=1, keepdims=True))
    for order, message in enumerate(messages):
        place = pl.multiple_of((index ^ order) * part, part)
        message[...] = scratch[pl.ds(place, part), :]


def last_second_kernel(shards, *refs):
    index = refs[0][0]
    length = refs[1][0]
    blocks, refs = refs[2 : 2 + shards], refs[2 + shards :]
    normed, w_gate, w_out, y_rows, gate_gain, z_out, hidden_out, grad_all, grad_hidden_out, sums_out = refs
    rows = y_rows.shape[0]
    gather_rows(grad_all, index, blocks, normed.shape[1])
    gate = dot(normed[...], w_gate[...])
    z_out[...] = gate
    gated = y_rows[...] * (gate * sigmoid(gate))
    squares = jnp.sum(gated * gated, axis=1, keepdims=True)
    weighted = gated * gate_gain[...] * live_column(length, rows)
    hidden_out[...] = weighted.astype(BF16)
    grad_hidden = dot(grad_all[...], w_out[...])
    grad_hidden_out[...] = grad_hidden
    products = jnp.sum(grad_hidden * weighted, axis=1, keepdims=True)
    lane = iota((rows, LANES), 1)
    table = jnp.where(lane == 0, squares, jnp.where(lane == 1, products, 0.0))
    sums_out[...] = table.T[:8, :]


def branch_kernel(shards, *refs):
    index = refs[0][0]
    hidden, w_out, scales = refs[1:4]
    messages, scratch = refs[4 : 4 + shards], refs[4 + shards]
    part = messages[0].shape[0]
    scratch[...] = (scales[:, 0:1] * dot(hidden[...], w_out[...], 1, 1)).astype(BF16)
    for order, message in enumerate(messages):
        place = pl.multiple_of((index ^ order) * part, part)
        message[...] = scratch[pl.ds(place, part), :]


def gate_back(length, scale, product, inner_all, y_rows, gate, grad_hidden, gate_gain):
    live = live_column(length, y_rows.shape[0])
    turn = sigmoid(gate)
    opened = gate * turn
    gated = y_rows * opened
    grad_live = grad_hidden * live
    grad_gain = jnp.sum(grad_live * gated * scale, axis=0, keepdims=True)
    grad_gated = scale * grad_live * gate_gain - gated * (
        scale * scale * scale * (product / inner_all)
    )
    hidden = (gated * scale * gate_gain * live).astype(BF16)
    grad_y = grad_gated * opened
    grad_gate = grad_gated * y_rows * (turn * (1.0 + gate * (1.0 - turn)))
    return hidden, grad_y, grad_gate.astype(BF16), grad_gain


def early_grads(normed, grad_all, hidden, grad_gate, out):
    inner = hidden.shape[1]
    out[:, :inner] = dot(normed[...], grad_gate, 0, 0).astype(BF16)
    out[:, inner:] = dot(grad_all[...], hidden, 0, 0).astype(BF16)


def last_gate_kernel(shards, inner_all, *refs):
    length = refs[0][0]
    sums, refs = refs[1 : 1 + shards], refs[1 + shards :]
    y_rows, gate, grad_hidden, gate_gain, normed, grad_all = refs[:6]
    grad_y_out, grad_gate_out, gain_out, grads_out, scale_out = refs[6:]
    rows = y_rows.shape[0]
    total = sums[0][...]
    for other in sums[1:]:
        total = total + other[...]
    table = jnp.concatenate([total, jnp.zeros((LANES - 8, rows), F32)], axis=0).T
    scale = lax.rsqrt(table[:, 0:1] / inner_all + EPSILON)
    scale_out[...] = jnp.broadcast_to(scale, scale_out.shape)
    hidden, grad_y, grad_gate, grad_gain = gate_back(
        length,
        scale,
        table[:, 1:2],
        inner_all,
        y_rows[...],
        gate[...],
        grad_hidden[...],
        gate_gain[...],
    )
    grad_y_out[...] = grad_y
    grad_gate_out[...] = grad_gate
    gain_out[...] = jnp.broadcast_to(grad_gain, gain_out.shape)
    early_grads(normed, grad_all, hidden, grad_gate, grads_out)


def gate_kernel(shards, inner_all, *refs):
    index = refs[0][0]
    length = refs[1][0]
    blocks, refs = refs[2 : 2 + shards], refs[2 + shards :]
    scales, w_out, y_rows, gate, gate_gain, normed = refs[:6]
    grad_y_out, grad_gate_out, gain_out, grads_out, grad_all, products = refs[6:]
    depth = grad_all.shape[1]
    part = blocks[0].shape[0]
    gather_rows(grad_all, index, blocks, depth)
    for order, block in enumerate(blocks):
        place = pl.multiple_of((index ^ order) * part, part)
        products[pl.ds(place, part), :] = jnp.broadcast_to(
            joined_parts(block, depth), (part, LANES)
        )
    hidden, grad_y, grad_gate, grad_gain = gate_back(
        length,
        scales[:, 0:1],
        products[:, 0:1],
        inner_all,
        y_rows[...],
        gate[...],
        dot(grad_all[...], w_out[...]),
        gate_gain[...],
    )
    grad_y_out[...] = grad_y
    grad_gate_out[...] = grad_gate
    gain_out[...] = jnp.broadcast_to(grad_gain, gain_out.shape)
    early_grads(normed, grad_all, hidden, grad_gate, grads_out)


def scan_back_kernel(width, index, *refs):
    (u_ref, bc_ref, q_ref, y_ref, grad_ref, conv_x, conv_bc, dt_bias, a_log, skips) = refs[:10]
    du_out, dbc_out, dq_out, sums_x, sums_bc = refs[10:15]
    pieces = refs[15:]
    u_rows, bc_rows, q_rows = u_ref[...], bc_ref[...], q_ref[...]
    grad_y = grad_ref[...]
    rows, inner = u_rows.shape
    states = bc_rows.shape[1] // 2
    taps_x, taps_bc = conv_x[...], conv_bc[...]
    pre_x = conv(u_rows, taps_x)
    turn_x = sigmoid(pre_x)
    mixed_in = pre_x * turn_x
    pre_bc = conv(bc_rows, taps_bc)
    turn_bc = sigmoid(pre_bc)
    maps = pre_bc * turn_bc
    shifted, steps, rates, running = step_state(q_rows, dt_bias[...], a_log[...])
    turned = running.T
    b_rows, c_rows = maps[:, :states], maps[:, states:]
    scores = dot(b_rows, c_rows, 1, 1, EXACT)
    spread = head_spread(inner, width)
    steps_wide = split_sum(steps, spread)
    scaled = (mixed_in * steps_wide).astype(BF16)
    grad_low = grad_y.astype(BF16)
    causal = iota((rows, rows), 0) <= iota((rows, rows), 1)
    lane = iota((rows, LANES), 1)
    per_block = LANES // width
    grad_scores = jnp.zeros((rows, rows), F32)
    parts = []
    for block in range(inner // LANES):
        cut = slice(block * LANES, (block + 1) * LANES)
        block_in, block_grad = scaled[:, cut], grad_low[:, cut]
        total = None
        for slot in range(per_block):
            head = block * per_block + slot
            gap = turned[head : head + 1, :] - running[:, head : head + 1]
            decay = jnp.exp(jnp.where(causal, gap, -1e30))
            part = dot((decay * scores).astype(BF16), block_grad)
            total = part if slot == 0 else jnp.where(lane < slot * width, total, part)
            own = jnp.where(
                (lane >= slot * width) & (lane < (slot + 1) * width), block_in, jnp.zeros_like(block_in)
            )
            grad_scores = grad_scores + dot(own, block_grad, 1, 1) * decay
        parts.append(total)
    grad_scaled = jnp.concatenate(parts, axis=1)
    grad_b = dot(grad_scores, c_rows, precision=EXACT)
    grad_c = dot(grad_scores, b_rows, 0, 0, EXACT)
    gather = head_gather(inner, width)
    within = y_ref[...] - skips[...] * mixed_in
    grad_running = split_sum(
        grad_low.astype(F32) * within - scaled.astype(F32) * grad_scaled, gather
    )
    grad_steps = split_sum(mixed_in * grad_scaled, gather)
    above = (iota((rows, rows), 0) <= iota((rows, rows), 1)).astype(F32)
    grad_decay = dot(above, grad_running, precision=EXACT)
    grad_steps = grad_steps + grad_decay * rates
    grad_q = grad_steps * sigmoid(shifted)
    dq_out[...] = grad_q.astype(BF16)
    bias_sum = jnp.sum(grad_q, axis=0, keepdims=True)
    rate_sum = jnp.sum(grad_decay * steps, axis=0, keepdims=True) * rates
    skip_sum = split_sum(
        jnp.broadcast_to(jnp.sum(grad_y * mixed_in, axis=0, keepdims=True), (8, inner)), gather
    )[:1, :]
    grad_x = steps_wide * grad_scaled + skips[...] * grad_y
    grad_x = grad_x * (turn_x * (1.0 + pre_x * (1.0 - turn_x)))
    du, tap_sums = conv_back(u_rows, taps_x, grad_x)
    du_out[...] = du.astype(BF16)
    for order, row in enumerate(tap_sums):
        sums_x[order : order + 1, :] = row
    sums_x[5:8, :] = jnp.zeros((3, inner), F32)
    sums_x[6:7, :LANES] = bias_sum
    sums_x[6:7, LANES : 2 * LANES] = rate_sum
    sums_x[6:7, 2 * LANES : 3 * LANES] = skip_sum
    grad_bc = jnp.concatenate([grad_b, grad_c], axis=1)
    grad_bc = grad_bc * (turn_bc * (1.0 + pre_bc * (1.0 - turn_bc)))
    dbc, tap_sums = conv_back(bc_rows, taps_bc, grad_bc)
    low = dbc.astype(BF16)
    dbc_out[...] = low
    piece = low.shape[1] // len(pieces)
    for order, out in enumerate(pieces):
        shape = (low.shape[1], LANES)
        ones = iota(shape, 0) - (index[0] ^ order) * piece == iota(shape, 1)
        ones = ones & (iota(shape, 1) < piece)
        out[...] = dot(low, ones.astype(BF16)).astype(BF16)
    sums_bc[...] = jnp.zeros(sums_bc.shape, F32)
    for order, row in enumerate(tap_sums):
        sums_bc[order : order + 1, :] = row


def halving_order(count):
    order = [0]
    step = count // 2
    while step > 1:
        order = order + [place + step for place in order]
        step //= 2
    return order


def late_grads_kernel(shards, slabs, place, normed, du, dq, *refs):
    parts, (mine, theirs, scratch) = refs[:shards], refs[shards:]
    inner = du.shape[1]
    total = parts[0][...].astype(F32)
    for other in parts[1:]:
        total = total + other[...].astype(F32)
    shape = (LANES, LANES)
    moved = (iota(shape, 1) - HALF == iota(shape, 0)).astype(BF16)
    tail = (total + dot(dq[...], moved)).astype(BF16)
    rows_in = normed[...]
    scratch[:, :inner] = dot(rows_in, du[...], 0, 0).astype(BF16)
    scratch[:, inner:] = dot(rows_in, tail, 0, 0).astype(BF16)
    slab = scratch.shape[0] // slabs
    for slot, order in enumerate(halving_order(slabs)):
        cut = slice(slot * slab, (slot + 1) * slab)
        for out, flip in ((mine, 0), (theirs, 1)):
            start = pl.multiple_of((place[0] ^ (order + flip)) * slab, slab)
            out[cut, :] = scratch[pl.ds(start, slab), :]


def fold_kernel(mine, other, kept, sent):
    half = kept.shape[0]
    kept[...] = mine[:half, :].astype(F32) + other[:half, :].astype(F32)
    sent[...] = (mine[half:, :].astype(F32) + other[half:, :].astype(F32)).astype(BF16)


def finish_kernel(kept, part, x_out, tail_out, low_out):
    total = kept[...] + part[...].astype(F32)
    inner = x_out.shape[1]
    x_out[...] = total[:, :inner]
    tail_out[...] = total[:, inner:]
    low_out[...] = total[:, inner:].astype(BF16)


def widen_kernel(index, *refs):
    blocks, (out,) = refs[:-1], refs[-1:]
    wide = out.shape[1]
    piece = wide // len(blocks)
    total = None
    for order, block in enumerate(blocks):
        shape = (LANES, wide)
        lane = iota(shape, 1) - (index[0] ^ order) * piece
        ones = (lane == iota(shape, 0)) & (iota(shape, 0) < piece)
        part = dot(block[...], ones.astype(BF16))
        total = part if total is None else total + part
    out[...] = total


def input_grad_kernel(shards, *refs):
    index = refs[0][0]
    grad_gate, du, dbc, dq, w_in, w_gate, w_bc, w_dt = refs[1:9]
    outs = refs[9 : 9 + shards]
    scratch = refs[9 + shards]
    part = outs[0].shape[0]
    scratch[...] = (
        dot(grad_gate[...], w_gate[...], 1, 1)
        + dot(du[...], w_in[...], 1, 1)
        + dot(dbc[...], w_bc[...], 1, 1)
        + dot(dq[...], w_dt[...])
    ).astype(BF16)
    for order, out in enumerate(outs):
        place = pl.multiple_of((index ^ order) * part, part)
        out[...] = scratch[pl.ds(place, part), :]


def branch_total(messages, depth, inner_all):
    total = messages[0][:, :depth].astype(F32)
    squares = joined_parts(messages[0], depth)
    for other in messages[1:]:
        total = total + other[:, :depth].astype(F32)
        squares = squares + joined_parts(other, depth)
    return total, lax.rsqrt(squares / inner_all + EPSILON)


def residual_kernel(shards, inner_all, *refs):
    messages = refs[:shards]
    start, gain, current_out, branch_out, message_out = refs[shards:]
    depth = start.shape[1]
    branch, scale = branch_total(messages, depth, inner_all)
    current = start[...].astype(F32) + scale * branch
    current_out[...] = current
    branch_out[...] = branch
    norm = lax.rsqrt(jnp.mean(current * current, axis=1, keepdims=True) + EPSILON)
    message_out[:, :depth] = (current * norm * gain[...]).astype(BF16)
    message_out[:, depth:] = pair_of_parts(scale)


def output_kernel(shards, *refs):
    messages = refs[:shards]
    start, out = refs[shards:]
    total = start[...]
    for message in messages:
        total = total + message[...].astype(F32)
    out[...] = total


def norm_back_kernel(shards, last, *refs):
    blocks = refs[:shards]
    refs = refs[shards:]
    rows_in, gain, grad_in = refs[:3]
    current = rows_in[...].astype(F32)
    depth = current.shape[1]
    grad_normed = blocks[0][...].astype(F32)
    for other in blocks[1:]:
        grad_normed = grad_normed + other[...].astype(F32)
    norm = lax.rsqrt(jnp.mean(current * current, axis=1, keepdims=True) + EPSILON)
    weighted = grad_normed * gain[...]
    inner_product = jnp.mean(weighted * current, axis=1, keepdims=True)
    grad = grad_in[...].astype(F32) + norm * weighted - current * (norm * norm * norm * inner_product)
    gain_row = jnp.sum(grad_normed * current * norm, axis=0, keepdims=True)
    if last:
        branch, grad_out, gain_out, message_out = refs[3:]
        low = grad.astype(BF16)
        message_out[:, :depth] = low
        message_out[:, depth:] = pair_of_parts(
            jnp.sum(low.astype(F32) * branch[...], axis=1, keepdims=True)
        )
    else:
        grad_out, gain_out = refs[3:]
    grad_out[...] = grad
    gain_out[...] = jnp.broadcast_to(gain_row, gain_out.shape)


def call(kernel, name, scalars, arrays, outs, flops=0, scratch=()):
    specs, given, held = [], [], 0
    for item in arrays:
        if isinstance(item, tuple):
            item, columns, column = item
            shape = (item.shape[0], columns)
            specs.append(pl.BlockSpec(shape, functools.partial(lambda at, step: (0, at), column)))
        else:
            shape = item.shape
            specs.append(pl.BlockSpec(shape, functools.partial(lambda dims, step: (0,) * dims, len(shape))))
        given.append(pltpu.with_memory_space_constraint(item, pltpu.HBM))
        held += math.prod(shape) * item.dtype.itemsize
    held += sum(jnp.dtype(d).itemsize * math.prod(s) for s, d in outs)
    return pl.pallas_call(
        kernel,
        grid=(1,),
        out_shape=tuple(pltpu.HBM(s, d) for s, d in outs),
        in_specs=[pl.BlockSpec(memory_space=pltpu.SMEM)] * len(scalars) + specs,
        out_specs=tuple(
            pl.BlockSpec(s, functools.partial(lambda dims, step: (0,) * dims, len(s))) for s, d in outs
        ),
        scratch_shapes=list(scratch),
        compiler_params=pltpu.CompilerParams(vmem_limit_bytes=40 * 1024 * 1024),
        cost_estimate=pl.CostEstimate(flops=int(flops), bytes_accessed=int(held), transcendentals=0),
        name=name,
    )(*scalars, *given)


def exchange(blocks, axis):
    count = lax.axis_size(axis)
    return [blocks[0]] + [
        lax.ppermute(blocks[k], axis, [(i, i ^ k) for i in range(count)]) for k in range(1, count)
    ]


def spread_out(block, axis):
    return exchange([block] * lax.axis_size(axis), axis)


def gather_dp(block):
    count = lax.axis_size("dp")
    even = [block] + [
        lax.ppermute(block, "dp", [(i, i ^ k) for i in range(count)]) for k in range(2, count, 2)
    ]
    odd = [lax.ppermute(part, "dp", [(i, i ^ 1) for i in range(count)]) for part in even]
    return [part for pair in zip(even, odd) for part in pair]


class Fold:
    def __init__(self, layer, mine, theirs):
        self.layer, self.kept, self.sent, self.hop = layer, mine, theirs, 1
        self.step()

    def receive(self):
        count = lax.axis_size("dp")
        hop = self.hop
        self.hop *= 2
        return lax.ppermute(self.sent, "dp", [(i, i ^ hop) for i in range(count)])

    def step(self):
        other = self.receive()
        half = (self.kept.shape[0] // 2, self.kept.shape[1])
        self.kept, self.sent = call(
            fold_kernel,
            f"fold_{self.layer}",
            [],
            [self.kept, other],
            [(half, F32), (half, BF16)],
        )

    def last(self):
        while self.hop * 2 < lax.axis_size("dp"):
            self.step()
        return self.kept, self.receive()


def sum_over_dp(values):
    count = lax.axis_size("dp")
    values = values + lax.ppermute(values, "dp", [(i, i ^ 1) for i in range(count)])
    others = [
        lax.ppermute(values, "dp", [(i, i ^ k) for i in range(count)]) for k in range(2, count, 2)
    ]
    for other in others:
        values = values + other
    return values


def body(
    residual_in,
    norm_gain,
    w_zx,
    w_bc,
    w_dt,
    conv_x,
    conv_bc,
    dt_bias,
    a_log,
    d_skip,
    gate_gain,
    w_out,
    lengths,
    cotangent,
):
    shards = lax.axis_size("tensor")
    dp_count = lax.axis_size("dp")
    rows, depth = residual_in.shape
    inner = gate_gain.shape[1]
    heads = dt_bias.shape[1]
    width = inner // heads
    wide = w_bc.shape[2]
    total_rows = rows * shards
    inner_all = inner * shards
    slab = norm_gain.shape[1]
    index = lax.axis_index("tensor").reshape(1).astype(jnp.int32)
    place = lax.axis_index("dp").reshape(1).astype(jnp.int32)
    message = (rows, depth + LANES)

    residual_blocks = spread_out(residual_in, "tensor")
    late_blocks = spread_out(cotangent, "tensor")
    columns = []
    for layer in range(LAYERS):
        columns += [w_zx[layer, :, 1, :], w_zx[layer, :, 0, :], w_out[layer].T]
    ahead = [lax.all_gather(jnp.concatenate(part, axis=1), "dp", axis=0, tiled=True) for part in (columns[:4], columns[4:])]
    w_x = [(ahead[0], inner, 0), (ahead[0], inner, 3)]
    w_gates = [(ahead[0], inner, 1), (ahead[1], inner, 0)]
    w_outs = [(ahead[0], inner, 2), (ahead[1], inner, 1)]
    piece = wide // shards
    maps = lax.dynamic_slice_in_dim(w_bc, index[0] * piece, piece, 2)
    (maps,) = call(
        pack_kernel,
        "pack_maps",
        [place],
        gather_dp(jnp.concatenate([maps[layer] for layer in range(LAYERS)], axis=1)),
        [((depth, LAYERS * piece), BF16)],
    )
    w_bcs = call(
        unpack_maps_kernel,
        "unpack_maps",
        [index],
        spread_out(maps, "tensor"),
        [((depth, wide), BF16)] * LAYERS,
    )
    few = jnp.concatenate(
        [
            w_dt.transpose(0, 2, 1).reshape(LAYERS * heads, slab),
            norm_gain,
            jnp.pad(conv_bc.reshape(LAYERS * 5, -1), ((0, 0), (0, slab - wide // dp_count))),
        ],
        axis=0,
    )
    few = jnp.pad(few, ((0, -few.shape[0] % 16), (0, 0)))
    few = call(
        functools.partial(unpack_kernel, heads),
        "unpack",
        [place],
        spread_out(few, "dp"),
        [((LANES, depth), BF16)] * LAYERS + [((1, depth), F32)] * LAYERS + [((5, wide), F32)] * LAYERS,
    )
    w_steps, gains, taps_bc = few[:LAYERS], few[LAYERS : 2 * LAYERS], few[2 * LAYERS :]
    bias = jnp.pad(dt_bias, ((0, 0), (0, LANES - heads)))[:, None, :]
    rates = jnp.pad(a_log, ((0, 0), (0, LANES - heads)))[:, None, :]
    skips = jnp.repeat(d_skip, width, axis=1)[:, None, :]

    flops = 2 * total_rows * depth * inner
    kept = []
    blocks = residual_blocks
    scales = None
    current = residual_in
    for layer in range(LAYERS):
        last = layer == LAYERS - 1
        outs = [
            ((total_rows, depth), BF16),
            ((total_rows, inner), F32),
            ((total_rows, wide), F32),
            ((total_rows, LANES), F32),
            ((total_rows, inner), F32),
        ]
        if layer:
            outs.append(((total_rows, LANES), F32))
        first = call(
            functools.partial(first_kernel, layer, shards, width),
            f"mix_{layer}",
            [index],
            [*blocks, w_x[layer], w_bcs[layer], gains[layer], w_steps[layer], conv_x[layer], taps_bc[layer], bias[layer], rates[layer], skips[layer]],
            outs,
            flops * 3,
        )
        normed, u_rows, bc_rows, q_rows, y_rows = first[:5]
        if layer:
            scales = first[5]
        arrays = [normed, w_gates[layer], w_outs[layer], y_rows, gate_gain[layer][None]]
        if last:
            gate, hidden, grad_all, grad_hidden, sums = call(
                functools.partial(last_second_kernel, shards),
                f"gate_{layer}",
                [index, lengths],
                [*late_blocks, *arrays],
                [
                    ((total_rows, inner), F32),
                    ((total_rows, inner), BF16),
                    ((total_rows, depth), BF16),
                    ((total_rows, inner), F32),
                    ((8, total_rows), F32),
                ],
                flops * 2,
            )
            sums = spread_out(sums, "tensor")
        else:
            gate, *sent = call(
                functools.partial(second_kernel, shards),
                f"gate_{layer}",
                [index, lengths],
                arrays,
                [((total_rows, inner), F32)] + [(message, BF16)] * shards,
                flops * 2,
                [pltpu.VMEM((total_rows, depth + LANES), BF16)],
            )
            sent = exchange(sent, "tensor")
        kept.append([normed, u_rows, bc_rows, q_rows, y_rows, gate, current])
        if not last:
            current, branch, packed = call(
                functools.partial(residual_kernel, shards, inner_all),
                f"residual_{layer}",
                [],
                [*sent, current, gains[layer + 1]],
                [((rows, depth), F32), ((rows, depth), F32), (message, BF16)],
            )
            blocks = spread_out(packed, "tensor")

    grad_now = cotangent
    early, folds, few_x, few_bc, few_gain = {}, {}, {}, {}, {}
    for layer in reversed(range(LAYERS)):
        last = layer == LAYERS - 1
        normed, u_rows, bc_rows, q_rows, y_rows, gate, rows_in = kept[layer]
        outs = [
            ((total_rows, inner), F32),
            ((total_rows, inner), BF16),
            ((8, inner), F32),
            ((depth, 2 * inner), BF16),
        ]
        if last:
            grad_y, grad_gate, gain_sum, grads, out_scales = call(
                functools.partial(last_gate_kernel, shards, inner_all),
                f"gate_back_{layer}",
                [lengths],
                [*sums, y_rows, gate, grad_hidden, gate_gain[layer][None], normed, grad_all],
                outs + [((total_rows, LANES), F32)],
                flops * 2,
            )
        else:
            grad_y, grad_gate, gain_sum, grads = call(
                functools.partial(gate_kernel, shards, inner_all),
                f"gate_back_{layer}",
                [index, lengths],
                [*blocks, scales, w_outs[layer], y_rows, gate, gate_gain[layer][None], normed],
                outs,
                flops * 3,
                [pltpu.VMEM((total_rows, depth), BF16), pltpu.VMEM((total_rows, LANES), F32)],
            )
        grads, grad_y = lax.optimization_barrier((grads, grad_y))
        early[layer] = lax.psum_scatter(grads, "dp", scatter_dimension=0, tiled=True)
        du, dbc, dq, sums_x, sums_bc, *pieces_bc = call(
            functools.partial(scan_back_kernel, width),
            f"mix_back_{layer}",
            [index],
            [u_rows, bc_rows, q_rows, y_rows, grad_y, conv_x[layer], taps_bc[layer], bias[layer], rates[layer], skips[layer]],
            [
                ((total_rows, inner), BF16),
                ((total_rows, wide), BF16),
                ((total_rows, LANES), BF16),
                ((8, inner), F32),
                ((8, wide), F32),
            ]
            + [((total_rows, LANES), BF16)] * shards,
            flops * 2,
        )
        few_x[layer] = sums_x.at[5].set(gain_sum[0])
        few_bc[layer] = sums_bc
        pieces = call(
            functools.partial(input_grad_kernel, shards),
            f"input_grad_{layer}",
            [index],
            [
                grad_gate,
                du,
                dbc,
                dq,
                w_x[layer],
                w_gates[layer],
                w_bcs[layer],
                w_steps[layer],
            ],
            [((rows, depth), BF16)] * shards,
            flops * 2,
            [pltpu.VMEM((total_rows, depth), BF16)],
        )
        pieces = exchange(pieces, "tensor")
        pieces_bc = exchange(pieces_bc, "tensor")
        if last:
            messages = call(
                functools.partial(branch_kernel, shards),
                "branch",
                [index],
                [hidden, w_outs[layer], out_scales],
                [((rows, depth), BF16)] * shards,
                flops,
                [pltpu.VMEM((total_rows, depth), BF16)],
            )
            (output,) = call(
                functools.partial(output_kernel, shards),
                "output",
                [],
                [*exchange(messages, "tensor"), current],
                [((rows, depth), F32)],
            )
        else:
            folds[layer + 1].step()
            pieces_bc[1], folds[layer + 1].sent = lax.optimization_barrier(
                (pieces_bc[1], folds[layer + 1].sent)
            )
        tall = (depth // 2, inner + LANES)
        mine, theirs = call(
            functools.partial(late_grads_kernel, shards, dp_count),
            f"late_{layer}",
            [place],
            [normed, du, dq, *pieces_bc],
            [(tall, BF16)] * 2,
            flops * 2,
            [pltpu.VMEM((depth, inner + LANES), BF16)],
        )
        if layer:
            pieces[1], mine, theirs = lax.optimization_barrier((pieces[1], mine, theirs))
        fold = Fold(layer, mine, theirs)
        if not layer:
            pieces[1], fold.sent = lax.optimization_barrier((pieces[1], fold.sent))
        folds[layer] = fold
        arrays = [*pieces, rows_in, gains[layer], grad_now]
        outs = [((rows, depth), F32), ((8, depth), F32)]
        if layer:
            arrays.append(branch)
            outs.append((message, BF16))
        back = call(
            functools.partial(norm_back_kernel, shards, bool(layer)),
            f"norm_back_{layer}",
            [],
            arrays,
            outs,
        )
        grad_now, few_gain[layer] = back[:2]
        if layer:
            blocks = spread_out(back[2], "tensor")
            blocks[1], fold.sent = lax.optimization_barrier((blocks[1], fold.sent))

    order = range(LAYERS)
    shared = jnp.stack(
        [
            jnp.concatenate([few_gain[layer][0], few_bc[layer][:5].reshape(-1)])
            for layer in order
        ]
    )
    shared = functools.reduce(jnp.add, spread_out(shared, "tensor"))
    own = jnp.stack([few_x[layer] for layer in order]).reshape(-1, LANES)
    few = jnp.concatenate([own, shared.reshape(-1, LANES)], axis=0)
    few = sum_over_dp(few)
    own = few[: own.shape[0]].reshape(LAYERS, 8, inner)
    shared = few[own.size // LANES :].reshape(LAYERS, -1)
    grad_gain = lax.dynamic_slice_in_dim(shared[:, :depth], place[0] * slab, slab, 1)
    grad_conv_bc = lax.dynamic_slice_in_dim(
        shared[:, depth:].reshape(LAYERS, 5, wide), place[0] * (wide // dp_count), wide // dp_count, 2
    )
    grad_x, grad_tail, grad_bc = {}, {}, {}
    for layer in reversed(order):
        kept_part, part = folds[layer].last()
        grad_x[layer], grad_tail[layer], low = call(
            finish_kernel,
            f"finish_{layer}",
            [],
            [kept_part, part],
            [((slab, inner), F32), ((slab, LANES), F32), ((slab, LANES), BF16)],
        )
        (grad_bc[layer],) = call(
            widen_kernel,
            f"widen_{layer}",
            [index],
            spread_out(low, "tensor"),
            [((slab, wide), F32)],
        )
    grad_bc = jnp.stack([grad_bc[layer] for layer in order])
    grad_zx = jnp.stack(
        [jnp.stack([early[layer][:, :inner].astype(F32), grad_x[layer]], axis=1) for layer in order]
    )
    grad_dt = jnp.stack([grad_tail[layer][:, HALF : HALF + heads] for layer in order])
    grad_out = jnp.stack([early[layer][:, inner:].T for layer in order]).astype(F32)
    return (
        output,
        grad_now,
        grad_gain,
        grad_zx,
        grad_bc,
        grad_dt,
        own[:, :5],
        grad_conv_bc,
        own[:, 6, :heads],
        own[:, 6, LANES : LANES + heads],
        own[:, 6, 2 * LANES : 2 * LANES + heads],
        own[:, 5],
        grad_out,
    )


def solution(mesh):
    return jax.shard_map(
        body,
        mesh=mesh,
        in_specs=(
            P(("dp", "tensor"), None),
            P(None, "dp"),
            P(None, "dp", None, "tensor"),
            P(None, "dp", None),
            P(None, "dp", "tensor"),
            P(None, None, "tensor"),
            P(None, None, "dp"),
            P(None, "tensor"),
            P(None, "tensor"),
            P(None, "tensor"),
            P(None, "tensor"),
            P(None, "tensor", "dp"),
            P("dp"),
            P(("dp", "tensor"), None),
        ),
        out_specs=(
            P(("dp", "tensor"), None),
            P(("dp", "tensor"), None),
            P(None, "dp"),
            P(None, "dp", None, "tensor"),
            P(None, "dp", None),
            P(None, "dp", "tensor"),
            P(None, None, "tensor"),
            P(None, None, "dp"),
            P(None, "tensor"),
            P(None, "tensor"),
            P(None, "tensor"),
            P(None, "tensor"),
            P(None, "tensor", "dp"),
        ),
        check_vma=False,
    )
```

```python
import functools
import math

import jax
import jax.numpy as jnp
from jax import lax
from jax.experimental import pallas as pl
from jax.experimental.pallas import tpu as pltpu
from jax.sharding import PartitionSpec as P

LAYERS = 2
EPSILON = 1e-05
LANES = 128
HALF = 64
F32 = jnp.float32
BF16 = jnp.bfloat16
EXACT = lax.Precision.HIGHEST


class Far:
    def __init__(self, array, columns=None, place=0):
        self.array, self.place = array, place
        self.columns = array.shape[1] if columns is None else columns
        self.shape, self.dtype = (array.shape[0], self.columns), array.dtype


class Arrival:
    def __init__(self, copy, ref):
        self.copy, self.ref, self.waiting = copy, ref, True
        self.shape = ref.shape
        copy.start()

    def wait(self):
        if self.waiting:
            self.copy.wait()
            self.waiting = False

    def __getitem__(self, at):
        self.wait()
        return self.ref[at]


class Departure:
    def __init__(self, copy, ref):
        self.copy, self.ref, self.started = copy, ref, False
        self.shape = ref.shape

    def send(self):
        if not self.started:
            self.copy.start()
            self.started = True

    def __getitem__(self, at):
        return self.ref[at]

    def __setitem__(self, at, values):
        self.ref[at] = values
        if at is Ellipsis:
            self.send()


def dot(left, right, left_dim=1, right_dim=0, precision=None):
    return lax.dot_general(
        left,
        right,
        (((left_dim,), (right_dim,)), ((), ())),
        precision=precision,
        preferred_element_type=F32,
    )


def iota(shape, dim):
    return lax.broadcasted_iota(jnp.int32, shape, dim)


def sigmoid(values):
    return 1.0 / (1.0 + jnp.exp(-values))


def softplus(values):
    return jnp.maximum(values, 0.0) + jnp.log1p(jnp.exp(-jnp.abs(values)))


def rows_later(values, steps):
    return jnp.where(iota(values.shape, 0) >= steps, pltpu.roll(values, steps, 0), 0.0)


def rows_earlier(values, steps):
    total = values.shape[0]
    return jnp.where(
        iota(values.shape, 0) < total - steps, pltpu.roll(values, total - steps, 0), 0.0
    )


def conv(values, taps):
    result = taps[4:5, :] + taps[3:4, :] * values
    for offset in range(3):
        result = result + taps[offset : offset + 1, :] * rows_later(values, 3 - offset)
    return result


def conv_back(values, taps, grad):
    back = taps[3:4, :] * grad
    for offset in range(3):
        back = back + taps[offset : offset + 1, :] * rows_earlier(grad, 3 - offset)
    sums = [
        jnp.sum(grad * rows_later(values, 3 - offset), axis=0, keepdims=True)
        for offset in range(3)
    ]
    sums.append(jnp.sum(grad * values, axis=0, keepdims=True))
    sums.append(jnp.sum(grad, axis=0, keepdims=True))
    return back, sums


def pair_of_parts(column):
    high = column.astype(BF16).astype(F32)
    wide = jnp.broadcast_to(high, (column.shape[0], LANES))
    rest = jnp.broadcast_to(column - high, (column.shape[0], LANES))
    return jnp.where(iota(wide.shape, 1) < HALF, wide, rest).astype(BF16)


def joined_parts(message, width):
    return message[:, width : width + 1].astype(F32) + message[
        :, width + HALF : width + HALF + 1
    ].astype(F32)


def three_parts(values):
    high = values.astype(BF16)
    rest = values - high.astype(F32)
    middle = rest.astype(BF16)
    return high, middle, (rest - middle.astype(F32)).astype(BF16)


def spread_sum(parts, spread):
    spread = spread.astype(BF16)
    return dot(parts[0], spread) + dot(parts[1], spread) + dot(parts[2], spread)


def ready(operand):
    if isinstance(operand, Arrival):
        operand.wait()
    return operand.ref if isinstance(operand, (Arrival, Departure)) else operand


def step_state(q_rows, dt_bias, a_log):
    rows = q_rows.shape[0]
    shifted = q_rows + dt_bias
    steps = softplus(shifted)
    rates = -jnp.exp(a_log)
    below = (iota((rows, rows), 0) >= iota((rows, rows), 1)).astype(F32)
    running = dot(below, steps * rates, precision=EXACT)
    return shifted, steps, rates, running


SKIP_ROW, GAIN_ROW, BIAS_ROW, RATE_ROW = 5, 6, 7, 8


def mixer_forward(u_ref, y_ref, params, turned, bc_rows, q_rows, conv_bc, width):
    rows, inner = u_ref.shape
    states = bc_rows.shape[1] // 2
    maps = conv(bc_rows, conv_bc)
    maps = maps * sigmoid(maps)
    _, steps, _, running = step_state(
        q_rows, params[BIAS_ROW : BIAS_ROW + 1, :LANES], params[RATE_ROW : RATE_ROW + 1, :LANES]
    )
    turned[...] = running.T
    scores = dot(maps[:, states:], maps[:, :states], 1, 1, EXACT)
    steps = three_parts(steps)
    causal = iota((rows, rows), 0) >= iota((rows, rows), 1)
    lane = iota((rows, LANES), 1)
    per_block = LANES // width

    def block_step(block):
        at = pl.ds(block * LANES, LANES)
        mixed_in = conv(u_ref[:, at], params[:5, at])
        mixed_in = mixed_in * sigmoid(mixed_in)
        shape = (LANES, LANES)
        heads = block * per_block + iota(shape, 1) // width
        scaled = (mixed_in * spread_sum(steps, heads == iota(shape, 0))).astype(BF16)
        total = None
        for slot in range(per_block):
            head = block * per_block + slot
            gap = running[:, head : head + 1] - turned[head : head + 1, :]
            decay = jnp.exp(jnp.where(causal, gap, -1e30))
            part = dot((decay * scores).astype(BF16), scaled)
            total = part if slot == 0 else jnp.where(lane < slot * width, total, part)
        y_ref[:, at] = total + params[SKIP_ROW : SKIP_ROW + 1, at] * mixed_in

    for block in range(inner // LANES):
        block_step(block)


def gather_rows(target, index, blocks, width):
    rows = blocks[0].shape[0]
    for order, block in enumerate(blocks):
        place = pl.multiple_of((index ^ order) * rows, rows)
        target[pl.ds(place, rows), :] = block[:, :width]


def unpack_kernel(heads, *refs):
    index = refs[0][0]
    outs = refs[-3 * LAYERS :]
    blocks = refs[1 : -3 * LAYERS]
    slab = blocks[0].shape[1]
    depth, wide = outs[LAYERS].shape[1], outs[2 * LAYERS].shape[1]
    piece = wide // len(blocks)

    def placed(start, stop, held, total):
        result = None
        for order, block in enumerate(blocks):
            shape = (held, total)
            ones = iota(shape, 1) - (index ^ order) * held == iota(shape, 0)
            part = dot(block[...][start:stop, :held], ones.astype(BF16))
            result = part if result is None else result + part
        return result

    norm_at = LAYERS * heads
    taps_at = norm_at + LAYERS
    rows = placed(0, taps_at, slab, depth)
    taps = placed(taps_at, taps_at + 5 * LAYERS, piece, wide)
    for layer in range(LAYERS):
        steps = rows[layer * heads : (layer + 1) * heads, :]
        padding = jnp.zeros((LANES - heads, depth), F32)
        outs[layer][...] = jnp.concatenate([steps, padding], axis=0).astype(BF16)
        outs[LAYERS + layer][...] = rows[norm_at + layer : norm_at + layer + 1, :]
        outs[2 * LAYERS + layer][...] = taps[5 * layer : 5 * layer + 5, :]


def pack_kernel(index, *refs):
    blocks, (out,) = refs[:-1], refs[-1:]
    gather_rows(out, index[0], blocks, out.shape[1])


def unpack_maps_kernel(index, *refs):
    blocks, outs = refs[:-LAYERS], refs[-LAYERS:]
    piece = blocks[0].shape[1] // LAYERS
    for layer, out in enumerate(outs):
        total = None
        for order, block in enumerate(blocks):
            shape = (LAYERS * piece, out.shape[1])
            row = iota(shape, 0) - layer * piece
            ones = (row == iota(shape, 1) - (index[0] ^ order) * piece) & (row >= 0) & (row < piece)
            part = dot(block[...], ones.astype(BF16))
            total = part if total is None else total + part
        out[...] = total.astype(BF16)


def first_kernel(layer, shards, slabs, width, *refs):
    index, place = refs[0][0], refs[1][0]
    blocks, refs = refs[2 : 2 + shards], refs[2 + shards :]
    if layer:
        weights, refs = refs[:slabs], refs[slabs:]
        w_in, scales_out = refs[-3:-1]
        refs = refs[:-3] + refs[-1:]
    else:
        w_in, refs = refs[0], refs[1:]
    w_bc, gain, w_dt, conv_bc, params, normed, u_out, bc_out, q_out, y_out, turned = refs
    depth = normed.shape[1]
    inner = u_out.shape[1]
    rows = blocks[0].shape[0]
    if layer == 0:
        for order, block in enumerate(blocks):
            values = block[...].astype(F32)
            scale = lax.rsqrt(jnp.mean(values * values, axis=1, keepdims=True) + EPSILON)
            start = pl.multiple_of((index ^ order) * rows, rows)
            normed[pl.ds(start, rows), :] = (values * scale * gain[...]).astype(BF16)
    else:
        gather_rows(normed, index, blocks, depth)
        for order, block in enumerate(blocks):
            start = pl.multiple_of((index ^ order) * rows, rows)
            scales_out[pl.ds(start, rows), :] = jnp.broadcast_to(
                joined_parts(block, depth), (rows, LANES)
            )
        gather_rows(w_in, place, weights, inner)
        scales_out.send()
        w_in.send()
    normed.send()
    rows_in = normed[...]
    bc_rows = dot(rows_in, w_bc[...])
    q_rows = dot(rows_in, w_dt[...], 1, 1)
    u_rows = dot(rows_in, w_in[...])
    u_out[...] = u_rows
    bc_out[...] = bc_rows
    q_out[...] = q_rows
    mixer_forward(
        ready(u_out), ready(y_out), ready(params), turned, bc_rows, q_rows, conv_bc[...], width
    )


def live_column(length, rows):
    return (iota((rows, 1), 0) < length).astype(F32)


def second_kernel(shards, *refs):
    index = refs[0][0]
    length = refs[1][0]
    normed, w_gate, w_out, y_rows, params, z_out = refs[2:8]
    messages, scratch = refs[8 : 8 + shards], refs[8 + shards]
    depth = normed.shape[1]
    part = messages[0].shape[0]
    gate = dot(normed[...], w_gate[...])
    z_out[...] = gate
    gated = y_rows[...] * (gate * sigmoid(gate))
    live = live_column(length, y_rows.shape[0])
    hidden = (gated * params[GAIN_ROW : GAIN_ROW + 1, :] * live).astype(BF16)
    scratch[:, :depth] = dot(hidden, w_out[...], 1, 1).astype(BF16)
    scratch[:, depth:] = pair_of_parts(jnp.sum(gated * gated, axis=1, keepdims=True))
    for order, message in enumerate(messages):
        place = pl.multiple_of((index ^ order) * part, part)
        message[...] = scratch[pl.ds(place, part), :]


def last_second_kernel(shards, *refs):
    index = refs[0][0]
    length = refs[1][0]
    blocks, refs = refs[2 : 2 + shards], refs[2 + shards :]
    normed, w_gate, w_out, y_rows, params = refs[:5]
    z_out, hidden_out, grad_all, grad_hidden_out, sums_out = refs[5:]
    rows = y_rows.shape[0]
    gather_rows(grad_all, index, blocks, normed.shape[1])
    grad_all.send()
    grad_hidden = dot(grad_all[...], w_out[...])
    grad_hidden_out[...] = grad_hidden
    gate = dot(normed[...], w_gate[...])
    z_out[...] = gate
    gated = y_rows[...] * (gate * sigmoid(gate))
    squares = jnp.sum(gated * gated, axis=1, keepdims=True)
    weighted = gated * params[GAIN_ROW : GAIN_ROW + 1, :] * live_column(length, rows)
    hidden_out[...] = weighted.astype(BF16)
    products = jnp.sum(grad_hidden * weighted, axis=1, keepdims=True)
    lane = iota((rows, LANES), 1)
    table = jnp.where(lane == 0, squares, jnp.where(lane == 1, products, 0.0))
    sums_out[...] = table.T[:8, :]


def branch_kernel(shards, *refs):
    index = refs[0][0]
    hidden, w_out, scales = refs[1:4]
    messages, scratch = refs[4 : 4 + shards], refs[4 + shards]
    part = messages[0].shape[0]
    scratch[...] = (scales[:, 0:1] * dot(hidden[...], w_out[...], 1, 1)).astype(BF16)
    for order, message in enumerate(messages):
        place = pl.multiple_of((index ^ order) * part, part)
        message[...] = scratch[pl.ds(place, part), :]


def gate_back(length, scale, product, inner_all, y_rows, gate, grad_hidden, gate_gain):
    live = live_column(length, y_rows.shape[0])
    turn = sigmoid(gate)
    opened = gate * turn
    gated = y_rows * opened
    grad_live = grad_hidden * live
    grad_gain = jnp.sum(grad_live * gated * scale, axis=0, keepdims=True)
    grad_gated = scale * grad_live * gate_gain - gated * (
        scale * scale * scale * (product / inner_all)
    )
    hidden = (gated * scale * gate_gain * live).astype(BF16)
    grad_y = grad_gated * opened
    grad_gate = grad_gated * y_rows * (turn * (1.0 + gate * (1.0 - turn)))
    return hidden, grad_y, grad_gate.astype(BF16), grad_gain


def weight_grads(pairs, out, staged, sems):
    slots, part = staged.shape[:2]
    copies = []
    for slot in range(slots):
        cut = slice(slot * part, (slot + 1) * part)
        at = 0
        for left, right in pairs:
            columns = right.shape[1]
            staged[slot, :, at : at + columns] = dot(left[:, cut], right[...], 0, 0).astype(BF16)
            at += columns
        copies.append(
            pltpu.make_async_copy(staged.at[slot], out.at[pl.ds(slot * part, part), :], sems.at[slot])
        )
        copies[-1].start()
    for copy in copies:
        copy.wait()


def last_gate_kernel(shards, inner_all, *refs):
    length = refs[0][0]
    sums, refs = refs[1 : 1 + shards], refs[1 + shards :]
    y_rows, gate, grad_hidden, params, normed, grad_all = refs[:6]
    grad_y_out, grad_gate_out, gain_out, grads_out, scale_out, staged, sems = refs[6:]
    rows = y_rows.shape[0]
    total = sums[0][...]
    for other in sums[1:]:
        total = total + other[...]
    table = jnp.concatenate([total, jnp.zeros((LANES - 8, rows), F32)], axis=0).T
    scale = lax.rsqrt(table[:, 0:1] / inner_all + EPSILON)
    scale_out[...] = jnp.broadcast_to(scale, scale_out.shape)
    hidden, grad_y, grad_gate, grad_gain = gate_back(
        length,
        scale,
        table[:, 1:2],
        inner_all,
        y_rows[...],
        gate[...],
        grad_hidden[...],
        params[GAIN_ROW : GAIN_ROW + 1, :],
    )
    grad_y_out[...] = grad_y
    grad_gate_out[...] = grad_gate
    gain_out[...] = jnp.broadcast_to(grad_gain, gain_out.shape)
    weight_grads(((normed, grad_gate), (grad_all, hidden)), grads_out, staged, sems)


def gate_kernel(shards, inner_all, *refs):
    index = refs[0][0]
    length = refs[1][0]
    blocks, refs = refs[2 : 2 + shards], refs[2 + shards :]
    scales, w_out, y_rows, gate, params, normed = refs[:6]
    grad_y_out, grad_gate_out, gain_out, hidden_out, grad_all, products = refs[6:]
    depth = grad_all.shape[1]
    part = blocks[0].shape[0]
    gather_rows(grad_all, index, blocks, depth)
    for order, block in enumerate(blocks):
        place = pl.multiple_of((index ^ order) * part, part)
        products[pl.ds(place, part), :] = jnp.broadcast_to(
            joined_parts(block, depth), (part, LANES)
        )
    hidden, grad_y, grad_gate, grad_gain = gate_back(
        length,
        scales[:, 0:1],
        products[:, 0:1],
        inner_all,
        y_rows[...],
        gate[...],
        dot(grad_all[...], w_out[...]),
        params[GAIN_ROW : GAIN_ROW + 1, :],
    )
    grad_y_out[...] = grad_y
    grad_gate_out[...] = grad_gate
    hidden_out[...] = hidden
    gain_out[...] = jnp.broadcast_to(grad_gain, gain_out.shape)


def grads_kernel(normed, grad_gate, grad_all, hidden, du, out, staged, sems):
    weight_grads(((normed, grad_gate), (grad_all, hidden), (normed, du)), out, staged, sems)


def scan_back_kernel(width, index, *refs):
    u_ref, bc_ref, q_ref, y_ref, grad_ref, gain_sum, conv_bc, params_ref = refs[:8]
    du_out, dbc_out, dq_out, sums_out, sums_bc = refs[8:13]
    pieces = refs[13:-5]
    turned, grad_scores, grad_running, grad_steps, skip_sum = refs[-5:]
    params, u_ref, y_ref, grad_ref = ready(params_ref), ready(u_ref), ready(y_ref), ready(grad_ref)
    sums_x, du_ref = ready(sums_out), ready(du_out)
    bc_rows, q_rows = bc_ref[...], q_ref[...]
    rows, inner = u_ref.shape
    states = bc_rows.shape[1] // 2
    taps_bc = conv_bc[...]
    pre_bc = conv(bc_rows, taps_bc)
    turn_bc = sigmoid(pre_bc)
    maps = pre_bc * turn_bc
    shifted, steps, rates, running = step_state(
        q_rows, params[BIAS_ROW : BIAS_ROW + 1, :LANES], params[RATE_ROW : RATE_ROW + 1, :LANES]
    )
    turned[...] = running.T
    b_rows, c_rows = maps[:, :states], maps[:, states:]
    scores = dot(b_rows, c_rows, 1, 1, EXACT)
    steps_parts = three_parts(steps)
    causal = iota((rows, rows), 0) <= iota((rows, rows), 1)
    lane = iota((rows, LANES), 1)
    per_block = LANES // width
    for total in (grad_scores, grad_running, grad_steps, skip_sum):
        total[...] = jnp.zeros(total.shape, F32)

    def block_step(block):
        at = pl.ds(block * LANES, LANES)
        u_rows, grad_y = u_ref[:, at], grad_ref[:, at]
        taps_x, skips = params[:5, at], params[SKIP_ROW : SKIP_ROW + 1, at]
        pre_x = conv(u_rows, taps_x)
        turn_x = sigmoid(pre_x)
        mixed_in = pre_x * turn_x
        shape = (LANES, LANES)
        heads = block * per_block + iota(shape, 1) // width
        steps_wide = spread_sum(steps_parts, heads == iota(shape, 0))
        scaled = (mixed_in * steps_wide).astype(BF16)
        grad_low = grad_y.astype(BF16)
        grad_scaled = None
        for slot in range(per_block):
            head = block * per_block + slot
            gap = turned[head : head + 1, :] - running[:, head : head + 1]
            decay = jnp.exp(jnp.where(causal, gap, -1e30))
            part = dot((decay * scores).astype(BF16), grad_low)
            grad_scaled = part if slot == 0 else jnp.where(lane < slot * width, grad_scaled, part)
            own = jnp.where(
                (lane >= slot * width) & (lane < (slot + 1) * width), scaled, jnp.zeros_like(scaled)
            )
            grad_scores[...] += dot(own, grad_low, 1, 1) * decay
        gather = block * per_block + iota(shape, 0) // width == iota(shape, 1)
        within = y_ref[:, at] - skips * mixed_in
        moved = grad_low.astype(F32) * within - scaled.astype(F32) * grad_scaled
        grad_running[...] += spread_sum(three_parts(moved), gather)
        grad_steps[...] += spread_sum(three_parts(mixed_in * grad_scaled), gather)
        skip_row = jnp.sum(grad_y * mixed_in, axis=0, keepdims=True)
        skip_sum[...] += spread_sum(three_parts(jnp.broadcast_to(skip_row, (8, LANES))), gather)
        grad_x = steps_wide * grad_scaled + skips * grad_y
        grad_x = grad_x * (turn_x * (1.0 + pre_x * (1.0 - turn_x)))
        du, tap_sums = conv_back(u_rows, taps_x, grad_x)
        du_ref[:, at] = du.astype(BF16)
        tap_sums.append(gain_sum[0:1, at])
        tap_sums.append(jnp.zeros((2, LANES), F32))
        sums_x[:, at] = jnp.concatenate(tap_sums, axis=0)

    for block in range(inner // LANES):
        block_step(block)
    grad_b = dot(grad_scores[...], c_rows, precision=EXACT)
    grad_c = dot(grad_scores[...], b_rows, 0, 0, EXACT)
    above = (iota((rows, rows), 0) <= iota((rows, rows), 1)).astype(F32)
    grad_decay = dot(above, grad_running[...], precision=EXACT)
    grad_q = (grad_steps[...] + grad_decay * rates) * sigmoid(shifted)
    dq_out[...] = grad_q.astype(BF16)
    sums_x[6:7, :LANES] = jnp.sum(grad_q, axis=0, keepdims=True)
    sums_x[6:7, LANES : 2 * LANES] = jnp.sum(grad_decay * steps, axis=0, keepdims=True) * rates
    sums_x[6:7, 2 * LANES : 3 * LANES] = skip_sum[0:1, :]
    grad_bc = jnp.concatenate([grad_b, grad_c], axis=1)
    grad_bc = grad_bc * (turn_bc * (1.0 + pre_bc * (1.0 - turn_bc)))
    dbc, tap_sums = conv_back(bc_rows, taps_bc, grad_bc)
    low = dbc.astype(BF16)
    dbc_out[...] = low
    piece = low.shape[1] // len(pieces)
    for order, out in enumerate(pieces):
        shape = (low.shape[1], LANES)
        ones = iota(shape, 0) - (index[0] ^ order) * piece == iota(shape, 1)
        ones = ones & (iota(shape, 1) < piece)
        out[...] = dot(low, ones.astype(BF16)).astype(BF16)
    tap_sums.append(jnp.zeros((3, low.shape[1]), F32))
    sums_bc[...] = jnp.concatenate(tap_sums, axis=0)


def halving_order(count):
    order = [0]
    step = count // 2
    while step > 1:
        order = order + [place + step for place in order]
        step //= 2
    return order


def late_tail(parts, dq):
    total = parts[0][...].astype(F32)
    for other in parts[1:]:
        total = total + other[...].astype(F32)
    shape = (LANES, LANES)
    moved = (iota(shape, 1) - HALF == iota(shape, 0)).astype(BF16)
    tail = (total + dot(dq[...], moved)).astype(BF16)
    return tail


def split_slabs(place, slabs, scratch, mine, theirs):
    slab = scratch.shape[0] // slabs
    for slot, order in enumerate(halving_order(slabs)):
        cut = slice(slot * slab, (slot + 1) * slab)
        for out, flip in ((mine, 0), (theirs, 1)):
            start = pl.multiple_of((place[0] ^ (order + flip)) * slab, slab)
            out[cut, :] = scratch[pl.ds(start, slab), :]


def late_tail_kernel(shards, slabs, place, normed, dq, *refs):
    parts, (mine, theirs, scratch) = refs[:shards], refs[shards:]
    scratch[...] = dot(normed[...], late_tail(parts, dq), 0, 0).astype(BF16)
    split_slabs(place, slabs, scratch, mine, theirs)


def late_grads_kernel(shards, slabs, place, normed, du, dq, *refs):
    parts, (mine, theirs, scratch) = refs[:shards], refs[shards:]
    inner = du.shape[1]
    rows_in = normed[...]
    scratch[:, :inner] = dot(rows_in, du[...], 0, 0).astype(BF16)
    scratch[:, inner:] = dot(rows_in, late_tail(parts, dq), 0, 0).astype(BF16)
    split_slabs(place, slabs, scratch, mine, theirs)


def fold_kernel(mine, other, kept, sent):
    half = kept.shape[0]
    kept[...] = mine[:half, :].astype(F32) + other[:half, :].astype(F32)
    sent[...] = (mine[half:, :].astype(F32) + other[half:, :].astype(F32)).astype(BF16)


def tails_kernel(first_kept, first_part, last_kept, last_part, tail_out, low_out):
    tails = []
    for kept, part in ((first_kept, first_part), (last_kept, last_part)):
        inner = kept.shape[1] - LANES
        tails.append(kept[:, inner:] + part[:, inner:].astype(F32))
    tail = jnp.concatenate(tails, axis=1)
    low_out[...] = tail.astype(BF16)
    tail_out[...] = tail


def finish_kernel(first, early, kept, part, zx_out, out_out):
    inner = early.shape[1] // 2
    zx_out[1, :, 0, :] = early[:, :inner].astype(F32)
    zx_out[1, :, 1, :] = kept[:, :inner] + part[:, :inner].astype(F32)
    out_out[1, :, :] = early[:, inner:].astype(F32)
    zx_out[0, :, 0, :] = first[:, :inner].astype(F32)
    zx_out[0, :, 1, :] = first[:, 2 * inner :].astype(F32)
    out_out[0, :, :] = first[:, inner : 2 * inner].astype(F32)


def widen_kernel(index, *refs):
    blocks, outs = refs[:-LAYERS], refs[-LAYERS:]
    wide = outs[0].shape[1]
    piece = wide // len(blocks)
    for layer, out in enumerate(outs):
        total = None
        for order, block in enumerate(blocks):
            shape = (LANES, wide)
            lane = iota(shape, 1) - (index[0] ^ order) * piece
            ones = (lane == iota(shape, 0)) & (iota(shape, 0) < piece)
            part = dot(block[:, layer * LANES : (layer + 1) * LANES], ones.astype(BF16))
            total = part if total is None else total + part
        out[...] = total


def input_grad_kernel(shards, *refs):
    index = refs[0][0]
    grad_gate, du, dbc, dq, w_in, w_gate, w_bc, w_dt = refs[1:9]
    outs, scratch = refs[9 : 9 + shards], refs[9 + shards]
    part = outs[0].shape[0]
    total = dot(dbc[...], w_bc[...], 1, 1) + dot(dq[...], w_dt[...])
    total = total + dot(du[...], w_in[...], 1, 1)
    scratch[...] = (total + dot(grad_gate[...], w_gate[...], 1, 1)).astype(BF16)
    for order, out in enumerate(outs):
        place = pl.multiple_of((index ^ order) * part, part)
        out[...] = scratch[pl.ds(place, part), :]


def branch_total(messages, depth, inner_all):
    total = messages[0][:, :depth].astype(F32)
    squares = joined_parts(messages[0], depth)
    for other in messages[1:]:
        total = total + other[:, :depth].astype(F32)
        squares = squares + joined_parts(other, depth)
    return total, lax.rsqrt(squares / inner_all + EPSILON)


def residual_kernel(shards, inner_all, *refs):
    messages = refs[:shards]
    start, gain, current_out, branch_out, message_out = refs[shards:]
    depth = start.shape[1]
    branch, scale = branch_total(messages, depth, inner_all)
    current = start[...].astype(F32) + scale * branch
    current_out[...] = current
    branch_out[...] = branch
    norm = lax.rsqrt(jnp.mean(current * current, axis=1, keepdims=True) + EPSILON)
    message_out[:, :depth] = (current * norm * gain[...]).astype(BF16)
    message_out[:, depth:] = pair_of_parts(scale)


def output_kernel(shards, *refs):
    messages = refs[:shards]
    start, out = refs[shards:]
    total = start[...]
    for message in messages:
        total = total + message[...].astype(F32)
    out[...] = total


def norm_back_kernel(shards, last, *refs):
    blocks = refs[:shards]
    refs = refs[shards:]
    rows_in, gain, grad_in = refs[:3]
    current = rows_in[...].astype(F32)
    depth = current.shape[1]
    grad_normed = blocks[0][...].astype(F32)
    for other in blocks[1:]:
        grad_normed = grad_normed + other[...].astype(F32)
    norm = lax.rsqrt(jnp.mean(current * current, axis=1, keepdims=True) + EPSILON)
    weighted = grad_normed * gain[...]
    inner_product = jnp.mean(weighted * current, axis=1, keepdims=True)
    grad = grad_in[...].astype(F32) + norm * weighted - current * (norm * norm * norm * inner_product)
    gain_row = jnp.sum(grad_normed * current * norm, axis=0, keepdims=True)
    if last:
        branch, grad_out, gain_out, message_out = refs[3:]
        low = grad.astype(BF16)
        message_out[:, :depth] = low
        message_out[:, depth:] = pair_of_parts(
            jnp.sum(low.astype(F32) * branch[...], axis=1, keepdims=True)
        )
    else:
        grad_out, gain_out = refs[3:]
    grad_out[...] = grad
    gain_out[...] = jnp.broadcast_to(gain_row, gain_out.shape)


def call(kernel, name, scalars, arrays, outs, flops=0, scratch=(), vmem=24):
    far_in = [item for item in arrays if isinstance(item, Far)]
    far_out = [out for out in outs if out[2:] == ("far",)]
    specs, given, out_specs, shapes, held = [], [], [], [], 0
    for item in arrays:
        if isinstance(item, Far):
            specs.append(pl.BlockSpec(memory_space=pl.ANY))
            given.append(pltpu.with_memory_space_constraint(item.array, pltpu.HBM))
        else:
            specs.append(pl.BlockSpec(memory_space=pltpu.VMEM))
            given.append(item)
        held += math.prod(item.shape) * item.dtype.itemsize
    for shape, dtype, *kind in outs:
        out_specs.append(pl.BlockSpec(memory_space=pl.ANY if kind else pltpu.VMEM))
        shapes.append(pltpu.HBM(shape, dtype) if kind else jax.ShapeDtypeStruct(shape, dtype))
        held += math.prod(shape) * jnp.dtype(dtype).itemsize
    extra = [pltpu.VMEM(item.shape, item.dtype) for item in far_in]
    extra += [pltpu.VMEM(out[0], out[1]) for out in far_out]
    extra += [pltpu.SemaphoreType.DMA((max(1, len(far_in) + len(far_out)),))]

    def whole(*refs):
        refs = list(refs)
        own = len(refs) - len(extra)
        places, sems = refs[own:-1], refs[-1]
        refs = refs[:own]
        moved, slot = [], 0
        for order, item in enumerate(arrays):
            if isinstance(item, Far):
                at = len(scalars) + order
                source = refs[at]
                if item.columns != item.array.shape[1]:
                    source = source.at[:, pl.ds(item.place * item.columns, item.columns)]
                copy = pltpu.make_async_copy(source, places[slot], sems.at[slot])
                refs[at] = Arrival(copy, places[slot])
                moved.append(refs[at])
                slot += 1
        leaving = []
        for order, out in enumerate(outs):
            if out[2:] == ("far",):
                at = len(scalars) + len(arrays) + order
                copy = pltpu.make_async_copy(places[slot], refs[at], sems.at[slot])
                refs[at] = Departure(copy, places[slot])
                leaving.append(refs[at])
                slot += 1
        kernel(*refs)
        for item in moved:
            item.wait()
        for item in leaving:
            item.send()
        for item in leaving:
            item.copy.wait()

    return pl.pallas_call(
        whole,
        out_shape=tuple(shapes),
        in_specs=[pl.BlockSpec(memory_space=pltpu.SMEM)] * len(scalars) + specs,
        out_specs=tuple(out_specs),
        scratch_shapes=list(scratch) + extra,
        compiler_params=pltpu.CompilerParams(vmem_limit_bytes=vmem * 1024 * 1024),
        cost_estimate=pl.CostEstimate(flops=1, bytes_accessed=1, transcendentals=0),
        name=name,
    )(*scalars, *given)


def far(shape, dtype):
    return (shape, dtype, "far")


def exchange(blocks, axis):
    count = lax.axis_size(axis)
    return [blocks[0]] + [
        lax.ppermute(blocks[k], axis, [(i, i ^ k) for i in range(count)]) for k in range(1, count)
    ]


def spread_out(block, axis):
    return exchange([block] * lax.axis_size(axis), axis)


def gather_dp(block):
    count = lax.axis_size("dp")
    blocks, hop = {0: block}, count // 2
    while hop:
        for k in list(blocks):
            blocks[k ^ hop] = lax.ppermute(blocks[k], "dp", [(i, i ^ hop) for i in range(count)])
        hop //= 2
    return [blocks[k] for k in range(count)]


def over_dp(block, hop):
    count = lax.axis_size("dp")
    return lax.ppermute(block, "dp", [(i, i ^ hop) for i in range(count)])


class Halves:
    def __init__(self, name, mine, theirs):
        self.name, self.kept, self.sent, self.hop = name, mine, theirs, 1

    def receive(self):
        other = over_dp(self.sent, self.hop)
        self.hop *= 2
        return other

    def step(self, other=None):
        half = (self.kept.shape[0] // 2, self.kept.shape[1])
        self.kept, self.sent = call(
            fold_kernel,
            self.name,
            [],
            [Far(self.kept), self.receive() if other is None else other],
            [far(half, F32), (half, BF16)],
        )

    def last(self):
        while self.hop * 2 < lax.axis_size("dp"):
            self.step()
        return self.kept, self.receive()


def sum_over_dp(values):
    count = lax.axis_size("dp")
    values = values + lax.ppermute(values, "dp", [(i, i ^ 1) for i in range(count)])
    others = [
        lax.ppermute(values, "dp", [(i, i ^ k) for i in range(count)]) for k in range(2, count, 2)
    ]
    for other in others:
        values = values + other
    return values


def body(
    residual_in,
    norm_gain,
    w_zx,
    w_bc,
    w_dt,
    conv_x,
    conv_bc,
    dt_bias,
    a_log,
    d_skip,
    gate_gain,
    w_out,
    lengths,
    cotangent,
):
    shards = lax.axis_size("tensor")
    dp_count = lax.axis_size("dp")
    rows, depth = residual_in.shape
    inner = gate_gain.shape[1]
    heads = dt_bias.shape[1]
    width = inner // heads
    wide = w_bc.shape[2]
    total_rows = rows * shards
    inner_all = inner * shards
    slab = norm_gain.shape[1]
    index = lax.axis_index("tensor").reshape(1).astype(jnp.int32)
    place = lax.axis_index("dp").reshape(1).astype(jnp.int32)
    message = (rows, depth + LANES)

    order = range(LAYERS)
    few = jnp.concatenate(
        [
            w_dt.transpose(0, 2, 1).reshape(LAYERS * heads, slab),
            norm_gain,
            jnp.pad(conv_bc.reshape(LAYERS * 5, -1), ((0, 0), (0, slab - wide // dp_count))),
        ],
        axis=0,
    )
    few = jnp.pad(few, ((0, -few.shape[0] % 16), (0, 0)))
    x_blocks = gather_dp(w_zx[1, :, 1, :])
    few, x_blocks[dp_count // 2] = lax.optimization_barrier((few, x_blocks[dp_count // 2]))
    few = spread_out(few, "dp")
    residual_blocks = spread_out(residual_in, "tensor")
    late_blocks = spread_out(cotangent, "tensor")
    w_first = lax.all_gather(
        jnp.concatenate([w_zx[0, :, 1, :], w_zx[0, :, 0, :], w_out[0].T], axis=1), "dp", axis=0, tiled=True
    )
    w_last = lax.all_gather(
        jnp.concatenate([w_zx[1, :, 0, :], w_out[1].T], axis=1), "dp", axis=0, tiled=True
    )
    w_x = [Far(w_first, inner, 0)]
    w_gates = [Far(w_first, inner, 1), Far(w_last, inner, 0)]
    w_outs = [Far(w_first, inner, 2), Far(w_last, inner, 1)]
    piece = wide // shards
    maps = lax.dynamic_slice_in_dim(w_bc, index[0] * piece, piece, 2)
    (maps,) = call(
        pack_kernel,
        "pack_maps",
        [place],
        gather_dp(jnp.concatenate([maps[layer] for layer in order], axis=1)),
        [((depth, LAYERS * piece), BF16)],
    )
    w_bcs = call(
        unpack_maps_kernel,
        "unpack_maps",
        [index],
        spread_out(maps, "tensor"),
        [far((depth, wide), BF16)] * LAYERS,
    )
    params = []
    for layer in order:
        ends = jnp.stack([dt_bias[layer], a_log[layer]])
        params.append(
            jnp.concatenate(
                [
                    conv_x[layer],
                    jnp.repeat(d_skip[layer], width)[None],
                    gate_gain[layer][None],
                    jnp.pad(ends, ((0, 7), (0, inner - heads))),
                ],
                axis=0,
            )
        )
    few[1], params[0], params[1] = lax.optimization_barrier((few[1], params[0], params[1]))
    few = call(
        functools.partial(unpack_kernel, heads),
        "unpack",
        [place],
        few,
        [far((LANES, depth), BF16)] * LAYERS + [far((1, depth), F32)] * LAYERS + [far((5, wide), F32)] * LAYERS,
    )
    w_steps, gains, taps_bc = few[:LAYERS], few[LAYERS : 2 * LAYERS], few[2 * LAYERS :]
    params = [Far(part) for part in params]
    w_steps, gains, taps_bc, w_bcs = (
        [Far(part) for part in parts] for parts in (w_steps, gains, taps_bc, w_bcs)
    )

    flops = 2 * total_rows * depth * inner
    kept = []
    blocks = residual_blocks
    current = residual_in
    for layer in order:
        last = layer == LAYERS - 1
        outs = [
            far((total_rows, depth), BF16),
            far((total_rows, inner), F32),
            far((total_rows, wide), F32),
            far((total_rows, LANES), F32),
            far((total_rows, inner), F32),
        ]
        if layer:
            outs += [far((depth, inner), BF16), far((total_rows, LANES), F32)]
        normed, u_rows, bc_rows, q_rows, y_rows, *more = call(
            functools.partial(first_kernel, layer, shards, dp_count, width),
            f"mix_{layer}",
            [index, place],
            [
                *blocks,
                *(x_blocks if layer else w_x),
                w_bcs[layer],
                gains[layer],
                w_steps[layer],
                taps_bc[layer],
                params[layer],
            ],
            outs,
            flops * 3,
            [pltpu.VMEM((LANES, total_rows), F32)],
        )
        if layer:
            w_x.append(Far(more[0]))
            scales = more[1]
        arrays = [Far(normed), w_gates[layer], w_outs[layer], Far(y_rows), params[layer]]
        if last:
            gate, hidden, grad_all, grad_hidden, sums = call(
                functools.partial(last_second_kernel, shards),
                f"gate_{layer}",
                [index, lengths],
                [*late_blocks, *arrays],
                [
                    far((total_rows, inner), F32),
                    far((total_rows, inner), BF16),
                    far((total_rows, depth), BF16),
                    far((total_rows, inner), F32),
                    ((8, total_rows), F32),
                ],
                flops * 2,
            )
            sums = spread_out(sums, "tensor")
        else:
            gate, *sent = call(
                functools.partial(second_kernel, shards),
                f"gate_{layer}",
                [index, lengths],
                arrays,
                [far((total_rows, inner), F32)] + [(message, BF16)] * shards,
                flops * 2,
                [pltpu.VMEM((total_rows, depth + LANES), BF16)],
            )
            sent = exchange(sent, "tensor")
        kept.append([normed, u_rows, bc_rows, q_rows, y_rows, gate, current])
        if not last:
            current, branch, packed = call(
                functools.partial(residual_kernel, shards, inner_all),
                f"residual_{layer}",
                [],
                [*sent, Far(current), gains[layer + 1]],
                [far((rows, depth), F32), far((rows, depth), F32), (message, BF16)],
            )
            blocks = spread_out(packed, "tensor")

    grad_now = cotangent
    few_x, few_bc, few_gain = {}, {}, {}
    for layer in reversed(order):
        last = layer == LAYERS - 1
        normed, u_rows, bc_rows, q_rows, y_rows, gate, rows_in = kept[layer]
        outs = [
            ((total_rows, inner), F32),
            ((total_rows, inner), BF16),
            ((8, inner), F32),
        ]
        slots = depth // 512
        if last:
            grad_y, grad_gate, gain_sum, grads, out_scales = call(
                functools.partial(last_gate_kernel, shards, inner_all),
                f"gate_back_{layer}",
                [lengths],
                [*sums, Far(y_rows), Far(gate), Far(grad_hidden), params[layer], Far(normed), Far(grad_all)],
                outs
                + [((depth, 2 * inner), BF16, "raw"), far((total_rows, LANES), F32)],
                flops * 2,
                [pltpu.VMEM((slots, 512, 2 * inner), BF16), pltpu.SemaphoreType.DMA((slots,))],
            )
            grads, grad_y = lax.optimization_barrier((grads, grad_y))
            last_early = lax.psum_scatter(grads, "dp", scatter_dimension=0, tiled=True)
        else:
            grad_y, grad_gate, gain_sum, hidden, grad_all = call(
                functools.partial(gate_kernel, shards, inner_all),
                f"gate_back_{layer}",
                [index, lengths],
                [*blocks, Far(scales), w_outs[layer], Far(y_rows), Far(gate), params[layer], Far(normed)],
                outs + [((total_rows, inner), BF16), ((total_rows, depth), BF16)],
                flops * 3,
                [pltpu.VMEM((total_rows, LANES), F32)],
            )
        du, dbc, dq, few_x[layer], few_bc[layer], *pieces_bc = call(
            functools.partial(scan_back_kernel, width),
            f"mix_back_{layer}",
            [index],
            [
                Far(u_rows),
                Far(bc_rows),
                Far(q_rows),
                Far(y_rows),
                grad_y,
                gain_sum,
                taps_bc[layer],
                params[layer],
            ],
            [
                ((total_rows, inner), BF16),
                ((total_rows, wide), BF16),
                ((total_rows, LANES), BF16),
                far((8, inner), F32),
                far((8, wide), F32),
            ]
            + [((total_rows, LANES), BF16)] * shards,
            flops * 2,
            [
                pltpu.VMEM((LANES, total_rows), F32),
                pltpu.VMEM((total_rows, total_rows), F32),
                pltpu.VMEM((total_rows, LANES), F32),
                pltpu.VMEM((total_rows, LANES), F32),
                pltpu.VMEM((8, LANES), F32),
            ],
        )
        if not last:
            other = last_halves.receive()
            du, other = lax.optimization_barrier((du, other))
            (grads,) = call(
                grads_kernel,
                f"grads_{layer}",
                [],
                [Far(normed), grad_gate, grad_all, hidden, du],
                [((depth, 3 * inner), BF16, "raw")],
                flops * 3,
                [pltpu.VMEM((slots, 512, 3 * inner), BF16), pltpu.SemaphoreType.DMA((slots,))],
            )
            grads, du, dq, last_halves.kept = lax.optimization_barrier((grads, du, dq, last_halves.kept))
            last_halves.step(other)
            first_early = lax.psum_scatter(grads, "dp", scatter_dimension=0, tiled=True)
        pieces = call(
            functools.partial(input_grad_kernel, shards),
            f"input_grad_{layer}",
            [index],
            [
                grad_gate,
                du,
                dbc,
                dq,
                w_x[layer],
                w_gates[layer],
                w_bcs[layer],
                w_steps[layer],
            ],
            [((rows, depth), BF16)] * shards,
            flops * 2,
            [pltpu.VMEM((total_rows, depth), BF16)],
        )
        pieces = exchange(pieces, "tensor")
        pieces_bc = exchange(pieces_bc, "tensor")
        if last:
            messages = call(
                functools.partial(branch_kernel, shards),
                "branch",
                [index],
                [Far(hidden), w_outs[layer], Far(out_scales)],
                [((rows, depth), BF16)] * shards,
                flops,
                [pltpu.VMEM((total_rows, depth), BF16)],
            )
            (output,) = call(
                functools.partial(output_kernel, shards),
                "output",
                [],
                [*exchange(messages, "tensor"), Far(current)],
                [far((rows, depth), F32)],
            )
        if last:
            tall = (depth // 2, inner + LANES)
            mine, theirs = call(
                functools.partial(late_grads_kernel, shards, dp_count),
                f"late_{layer}",
                [place],
                [Far(normed), du, dq, *pieces_bc],
                [far(tall, BF16), (tall, BF16)],
                flops * 2,
                [pltpu.VMEM((depth, inner + LANES), BF16)],
            )
            last_halves = Halves(f"fold_{layer}", mine, theirs)
            last_halves.step()
            pieces[-1], last_halves.sent = lax.optimization_barrier((pieces[-1], last_halves.sent))
        else:
            tall = (depth // 2, LANES)
            mine, theirs = call(
                functools.partial(late_tail_kernel, shards, dp_count),
                f"late_{layer}",
                [place],
                [Far(normed), dq, *pieces_bc],
                [far(tall, BF16), (tall, BF16)],
                flops * 2,
                [pltpu.VMEM((depth, LANES), BF16)],
            )
            halves = Halves(f"fold_{layer}", mine, theirs)
            halves.step()
            first_kept, first_part = halves.last()
            last_kept, last_part = last_halves.last()
            pieces[1], last_part = lax.optimization_barrier((pieces[1], last_part))
        arrays = [*pieces, Far(rows_in), gains[layer], Far(grad_now)]
        outs = [far((rows, depth), F32), far((8, depth), F32)]
        if layer:
            arrays.append(Far(branch))
            outs.append((message, BF16))
        back = call(
            functools.partial(norm_back_kernel, shards, bool(layer)),
            f"norm_back_{layer}",
            [],
            arrays,
            outs,
        )
        grad_now, few_gain[layer] = back[:2]
        if layer:
            blocks = spread_out(back[2], "tensor")

    shared = jnp.stack(
        [
            jnp.concatenate([few_gain[layer][0], few_bc[layer][:5].reshape(-1)])
            for layer in order
        ]
    )
    shared = functools.reduce(jnp.add, spread_out(shared, "tensor"))
    own = jnp.stack([few_x[layer] for layer in order]).reshape(-1, LANES)
    few = jnp.concatenate([own, shared.reshape(-1, LANES)], axis=0)
    few = sum_over_dp(few)
    own = few[: own.shape[0]].reshape(LAYERS, 8, inner)
    shared = few[own.size // LANES :].reshape(LAYERS, -1)
    grad_gain = lax.dynamic_slice_in_dim(shared[:, :depth], place[0] * slab, slab, 1)
    grad_conv_bc = lax.dynamic_slice_in_dim(
        shared[:, depth:].reshape(LAYERS, 5, wide), place[0] * (wide // dp_count), wide // dp_count, 2
    )
    grad_tail, low = call(
        tails_kernel,
        "tails",
        [],
        [Far(first_kept), first_part, Far(last_kept), last_part],
        [far((slab, LAYERS * LANES), F32), ((slab, LAYERS * LANES), BF16)],
    )
    grad_bc = call(
        widen_kernel,
        "widen",
        [index],
        spread_out(low, "tensor"),
        [far((slab, wide), F32)] * LAYERS,
    )
    grad_zx, grad_out = call(
        finish_kernel,
        "finish",
        [],
        [Far(first_early), Far(last_early), Far(last_kept), last_part],
        [far((LAYERS, slab, 2, inner), F32), far((LAYERS, slab, inner), F32)],
    )
    grad_out = grad_out.transpose(0, 2, 1)
    grad_bc = jnp.stack([grad_bc[layer] for layer in order])
    grad_dt = jnp.stack(
        [grad_tail[:, layer * LANES + HALF : layer * LANES + HALF + heads] for layer in order]
    )
    return (
        output,
        grad_now,
        grad_gain,
        grad_zx,
        grad_bc,
        grad_dt,
        own[:, :5],
        grad_conv_bc,
        own[:, 6, :heads],
        own[:, 6, LANES : LANES + heads],
        own[:, 6, 2 * LANES : 2 * LANES + heads],
        own[:, 5],
        grad_out,
    )


def solution(mesh):
    return jax.shard_map(
        body,
        mesh=mesh,
        in_specs=(
            P(("dp", "tensor"), None),
            P(None, "dp"),
            P(None, "dp", None, "tensor"),
            P(None, "dp", None),
            P(None, "dp", "tensor"),
            P(None, None, "tensor"),
            P(None, None, "dp"),
            P(None, "tensor"),
            P(None, "tensor"),
            P(None, "tensor"),
            P(None, "tensor"),
            P(None, "tensor", "dp"),
            P("dp"),
            P(("dp", "tensor"), None),
        ),
        out_specs=(
            P(("dp", "tensor"), None),
            P(("dp", "tensor"), None),
            P(None, "dp"),
            P(None, "dp", None, "tensor"),
            P(None, "dp", None),
            P(None, "dp", "tensor"),
            P(None, None, "tensor"),
            P(None, None, "dp"),
            P(None, "tensor"),
            P(None, "tensor"),
            P(None, "tensor"),
            P(None, "tensor"),
            P(None, "tensor", "dp"),
        ),
        check_vma=False,
    )
```

```python
import functools
import math

import jax
import jax.numpy as jnp
from jax import lax
from jax.experimental import pallas as pl
from jax.experimental.pallas import tpu as pltpu
from jax.sharding import PartitionSpec as P

LAYERS = 2
EPSILON = 1e-05
LANES = 128
HALF = 64
F32 = jnp.float32
BF16 = jnp.bfloat16
EXACT = lax.Precision.HIGHEST


class Far:
    def __init__(self, array, columns=None, place=0):
        self.array, self.place = array, place
        self.columns = array.shape[1] if columns is None else columns
        self.shape, self.dtype = (array.shape[0], self.columns), array.dtype


class Raw:
    def __init__(self, array):
        self.array, self.shape, self.dtype = array, array.shape, array.dtype


class Arrival:
    def __init__(self, copy, ref):
        self.copy, self.ref, self.waiting = copy, ref, True
        self.shape = ref.shape
        copy.start()

    def wait(self):
        if self.waiting:
            self.copy.wait()
            self.waiting = False

    def __getitem__(self, at):
        self.wait()
        return self.ref[at]


class Departure:
    def __init__(self, copy, ref):
        self.copy, self.ref, self.started = copy, ref, False
        self.shape = ref.shape

    def send(self):
        if not self.started:
            self.copy.start()
            self.started = True

    def __getitem__(self, at):
        return self.ref[at]

    def __setitem__(self, at, values):
        self.ref[at] = values
        if at is Ellipsis:
            self.send()


def dot(left, right, left_dim=1, right_dim=0, precision=None):
    return lax.dot_general(
        left,
        right,
        (((left_dim,), (right_dim,)), ((), ())),
        precision=precision,
        preferred_element_type=F32,
    )


def iota(shape, dim):
    return lax.broadcasted_iota(jnp.int32, shape, dim)


def sigmoid(values):
    return 1.0 / (1.0 + jnp.exp(-values))


def softplus(values):
    return jnp.maximum(values, 0.0) + jnp.log1p(jnp.exp(-jnp.abs(values)))


def rows_later(values, steps):
    return jnp.where(iota(values.shape, 0) >= steps, pltpu.roll(values, steps, 0), 0.0)


def rows_earlier(values, steps):
    total = values.shape[0]
    return jnp.where(
        iota(values.shape, 0) < total - steps, pltpu.roll(values, total - steps, 0), 0.0
    )


def conv(values, taps):
    result = taps[4:5, :] + taps[3:4, :] * values
    for offset in range(3):
        result = result + taps[offset : offset + 1, :] * rows_later(values, 3 - offset)
    return result


def conv_back(values, taps, grad):
    back = taps[3:4, :] * grad
    for offset in range(3):
        back = back + taps[offset : offset + 1, :] * rows_earlier(grad, 3 - offset)
    sums = [
        jnp.sum(grad * rows_later(values, 3 - offset), axis=0, keepdims=True)
        for offset in range(3)
    ]
    sums.append(jnp.sum(grad * values, axis=0, keepdims=True))
    sums.append(jnp.sum(grad, axis=0, keepdims=True))
    return back, sums


def pair_of_parts(column):
    high = column.astype(BF16).astype(F32)
    wide = jnp.broadcast_to(high, (column.shape[0], LANES))
    rest = jnp.broadcast_to(column - high, (column.shape[0], LANES))
    return jnp.where(iota(wide.shape, 1) < HALF, wide, rest).astype(BF16)


def joined_parts(message, width):
    return message[:, width : width + 1].astype(F32) + message[
        :, width + HALF : width + HALF + 1
    ].astype(F32)


def three_parts(values):
    high = values.astype(BF16)
    rest = values - high.astype(F32)
    middle = rest.astype(BF16)
    return high, middle, (rest - middle.astype(F32)).astype(BF16)


def spread_sum(parts, spread):
    spread = spread.astype(BF16)
    return dot(parts[0], spread) + dot(parts[1], spread) + dot(parts[2], spread)


def send(output):
    if isinstance(output, Departure):
        output.send()


def ready(operand):
    if isinstance(operand, Arrival):
        operand.wait()
    return operand.ref if isinstance(operand, (Arrival, Departure)) else operand


def step_state(q_rows, dt_bias, a_log):
    rows = q_rows.shape[0]
    shifted = q_rows + dt_bias
    steps = softplus(shifted)
    rates = -jnp.exp(a_log)
    below = (iota((rows, rows), 0) >= iota((rows, rows), 1)).astype(F32)
    running = dot(below, steps * rates, precision=EXACT)
    return shifted, steps, rates, running


SKIP_ROW, GAIN_ROW, BIAS_ROW, RATE_ROW = 5, 6, 7, 8


def mixer_forward(u_ref, y_ref, params, turned, bc_rows, q_rows, conv_bc, width):
    rows, inner = u_ref.shape
    states = bc_rows.shape[1] // 2
    maps = conv(bc_rows, conv_bc)
    maps = maps * sigmoid(maps)
    _, steps, _, running = step_state(
        q_rows, params[BIAS_ROW : BIAS_ROW + 1, :LANES], params[RATE_ROW : RATE_ROW + 1, :LANES]
    )
    turned[...] = running.T
    scores = dot(maps[:, states:], maps[:, :states], 1, 1, EXACT)
    steps = three_parts(steps)
    causal = iota((rows, rows), 0) >= iota((rows, rows), 1)
    lane = iota((rows, LANES), 1)
    per_block = LANES // width

    def block_step(block):
        at = pl.ds(block * LANES, LANES)
        mixed_in = conv(u_ref[:, at], params[:5, at])
        mixed_in = mixed_in * sigmoid(mixed_in)
        shape = (LANES, LANES)
        heads = block * per_block + iota(shape, 1) // width
        scaled = (mixed_in * spread_sum(steps, heads == iota(shape, 0))).astype(BF16)
        total = None
        for slot in range(per_block):
            head = block * per_block + slot
            gap = running[:, head : head + 1] - turned[head : head + 1, :]
            decay = jnp.exp(jnp.where(causal, gap, -1e30))
            part = dot((decay * scores).astype(BF16), scaled)
            total = part if slot == 0 else jnp.where(lane < slot * width, total, part)
        y_ref[:, at] = total + params[SKIP_ROW : SKIP_ROW + 1, at] * mixed_in

    for block in range(inner // LANES):
        block_step(block)


def gather_rows(target, index, blocks, width):
    rows = blocks[0].shape[0]
    for order, block in enumerate(blocks):
        place = pl.multiple_of((index ^ order) * rows, rows)
        target[pl.ds(place, rows), :] = block[:, :width]


def unpack_kernel(heads, *refs):
    index = refs[0][0]
    outs = refs[-3 * LAYERS :]
    blocks = refs[1 : -3 * LAYERS]
    slab = blocks[0].shape[1]
    depth, wide = outs[LAYERS].shape[1], outs[2 * LAYERS].shape[1]
    piece = wide // len(blocks)

    def placed(start, stop, held, total):
        result = None
        for order, block in enumerate(blocks):
            shape = (held, total)
            ones = iota(shape, 1) - (index ^ order) * held == iota(shape, 0)
            part = dot(block[...][start:stop, :held], ones.astype(BF16))
            result = part if result is None else result + part
        return result

    norm_at = LAYERS * heads
    taps_at = norm_at + LAYERS
    rows = placed(0, taps_at, slab, depth)
    taps = placed(taps_at, taps_at + 5 * LAYERS, piece, wide)
    for layer in range(LAYERS):
        steps = rows[layer * heads : (layer + 1) * heads, :]
        padding = jnp.zeros((LANES - heads, depth), F32)
        outs[layer][...] = jnp.concatenate([steps, padding], axis=0).astype(BF16)
        outs[LAYERS + layer][...] = rows[norm_at + layer : norm_at + layer + 1, :]
        outs[2 * LAYERS + layer][...] = taps[5 * layer : 5 * layer + 5, :]


def pack_kernel(index, *refs):
    blocks, (out,) = refs[:-1], refs[-1:]
    gather_rows(out, index[0], blocks, out.shape[1])


def unpack_maps_kernel(index, *refs):
    blocks, outs = refs[:-LAYERS], refs[-LAYERS:]
    piece = blocks[0].shape[1] // LAYERS
    for layer, out in enumerate(outs):
        total = None
        for order, block in enumerate(blocks):
            shape = (LAYERS * piece, out.shape[1])
            row = iota(shape, 0) - layer * piece
            ones = (row == iota(shape, 1) - (index[0] ^ order) * piece) & (row >= 0) & (row < piece)
            part = dot(block[...], ones.astype(BF16))
            total = part if total is None else total + part
        out[...] = total.astype(BF16)


def first_kernel(layer, shards, slabs, width, *refs):
    index, place = refs[0][0], refs[1][0]
    blocks, refs = refs[2 : 2 + shards], refs[2 + shards :]
    if layer:
        weights, refs = refs[:slabs], refs[slabs:]
        w_in, scales_out = refs[-3:-1]
        refs = refs[:-3] + refs[-1:]
    else:
        w_in, refs = refs[0], refs[1:]
    w_bc, gain, w_dt, conv_bc, params, normed, u_out, bc_out, q_out, y_out, turned = refs
    depth = normed.shape[1]
    inner = u_out.shape[1]
    rows = blocks[0].shape[0]
    if layer == 0:
        for order, block in enumerate(blocks):
            values = block[...].astype(F32)
            scale = lax.rsqrt(jnp.mean(values * values, axis=1, keepdims=True) + EPSILON)
            start = pl.multiple_of((index ^ order) * rows, rows)
            normed[pl.ds(start, rows), :] = (values * scale * gain[...]).astype(BF16)
    else:
        gather_rows(normed, index, blocks, depth)
        for order, block in enumerate(blocks):
            start = pl.multiple_of((index ^ order) * rows, rows)
            scales_out[pl.ds(start, rows), :] = jnp.broadcast_to(
                joined_parts(block, depth), (rows, LANES)
            )
        gather_rows(w_in, place, weights, inner)
        send(scales_out)
        send(w_in)
    send(normed)
    rows_in = normed[...]
    bc_rows = dot(rows_in, w_bc[...])
    q_rows = dot(rows_in, w_dt[...], 1, 1)
    u_rows = dot(rows_in, w_in[...])
    u_out[...] = u_rows
    bc_out[...] = bc_rows
    q_out[...] = q_rows
    mixer_forward(
        ready(u_out), ready(y_out), ready(params), turned, bc_rows, q_rows, conv_bc[...], width
    )


def live_column(length, rows):
    return (iota((rows, 1), 0) < length).astype(F32)


def second_kernel(shards, *refs):
    index = refs[0][0]
    length = refs[1][0]
    normed, w_gate, w_out, y_rows, params, z_out = refs[2:8]
    messages, scratch = refs[8 : 8 + shards], refs[8 + shards]
    depth = normed.shape[1]
    part = messages[0].shape[0]
    gate = dot(normed[...], w_gate[...])
    z_out[...] = gate
    gated = y_rows[...] * (gate * sigmoid(gate))
    live = live_column(length, y_rows.shape[0])
    hidden = (gated * params[GAIN_ROW : GAIN_ROW + 1, :] * live).astype(BF16)
    scratch[:, :depth] = dot(hidden, w_out[...], 1, 1).astype(BF16)
    scratch[:, depth:] = pair_of_parts(jnp.sum(gated * gated, axis=1, keepdims=True))
    for order, message in enumerate(messages):
        place = pl.multiple_of((index ^ order) * part, part)
        message[...] = scratch[pl.ds(place, part), :]


def last_second_kernel(shards, *refs):
    index = refs[0][0]
    length = refs[1][0]
    blocks, refs = refs[2 : 2 + shards], refs[2 + shards :]
    normed, w_gate, w_out, y_rows, params = refs[:5]
    z_out, hidden_out, grad_all, grad_hidden_out, sums_out = refs[5:]
    rows = y_rows.shape[0]
    gather_rows(grad_all, index, blocks, normed.shape[1])
    send(grad_all)
    grad_hidden = dot(grad_all[...], w_out[...])
    grad_hidden_out[...] = grad_hidden
    gate = dot(normed[...], w_gate[...])
    z_out[...] = gate
    gated = y_rows[...] * (gate * sigmoid(gate))
    squares = jnp.sum(gated * gated, axis=1, keepdims=True)
    weighted = gated * params[GAIN_ROW : GAIN_ROW + 1, :] * live_column(length, rows)
    hidden_out[...] = weighted.astype(BF16)
    products = jnp.sum(grad_hidden * weighted, axis=1, keepdims=True)
    lane = iota((rows, LANES), 1)
    table = jnp.where(lane == 0, squares, jnp.where(lane == 1, products, 0.0))
    sums_out[...] = table.T[:8, :]


def branch_kernel(shards, *refs):
    index = refs[0][0]
    hidden, w_out, scales = refs[1:4]
    messages, scratch = refs[4 : 4 + shards], refs[4 + shards]
    part = messages[0].shape[0]
    scratch[...] = (scales[:, 0:1] * dot(hidden[...], w_out[...], 1, 1)).astype(BF16)
    for order, message in enumerate(messages):
        place = pl.multiple_of((index ^ order) * part, part)
        message[...] = scratch[pl.ds(place, part), :]


def gate_back(length, scale, product, inner_all, y_rows, gate, grad_hidden, gate_gain):
    live = live_column(length, y_rows.shape[0])
    turn = sigmoid(gate)
    opened = gate * turn
    gated = y_rows * opened
    grad_live = grad_hidden * live
    grad_gain = jnp.sum(grad_live * gated * scale, axis=0, keepdims=True)
    grad_gated = scale * grad_live * gate_gain - gated * (
        scale * scale * scale * (product / inner_all)
    )
    hidden = (gated * scale * gate_gain * live).astype(BF16)
    grad_y = grad_gated * opened
    grad_gate = grad_gated * y_rows * (turn * (1.0 + gate * (1.0 - turn)))
    return hidden, grad_y, grad_gate.astype(BF16), grad_gain


def weight_grads(pairs, out, staged, sems):
    slots, part = staged.shape[:2]
    copies = []
    for slot in range(slots):
        cut = slice(slot * part, (slot + 1) * part)
        at = 0
        for left, right in pairs:
            columns = right.shape[1]
            staged[slot, :, at : at + columns] = dot(left[:, cut], right[...], 0, 0).astype(BF16)
            at += columns
        copies.append(
            pltpu.make_async_copy(staged.at[slot], out.at[pl.ds(slot * part, part), :], sems.at[slot])
        )
        copies[-1].start()
    for copy in copies:
        copy.wait()


def last_gate_kernel(shards, inner_all, *refs):
    length = refs[0][0]
    sums, refs = refs[1 : 1 + shards], refs[1 + shards :]
    y_rows, gate, grad_hidden, params, normed, grad_all = refs[:6]
    grad_y_out, grad_gate_out, gain_out, grads_out, scale_out, staged, sems = refs[6:]
    rows = y_rows.shape[0]
    total = sums[0][...]
    for other in sums[1:]:
        total = total + other[...]
    table = jnp.concatenate([total, jnp.zeros((LANES - 8, rows), F32)], axis=0).T
    scale = lax.rsqrt(table[:, 0:1] / inner_all + EPSILON)
    scale_out[...] = jnp.broadcast_to(scale, scale_out.shape)
    hidden, grad_y, grad_gate, grad_gain = gate_back(
        length,
        scale,
        table[:, 1:2],
        inner_all,
        y_rows[...],
        gate[...],
        grad_hidden[...],
        params[GAIN_ROW : GAIN_ROW + 1, :],
    )
    grad_y_out[...] = grad_y
    grad_gate_out[...] = grad_gate
    gain_out[...] = jnp.broadcast_to(grad_gain, gain_out.shape)
    weight_grads(((normed, grad_gate), (grad_all, hidden)), grads_out, staged, sems)


def gate_kernel(shards, inner_all, *refs):
    index = refs[0][0]
    length = refs[1][0]
    blocks, refs = refs[2 : 2 + shards], refs[2 + shards :]
    scales, w_out, y_rows, gate, params, normed = refs[:6]
    grad_y_out, grad_gate_out, gain_out, hidden_out, grad_all, products = refs[6:]
    depth = grad_all.shape[1]
    part = blocks[0].shape[0]
    gather_rows(grad_all, index, blocks, depth)
    for order, block in enumerate(blocks):
        place = pl.multiple_of((index ^ order) * part, part)
        products[pl.ds(place, part), :] = jnp.broadcast_to(
            joined_parts(block, depth), (part, LANES)
        )
    hidden, grad_y, grad_gate, grad_gain = gate_back(
        length,
        scales[:, 0:1],
        products[:, 0:1],
        inner_all,
        y_rows[...],
        gate[...],
        dot(grad_all[...], w_out[...]),
        params[GAIN_ROW : GAIN_ROW + 1, :],
    )
    grad_y_out[...] = grad_y
    grad_gate_out[...] = grad_gate
    hidden_out[...] = hidden
    gain_out[...] = jnp.broadcast_to(grad_gain, gain_out.shape)


def grads_kernel(normed, grad_gate, grad_all, hidden, du, out, staged, sems):
    weight_grads(((normed, grad_gate), (grad_all, hidden), (normed, du)), out, staged, sems)


def scan_back_kernel(width, index, *refs):
    u_ref, bc_ref, q_ref, y_ref, grad_ref, gain_sum, conv_bc, params_ref = refs[:8]
    du_out, dbc_out, dq_out, sums_out, sums_bc = refs[8:13]
    pieces = refs[13:-5]
    turned, grad_scores, grad_running, grad_steps, skip_sum = refs[-5:]
    params, u_ref, y_ref, grad_ref = ready(params_ref), ready(u_ref), ready(y_ref), ready(grad_ref)
    sums_x, du_ref = ready(sums_out), ready(du_out)
    bc_rows, q_rows = bc_ref[...], q_ref[...]
    rows, inner = u_ref.shape
    states = bc_rows.shape[1] // 2
    taps_bc = conv_bc[...]
    pre_bc = conv(bc_rows, taps_bc)
    turn_bc = sigmoid(pre_bc)
    maps = pre_bc * turn_bc
    shifted, steps, rates, running = step_state(
        q_rows, params[BIAS_ROW : BIAS_ROW + 1, :LANES], params[RATE_ROW : RATE_ROW + 1, :LANES]
    )
    turned[...] = running.T
    b_rows, c_rows = maps[:, :states], maps[:, states:]
    scores = dot(b_rows, c_rows, 1, 1, EXACT)
    steps_parts = three_parts(steps)
    causal = iota((rows, rows), 0) <= iota((rows, rows), 1)
    lane = iota((rows, LANES), 1)
    per_block = LANES // width
    for total in (grad_scores, grad_running, grad_steps, skip_sum):
        total[...] = jnp.zeros(total.shape, F32)

    def block_step(block):
        at = pl.ds(block * LANES, LANES)
        u_rows, grad_y = u_ref[:, at], grad_ref[:, at]
        taps_x, skips = params[:5, at], params[SKIP_ROW : SKIP_ROW + 1, at]
        pre_x = conv(u_rows, taps_x)
        turn_x = sigmoid(pre_x)
        mixed_in = pre_x * turn_x
        shape = (LANES, LANES)
        heads = block * per_block + iota(shape, 1) // width
        steps_wide = spread_sum(steps_parts, heads == iota(shape, 0))
        scaled = (mixed_in * steps_wide).astype(BF16)
        grad_low = grad_y.astype(BF16)
        grad_scaled = None
        for slot in range(per_block):
            head = block * per_block + slot
            gap = turned[head : head + 1, :] - running[:, head : head + 1]
            decay = jnp.exp(jnp.where(causal, gap, -1e30))
            part = dot((decay * scores).astype(BF16), grad_low)
            grad_scaled = part if slot == 0 else jnp.where(lane < slot * width, grad_scaled, part)
            own = jnp.where(
                (lane >= slot * width) & (lane < (slot + 1) * width), scaled, jnp.zeros_like(scaled)
            )
            grad_scores[...] += dot(own, grad_low, 1, 1) * decay
        gather = block * per_block + iota(shape, 0) // width == iota(shape, 1)
        within = y_ref[:, at] - skips * mixed_in
        moved = grad_low.astype(F32) * within - scaled.astype(F32) * grad_scaled
        grad_running[...] += spread_sum(three_parts(moved), gather)
        grad_steps[...] += spread_sum(three_parts(mixed_in * grad_scaled), gather)
        skip_row = jnp.sum(grad_y * mixed_in, axis=0, keepdims=True)
        skip_sum[...] += spread_sum(three_parts(jnp.broadcast_to(skip_row, (8, LANES))), gather)
        grad_x = steps_wide * grad_scaled + skips * grad_y
        grad_x = grad_x * (turn_x * (1.0 + pre_x * (1.0 - turn_x)))
        du, tap_sums = conv_back(u_rows, taps_x, grad_x)
        du_ref[:, at] = du.astype(BF16)
        tap_sums.append(gain_sum[0:1, at])
        tap_sums.append(jnp.zeros((2, LANES), F32))
        sums_x[:, at] = jnp.concatenate(tap_sums, axis=0)

    for block in range(inner // LANES):
        block_step(block)
    grad_b = dot(grad_scores[...], c_rows, precision=EXACT)
    grad_c = dot(grad_scores[...], b_rows, 0, 0, EXACT)
    above = (iota((rows, rows), 0) <= iota((rows, rows), 1)).astype(F32)
    grad_decay = dot(above, grad_running[...], precision=EXACT)
    grad_q = (grad_steps[...] + grad_decay * rates) * sigmoid(shifted)
    dq_out[...] = grad_q.astype(BF16)
    sums_x[6:7, :LANES] = jnp.sum(grad_q, axis=0, keepdims=True)
    sums_x[6:7, LANES : 2 * LANES] = jnp.sum(grad_decay * steps, axis=0, keepdims=True) * rates
    sums_x[6:7, 2 * LANES : 3 * LANES] = skip_sum[0:1, :]
    grad_bc = jnp.concatenate([grad_b, grad_c], axis=1)
    grad_bc = grad_bc * (turn_bc * (1.0 + pre_bc * (1.0 - turn_bc)))
    dbc, tap_sums = conv_back(bc_rows, taps_bc, grad_bc)
    low = dbc.astype(BF16)
    dbc_out[...] = low
    piece = low.shape[1] // len(pieces)
    for order, out in enumerate(pieces):
        shape = (low.shape[1], LANES)
        ones = iota(shape, 0) - (index[0] ^ order) * piece == iota(shape, 1)
        ones = ones & (iota(shape, 1) < piece)
        out[...] = dot(low, ones.astype(BF16)).astype(BF16)
    tap_sums.append(jnp.zeros((3, low.shape[1]), F32))
    sums_bc[...] = jnp.concatenate(tap_sums, axis=0)


def halving_order(count):
    order = [0]
    step = count // 2
    while step > 1:
        order = order + [place + step for place in order]
        step //= 2
    return order


def late_tail(parts, dq):
    total = parts[0][...].astype(F32)
    for other in parts[1:]:
        total = total + other[...].astype(F32)
    shape = (LANES, LANES)
    moved = (iota(shape, 1) - HALF == iota(shape, 0)).astype(BF16)
    tail = (total + dot(dq[...], moved)).astype(BF16)
    return tail


def split_slabs(place, slabs, scratch, mine, theirs):
    slab = scratch.shape[0] // slabs
    for slot, order in enumerate(halving_order(slabs)):
        cut = slice(slot * slab, (slot + 1) * slab)
        for out, flip in ((mine, 0), (theirs, 1)):
            start = pl.multiple_of((place[0] ^ (order + flip)) * slab, slab)
            out[cut, :] = scratch[pl.ds(start, slab), :]


def late_tail_kernel(shards, slabs, place, normed, dq, *refs):
    parts, (mine, theirs, scratch) = refs[:shards], refs[shards:]
    scratch[...] = dot(normed[...], late_tail(parts, dq), 0, 0).astype(BF16)
    split_slabs(place, slabs, scratch, mine, theirs)


def late_grads_kernel(shards, slabs, place, normed, du, dq, *refs):
    parts, (mine, theirs, scratch) = refs[:shards], refs[shards:]
    inner = du.shape[1]
    rows_in = normed[...]
    scratch[:, :inner] = dot(rows_in, du[...], 0, 0).astype(BF16)
    scratch[:, inner:] = dot(rows_in, late_tail(parts, dq), 0, 0).astype(BF16)
    split_slabs(place, slabs, scratch, mine, theirs)


def fold_kernel(mine, other, kept, sent):
    half = kept.shape[0]
    kept[...] = mine[:half, :].astype(F32) + other[:half, :].astype(F32)
    sent[...] = (mine[half:, :].astype(F32) + other[half:, :].astype(F32)).astype(BF16)


def tails_kernel(first_kept, first_part, last_kept, last_part, tail_out, low_out):
    tails = []
    for kept, part in ((first_kept, first_part), (last_kept, last_part)):
        inner = kept.shape[1] - LANES
        tails.append(kept[:, inner:] + part[:, inner:].astype(F32))
    tail = jnp.concatenate(tails, axis=1)
    low_out[...] = tail.astype(BF16)
    tail_out[...] = tail


def finish_kernel(layer, early, *refs):
    zx_out, out_out, zx_rows, out_rows, sems = refs[-5:]
    inner = out_rows.shape[1]
    zx_rows[:, 0, :] = early[:, :inner].astype(F32)
    if layer:
        kept, part = refs[:2]
        zx_rows[:, 1, :] = kept[:, :inner] + part[:, :inner].astype(F32)
    else:
        zx_rows[:, 1, :] = early[:, 2 * inner :].astype(F32)
    first = pltpu.make_async_copy(zx_rows, zx_out.at[layer], sems.at[0])
    first.start()
    out_rows[...] = early[:, inner : 2 * inner].astype(F32)
    second = pltpu.make_async_copy(out_rows, out_out.at[layer], sems.at[1])
    second.start()
    first.wait()
    second.wait()


def widen_kernel(index, *refs):
    blocks, outs = refs[:-LAYERS], refs[-LAYERS:]
    wide = outs[0].shape[1]
    piece = wide // len(blocks)
    for layer, out in enumerate(outs):
        total = None
        for order, block in enumerate(blocks):
            shape = (LANES, wide)
            lane = iota(shape, 1) - (index[0] ^ order) * piece
            ones = (lane == iota(shape, 0)) & (iota(shape, 0) < piece)
            part = dot(block[:, layer * LANES : (layer + 1) * LANES], ones.astype(BF16))
            total = part if total is None else total + part
        out[...] = total


def input_grad_kernel(shards, *refs):
    index = refs[0][0]
    grad_gate, du, dbc, dq, w_in, w_gate, w_bc, w_dt = refs[1:9]
    outs, scratch = refs[9 : 9 + shards], refs[9 + shards]
    part = outs[0].shape[0]
    total = dot(dbc[...], w_bc[...], 1, 1) + dot(dq[...], w_dt[...])
    total = total + dot(du[...], w_in[...], 1, 1)
    scratch[...] = (total + dot(grad_gate[...], w_gate[...], 1, 1)).astype(BF16)
    for order, out in enumerate(outs):
        place = pl.multiple_of((index ^ order) * part, part)
        out[...] = scratch[pl.ds(place, part), :]


def branch_total(messages, depth, inner_all):
    total = messages[0][:, :depth].astype(F32)
    squares = joined_parts(messages[0], depth)
    for other in messages[1:]:
        total = total + other[:, :depth].astype(F32)
        squares = squares + joined_parts(other, depth)
    return total, lax.rsqrt(squares / inner_all + EPSILON)


def residual_kernel(shards, inner_all, *refs):
    messages = refs[:shards]
    start, gain, current_out, branch_out, message_out = refs[shards:]
    depth = start.shape[1]
    branch, scale = branch_total(messages, depth, inner_all)
    current = start[...].astype(F32) + scale * branch
    current_out[...] = current
    branch_out[...] = branch
    norm = lax.rsqrt(jnp.mean(current * current, axis=1, keepdims=True) + EPSILON)
    message_out[:, :depth] = (current * norm * gain[...]).astype(BF16)
    message_out[:, depth:] = pair_of_parts(scale)


def output_kernel(shards, *refs):
    messages = refs[:shards]
    start, out = refs[shards:]
    total = start[...]
    for message in messages:
        total = total + message[...].astype(F32)
    out[...] = total


def norm_back_kernel(shards, last, *refs):
    blocks = refs[:shards]
    refs = refs[shards:]
    rows_in, gain, grad_in = refs[:3]
    current = rows_in[...].astype(F32)
    depth = current.shape[1]
    grad_normed = blocks[0][...].astype(F32)
    for other in blocks[1:]:
        grad_normed = grad_normed + other[...].astype(F32)
    norm = lax.rsqrt(jnp.mean(current * current, axis=1, keepdims=True) + EPSILON)
    weighted = grad_normed * gain[...]
    inner_product = jnp.mean(weighted * current, axis=1, keepdims=True)
    grad = grad_in[...].astype(F32) + norm * weighted - current * (norm * norm * norm * inner_product)
    gain_row = jnp.sum(grad_normed * current * norm, axis=0, keepdims=True)
    if last:
        branch, grad_out, gain_out, message_out = refs[3:]
        low = grad.astype(BF16)
        message_out[:, :depth] = low
        message_out[:, depth:] = pair_of_parts(
            jnp.sum(low.astype(F32) * branch[...], axis=1, keepdims=True)
        )
    else:
        grad_out, gain_out = refs[3:]
    grad_out[...] = grad
    gain_out[...] = jnp.broadcast_to(gain_row, gain_out.shape)


def call(kernel, name, scalars, arrays, outs, flops=0, scratch=(), vmem=24, aliases=None):
    far_in = [item for item in arrays if isinstance(item, Far)]
    far_out = [out for out in outs if out[2:] == ("far",)]
    specs, given, out_specs, shapes, held = [], [], [], [], 0
    for item in arrays:
        if isinstance(item, (Far, Raw)):
            specs.append(pl.BlockSpec(memory_space=pl.ANY))
            given.append(pltpu.with_memory_space_constraint(item.array, pltpu.HBM))
        else:
            specs.append(pl.BlockSpec(memory_space=pltpu.VMEM))
            given.append(item)
        held += math.prod(item.shape) * item.dtype.itemsize
    for shape, dtype, *kind in outs:
        out_specs.append(pl.BlockSpec(memory_space=pl.ANY if kind else pltpu.VMEM))
        shapes.append(pltpu.HBM(shape, dtype) if kind else jax.ShapeDtypeStruct(shape, dtype))
        held += math.prod(shape) * jnp.dtype(dtype).itemsize
    extra = [pltpu.VMEM(item.shape, item.dtype) for item in far_in]
    extra += [pltpu.VMEM(out[0], out[1]) for out in far_out]
    extra += [pltpu.SemaphoreType.DMA((max(1, len(far_in) + len(far_out)),))]

    def whole(*refs):
        refs = list(refs)
        own = len(refs) - len(extra)
        places, sems = refs[own:-1], refs[-1]
        refs = refs[:own]
        moved, slot = [], 0
        for order, item in enumerate(arrays):
            if isinstance(item, Far):
                at = len(scalars) + order
                source = refs[at]
                if item.columns != item.array.shape[1]:
                    source = source.at[:, pl.ds(item.place * item.columns, item.columns)]
                copy = pltpu.make_async_copy(source, places[slot], sems.at[slot])
                refs[at] = Arrival(copy, places[slot])
                moved.append(refs[at])
                slot += 1
        leaving = []
        for order, out in enumerate(outs):
            if out[2:] == ("far",):
                at = len(scalars) + len(arrays) + order
                copy = pltpu.make_async_copy(places[slot], refs[at], sems.at[slot])
                refs[at] = Departure(copy, places[slot])
                leaving.append(refs[at])
                slot += 1
        kernel(*refs)
        for item in moved:
            item.wait()
        for item in leaving:
            item.send()
        for item in leaving:
            item.copy.wait()

    return pl.pallas_call(
        whole,
        out_shape=tuple(shapes),
        in_specs=[pl.BlockSpec(memory_space=pltpu.SMEM)] * len(scalars) + specs,
        out_specs=tuple(out_specs),
        scratch_shapes=list(scratch) + extra,
        input_output_aliases=aliases or {},
        compiler_params=pltpu.CompilerParams(vmem_limit_bytes=vmem * 1024 * 1024),
        cost_estimate=pl.CostEstimate(flops=1, bytes_accessed=1, transcendentals=0),
        name=name,
    )(*scalars, *given)


def near(*parts):
    return parts if len(parts) > 1 else parts[0]


def far(shape, dtype):
    return (shape, dtype, "far")


def exchange(blocks, axis):
    count = lax.axis_size(axis)
    return [blocks[0]] + [
        lax.ppermute(blocks[k], axis, [(i, i ^ k) for i in range(count)]) for k in range(1, count)
    ]


def spread_out(block, axis):
    return exchange([block] * lax.axis_size(axis), axis)


def gather_dp(blocks):
    count = lax.axis_size("dp")
    hop = count // 2 // len(blocks)
    while hop:
        for k in list(blocks):
            blocks[k ^ hop] = lax.ppermute(blocks[k], "dp", [(i, i ^ hop) for i in range(count)])
        hop //= 2
    return [blocks[k] for k in range(count)]


def over_dp(block, hop):
    count = lax.axis_size("dp")
    return lax.ppermute(block, "dp", [(i, i ^ hop) for i in range(count)])


class Halves:
    def __init__(self, name, mine, theirs):
        self.name, self.kept, self.sent, self.hop = name, mine, theirs, 1

    def receive(self):
        other = over_dp(self.sent, self.hop)
        self.hop *= 2
        return other

    def step(self, other=None):
        half = (self.kept.shape[0] // 2, self.kept.shape[1])
        self.kept, self.sent = call(
            fold_kernel,
            self.name,
            [],
            [Far(self.kept), self.receive() if other is None else other],
            [far(half, F32), (half, BF16)],
        )

    def last(self):
        while self.hop * 2 < lax.axis_size("dp"):
            self.step()
        return self.kept, self.receive()


def sum_over_dp(values):
    count = lax.axis_size("dp")
    values = values + lax.ppermute(values, "dp", [(i, i ^ 1) for i in range(count)])
    others = [
        lax.ppermute(values, "dp", [(i, i ^ k) for i in range(count)]) for k in range(2, count, 2)
    ]
    for other in others:
        values = values + other
    return values


def body(
    residual_in,
    norm_gain,
    w_zx,
    w_bc,
    w_dt,
    conv_x,
    conv_bc,
    dt_bias,
    a_log,
    d_skip,
    gate_gain,
    w_out,
    lengths,
    cotangent,
):
    shards = lax.axis_size("tensor")
    dp_count = lax.axis_size("dp")
    rows, depth = residual_in.shape
    inner = gate_gain.shape[1]
    heads = dt_bias.shape[1]
    width = inner // heads
    wide = w_bc.shape[2]
    total_rows = rows * shards
    inner_all = inner * shards
    slab = norm_gain.shape[1]
    index = lax.axis_index("tensor").reshape(1).astype(jnp.int32)
    place = lax.axis_index("dp").reshape(1).astype(jnp.int32)
    message = (rows, depth + LANES)

    order = range(LAYERS)
    columns = [w_zx[0, :, 1, :], w_zx[0, :, 0, :], w_out[0].T]
    packed = jnp.concatenate(columns, axis=1)
    packed, w_dt = lax.optimization_barrier((packed, w_dt))
    w_first = lax.all_gather(packed, "dp", axis=0, tiled=True)
    x_half = [w_zx[1, :, 1, :], over_dp(w_zx[1, :, 1, :], dp_count // 2)]
    few = jnp.concatenate(
        [
            w_dt.transpose(0, 2, 1).reshape(LAYERS * heads, slab),
            norm_gain,
            jnp.pad(conv_bc.reshape(LAYERS * 5, -1), ((0, 0), (0, slab - wide // dp_count))),
        ],
        axis=0,
    )
    few = jnp.pad(few, ((0, -few.shape[0] % 16), (0, 0)))
    few, x_half[1] = lax.optimization_barrier((few, x_half[1]))
    few = spread_out(few, "dp")
    x_blocks = gather_dp({0: x_half[0], dp_count // 2: x_half[1]})
    residual_blocks = spread_out(residual_in, "tensor")
    late_blocks = spread_out(cotangent, "tensor")
    w_last = lax.all_gather(
        jnp.concatenate([w_zx[1, :, 0, :], w_out[1].T], axis=1), "dp", axis=0, tiled=True
    )
    w_x = [Far(w_first, inner, 0)]
    w_gates = [Far(w_first, inner, 1), Far(w_last, inner, 0)]
    w_outs = [Far(w_first, inner, 2), Far(w_last, inner, 1)]
    piece = wide // shards
    maps = lax.dynamic_slice_in_dim(w_bc, index[0] * piece, piece, 2)
    (maps,) = call(
        pack_kernel,
        "pack_maps",
        [place],
        gather_dp({0: jnp.concatenate([maps[layer] for layer in order], axis=1)}),
        [((depth, LAYERS * piece), BF16)],
    )
    w_bcs = call(
        unpack_maps_kernel,
        "unpack_maps",
        [index],
        spread_out(maps, "tensor"),
        [far((depth, wide), BF16)] * LAYERS,
    )
    params = []
    for layer in order:
        ends = jnp.stack([dt_bias[layer], a_log[layer]])
        params.append(
            jnp.concatenate(
                [
                    conv_x[layer],
                    jnp.repeat(d_skip[layer], width)[None],
                    gate_gain[layer][None],
                    jnp.pad(ends, ((0, 7), (0, inner - heads))),
                ],
                axis=0,
            )
        )
    few[1], params[0], params[1] = lax.optimization_barrier((few[1], params[0], params[1]))
    few = call(
        functools.partial(unpack_kernel, heads),
        "unpack",
        [place],
        few,
        [far((LANES, depth), BF16)] * LAYERS + [far((1, depth), F32)] * LAYERS + [far((5, wide), F32)] * LAYERS,
    )
    w_steps, gains, taps_bc = few[:LAYERS], few[LAYERS : 2 * LAYERS], few[2 * LAYERS :]
    params = [Far(part) for part in params]
    w_steps, gains, taps_bc, w_bcs = (
        [Far(part) for part in parts] for parts in (w_steps, gains, taps_bc, w_bcs)
    )

    flops = 2 * total_rows * depth * inner
    kept = []
    blocks = residual_blocks
    current = residual_in
    for layer in order:
        last = layer == LAYERS - 1
        long = near if last else far
        hold = near if last else Far
        outs = [
            long((total_rows, depth), BF16),
            far((total_rows, inner), F32),
            far((total_rows, wide), F32),
            far((total_rows, LANES), F32),
            long((total_rows, inner), F32),
        ]
        if layer:
            outs += [far((depth, inner), BF16), far((total_rows, LANES), F32)]
        normed, u_rows, bc_rows, q_rows, y_rows, *more = call(
            functools.partial(first_kernel, layer, shards, dp_count, width),
            f"mix_{layer}",
            [index, place],
            [
                *blocks,
                *(x_blocks if layer else w_x),
                w_bcs[layer],
                gains[layer],
                w_steps[layer],
                taps_bc[layer],
                params[layer],
            ],
            outs,
            flops * 3,
            [pltpu.VMEM((LANES, total_rows), F32)],
        )
        if layer:
            w_x.append(Far(more[0]))
            scales = more[1]
        arrays = [hold(normed), w_gates[layer], w_outs[layer], hold(y_rows), params[layer]]
        if last:
            gate, last_hidden, grad_all, grad_hidden, sums = call(
                functools.partial(last_second_kernel, shards),
                f"gate_{layer}",
                [index, lengths],
                [*late_blocks, *arrays],
                [
                    ((total_rows, inner), F32),
                    ((total_rows, inner), BF16),
                    ((total_rows, depth), BF16),
                    ((total_rows, inner), F32),
                    ((8, total_rows), F32),
                ],
                flops * 2,
            )
            sums = spread_out(sums, "tensor")
        else:
            gate, *sent = call(
                functools.partial(second_kernel, shards),
                f"gate_{layer}",
                [index, lengths],
                arrays,
                [far((total_rows, inner), F32)] + [(message, BF16)] * shards,
                flops * 2,
                [pltpu.VMEM((total_rows, depth + LANES), BF16)],
            )
            sent = exchange(sent, "tensor")
        kept.append([normed, u_rows, bc_rows, q_rows, y_rows, gate, current])
        if not last:
            current, branch, packed = call(
                functools.partial(residual_kernel, shards, inner_all),
                f"residual_{layer}",
                [],
                [*sent, Far(current), gains[layer + 1]],
                [far((rows, depth), F32), far((rows, depth), F32), (message, BF16)],
            )
            blocks = spread_out(packed, "tensor")

    grad_now = cotangent
    few_x, few_bc, few_gain = {}, {}, {}
    for layer in reversed(order):
        last = layer == LAYERS - 1
        normed, u_rows, bc_rows, q_rows, y_rows, gate, rows_in = kept[layer]
        hold = near if last else Far
        outs = [
            ((total_rows, inner), F32),
            ((total_rows, inner), BF16),
            ((8, inner), F32),
        ]
        slots = depth // 512
        if last:
            grad_y, grad_gate, gain_sum, grads, out_scales = call(
                functools.partial(last_gate_kernel, shards, inner_all),
                f"gate_back_{layer}",
                [lengths],
                [*sums, y_rows, gate, grad_hidden, params[layer], normed, grad_all],
                outs
                + [((depth, 2 * inner), BF16, "raw"), far((total_rows, LANES), F32)],
                flops * 2,
                [pltpu.VMEM((slots, 512, 2 * inner), BF16), pltpu.SemaphoreType.DMA((slots,))],
            )
            grads, grad_y = lax.optimization_barrier((grads, grad_y))
            last_early = lax.psum_scatter(grads, "dp", scatter_dimension=0, tiled=True)
        else:
            grad_y, grad_gate, gain_sum, hidden, grad_all = call(
                functools.partial(gate_kernel, shards, inner_all),
                f"gate_back_{layer}",
                [index, lengths],
                [*blocks, Far(scales), w_outs[layer], Far(y_rows), Far(gate), params[layer], Far(normed)],
                outs + [((total_rows, inner), BF16), ((total_rows, depth), BF16)],
                flops * 3,
                [pltpu.VMEM((total_rows, LANES), F32)],
            )
        du, dbc, dq, few_x[layer], few_bc[layer], *pieces_bc = call(
            functools.partial(scan_back_kernel, width),
            f"mix_back_{layer}",
            [index],
            [
                Far(u_rows),
                Far(bc_rows),
                Far(q_rows),
                hold(y_rows),
                grad_y,
                gain_sum,
                taps_bc[layer],
                params[layer],
            ],
            [
                ((total_rows, inner), BF16),
                ((total_rows, wide), BF16),
                ((total_rows, LANES), BF16),
                far((8, inner), F32),
                far((8, wide), F32),
            ]
            + [((total_rows, LANES), BF16)] * shards,
            flops * 2,
            [
                pltpu.VMEM((LANES, total_rows), F32),
                pltpu.VMEM((total_rows, total_rows), F32),
                pltpu.VMEM((total_rows, LANES), F32),
                pltpu.VMEM((total_rows, LANES), F32),
                pltpu.VMEM((8, LANES), F32),
            ],
        )
        if not last:
            other = last_halves.receive()
            du, other = lax.optimization_barrier((du, other))
            (grads,) = call(
                grads_kernel,
                f"grads_{layer}",
                [],
                [Far(normed), grad_gate, grad_all, hidden, du],
                [((depth, 3 * inner), BF16, "raw")],
                flops * 3,
                [pltpu.VMEM((slots, 512, 3 * inner), BF16), pltpu.SemaphoreType.DMA((slots,))],
            )
            grads, du, dq, last_halves.kept = lax.optimization_barrier((grads, du, dq, last_halves.kept))
            last_halves.step(other)
            last_hidden, last_halves.sent = lax.optimization_barrier((last_hidden, last_halves.sent))
            first_early = lax.psum_scatter(grads, "dp", scatter_dimension=0, tiled=True)
        pieces = call(
            functools.partial(input_grad_kernel, shards),
            f"input_grad_{layer}",
            [index],
            [
                grad_gate,
                du,
                dbc,
                dq,
                w_x[layer],
                w_gates[layer],
                w_bcs[layer],
                w_steps[layer],
            ],
            [((rows, depth), BF16)] * shards,
            flops * 2,
            [pltpu.VMEM((total_rows, depth), BF16)],
        )
        pieces = exchange(pieces, "tensor")
        pieces_bc = exchange(pieces_bc, "tensor")
        if not last:
            messages = call(
                functools.partial(branch_kernel, shards),
                "branch",
                [index],
                [last_hidden, w_outs[-1], Far(out_scales)],
                [((rows, depth), BF16)] * shards,
                flops,
                [pltpu.VMEM((total_rows, depth), BF16)],
            )
            (output,) = call(
                functools.partial(output_kernel, shards),
                "output",
                [],
                [*exchange(messages, "tensor"), Far(current)],
                [far((rows, depth), F32)],
            )
        if last:
            tall = (depth // 2, inner + LANES)
            mine, theirs = call(
                functools.partial(late_grads_kernel, shards, dp_count),
                f"late_{layer}",
                [place],
                [normed, du, dq, *pieces_bc],
                [far(tall, BF16), (tall, BF16)],
                flops * 2,
                [pltpu.VMEM((depth, inner + LANES), BF16)],
            )
            last_halves = Halves(f"fold_{layer}", mine, theirs)
            last_halves.step()
            pieces[-1], last_halves.sent = lax.optimization_barrier((pieces[-1], last_halves.sent))
        else:
            tall = (depth // 2, LANES)
            mine, theirs = call(
                functools.partial(late_tail_kernel, shards, dp_count),
                f"late_{layer}",
                [place],
                [Far(normed), dq, *pieces_bc],
                [far(tall, BF16), (tall, BF16)],
                flops * 2,
                [pltpu.VMEM((depth, LANES), BF16)],
            )
            halves = Halves(f"fold_{layer}", mine, theirs)
            halves.step()
            first_kept, first_part = halves.last()
            last_kept, last_part = last_halves.last()
            pieces[1], last_part = lax.optimization_barrier((pieces[1], last_part))
        arrays = [*pieces, Far(rows_in), gains[layer], Far(grad_now)]
        outs = [far((rows, depth), F32), far((8, depth), F32)]
        if layer:
            arrays.append(Far(branch))
            outs.append((message, BF16))
        back = call(
            functools.partial(norm_back_kernel, shards, bool(layer)),
            f"norm_back_{layer}",
            [],
            arrays,
            outs,
        )
        grad_now, few_gain[layer] = back[:2]
        if layer:
            blocks = spread_out(back[2], "tensor")

    shared = jnp.stack(
        [
            jnp.concatenate([few_gain[layer][0], few_bc[layer][:5].reshape(-1)])
            for layer in order
        ]
    )
    shared = functools.reduce(jnp.add, spread_out(shared, "tensor"))
    own = jnp.stack([few_x[layer] for layer in order]).reshape(-1, LANES)
    few = jnp.concatenate([own, shared.reshape(-1, LANES)], axis=0)
    few = sum_over_dp(few)
    own = few[: own.shape[0]].reshape(LAYERS, 8, inner)
    shared = few[own.size // LANES :].reshape(LAYERS, -1)
    grad_gain = lax.dynamic_slice_in_dim(shared[:, :depth], place[0] * slab, slab, 1)
    grad_conv_bc = lax.dynamic_slice_in_dim(
        shared[:, depth:].reshape(LAYERS, 5, wide), place[0] * (wide // dp_count), wide // dp_count, 2
    )
    grad_tail, low = call(
        tails_kernel,
        "tails",
        [],
        [Far(first_kept), first_part, Far(last_kept), last_part],
        [far((slab, LAYERS * LANES), F32), ((slab, LAYERS * LANES), BF16)],
    )
    grad_bc = call(
        widen_kernel,
        "widen",
        [index],
        spread_out(low, "tensor"),
        [far((slab, wide), F32)] * LAYERS,
    )
    outs = [((LAYERS, slab, 2, inner), F32, "raw"), ((LAYERS, slab, inner), F32, "raw")]
    staged = [
        pltpu.VMEM((slab, 2, inner), F32),
        pltpu.VMEM((slab, inner), F32),
        pltpu.SemaphoreType.DMA((2,)),
    ]
    grads = call(
        functools.partial(finish_kernel, 1),
        "finish_1",
        [],
        [Far(last_early), Far(last_kept), last_part],
        outs,
        0,
        staged,
    )
    grad_zx, grad_out = call(
        functools.partial(finish_kernel, 0),
        "finish_0",
        [],
        [Far(first_early), *(Raw(part) for part in grads)],
        outs,
        0,
        staged,
        aliases={1: 0, 2: 1},
    )
    grad_out = grad_out.transpose(0, 2, 1)
    grad_bc = jnp.stack([grad_bc[layer] for layer in order])
    grad_dt = jnp.stack(
        [grad_tail[:, layer * LANES + HALF : layer * LANES + HALF + heads] for layer in order]
    )
    return (
        output,
        grad_now,
        grad_gain,
        grad_zx,
        grad_bc,
        grad_dt,
        own[:, :5],
        grad_conv_bc,
        own[:, 6, :heads],
        own[:, 6, LANES : LANES + heads],
        own[:, 6, 2 * LANES : 2 * LANES + heads],
        own[:, 5],
        grad_out,
    )


def solution(mesh):
    return jax.shard_map(
        body,
        mesh=mesh,
        in_specs=(
            P(("dp", "tensor"), None),
            P(None, "dp"),
            P(None, "dp", None, "tensor"),
            P(None, "dp", None),
            P(None, "dp", "tensor"),
            P(None, None, "tensor"),
            P(None, None, "dp"),
            P(None, "tensor"),
            P(None, "tensor"),
            P(None, "tensor"),
            P(None, "tensor"),
            P(None, "tensor", "dp"),
            P("dp"),
            P(("dp", "tensor"), None),
        ),
        out_specs=(
            P(("dp", "tensor"), None),
            P(("dp", "tensor"), None),
            P(None, "dp"),
            P(None, "dp", None, "tensor"),
            P(None, "dp", None),
            P(None, "dp", "tensor"),
            P(None, None, "tensor"),
            P(None, None, "dp"),
            P(None, "tensor"),
            P(None, "tensor"),
            P(None, "tensor"),
            P(None, "tensor"),
            P(None, "tensor", "dp"),
        ),
        check_vma=False,
    )
```

```python
import functools
import math

import jax
import jax.numpy as jnp
from jax import lax
from jax.experimental import pallas as pl
from jax.experimental.pallas import tpu as pltpu
from jax.sharding import PartitionSpec as P

LAYERS = 2
EPSILON = 1e-05
LANES = 128
HALF = 64
F32 = jnp.float32
BF16 = jnp.bfloat16
EXACT = lax.Precision.HIGHEST


class Far:
    def __init__(self, array, columns=None, place=0):
        self.array, self.place = array, place
        self.columns = array.shape[1] if columns is None else columns
        self.shape, self.dtype = (array.shape[0], self.columns), array.dtype


class Raw:
    def __init__(self, array):
        self.array, self.shape, self.dtype = array, array.shape, array.dtype


class Arrival:
    def __init__(self, copy, ref):
        self.copy, self.ref, self.waiting = copy, ref, True
        self.shape = ref.shape
        copy.start()

    def wait(self):
        if self.waiting:
            self.copy.wait()
            self.waiting = False

    def __getitem__(self, at):
        self.wait()
        return self.ref[at]


class Departure:
    def __init__(self, copy, ref):
        self.copy, self.ref, self.started = copy, ref, False
        self.shape = ref.shape

    def send(self):
        if not self.started:
            self.copy.start()
            self.started = True

    def __getitem__(self, at):
        return self.ref[at]

    def __setitem__(self, at, values):
        self.ref[at] = values
        if at is Ellipsis:
            self.send()


def dot(left, right, left_dim=1, right_dim=0, precision=None):
    return lax.dot_general(
        left,
        right,
        (((left_dim,), (right_dim,)), ((), ())),
        precision=precision,
        preferred_element_type=F32,
    )


def iota(shape, dim):
    return lax.broadcasted_iota(jnp.int32, shape, dim)


def sigmoid(values):
    return 1.0 / (1.0 + jnp.exp(-values))


def softplus(values):
    return jnp.maximum(values, 0.0) + jnp.log1p(jnp.exp(-jnp.abs(values)))


def rows_later(values, steps):
    return jnp.where(iota(values.shape, 0) >= steps, pltpu.roll(values, steps, 0), 0.0)


def rows_earlier(values, steps):
    total = values.shape[0]
    return jnp.where(
        iota(values.shape, 0) < total - steps, pltpu.roll(values, total - steps, 0), 0.0
    )


def conv(values, taps):
    result = taps[4:5, :] + taps[3:4, :] * values
    for offset in range(3):
        result = result + taps[offset : offset + 1, :] * rows_later(values, 3 - offset)
    return result


def conv_back(values, taps, grad):
    back = taps[3:4, :] * grad
    for offset in range(3):
        back = back + taps[offset : offset + 1, :] * rows_earlier(grad, 3 - offset)
    sums = [
        jnp.sum(grad * rows_later(values, 3 - offset), axis=0, keepdims=True)
        for offset in range(3)
    ]
    sums.append(jnp.sum(grad * values, axis=0, keepdims=True))
    sums.append(jnp.sum(grad, axis=0, keepdims=True))
    return back, sums


def pair_of_parts(column):
    high = column.astype(BF16).astype(F32)
    wide = jnp.broadcast_to(high, (column.shape[0], LANES))
    rest = jnp.broadcast_to(column - high, (column.shape[0], LANES))
    return jnp.where(iota(wide.shape, 1) < HALF, wide, rest).astype(BF16)


def joined_parts(message, width):
    return message[:, width : width + 1].astype(F32) + message[
        :, width + HALF : width + HALF + 1
    ].astype(F32)


def three_parts(values):
    high = values.astype(BF16)
    rest = values - high.astype(F32)
    middle = rest.astype(BF16)
    return high, middle, (rest - middle.astype(F32)).astype(BF16)


def spread_sum(parts, spread):
    spread = spread.astype(BF16)
    return dot(parts[0], spread) + dot(parts[1], spread) + dot(parts[2], spread)


def send(output):
    if isinstance(output, Departure):
        output.send()


def ready(operand):
    if isinstance(operand, Arrival):
        operand.wait()
    return operand.ref if isinstance(operand, (Arrival, Departure)) else operand


def step_state(q_rows, dt_bias, a_log):
    rows = q_rows.shape[0]
    shifted = q_rows + dt_bias
    steps = softplus(shifted)
    rates = -jnp.exp(a_log)
    below = (iota((rows, rows), 0) >= iota((rows, rows), 1)).astype(F32)
    running = dot(below, steps * rates, precision=EXACT)
    return shifted, steps, rates, running


SKIP_ROW, GAIN_ROW, BIAS_ROW, RATE_ROW = 5, 6, 7, 8


def mixer_forward(u_ref, y_ref, params, turned, bc_rows, q_rows, conv_bc, width):
    rows, inner = u_ref.shape
    states = bc_rows.shape[1] // 2
    maps = conv(bc_rows, conv_bc)
    maps = maps * sigmoid(maps)
    _, steps, _, running = step_state(
        q_rows, params[BIAS_ROW : BIAS_ROW + 1, :LANES], params[RATE_ROW : RATE_ROW + 1, :LANES]
    )
    turned[...] = running.T
    scores = dot(maps[:, states:], maps[:, :states], 1, 1, EXACT)
    steps = three_parts(steps)
    causal = iota((rows, rows), 0) >= iota((rows, rows), 1)
    lane = iota((rows, LANES), 1)
    per_block = LANES // width

    def block_step(block):
        at = pl.ds(block * LANES, LANES)
        mixed_in = conv(u_ref[:, at], params[:5, at])
        mixed_in = mixed_in * sigmoid(mixed_in)
        shape = (LANES, LANES)
        heads = block * per_block + iota(shape, 1) // width
        scaled = (mixed_in * spread_sum(steps, heads == iota(shape, 0))).astype(BF16)
        total = None
        for slot in range(per_block):
            head = block * per_block + slot
            gap = running[:, head : head + 1] - turned[head : head + 1, :]
            decay = jnp.exp(jnp.where(causal, gap, -1e30))
            part = dot((decay * scores).astype(BF16), scaled)
            total = part if slot == 0 else jnp.where(lane < slot * width, total, part)
        y_ref[:, at] = total + params[SKIP_ROW : SKIP_ROW + 1, at] * mixed_in

    for block in range(inner // LANES):
        block_step(block)


def gather_rows(target, index, blocks, width):
    rows = blocks[0].shape[0]
    for order, block in enumerate(blocks):
        place = pl.multiple_of((index ^ order) * rows, rows)
        target[pl.ds(place, rows), :] = block[:, :width]


def unpack_kernel(heads, *refs):
    index = refs[0][0]
    outs = refs[-3 * LAYERS :]
    blocks = refs[1 : -3 * LAYERS]
    slab = blocks[0].shape[1]
    depth, wide = outs[LAYERS].shape[1], outs[2 * LAYERS].shape[1]
    piece = wide // len(blocks)

    def placed(start, stop, held, total):
        result = None
        for order, block in enumerate(blocks):
            shape = (held, total)
            ones = iota(shape, 1) - (index ^ order) * held == iota(shape, 0)
            part = dot(block[...][start:stop, :held], ones.astype(BF16))
            result = part if result is None else result + part
        return result

    norm_at = LAYERS * heads
    taps_at = norm_at + LAYERS
    rows = placed(0, taps_at, slab, depth)
    taps = placed(taps_at, taps_at + 5 * LAYERS, piece, wide)
    for layer in range(LAYERS):
        steps = rows[layer * heads : (layer + 1) * heads, :]
        padding = jnp.zeros((LANES - heads, depth), F32)
        outs[layer][...] = jnp.concatenate([steps, padding], axis=0).astype(BF16)
        outs[LAYERS + layer][...] = rows[norm_at + layer : norm_at + layer + 1, :]
        outs[2 * LAYERS + layer][...] = taps[5 * layer : 5 * layer + 5, :]


def pack_kernel(index, *refs):
    blocks, (out,) = refs[:-1], refs[-1:]
    gather_rows(out, index[0], blocks, out.shape[1])


def unpack_maps_kernel(index, *refs):
    blocks, outs = refs[:-LAYERS], refs[-LAYERS:]
    piece = blocks[0].shape[1] // LAYERS
    for layer, out in enumerate(outs):
        total = None
        for order, block in enumerate(blocks):
            shape = (LAYERS * piece, out.shape[1])
            row = iota(shape, 0) - layer * piece
            ones = (row == iota(shape, 1) - (index[0] ^ order) * piece) & (row >= 0) & (row < piece)
            part = dot(block[...], ones.astype(BF16))
            total = part if total is None else total + part
        out[...] = total.astype(BF16)


def first_kernel(layer, shards, slabs, width, *refs):
    index, place = refs[0][0], refs[1][0]
    blocks, refs = refs[2 : 2 + shards], refs[2 + shards :]
    if layer:
        weights, refs = refs[:slabs], refs[slabs:]
        w_in, scales_out = refs[-3:-1]
        refs = refs[:-3] + refs[-1:]
    else:
        w_in, refs = refs[0], refs[1:]
    w_bc, gain, w_dt, conv_bc, params, normed, u_out, bc_out, q_out, y_out, turned = refs
    depth = normed.shape[1]
    inner = u_out.shape[1]
    rows = blocks[0].shape[0]
    if layer == 0:
        for order, block in enumerate(blocks):
            values = block[...].astype(F32)
            scale = lax.rsqrt(jnp.mean(values * values, axis=1, keepdims=True) + EPSILON)
            start = pl.multiple_of((index ^ order) * rows, rows)
            normed[pl.ds(start, rows), :] = (values * scale * gain[...]).astype(BF16)
    else:
        gather_rows(normed, index, blocks, depth)
        for order, block in enumerate(blocks):
            start = pl.multiple_of((index ^ order) * rows, rows)
            scales_out[pl.ds(start, rows), :] = jnp.broadcast_to(
                joined_parts(block, depth), (rows, LANES)
            )
        gather_rows(w_in, place, weights, inner)
        send(scales_out)
        send(w_in)
    send(normed)
    rows_in = normed[...]
    bc_rows = dot(rows_in, w_bc[...])
    q_rows = dot(rows_in, w_dt[...], 1, 1)
    u_rows = dot(rows_in, w_in[...])
    u_out[...] = u_rows
    bc_out[...] = bc_rows
    q_out[...] = q_rows
    mixer_forward(
        ready(u_out), ready(y_out), ready(params), turned, bc_rows, q_rows, conv_bc[...], width
    )


def live_column(length, rows):
    return (iota((rows, 1), 0) < length).astype(F32)


def second_kernel(shards, *refs):
    index = refs[0][0]
    length = refs[1][0]
    normed, w_gate, w_out, y_rows, params, z_out = refs[2:8]
    messages, scratch = refs[8 : 8 + shards], refs[8 + shards]
    depth = normed.shape[1]
    part = messages[0].shape[0]
    gate = dot(normed[...], w_gate[...])
    z_out[...] = gate
    gated = y_rows[...] * (gate * sigmoid(gate))
    live = live_column(length, y_rows.shape[0])
    hidden = (gated * params[GAIN_ROW : GAIN_ROW + 1, :] * live).astype(BF16)
    scratch[:, :depth] = dot(hidden, w_out[...], 1, 1).astype(BF16)
    scratch[:, depth:] = pair_of_parts(jnp.sum(gated * gated, axis=1, keepdims=True))
    for order, message in enumerate(messages):
        place = pl.multiple_of((index ^ order) * part, part)
        message[...] = scratch[pl.ds(place, part), :]


def last_second_kernel(shards, *refs):
    index = refs[0][0]
    length = refs[1][0]
    blocks, refs = refs[2 : 2 + shards], refs[2 + shards :]
    normed, w_gate, w_out, y_rows, params = refs[:5]
    z_out, hidden_out, grad_all, grad_hidden_out, sums_out = refs[5:]
    rows = y_rows.shape[0]
    gather_rows(grad_all, index, blocks, normed.shape[1])
    send(grad_all)
    grad_hidden = dot(grad_all[...], w_out[...])
    grad_hidden_out[...] = grad_hidden
    gate = dot(normed[...], w_gate[...])
    z_out[...] = gate
    gated = y_rows[...] * (gate * sigmoid(gate))
    squares = jnp.sum(gated * gated, axis=1, keepdims=True)
    weighted = gated * params[GAIN_ROW : GAIN_ROW + 1, :] * live_column(length, rows)
    hidden_out[...] = weighted.astype(BF16)
    products = jnp.sum(grad_hidden * weighted, axis=1, keepdims=True)
    lane = iota((rows, LANES), 1)
    table = jnp.where(lane == 0, squares, jnp.where(lane == 1, products, 0.0))
    sums_out[...] = table.T[:8, :]


def branch_kernel(shards, *refs):
    index = refs[0][0]
    hidden, w_out, scales = refs[1:4]
    messages, scratch = refs[4 : 4 + shards], refs[4 + shards]
    part = messages[0].shape[0]
    scratch[...] = (scales[:, 0:1] * dot(hidden[...], w_out[...], 1, 1)).astype(BF16)
    for order, message in enumerate(messages):
        place = pl.multiple_of((index ^ order) * part, part)
        message[...] = scratch[pl.ds(place, part), :]


def gate_back(length, scale, product, inner_all, y_rows, gate, grad_hidden, gate_gain):
    live = live_column(length, y_rows.shape[0])
    turn = sigmoid(gate)
    opened = gate * turn
    gated = y_rows * opened
    grad_live = grad_hidden * live
    grad_gain = jnp.sum(grad_live * gated * scale, axis=0, keepdims=True)
    grad_gated = scale * grad_live * gate_gain - gated * (
        scale * scale * scale * (product / inner_all)
    )
    hidden = (gated * scale * gate_gain * live).astype(BF16)
    grad_y = grad_gated * opened
    grad_gate = grad_gated * y_rows * (turn * (1.0 + gate * (1.0 - turn)))
    return hidden, grad_y, grad_gate.astype(BF16), grad_gain


def weight_grads(pairs, out, staged, sems):
    slots, part = staged.shape[:2]
    copies = []
    for slot in range(slots):
        cut = slice(slot * part, (slot + 1) * part)
        at = 0
        for left, right in pairs:
            columns = right.shape[1]
            staged[slot, :, at : at + columns] = dot(left[:, cut], right[...], 0, 0).astype(BF16)
            at += columns
        copies.append(
            pltpu.make_async_copy(staged.at[slot], out.at[pl.ds(slot * part, part), :], sems.at[slot])
        )
        copies[-1].start()
    for copy in copies:
        copy.wait()


def last_gate_kernel(shards, inner_all, *refs):
    length = refs[0][0]
    sums, refs = refs[1 : 1 + shards], refs[1 + shards :]
    y_rows, gate, grad_hidden, params, normed, grad_all = refs[:6]
    grad_y_out, grad_gate_out, gain_out, grads_out, scale_out, staged, sems = refs[6:]
    rows = y_rows.shape[0]
    total = sums[0][...]
    for other in sums[1:]:
        total = total + other[...]
    table = jnp.concatenate([total, jnp.zeros((LANES - 8, rows), F32)], axis=0).T
    scale = lax.rsqrt(table[:, 0:1] / inner_all + EPSILON)
    scale_out[...] = jnp.broadcast_to(scale, scale_out.shape)
    hidden, grad_y, grad_gate, grad_gain = gate_back(
        length,
        scale,
        table[:, 1:2],
        inner_all,
        y_rows[...],
        gate[...],
        grad_hidden[...],
        params[GAIN_ROW : GAIN_ROW + 1, :],
    )
    grad_y_out[...] = grad_y
    grad_gate_out[...] = grad_gate
    gain_out[...] = jnp.broadcast_to(grad_gain, gain_out.shape)
    weight_grads(((normed, grad_gate), (grad_all, hidden)), grads_out, staged, sems)


def gate_kernel(shards, inner_all, *refs):
    index = refs[0][0]
    length = refs[1][0]
    blocks, refs = refs[2 : 2 + shards], refs[2 + shards :]
    scales, w_out, y_rows, gate, params, normed = refs[:6]
    grad_y_out, grad_gate_out, gain_out, hidden_out, grad_all, products = refs[6:]
    depth = grad_all.shape[1]
    part = blocks[0].shape[0]
    gather_rows(grad_all, index, blocks, depth)
    for order, block in enumerate(blocks):
        place = pl.multiple_of((index ^ order) * part, part)
        products[pl.ds(place, part), :] = jnp.broadcast_to(
            joined_parts(block, depth), (part, LANES)
        )
    hidden, grad_y, grad_gate, grad_gain = gate_back(
        length,
        scales[:, 0:1],
        products[:, 0:1],
        inner_all,
        y_rows[...],
        gate[...],
        dot(grad_all[...], w_out[...]),
        params[GAIN_ROW : GAIN_ROW + 1, :],
    )
    grad_y_out[...] = grad_y
    grad_gate_out[...] = grad_gate
    hidden_out[...] = hidden
    gain_out[...] = jnp.broadcast_to(grad_gain, gain_out.shape)


def grads_kernel(normed, grad_gate, grad_all, hidden, du, out, staged, sems):
    weight_grads(((normed, grad_gate), (grad_all, hidden), (normed, du)), out, staged, sems)


def scan_back_kernel(width, index, *refs):
    u_ref, bc_ref, q_ref, y_ref, grad_ref, gain_sum, conv_bc, params_ref = refs[:8]
    du_out, dbc_out, dq_out, sums_out, sums_bc = refs[8:13]
    pieces = refs[13:-5]
    turned, grad_scores, grad_running, grad_steps, skip_sum = refs[-5:]
    params, u_ref, y_ref, grad_ref = ready(params_ref), ready(u_ref), ready(y_ref), ready(grad_ref)
    sums_x, du_ref = ready(sums_out), ready(du_out)
    bc_rows, q_rows = bc_ref[...], q_ref[...]
    rows, inner = u_ref.shape
    states = bc_rows.shape[1] // 2
    taps_bc = conv_bc[...]
    pre_bc = conv(bc_rows, taps_bc)
    turn_bc = sigmoid(pre_bc)
    maps = pre_bc * turn_bc
    shifted, steps, rates, running = step_state(
        q_rows, params[BIAS_ROW : BIAS_ROW + 1, :LANES], params[RATE_ROW : RATE_ROW + 1, :LANES]
    )
    turned[...] = running.T
    b_rows, c_rows = maps[:, :states], maps[:, states:]
    scores = dot(b_rows, c_rows, 1, 1, EXACT)
    steps_parts = three_parts(steps)
    causal = iota((rows, rows), 0) <= iota((rows, rows), 1)
    lane = iota((rows, LANES), 1)
    per_block = LANES // width
    for total in (grad_scores, grad_running, grad_steps, skip_sum):
        total[...] = jnp.zeros(total.shape, F32)

    def block_step(block):
        at = pl.ds(block * LANES, LANES)
        u_rows, grad_y = u_ref[:, at], grad_ref[:, at]
        taps_x, skips = params[:5, at], params[SKIP_ROW : SKIP_ROW + 1, at]
        pre_x = conv(u_rows, taps_x)
        turn_x = sigmoid(pre_x)
        mixed_in = pre_x * turn_x
        shape = (LANES, LANES)
        heads = block * per_block + iota(shape, 1) // width
        steps_wide = spread_sum(steps_parts, heads == iota(shape, 0))
        scaled = (mixed_in * steps_wide).astype(BF16)
        grad_low = grad_y.astype(BF16)
        grad_scaled = None
        for slot in range(per_block):
            head = block * per_block + slot
            gap = turned[head : head + 1, :] - running[:, head : head + 1]
            decay = jnp.exp(jnp.where(causal, gap, -1e30))
            part = dot((decay * scores).astype(BF16), grad_low)
            grad_scaled = part if slot == 0 else jnp.where(lane < slot * width, grad_scaled, part)
            own = jnp.where(
                (lane >= slot * width) & (lane < (slot + 1) * width), scaled, jnp.zeros_like(scaled)
            )
            grad_scores[...] += dot(own, grad_low, 1, 1) * decay
        gather = block * per_block + iota(shape, 0) // width == iota(shape, 1)
        within = y_ref[:, at] - skips * mixed_in
        moved = grad_low.astype(F32) * within - scaled.astype(F32) * grad_scaled
        grad_running[...] += spread_sum(three_parts(moved), gather)
        grad_steps[...] += spread_sum(three_parts(mixed_in * grad_scaled), gather)
        skip_row = jnp.sum(grad_y * mixed_in, axis=0, keepdims=True)
        skip_sum[...] += spread_sum(three_parts(jnp.broadcast_to(skip_row, (8, LANES))), gather)
        grad_x = steps_wide * grad_scaled + skips * grad_y
        grad_x = grad_x * (turn_x * (1.0 + pre_x * (1.0 - turn_x)))
        du, tap_sums = conv_back(u_rows, taps_x, grad_x)
        du_ref[:, at] = du.astype(BF16)
        tap_sums.append(gain_sum[0:1, at])
        tap_sums.append(jnp.zeros((2, LANES), F32))
        sums_x[:, at] = jnp.concatenate(tap_sums, axis=0)

    for block in range(inner // LANES):
        block_step(block)
    grad_b = dot(grad_scores[...], c_rows, precision=EXACT)
    grad_c = dot(grad_scores[...], b_rows, 0, 0, EXACT)
    above = (iota((rows, rows), 0) <= iota((rows, rows), 1)).astype(F32)
    grad_decay = dot(above, grad_running[...], precision=EXACT)
    grad_q = (grad_steps[...] + grad_decay * rates) * sigmoid(shifted)
    dq_out[...] = grad_q.astype(BF16)
    sums_x[6:7, :LANES] = jnp.sum(grad_q, axis=0, keepdims=True)
    sums_x[6:7, LANES : 2 * LANES] = jnp.sum(grad_decay * steps, axis=0, keepdims=True) * rates
    sums_x[6:7, 2 * LANES : 3 * LANES] = skip_sum[0:1, :]
    grad_bc = jnp.concatenate([grad_b, grad_c], axis=1)
    grad_bc = grad_bc * (turn_bc * (1.0 + pre_bc * (1.0 - turn_bc)))
    dbc, tap_sums = conv_back(bc_rows, taps_bc, grad_bc)
    low = dbc.astype(BF16)
    dbc_out[...] = low
    piece = low.shape[1] // len(pieces)
    for order, out in enumerate(pieces):
        shape = (low.shape[1], LANES)
        ones = iota(shape, 0) - (index[0] ^ order) * piece == iota(shape, 1)
        ones = ones & (iota(shape, 1) < piece)
        out[...] = dot(low, ones.astype(BF16)).astype(BF16)
    tap_sums.append(jnp.zeros((3, low.shape[1]), F32))
    sums_bc[...] = jnp.concatenate(tap_sums, axis=0)


def halving_order(count):
    order = [0]
    step = count // 2
    while step > 1:
        order = order + [place + step for place in order]
        step //= 2
    return order


def late_tail(parts, dq):
    total = parts[0][...].astype(F32)
    for other in parts[1:]:
        total = total + other[...].astype(F32)
    shape = (LANES, LANES)
    moved = (iota(shape, 1) - HALF == iota(shape, 0)).astype(BF16)
    tail = (total + dot(dq[...], moved)).astype(BF16)
    return tail


def split_slabs(place, slabs, scratch, mine, theirs):
    slab = scratch.shape[0] // slabs
    for slot, order in enumerate(halving_order(slabs)):
        cut = slice(slot * slab, (slot + 1) * slab)
        for out, flip in ((mine, 0), (theirs, 1)):
            start = pl.multiple_of((place[0] ^ (order + flip)) * slab, slab)
            out[cut, :] = scratch[pl.ds(start, slab), :]


def late_tail_kernel(shards, slabs, place, normed, dq, *refs):
    parts, (mine, theirs, scratch) = refs[:shards], refs[shards:]
    scratch[...] = dot(normed[...], late_tail(parts, dq), 0, 0).astype(BF16)
    split_slabs(place, slabs, scratch, mine, theirs)


def late_grads_kernel(shards, slabs, place, normed, du, dq, *refs):
    parts, (mine, theirs, scratch) = refs[:shards], refs[shards:]
    inner = du.shape[1]
    rows_in = normed[...]
    scratch[:, :inner] = dot(rows_in, du[...], 0, 0).astype(BF16)
    scratch[:, inner:] = dot(rows_in, late_tail(parts, dq), 0, 0).astype(BF16)
    split_slabs(place, slabs, scratch, mine, theirs)


def fold_kernel(mine, other, kept, sent):
    half = kept.shape[0]
    kept[...] = mine[:half, :].astype(F32) + other[:half, :].astype(F32)
    sent[...] = (mine[half:, :].astype(F32) + other[half:, :].astype(F32)).astype(BF16)


def tails_kernel(first_kept, first_part, last_kept, last_part, tail_out, low_out):
    tails = []
    for kept, part in ((first_kept, first_part), (last_kept, last_part)):
        inner = kept.shape[1] - LANES
        tails.append(kept[:, inner:] + part[:, inner:].astype(F32))
    tail = jnp.concatenate(tails, axis=1)
    low_out[...] = tail.astype(BF16)
    tail_out[...] = tail


def finish_kernel(layer, early, *refs):
    zx_out, out_out, zx_rows, out_rows, sems = refs[-5:]
    inner = out_rows.shape[1]
    zx_rows[:, 0, :] = early[:, :inner].astype(F32)
    if layer:
        kept, part = refs[:2]
        zx_rows[:, 1, :] = kept[:, :inner] + part[:, :inner].astype(F32)
    else:
        zx_rows[:, 1, :] = early[:, 2 * inner :].astype(F32)
    first = pltpu.make_async_copy(zx_rows, zx_out.at[layer], sems.at[0])
    first.start()
    out_rows[...] = early[:, inner : 2 * inner].astype(F32)
    second = pltpu.make_async_copy(out_rows, out_out.at[layer], sems.at[1])
    second.start()
    first.wait()
    second.wait()


def widen_kernel(index, *refs):
    blocks, outs = refs[:-LAYERS], refs[-LAYERS:]
    wide = outs[0].shape[1]
    piece = wide // len(blocks)
    for layer, out in enumerate(outs):
        total = None
        for order, block in enumerate(blocks):
            shape = (LANES, wide)
            lane = iota(shape, 1) - (index[0] ^ order) * piece
            ones = (lane == iota(shape, 0)) & (iota(shape, 0) < piece)
            part = dot(block[:, layer * LANES : (layer + 1) * LANES], ones.astype(BF16))
            total = part if total is None else total + part
        out[...] = total


def input_grad_kernel(shards, *refs):
    index = refs[0][0]
    grad_gate, du, dbc, dq, w_in, w_gate, w_bc, w_dt = refs[1:9]
    outs, scratch = refs[9 : 9 + shards], refs[9 + shards]
    part = outs[0].shape[0]
    total = dot(dbc[...], w_bc[...], 1, 1) + dot(dq[...], w_dt[...])
    total = total + dot(du[...], w_in[...], 1, 1)
    scratch[...] = (total + dot(grad_gate[...], w_gate[...], 1, 1)).astype(BF16)
    for order, out in enumerate(outs):
        place = pl.multiple_of((index ^ order) * part, part)
        out[...] = scratch[pl.ds(place, part), :]


def branch_total(messages, depth, inner_all):
    total = messages[0][:, :depth].astype(F32)
    squares = joined_parts(messages[0], depth)
    for other in messages[1:]:
        total = total + other[:, :depth].astype(F32)
        squares = squares + joined_parts(other, depth)
    return total, lax.rsqrt(squares / inner_all + EPSILON)


def residual_kernel(shards, inner_all, *refs):
    messages = refs[:shards]
    start, gain, current_out, branch_out, message_out = refs[shards:]
    depth = start.shape[1]
    branch, scale = branch_total(messages, depth, inner_all)
    current = start[...].astype(F32) + scale * branch
    current_out[...] = current
    branch_out[...] = branch
    norm = lax.rsqrt(jnp.mean(current * current, axis=1, keepdims=True) + EPSILON)
    message_out[:, :depth] = (current * norm * gain[...]).astype(BF16)
    message_out[:, depth:] = pair_of_parts(scale)


def output_kernel(shards, *refs):
    messages = refs[:shards]
    start, out = refs[shards:]
    total = start[...]
    for message in messages:
        total = total + message[...].astype(F32)
    out[...] = total


def norm_back_kernel(shards, last, *refs):
    blocks = refs[:shards]
    refs = refs[shards:]
    rows_in, gain, grad_in = refs[:3]
    current = rows_in[...].astype(F32)
    depth = current.shape[1]
    grad_normed = blocks[0][...].astype(F32)
    for other in blocks[1:]:
        grad_normed = grad_normed + other[...].astype(F32)
    norm = lax.rsqrt(jnp.mean(current * current, axis=1, keepdims=True) + EPSILON)
    weighted = grad_normed * gain[...]
    inner_product = jnp.mean(weighted * current, axis=1, keepdims=True)
    grad = grad_in[...].astype(F32) + norm * weighted - current * (norm * norm * norm * inner_product)
    gain_row = jnp.sum(grad_normed * current * norm, axis=0, keepdims=True)
    if last:
        branch, grad_out, gain_out, message_out = refs[3:]
        low = grad.astype(BF16)
        message_out[:, :depth] = low
        message_out[:, depth:] = pair_of_parts(
            jnp.sum(low.astype(F32) * branch[...], axis=1, keepdims=True)
        )
    else:
        grad_out, gain_out = refs[3:]
    grad_out[...] = grad
    gain_out[...] = jnp.broadcast_to(gain_row, gain_out.shape)


def call(kernel, name, scalars, arrays, outs, flops=0, scratch=(), vmem=24, aliases=None):
    far_in = [item for item in arrays if isinstance(item, Far)]
    far_out = [out for out in outs if out[2:] == ("far",)]
    specs, given, out_specs, shapes, held = [], [], [], [], 0
    for item in arrays:
        if isinstance(item, (Far, Raw)):
            specs.append(pl.BlockSpec(memory_space=pl.ANY))
            given.append(pltpu.with_memory_space_constraint(item.array, pltpu.HBM))
        else:
            specs.append(pl.BlockSpec(memory_space=pltpu.VMEM))
            given.append(item)
        held += math.prod(item.shape) * item.dtype.itemsize
    for shape, dtype, *kind in outs:
        out_specs.append(pl.BlockSpec(memory_space=pl.ANY if kind else pltpu.VMEM))
        shapes.append(pltpu.HBM(shape, dtype) if kind else jax.ShapeDtypeStruct(shape, dtype))
        held += math.prod(shape) * jnp.dtype(dtype).itemsize
    extra = [pltpu.VMEM(item.shape, item.dtype) for item in far_in]
    extra += [pltpu.VMEM(out[0], out[1]) for out in far_out]
    extra += [pltpu.SemaphoreType.DMA((max(1, len(far_in) + len(far_out)),))]

    def whole(*refs):
        refs = list(refs)
        own = len(refs) - len(extra)
        places, sems = refs[own:-1], refs[-1]
        refs = refs[:own]
        moved, slot = [], 0
        for order, item in enumerate(arrays):
            if isinstance(item, Far):
                at = len(scalars) + order
                source = refs[at]
                if item.columns != item.array.shape[1]:
                    source = source.at[:, pl.ds(item.place * item.columns, item.columns)]
                copy = pltpu.make_async_copy(source, places[slot], sems.at[slot])
                refs[at] = Arrival(copy, places[slot])
                moved.append(refs[at])
                slot += 1
        leaving = []
        for order, out in enumerate(outs):
            if out[2:] == ("far",):
                at = len(scalars) + len(arrays) + order
                copy = pltpu.make_async_copy(places[slot], refs[at], sems.at[slot])
                refs[at] = Departure(copy, places[slot])
                leaving.append(refs[at])
                slot += 1
        kernel(*refs)
        for item in moved:
            item.wait()
        for item in leaving:
            item.send()
        for item in leaving:
            item.copy.wait()

    return pl.pallas_call(
        whole,
        out_shape=tuple(shapes),
        in_specs=[pl.BlockSpec(memory_space=pltpu.SMEM)] * len(scalars) + specs,
        out_specs=tuple(out_specs),
        scratch_shapes=list(scratch) + extra,
        input_output_aliases=aliases or {},
        compiler_params=pltpu.CompilerParams(vmem_limit_bytes=vmem * 1024 * 1024),
        cost_estimate=pl.CostEstimate(flops=1, bytes_accessed=1, transcendentals=0),
        name=name,
    )(*scalars, *given)


def near(*parts):
    return parts if len(parts) > 1 else parts[0]


def far(shape, dtype):
    return (shape, dtype, "far")


def exchange(blocks, axis):
    count = lax.axis_size(axis)
    return [blocks[0]] + [
        lax.ppermute(blocks[k], axis, [(i, i ^ k) for i in range(count)]) for k in range(1, count)
    ]


def spread_out(block, axis):
    return exchange([block] * lax.axis_size(axis), axis)


def gather_dp(blocks):
    count = lax.axis_size("dp")
    hop = count // 2 // len(blocks)
    while hop:
        for k in list(blocks):
            blocks[k ^ hop] = lax.ppermute(blocks[k], "dp", [(i, i ^ hop) for i in range(count)])
        hop //= 2
    return [blocks[k] for k in range(count)]


def over_dp(block, hop):
    count = lax.axis_size("dp")
    return lax.ppermute(block, "dp", [(i, i ^ hop) for i in range(count)])


class Halves:
    def __init__(self, name, mine, theirs):
        self.name, self.kept, self.sent, self.hop = name, mine, theirs, 1

    def receive(self):
        other = over_dp(self.sent, self.hop)
        self.hop *= 2
        return other

    def step(self, other=None):
        half = (self.kept.shape[0] // 2, self.kept.shape[1])
        self.kept, self.sent = call(
            fold_kernel,
            self.name,
            [],
            [Far(self.kept), self.receive() if other is None else other],
            [far(half, F32), (half, BF16)],
        )

    def last(self):
        while self.hop * 2 < lax.axis_size("dp"):
            self.step()
        return self.kept, self.receive()


def sum_over_dp(values):
    count = lax.axis_size("dp")
    values = values + lax.ppermute(values, "dp", [(i, i ^ 1) for i in range(count)])
    others = [
        lax.ppermute(values, "dp", [(i, i ^ k) for i in range(count)]) for k in range(2, count, 2)
    ]
    for other in others:
        values = values + other
    return values


def body(
    residual_in,
    norm_gain,
    w_zx,
    w_bc,
    w_dt,
    conv_x,
    conv_bc,
    dt_bias,
    a_log,
    d_skip,
    gate_gain,
    w_out,
    lengths,
    cotangent,
):
    shards = lax.axis_size("tensor")
    dp_count = lax.axis_size("dp")
    rows, depth = residual_in.shape
    inner = gate_gain.shape[1]
    heads = dt_bias.shape[1]
    width = inner // heads
    wide = w_bc.shape[2]
    total_rows = rows * shards
    inner_all = inner * shards
    slab = norm_gain.shape[1]
    index = lax.axis_index("tensor").reshape(1).astype(jnp.int32)
    place = lax.axis_index("dp").reshape(1).astype(jnp.int32)
    message = (rows, depth + LANES)

    order = range(LAYERS)
    columns = [w_zx[0, :, 1, :], w_zx[0, :, 0, :], w_out[0].T]
    packed = jnp.concatenate(columns, axis=1)
    packed, w_dt = lax.optimization_barrier((packed, w_dt))
    w_first = lax.all_gather(packed, "dp", axis=0, tiled=True)
    x_half = [w_zx[1, :, 1, :], over_dp(w_zx[1, :, 1, :], dp_count // 2)]
    few = jnp.concatenate(
        [
            w_dt.transpose(0, 2, 1).reshape(LAYERS * heads, slab),
            norm_gain,
            jnp.pad(conv_bc.reshape(LAYERS * 5, -1), ((0, 0), (0, slab - wide // dp_count))),
        ],
        axis=0,
    )
    few = jnp.pad(few, ((0, -few.shape[0] % 16), (0, 0)))
    few, x_half[1] = lax.optimization_barrier((few, x_half[1]))
    few = spread_out(few, "dp")
    x_blocks = gather_dp({0: x_half[0], dp_count // 2: x_half[1]})
    residual_blocks = spread_out(residual_in, "tensor")
    late_blocks = spread_out(cotangent, "tensor")
    w_last = lax.all_gather(
        jnp.concatenate([w_zx[1, :, 0, :], w_out[1].T], axis=1), "dp", axis=0, tiled=True
    )
    w_x = [Far(w_first, inner, 0)]
    w_gates = [Far(w_first, inner, 1), Far(w_last, inner, 0)]
    w_outs = [Far(w_first, inner, 2), Far(w_last, inner, 1)]
    piece = wide // shards
    maps = lax.dynamic_slice_in_dim(w_bc, index[0] * piece, piece, 2)
    (maps,) = call(
        pack_kernel,
        "pack_maps",
        [place],
        gather_dp({0: jnp.concatenate([maps[layer] for layer in order], axis=1)}),
        [((depth, LAYERS * piece), BF16)],
    )
    w_bcs = call(
        unpack_maps_kernel,
        "unpack_maps",
        [index],
        spread_out(maps, "tensor"),
        [far((depth, wide), BF16)] * LAYERS,
    )
    params = []
    for layer in order:
        ends = jnp.stack([dt_bias[layer], a_log[layer]])
        params.append(
            jnp.concatenate(
                [
                    conv_x[layer],
                    jnp.repeat(d_skip[layer], width)[None],
                    gate_gain[layer][None],
                    jnp.pad(ends, ((0, 7), (0, inner - heads))),
                ],
                axis=0,
            )
        )
    few[1], params[0], params[1] = lax.optimization_barrier((few[1], params[0], params[1]))
    few = call(
        functools.partial(unpack_kernel, heads),
        "unpack",
        [place],
        few,
        [far((LANES, depth), BF16)] * LAYERS + [far((1, depth), F32)] * LAYERS + [far((5, wide), F32)] * LAYERS,
    )
    w_steps, gains, taps_bc = few[:LAYERS], few[LAYERS : 2 * LAYERS], few[2 * LAYERS :]
    params = [Far(part) for part in params]
    w_steps, gains, taps_bc, w_bcs = (
        [Far(part) for part in parts] for parts in (w_steps, gains, taps_bc, w_bcs)
    )

    flops = 2 * total_rows * depth * inner
    kept = []
    blocks = residual_blocks
    current = residual_in
    for layer in order:
        last = layer == LAYERS - 1
        long = near if last else far
        hold = near if last else Far
        outs = [
            long((total_rows, depth), BF16),
            far((total_rows, inner), F32),
            far((total_rows, wide), F32),
            far((total_rows, LANES), F32),
            long((total_rows, inner), F32),
        ]
        if layer:
            outs += [far((depth, inner), BF16), far((total_rows, LANES), F32)]
        normed, u_rows, bc_rows, q_rows, y_rows, *more = call(
            functools.partial(first_kernel, layer, shards, dp_count, width),
            f"mix_{layer}",
            [index, place],
            [
                *blocks,
                *(x_blocks if layer else w_x),
                w_bcs[layer],
                gains[layer],
                w_steps[layer],
                taps_bc[layer],
                params[layer],
            ],
            outs,
            flops * 3,
            [pltpu.VMEM((LANES, total_rows), F32)],
        )
        if layer:
            w_x.append(Far(more[0]))
            scales = more[1]
        arrays = [hold(normed), w_gates[layer], w_outs[layer], hold(y_rows), params[layer]]
        if last:
            gate, last_hidden, grad_all, grad_hidden, sums = call(
                functools.partial(last_second_kernel, shards),
                f"gate_{layer}",
                [index, lengths],
                [*late_blocks, *arrays],
                [
                    ((total_rows, inner), F32),
                    ((total_rows, inner), BF16),
                    ((total_rows, depth), BF16),
                    ((total_rows, inner), F32),
                    ((8, total_rows), F32),
                ],
                flops * 2,
            )
            sums = spread_out(sums, "tensor")
        else:
            gate, *sent = call(
                functools.partial(second_kernel, shards),
                f"gate_{layer}",
                [index, lengths],
                arrays,
                [far((total_rows, inner), F32)] + [(message, BF16)] * shards,
                flops * 2,
                [pltpu.VMEM((total_rows, depth + LANES), BF16)],
            )
            sent = exchange(sent, "tensor")
        kept.append([normed, u_rows, bc_rows, q_rows, y_rows, gate, current])
        if not last:
            current, branch, packed = call(
                functools.partial(residual_kernel, shards, inner_all),
                f"residual_{layer}",
                [],
                [*sent, Far(current), gains[layer + 1]],
                [far((rows, depth), F32), far((rows, depth), F32), (message, BF16)],
            )
            blocks = spread_out(packed, "tensor")

    grad_now = cotangent
    few_x, few_bc, few_gain = {}, {}, {}
    for layer in reversed(order):
        last = layer == LAYERS - 1
        normed, u_rows, bc_rows, q_rows, y_rows, gate, rows_in = kept[layer]
        hold = near if last else Far
        outs = [
            ((total_rows, inner), F32),
            ((total_rows, inner), BF16),
            ((8, inner), F32),
        ]
        slots = depth // 512
        if last:
            grad_y, grad_gate, gain_sum, grads, out_scales = call(
                functools.partial(last_gate_kernel, shards, inner_all),
                f"gate_back_{layer}",
                [lengths],
                [*sums, y_rows, gate, grad_hidden, params[layer], normed, grad_all],
                outs
                + [((depth, 2 * inner), BF16, "raw"), far((total_rows, LANES), F32)],
                flops * 2,
                [pltpu.VMEM((slots, 512, 2 * inner), BF16), pltpu.SemaphoreType.DMA((slots,))],
            )
            grads, grad_y = lax.optimization_barrier((grads, grad_y))
            last_early = lax.psum_scatter(grads, "dp", scatter_dimension=0, tiled=True)
        else:
            grad_y, grad_gate, gain_sum, hidden, grad_all = call(
                functools.partial(gate_kernel, shards, inner_all),
                f"gate_back_{layer}",
                [index, lengths],
                [*blocks, Far(scales), w_outs[layer], Far(y_rows), Far(gate), params[layer], Far(normed)],
                outs + [((total_rows, inner), BF16), ((total_rows, depth), BF16)],
                flops * 3,
                [pltpu.VMEM((total_rows, LANES), F32)],
            )
        du, dbc, dq, few_x[layer], few_bc[layer], *pieces_bc = call(
            functools.partial(scan_back_kernel, width),
            f"mix_back_{layer}",
            [index],
            [
                Far(u_rows),
                Far(bc_rows),
                Far(q_rows),
                hold(y_rows),
                grad_y,
                gain_sum,
                taps_bc[layer],
                params[layer],
            ],
            [
                ((total_rows, inner), BF16),
                ((total_rows, wide), BF16),
                ((total_rows, LANES), BF16),
                far((8, inner), F32),
                far((8, wide), F32),
            ]
            + [((total_rows, LANES), BF16)] * shards,
            flops * 2,
            [
                pltpu.VMEM((LANES, total_rows), F32),
                pltpu.VMEM((total_rows, total_rows), F32),
                pltpu.VMEM((total_rows, LANES), F32),
                pltpu.VMEM((total_rows, LANES), F32),
                pltpu.VMEM((8, LANES), F32),
            ],
        )
        if not last:
            last_halves.step()
            du, last_halves.sent = lax.optimization_barrier((du, last_halves.sent))
            (grads,) = call(
                grads_kernel,
                f"grads_{layer}",
                [],
                [Far(normed), grad_gate, grad_all, hidden, du],
                [((depth, 3 * inner), BF16, "raw")],
                flops * 3,
                [pltpu.VMEM((slots, 512, 3 * inner), BF16), pltpu.SemaphoreType.DMA((slots,))],
            )
            grads, du, dq = lax.optimization_barrier((grads, du, dq))
            first_early = lax.psum_scatter(grads, "dp", scatter_dimension=0, tiled=True)
        pieces = call(
            functools.partial(input_grad_kernel, shards),
            f"input_grad_{layer}",
            [index],
            [
                grad_gate,
                du,
                dbc,
                dq,
                w_x[layer],
                w_gates[layer],
                w_bcs[layer],
                w_steps[layer],
            ],
            [((rows, depth), BF16)] * shards,
            flops * 2,
            [pltpu.VMEM((total_rows, depth), BF16)],
        )
        if last:
            pieces = list(pieces)
            pieces[0], dq = lax.optimization_barrier((pieces[0], dq))
        pieces = exchange(pieces, "tensor")
        pieces_bc = exchange(pieces_bc, "tensor")
        if last:
            tall = (depth // 2, inner + LANES)
            mine, theirs = call(
                functools.partial(late_grads_kernel, shards, dp_count),
                f"late_{layer}",
                [place],
                [normed, du, dq, *pieces_bc],
                [far(tall, BF16), (tall, BF16)],
                flops * 2,
                [pltpu.VMEM((depth, inner + LANES), BF16)],
            )
            last_halves = Halves(f"fold_{layer}", mine, theirs)
            last_halves.step()
            pieces[-1], last_halves.sent = lax.optimization_barrier((pieces[-1], last_halves.sent))
        else:
            tall = (depth // 2, LANES)
            mine, theirs = call(
                functools.partial(late_tail_kernel, shards, dp_count),
                f"late_{layer}",
                [place],
                [Far(normed), dq, *pieces_bc],
                [far(tall, BF16), (tall, BF16)],
                flops * 2,
                [pltpu.VMEM((depth, LANES), BF16)],
            )
            halves = Halves(f"fold_{layer}", mine, theirs)
            halves.step()
            first_kept, first_part = halves.last()
            last_kept, last_part = last_halves.last()
            pieces[1], last_part = lax.optimization_barrier((pieces[1], last_part))
        arrays = [*pieces, Far(rows_in), gains[layer], Far(grad_now)]
        outs = [far((rows, depth), F32), far((8, depth), F32)]
        if layer:
            arrays.append(Far(branch))
            outs.append((message, BF16))
        back = call(
            functools.partial(norm_back_kernel, shards, bool(layer)),
            f"norm_back_{layer}",
            [],
            arrays,
            outs,
        )
        grad_now, few_gain[layer] = back[:2]
        if not last:
            last_hidden, few_gain[0] = lax.optimization_barrier((last_hidden, few_gain[0]))
            messages = call(
                functools.partial(branch_kernel, shards),
                "branch",
                [index],
                [last_hidden, w_outs[-1], Far(out_scales)],
                [((rows, depth), BF16)] * shards,
                flops,
                [pltpu.VMEM((total_rows, depth), BF16)],
            )
            (output,) = call(
                functools.partial(output_kernel, shards),
                "output",
                [],
                [*exchange(messages, "tensor"), Far(current)],
                [far((rows, depth), F32)],
            )
        if layer:
            blocks = spread_out(back[2], "tensor")

    shared = jnp.stack(
        [
            jnp.concatenate([few_gain[layer][0], few_bc[layer][:5].reshape(-1)])
            for layer in order
        ]
    )
    shared = functools.reduce(jnp.add, spread_out(shared, "tensor"))
    own = jnp.stack([few_x[layer] for layer in order]).reshape(-1, LANES)
    few = jnp.concatenate([own, shared.reshape(-1, LANES)], axis=0)
    few = sum_over_dp(few)
    own = few[: own.shape[0]].reshape(LAYERS, 8, inner)
    shared = few[own.size // LANES :].reshape(LAYERS, -1)
    grad_gain = lax.dynamic_slice_in_dim(shared[:, :depth], place[0] * slab, slab, 1)
    grad_conv_bc = lax.dynamic_slice_in_dim(
        shared[:, depth:].reshape(LAYERS, 5, wide), place[0] * (wide // dp_count), wide // dp_count, 2
    )
    grad_tail, low = call(
        tails_kernel,
        "tails",
        [],
        [Far(first_kept), first_part, Far(last_kept), last_part],
        [far((slab, LAYERS * LANES), F32), ((slab, LAYERS * LANES), BF16)],
    )
    grad_bc = call(
        widen_kernel,
        "widen",
        [index],
        spread_out(low, "tensor"),
        [far((slab, wide), F32)] * LAYERS,
    )
    outs = [((LAYERS, slab, 2, inner), F32, "raw"), ((LAYERS, slab, inner), F32, "raw")]
    staged = [
        pltpu.VMEM((slab, 2, inner), F32),
        pltpu.VMEM((slab, inner), F32),
        pltpu.SemaphoreType.DMA((2,)),
    ]
    grads = call(
        functools.partial(finish_kernel, 1),
        "finish_1",
        [],
        [Far(last_early), Far(last_kept), last_part],
        outs,
        0,
        staged,
    )
    grad_zx, grad_out = call(
        functools.partial(finish_kernel, 0),
        "finish_0",
        [],
        [Far(first_early), *(Raw(part) for part in grads)],
        outs,
        0,
        staged,
        aliases={1: 0, 2: 1},
    )
    grad_out = grad_out.transpose(0, 2, 1)
    grad_bc = jnp.stack([grad_bc[layer] for layer in order])
    grad_dt = jnp.stack(
        [grad_tail[:, layer * LANES + HALF : layer * LANES + HALF + heads] for layer in order]
    )
    return (
        output,
        grad_now,
        grad_gain,
        grad_zx,
        grad_bc,
        grad_dt,
        own[:, :5],
        grad_conv_bc,
        own[:, 6, :heads],
        own[:, 6, LANES : LANES + heads],
        own[:, 6, 2 * LANES : 2 * LANES + heads],
        own[:, 5],
        grad_out,
    )


def solution(mesh):
    return jax.shard_map(
        body,
        mesh=mesh,
        in_specs=(
            P(("dp", "tensor"), None),
            P(None, "dp"),
            P(None, "dp", None, "tensor"),
            P(None, "dp", None),
            P(None, "dp", "tensor"),
            P(None, None, "tensor"),
            P(None, None, "dp"),
            P(None, "tensor"),
            P(None, "tensor"),
            P(None, "tensor"),
            P(None, "tensor"),
            P(None, "tensor", "dp"),
            P("dp"),
            P(("dp", "tensor"), None),
        ),
        out_specs=(
            P(("dp", "tensor"), None),
            P(("dp", "tensor"), None),
            P(None, "dp"),
            P(None, "dp", None, "tensor"),
            P(None, "dp", None),
            P(None, "dp", "tensor"),
            P(None, None, "tensor"),
            P(None, None, "dp"),
            P(None, "tensor"),
            P(None, "tensor"),
            P(None, "tensor"),
            P(None, "tensor"),
            P(None, "tensor", "dp"),
        ),
        check_vma=False,
    )
```

```python
import functools
import math

import jax
import jax.numpy as jnp
from jax import lax
from jax.experimental import pallas as pl
from jax.experimental.pallas import tpu as pltpu
from jax.sharding import PartitionSpec as P

LAYERS = 2
EPSILON = 1e-05
LANES = 128
HALF = 64
F32 = jnp.float32
BF16 = jnp.bfloat16
EXACT = lax.Precision.HIGHEST


class Far:
    def __init__(self, array, columns=None, place=0):
        self.array, self.place = array, place
        self.columns = array.shape[1] if columns is None else columns
        self.shape, self.dtype = (array.shape[0], self.columns), array.dtype


class Raw:
    def __init__(self, array):
        self.array, self.shape, self.dtype = array, array.shape, array.dtype


class Arrival:
    def __init__(self, copy, ref):
        self.copy, self.ref, self.waiting = copy, ref, True
        self.shape = ref.shape
        copy.start()

    def wait(self):
        if self.waiting:
            self.copy.wait()
            self.waiting = False

    def __getitem__(self, at):
        self.wait()
        return self.ref[at]


class Departure:
    def __init__(self, copy, ref):
        self.copy, self.ref, self.started = copy, ref, False
        self.shape = ref.shape

    def send(self):
        if not self.started:
            self.copy.start()
            self.started = True

    def __getitem__(self, at):
        return self.ref[at]

    def __setitem__(self, at, values):
        self.ref[at] = values
        if at is Ellipsis:
            self.send()


def dot(left, right, left_dim=1, right_dim=0, precision=None):
    return lax.dot_general(
        left,
        right,
        (((left_dim,), (right_dim,)), ((), ())),
        precision=precision,
        preferred_element_type=F32,
    )


def iota(shape, dim):
    return lax.broadcasted_iota(jnp.int32, shape, dim)


def sigmoid(values):
    return 1.0 / (1.0 + jnp.exp(-values))


def softplus(values):
    return jnp.maximum(values, 0.0) + jnp.log1p(jnp.exp(-jnp.abs(values)))


def rows_later(values, steps):
    return jnp.where(iota(values.shape, 0) >= steps, pltpu.roll(values, steps, 0), 0.0)


def rows_earlier(values, steps):
    total = values.shape[0]
    return jnp.where(
        iota(values.shape, 0) < total - steps, pltpu.roll(values, total - steps, 0), 0.0
    )


def conv(values, taps):
    result = taps[4:5, :] + taps[3:4, :] * values
    for offset in range(3):
        result = result + taps[offset : offset + 1, :] * rows_later(values, 3 - offset)
    return result


def conv_back(values, taps, grad):
    back = taps[3:4, :] * grad
    for offset in range(3):
        back = back + taps[offset : offset + 1, :] * rows_earlier(grad, 3 - offset)
    sums = [
        jnp.sum(grad * rows_later(values, 3 - offset), axis=0, keepdims=True)
        for offset in range(3)
    ]
    sums.append(jnp.sum(grad * values, axis=0, keepdims=True))
    sums.append(jnp.sum(grad, axis=0, keepdims=True))
    return back, sums


def pair_of_parts(column):
    high = column.astype(BF16).astype(F32)
    wide = jnp.broadcast_to(high, (column.shape[0], LANES))
    rest = jnp.broadcast_to(column - high, (column.shape[0], LANES))
    return jnp.where(iota(wide.shape, 1) < HALF, wide, rest).astype(BF16)


def joined_parts(message, width):
    return message[:, width : width + 1].astype(F32) + message[
        :, width + HALF : width + HALF + 1
    ].astype(F32)


def three_parts(values):
    high = values.astype(BF16)
    rest = values - high.astype(F32)
    middle = rest.astype(BF16)
    return high, middle, (rest - middle.astype(F32)).astype(BF16)


def spread_sum(parts, spread):
    spread = spread.astype(BF16)
    return dot(parts[0], spread) + dot(parts[1], spread) + dot(parts[2], spread)


def send(output):
    if isinstance(output, Departure):
        output.send()


def ready(operand):
    if isinstance(operand, Arrival):
        operand.wait()
    return operand.ref if isinstance(operand, (Arrival, Departure)) else operand


def step_state(q_rows, dt_bias, a_log):
    rows = q_rows.shape[0]
    shifted = q_rows + dt_bias
    steps = softplus(shifted)
    rates = -jnp.exp(a_log)
    below = (iota((rows, rows), 0) >= iota((rows, rows), 1)).astype(F32)
    running = dot(below, steps * rates, precision=EXACT)
    return shifted, steps, rates, running


SKIP_ROW, GAIN_ROW, BIAS_ROW, RATE_ROW = 5, 6, 7, 8


def mixer_forward(u_ref, y_ref, params, turned, bc_rows, q_rows, conv_bc, width):
    rows, inner = u_ref.shape
    states = bc_rows.shape[1] // 2
    maps = conv(bc_rows, conv_bc)
    maps = maps * sigmoid(maps)
    _, steps, _, running = step_state(
        q_rows, params[BIAS_ROW : BIAS_ROW + 1, :LANES], params[RATE_ROW : RATE_ROW + 1, :LANES]
    )
    turned[...] = running.T
    scores = dot(maps[:, states:], maps[:, :states], 1, 1, EXACT)
    steps = three_parts(steps)
    causal = iota((rows, rows), 0) >= iota((rows, rows), 1)
    lane = iota((rows, LANES), 1)
    per_block = LANES // width

    def block_step(block):
        at = pl.ds(block * LANES, LANES)
        mixed_in = conv(u_ref[:, at], params[:5, at])
        mixed_in = mixed_in * sigmoid(mixed_in)
        shape = (LANES, LANES)
        heads = block * per_block + iota(shape, 1) // width
        scaled = (mixed_in * spread_sum(steps, heads == iota(shape, 0))).astype(BF16)
        total = None
        for slot in range(per_block):
            head = block * per_block + slot
            gap = running[:, head : head + 1] - turned[head : head + 1, :]
            decay = jnp.exp(jnp.where(causal, gap, -1e30))
            part = dot((decay * scores).astype(BF16), scaled)
            total = part if slot == 0 else jnp.where(lane < slot * width, total, part)
        y_ref[:, at] = total + params[SKIP_ROW : SKIP_ROW + 1, at] * mixed_in

    for block in range(inner // LANES):
        block_step(block)


def gather_rows(target, index, blocks, width):
    rows = blocks[0].shape[0]
    for order, block in enumerate(blocks):
        place = pl.multiple_of((index ^ order) * rows, rows)
        target[pl.ds(place, rows), :] = block[:, :width]


def unpack_kernel(heads, *refs):
    index = refs[0][0]
    outs = refs[-3 * LAYERS :]
    blocks = refs[1 : -3 * LAYERS]
    slab = blocks[0].shape[1]
    depth, wide = outs[LAYERS].shape[1], outs[2 * LAYERS].shape[1]
    piece = wide // len(blocks)

    def placed(start, stop, held, total):
        result = None
        for order, block in enumerate(blocks):
            shape = (held, total)
            ones = iota(shape, 1) - (index ^ order) * held == iota(shape, 0)
            part = dot(block[...][start:stop, :held], ones.astype(BF16))
            result = part if result is None else result + part
        return result

    norm_at = LAYERS * heads
    taps_at = norm_at + LAYERS
    rows = placed(0, taps_at, slab, depth)
    taps = placed(taps_at, taps_at + 5 * LAYERS, piece, wide)
    for layer in range(LAYERS):
        steps = rows[layer * heads : (layer + 1) * heads, :]
        padding = jnp.zeros((LANES - heads, depth), F32)
        outs[layer][...] = jnp.concatenate([steps, padding], axis=0).astype(BF16)
        outs[LAYERS + layer][...] = rows[norm_at + layer : norm_at + layer + 1, :]
        outs[2 * LAYERS + layer][...] = taps[5 * layer : 5 * layer + 5, :]


def pack_kernel(index, *refs):
    blocks, (out,) = refs[:-1], refs[-1:]
    gather_rows(out, index[0], blocks, out.shape[1])


def unpack_maps_kernel(index, *refs):
    blocks, outs = refs[:-LAYERS], refs[-LAYERS:]
    piece = blocks[0].shape[1] // LAYERS
    for layer, out in enumerate(outs):
        total = None
        for order, block in enumerate(blocks):
            shape = (LAYERS * piece, out.shape[1])
            row = iota(shape, 0) - layer * piece
            ones = (row == iota(shape, 1) - (index[0] ^ order) * piece) & (row >= 0) & (row < piece)
            part = dot(block[...], ones.astype(BF16))
            total = part if total is None else total + part
        out[...] = total.astype(BF16)


def first_kernel(layer, shards, slabs, width, *refs):
    index, place = refs[0][0], refs[1][0]
    blocks, refs = refs[2 : 2 + shards], refs[2 + shards :]
    if layer:
        weights, refs = refs[:slabs], refs[slabs:]
        w_in, scales_out = refs[-3:-1]
        refs = refs[:-3] + refs[-1:]
    else:
        w_in, refs = refs[0], refs[1:]
    w_bc, gain, w_dt, conv_bc, params, normed, u_out, bc_out, q_out, y_out, turned = refs
    depth = normed.shape[1]
    inner = u_out.shape[1]
    rows = blocks[0].shape[0]
    if layer == 0:
        for order, block in enumerate(blocks):
            values = block[...].astype(F32)
            scale = lax.rsqrt(jnp.mean(values * values, axis=1, keepdims=True) + EPSILON)
            start = pl.multiple_of((index ^ order) * rows, rows)
            normed[pl.ds(start, rows), :] = (values * scale * gain[...]).astype(BF16)
    else:
        gather_rows(normed, index, blocks, depth)
        for order, block in enumerate(blocks):
            start = pl.multiple_of((index ^ order) * rows, rows)
            scales_out[pl.ds(start, rows), :] = jnp.broadcast_to(
                joined_parts(block, depth), (rows, LANES)
            )
        gather_rows(w_in, place, weights, inner)
        send(scales_out)
        send(w_in)
    send(normed)
    rows_in = normed[...]
    bc_rows = dot(rows_in, w_bc[...])
    q_rows = dot(rows_in, w_dt[...], 1, 1)
    u_rows = dot(rows_in, w_in[...])
    u_out[...] = u_rows
    bc_out[...] = bc_rows
    q_out[...] = q_rows
    mixer_forward(
        ready(u_out), ready(y_out), ready(params), turned, bc_rows, q_rows, conv_bc[...], width
    )


def live_column(length, rows):
    return (iota((rows, 1), 0) < length).astype(F32)


def second_kernel(shards, *refs):
    index = refs[0][0]
    length = refs[1][0]
    normed, w_gate, w_out, y_rows, params, z_out = refs[2:8]
    messages, scratch = refs[8 : 8 + shards], refs[8 + shards]
    depth = normed.shape[1]
    part = messages[0].shape[0]
    gate = dot(normed[...], w_gate[...])
    z_out[...] = gate
    gated = y_rows[...] * (gate * sigmoid(gate))
    live = live_column(length, y_rows.shape[0])
    hidden = (gated * params[GAIN_ROW : GAIN_ROW + 1, :] * live).astype(BF16)
    scratch[:, :depth] = dot(hidden, w_out[...], 1, 1).astype(BF16)
    scratch[:, depth:] = pair_of_parts(jnp.sum(gated * gated, axis=1, keepdims=True))
    for order, message in enumerate(messages):
        place = pl.multiple_of((index ^ order) * part, part)
        message[...] = scratch[pl.ds(place, part), :]


def last_second_kernel(shards, *refs):
    index = refs[0][0]
    length = refs[1][0]
    blocks, refs = refs[2 : 2 + shards], refs[2 + shards :]
    normed, w_gate, w_out, y_rows, params = refs[:5]
    z_out, hidden_out, grad_all, grad_hidden_out, sums_out = refs[5:]
    rows = y_rows.shape[0]
    gather_rows(grad_all, index, blocks, normed.shape[1])
    send(grad_all)
    grad_hidden = dot(grad_all[...], w_out[...])
    grad_hidden_out[...] = grad_hidden
    gate = dot(normed[...], w_gate[...])
    z_out[...] = gate
    gated = y_rows[...] * (gate * sigmoid(gate))
    squares = jnp.sum(gated * gated, axis=1, keepdims=True)
    weighted = gated * params[GAIN_ROW : GAIN_ROW + 1, :] * live_column(length, rows)
    hidden_out[...] = weighted.astype(BF16)
    products = jnp.sum(grad_hidden * weighted, axis=1, keepdims=True)
    lane = iota((rows, LANES), 1)
    table = jnp.where(lane == 0, squares, jnp.where(lane == 1, products, 0.0))
    sums_out[...] = table.T[:8, :]


def branch_kernel(shards, *refs):
    index = refs[0][0]
    hidden, w_out, scales = refs[1:4]
    messages, scratch = refs[4 : 4 + shards], refs[4 + shards]
    part = messages[0].shape[0]
    scratch[...] = (scales[:, 0:1] * dot(hidden[...], w_out[...], 1, 1)).astype(BF16)
    for order, message in enumerate(messages):
        place = pl.multiple_of((index ^ order) * part, part)
        message[...] = scratch[pl.ds(place, part), :]


def gate_back(length, scale, product, inner_all, y_rows, gate, grad_hidden, gate_gain):
    live = live_column(length, y_rows.shape[0])
    turn = sigmoid(gate)
    opened = gate * turn
    gated = y_rows * opened
    grad_live = grad_hidden * live
    grad_gain = jnp.sum(grad_live * gated * scale, axis=0, keepdims=True)
    grad_gated = scale * grad_live * gate_gain - gated * (
        scale * scale * scale * (product / inner_all)
    )
    hidden = (gated * scale * gate_gain * live).astype(BF16)
    grad_y = grad_gated * opened
    grad_gate = grad_gated * y_rows * (turn * (1.0 + gate * (1.0 - turn)))
    return hidden, grad_y, grad_gate.astype(BF16), grad_gain


def weight_grads(pairs, out, staged, sems):
    slots, part = staged.shape[:2]
    copies = []
    for slot in range(slots):
        cut = slice(slot * part, (slot + 1) * part)
        at = 0
        for left, right in pairs:
            columns = right.shape[1]
            staged[slot, :, at : at + columns] = dot(left[:, cut], right[...], 0, 0).astype(BF16)
            at += columns
        copies.append(
            pltpu.make_async_copy(staged.at[slot], out.at[pl.ds(slot * part, part), :], sems.at[slot])
        )
        copies[-1].start()
    for copy in copies:
        copy.wait()


def last_gate_kernel(shards, inner_all, *refs):
    length = refs[0][0]
    sums, refs = refs[1 : 1 + shards], refs[1 + shards :]
    y_rows, gate, grad_hidden, params, normed, grad_all = refs[:6]
    grad_y_out, grad_gate_out, gain_out, grads_out, scale_out, staged, sems = refs[6:]
    rows = y_rows.shape[0]
    total = sums[0][...]
    for other in sums[1:]:
        total = total + other[...]
    table = jnp.concatenate([total, jnp.zeros((LANES - 8, rows), F32)], axis=0).T
    scale = lax.rsqrt(table[:, 0:1] / inner_all + EPSILON)
    scale_out[...] = jnp.broadcast_to(scale, scale_out.shape)
    hidden, grad_y, grad_gate, grad_gain = gate_back(
        length,
        scale,
        table[:, 1:2],
        inner_all,
        y_rows[...],
        gate[...],
        grad_hidden[...],
        params[GAIN_ROW : GAIN_ROW + 1, :],
    )
    grad_y_out[...] = grad_y
    grad_gate_out[...] = grad_gate
    gain_out[...] = jnp.broadcast_to(grad_gain, gain_out.shape)
    weight_grads(((normed, grad_gate), (grad_all, hidden)), grads_out, staged, sems)


def gate_kernel(shards, inner_all, *refs):
    index = refs[0][0]
    length = refs[1][0]
    blocks, refs = refs[2 : 2 + shards], refs[2 + shards :]
    scales, w_out, y_rows, gate, params, normed = refs[:6]
    grad_y_out, grad_gate_out, gain_out, hidden_out, grad_all, products = refs[6:]
    depth = grad_all.shape[1]
    part = blocks[0].shape[0]
    gather_rows(grad_all, index, blocks, depth)
    for order, block in enumerate(blocks):
        place = pl.multiple_of((index ^ order) * part, part)
        products[pl.ds(place, part), :] = jnp.broadcast_to(
            joined_parts(block, depth), (part, LANES)
        )
    hidden, grad_y, grad_gate, grad_gain = gate_back(
        length,
        scales[:, 0:1],
        products[:, 0:1],
        inner_all,
        y_rows[...],
        gate[...],
        dot(grad_all[...], w_out[...]),
        params[GAIN_ROW : GAIN_ROW + 1, :],
    )
    grad_y_out[...] = grad_y
    grad_gate_out[...] = grad_gate
    hidden_out[...] = hidden
    gain_out[...] = jnp.broadcast_to(grad_gain, gain_out.shape)


def grads_kernel(normed, grad_gate, grad_all, hidden, du, out, staged, sems):
    weight_grads(((normed, grad_gate), (grad_all, hidden), (normed, du)), out, staged, sems)


def scan_back_kernel(width, index, *refs):
    u_ref, bc_ref, q_ref, y_ref, grad_ref, gain_sum, conv_bc, params_ref = refs[:8]
    du_out, dbc_out, dq_out, sums_out, sums_bc = refs[8:13]
    pieces = refs[13:-5]
    turned, grad_scores, grad_running, grad_steps, skip_sum = refs[-5:]
    params, u_ref, y_ref, grad_ref = ready(params_ref), ready(u_ref), ready(y_ref), ready(grad_ref)
    sums_x, du_ref = ready(sums_out), ready(du_out)
    bc_rows, q_rows = bc_ref[...], q_ref[...]
    rows, inner = u_ref.shape
    states = bc_rows.shape[1] // 2
    taps_bc = conv_bc[...]
    pre_bc = conv(bc_rows, taps_bc)
    turn_bc = sigmoid(pre_bc)
    maps = pre_bc * turn_bc
    shifted, steps, rates, running = step_state(
        q_rows, params[BIAS_ROW : BIAS_ROW + 1, :LANES], params[RATE_ROW : RATE_ROW + 1, :LANES]
    )
    turned[...] = running.T
    b_rows, c_rows = maps[:, :states], maps[:, states:]
    scores = dot(b_rows, c_rows, 1, 1, EXACT)
    steps_parts = three_parts(steps)
    causal = iota((rows, rows), 0) <= iota((rows, rows), 1)
    lane = iota((rows, LANES), 1)
    per_block = LANES // width
    for total in (grad_scores, grad_running, grad_steps, skip_sum):
        total[...] = jnp.zeros(total.shape, F32)

    def block_step(block):
        at = pl.ds(block * LANES, LANES)
        u_rows, grad_y = u_ref[:, at], grad_ref[:, at]
        taps_x, skips = params[:5, at], params[SKIP_ROW : SKIP_ROW + 1, at]
        pre_x = conv(u_rows, taps_x)
        turn_x = sigmoid(pre_x)
        mixed_in = pre_x * turn_x
        shape = (LANES, LANES)
        heads = block * per_block + iota(shape, 1) // width
        steps_wide = spread_sum(steps_parts, heads == iota(shape, 0))
        scaled = (mixed_in * steps_wide).astype(BF16)
        grad_low = grad_y.astype(BF16)
        grad_scaled = None
        for slot in range(per_block):
            head = block * per_block + slot
            gap = turned[head : head + 1, :] - running[:, head : head + 1]
            decay = jnp.exp(jnp.where(causal, gap, -1e30))
            part = dot((decay * scores).astype(BF16), grad_low)
            grad_scaled = part if slot == 0 else jnp.where(lane < slot * width, grad_scaled, part)
            own = jnp.where(
                (lane >= slot * width) & (lane < (slot + 1) * width), scaled, jnp.zeros_like(scaled)
            )
            grad_scores[...] += dot(own, grad_low, 1, 1) * decay
        gather = block * per_block + iota(shape, 0) // width == iota(shape, 1)
        within = y_ref[:, at] - skips * mixed_in
        moved = grad_low.astype(F32) * within - scaled.astype(F32) * grad_scaled
        grad_running[...] += spread_sum(three_parts(moved), gather)
        grad_steps[...] += spread_sum(three_parts(mixed_in * grad_scaled), gather)
        skip_row = jnp.sum(grad_y * mixed_in, axis=0, keepdims=True)
        skip_sum[...] += spread_sum(three_parts(jnp.broadcast_to(skip_row, (8, LANES))), gather)
        grad_x = steps_wide * grad_scaled + skips * grad_y
        grad_x = grad_x * (turn_x * (1.0 + pre_x * (1.0 - turn_x)))
        du, tap_sums = conv_back(u_rows, taps_x, grad_x)
        du_ref[:, at] = du.astype(BF16)
        tap_sums.append(gain_sum[0:1, at])
        tap_sums.append(jnp.zeros((2, LANES), F32))
        sums_x[:, at] = jnp.concatenate(tap_sums, axis=0)

    for block in range(inner // LANES):
        block_step(block)
    grad_b = dot(grad_scores[...], c_rows, precision=EXACT)
    grad_c = dot(grad_scores[...], b_rows, 0, 0, EXACT)
    above = (iota((rows, rows), 0) <= iota((rows, rows), 1)).astype(F32)
    grad_decay = dot(above, grad_running[...], precision=EXACT)
    grad_q = (grad_steps[...] + grad_decay * rates) * sigmoid(shifted)
    dq_out[...] = grad_q.astype(BF16)
    sums_x[6:7, :LANES] = jnp.sum(grad_q, axis=0, keepdims=True)
    sums_x[6:7, LANES : 2 * LANES] = jnp.sum(grad_decay * steps, axis=0, keepdims=True) * rates
    sums_x[6:7, 2 * LANES : 3 * LANES] = skip_sum[0:1, :]
    grad_bc = jnp.concatenate([grad_b, grad_c], axis=1)
    grad_bc = grad_bc * (turn_bc * (1.0 + pre_bc * (1.0 - turn_bc)))
    dbc, tap_sums = conv_back(bc_rows, taps_bc, grad_bc)
    low = dbc.astype(BF16)
    dbc_out[...] = low
    piece = low.shape[1] // len(pieces)
    for order, out in enumerate(pieces):
        shape = (low.shape[1], LANES)
        ones = iota(shape, 0) - (index[0] ^ order) * piece == iota(shape, 1)
        ones = ones & (iota(shape, 1) < piece)
        out[...] = dot(low, ones.astype(BF16)).astype(BF16)
    tap_sums.append(jnp.zeros((3, low.shape[1]), F32))
    sums_bc[...] = jnp.concatenate(tap_sums, axis=0)


def halving_order(count):
    order = [0]
    step = count // 2
    while step > 1:
        order = order + [place + step for place in order]
        step //= 2
    return order


def late_tail(parts, dq):
    total = parts[0][...].astype(F32)
    for other in parts[1:]:
        total = total + other[...].astype(F32)
    shape = (LANES, LANES)
    moved = (iota(shape, 1) - HALF == iota(shape, 0)).astype(BF16)
    tail = (total + dot(dq[...], moved)).astype(BF16)
    return tail


def split_slabs(place, slabs, scratch, mine, theirs):
    slab = scratch.shape[0] // slabs
    for slot, order in enumerate(halving_order(slabs)):
        cut = slice(slot * slab, (slot + 1) * slab)
        for out, flip in ((mine, 0), (theirs, 1)):
            start = pl.multiple_of((place[0] ^ (order + flip)) * slab, slab)
            out[cut, :] = scratch[pl.ds(start, slab), :]


def late_tail_kernel(shards, slabs, place, normed, dq, *refs):
    parts, (mine, theirs, scratch) = refs[:shards], refs[shards:]
    scratch[...] = dot(normed[...], late_tail(parts, dq), 0, 0).astype(BF16)
    split_slabs(place, slabs, scratch, mine, theirs)


def late_grads_kernel(shards, slabs, place, normed, du, dq, *refs):
    parts, (mine, theirs, scratch) = refs[:shards], refs[shards:]
    inner = du.shape[1]
    rows_in = normed[...]
    scratch[:, :inner] = dot(rows_in, du[...], 0, 0).astype(BF16)
    scratch[:, inner:] = dot(rows_in, late_tail(parts, dq), 0, 0).astype(BF16)
    split_slabs(place, slabs, scratch, mine, theirs)


def fold_kernel(mine, other, kept, sent):
    half = kept.shape[0]
    kept[...] = mine[:half, :].astype(F32) + other[:half, :].astype(F32)
    sent[...] = (mine[half:, :].astype(F32) + other[half:, :].astype(F32)).astype(BF16)


def tails_kernel(first_kept, first_part, last_kept, last_part, tail_out, low_out):
    tails = []
    for kept, part in ((first_kept, first_part), (last_kept, last_part)):
        inner = kept.shape[1] - LANES
        tails.append(kept[:, inner:] + part[:, inner:].astype(F32))
    tail = jnp.concatenate(tails, axis=1)
    low_out[...] = tail.astype(BF16)
    tail_out[...] = tail


def finish_kernel(layer, early, *refs):
    zx_out, out_out, zx_rows, out_rows, sems = refs[-5:]
    inner = out_rows.shape[1]
    zx_rows[:, 0, :] = early[:, :inner].astype(F32)
    if layer:
        kept, part = refs[:2]
        zx_rows[:, 1, :] = kept[:, :inner] + part[:, :inner].astype(F32)
    else:
        zx_rows[:, 1, :] = early[:, 2 * inner :].astype(F32)
    first = pltpu.make_async_copy(zx_rows, zx_out.at[layer], sems.at[0])
    first.start()
    out_rows[...] = early[:, inner : 2 * inner].astype(F32)
    second = pltpu.make_async_copy(out_rows, out_out.at[layer], sems.at[1])
    second.start()
    first.wait()
    second.wait()


def widen_kernel(index, *refs):
    blocks, outs = refs[:-LAYERS], refs[-LAYERS:]
    wide = outs[0].shape[1]
    piece = wide // len(blocks)
    for layer, out in enumerate(outs):
        total = None
        for order, block in enumerate(blocks):
            shape = (LANES, wide)
            lane = iota(shape, 1) - (index[0] ^ order) * piece
            ones = (lane == iota(shape, 0)) & (iota(shape, 0) < piece)
            part = dot(block[:, layer * LANES : (layer + 1) * LANES], ones.astype(BF16))
            total = part if total is None else total + part
        out[...] = total


def input_grad_kernel(shards, *refs):
    index = refs[0][0]
    grad_gate, du, dbc, dq, w_in, w_gate, w_bc, w_dt = refs[1:9]
    outs, scratch = refs[9 : 9 + shards], refs[9 + shards]
    part = outs[0].shape[0]
    total = dot(dbc[...], w_bc[...], 1, 1) + dot(dq[...], w_dt[...])
    total = total + dot(du[...], w_in[...], 1, 1)
    scratch[...] = (total + dot(grad_gate[...], w_gate[...], 1, 1)).astype(BF16)
    for order, out in enumerate(outs):
        place = pl.multiple_of((index ^ order) * part, part)
        out[...] = scratch[pl.ds(place, part), :]


def branch_total(messages, depth, inner_all):
    total = messages[0][:, :depth].astype(F32)
    squares = joined_parts(messages[0], depth)
    for other in messages[1:]:
        total = total + other[:, :depth].astype(F32)
        squares = squares + joined_parts(other, depth)
    return total, lax.rsqrt(squares / inner_all + EPSILON)


def residual_kernel(shards, inner_all, *refs):
    messages = refs[:shards]
    start, gain, current_out, branch_out, message_out = refs[shards:]
    depth = start.shape[1]
    branch, scale = branch_total(messages, depth, inner_all)
    current = start[...].astype(F32) + scale * branch
    current_out[...] = current
    branch_out[...] = branch
    norm = lax.rsqrt(jnp.mean(current * current, axis=1, keepdims=True) + EPSILON)
    message_out[:, :depth] = (current * norm * gain[...]).astype(BF16)
    message_out[:, depth:] = pair_of_parts(scale)


def output_kernel(shards, *refs):
    messages = refs[:shards]
    start, out = refs[shards:]
    total = start[...]
    for message in messages:
        total = total + message[...].astype(F32)
    out[...] = total


def norm_back_kernel(shards, last, *refs):
    blocks = refs[:shards]
    refs = refs[shards:]
    rows_in, gain, grad_in = refs[:3]
    current = rows_in[...].astype(F32)
    depth = current.shape[1]
    grad_normed = blocks[0][...].astype(F32)
    for other in blocks[1:]:
        grad_normed = grad_normed + other[...].astype(F32)
    norm = lax.rsqrt(jnp.mean(current * current, axis=1, keepdims=True) + EPSILON)
    weighted = grad_normed * gain[...]
    inner_product = jnp.mean(weighted * current, axis=1, keepdims=True)
    grad = grad_in[...].astype(F32) + norm * weighted - current * (norm * norm * norm * inner_product)
    gain_row = jnp.sum(grad_normed * current * norm, axis=0, keepdims=True)
    if last:
        branch, grad_out, gain_out, message_out = refs[3:]
        low = grad.astype(BF16)
        message_out[:, :depth] = low
        message_out[:, depth:] = pair_of_parts(
            jnp.sum(low.astype(F32) * branch[...], axis=1, keepdims=True)
        )
    else:
        grad_out, gain_out = refs[3:]
    grad_out[...] = grad
    gain_out[...] = jnp.broadcast_to(gain_row, gain_out.shape)


def call(kernel, name, scalars, arrays, outs, flops=0, scratch=(), vmem=24, aliases=None):
    far_in = [item for item in arrays if isinstance(item, Far)]
    far_out = [out for out in outs if out[2:] == ("far",)]
    specs, given, out_specs, shapes, held = [], [], [], [], 0
    for item in arrays:
        if isinstance(item, (Far, Raw)):
            specs.append(pl.BlockSpec(memory_space=pl.ANY))
            given.append(pltpu.with_memory_space_constraint(item.array, pltpu.HBM))
        else:
            specs.append(pl.BlockSpec(memory_space=pltpu.VMEM))
            given.append(item)
        held += math.prod(item.shape) * item.dtype.itemsize
    for shape, dtype, *kind in outs:
        out_specs.append(pl.BlockSpec(memory_space=pl.ANY if kind else pltpu.VMEM))
        shapes.append(pltpu.HBM(shape, dtype) if kind else jax.ShapeDtypeStruct(shape, dtype))
        held += math.prod(shape) * jnp.dtype(dtype).itemsize
    extra = [pltpu.VMEM(item.shape, item.dtype) for item in far_in]
    extra += [pltpu.VMEM(out[0], out[1]) for out in far_out]
    extra += [pltpu.SemaphoreType.DMA((max(1, len(far_in) + len(far_out)),))]

    def whole(*refs):
        refs = list(refs)
        own = len(refs) - len(extra)
        places, sems = refs[own:-1], refs[-1]
        refs = refs[:own]
        moved, slot = [], 0
        for order, item in enumerate(arrays):
            if isinstance(item, Far):
                at = len(scalars) + order
                source = refs[at]
                if item.columns != item.array.shape[1]:
                    source = source.at[:, pl.ds(item.place * item.columns, item.columns)]
                copy = pltpu.make_async_copy(source, places[slot], sems.at[slot])
                refs[at] = Arrival(copy, places[slot])
                moved.append(refs[at])
                slot += 1
        leaving = []
        for order, out in enumerate(outs):
            if out[2:] == ("far",):
                at = len(scalars) + len(arrays) + order
                copy = pltpu.make_async_copy(places[slot], refs[at], sems.at[slot])
                refs[at] = Departure(copy, places[slot])
                leaving.append(refs[at])
                slot += 1
        kernel(*refs)
        for item in moved:
            item.wait()
        for item in leaving:
            item.send()
        for item in leaving:
            item.copy.wait()

    return pl.pallas_call(
        whole,
        out_shape=tuple(shapes),
        in_specs=[pl.BlockSpec(memory_space=pltpu.SMEM)] * len(scalars) + specs,
        out_specs=tuple(out_specs),
        scratch_shapes=list(scratch) + extra,
        input_output_aliases=aliases or {},
        compiler_params=pltpu.CompilerParams(vmem_limit_bytes=vmem * 1024 * 1024),
        cost_estimate=pl.CostEstimate(flops=1, bytes_accessed=1, transcendentals=0),
        name=name,
    )(*scalars, *given)


def near(*parts):
    return parts if len(parts) > 1 else parts[0]


def far(shape, dtype):
    return (shape, dtype, "far")


def exchange(blocks, axis):
    count = lax.axis_size(axis)
    return [blocks[0]] + [
        lax.ppermute(blocks[k], axis, [(i, i ^ k) for i in range(count)]) for k in range(1, count)
    ]


def spread_out(block, axis):
    return exchange([block] * lax.axis_size(axis), axis)


def gather_dp(blocks):
    count = lax.axis_size("dp")
    hop = count // 2 // len(blocks)
    while hop:
        for k in list(blocks):
            blocks[k ^ hop] = lax.ppermute(blocks[k], "dp", [(i, i ^ hop) for i in range(count)])
        hop //= 2
    return [blocks[k] for k in range(count)]


def over_dp(block, hop):
    count = lax.axis_size("dp")
    return lax.ppermute(block, "dp", [(i, i ^ hop) for i in range(count)])


class Halves:
    def __init__(self, name, mine, theirs):
        self.name, self.kept, self.sent, self.hop = name, mine, theirs, 1

    def receive(self):
        other = over_dp(self.sent, self.hop)
        self.hop *= 2
        return other

    def step(self, other=None):
        half = (self.kept.shape[0] // 2, self.kept.shape[1])
        self.kept, self.sent = call(
            fold_kernel,
            self.name,
            [],
            [Far(self.kept), self.receive() if other is None else other],
            [far(half, F32), (half, BF16)],
        )

    def more(self):
        return self.hop * 2 < lax.axis_size("dp")

    def last(self):
        while self.more():
            self.step()
        return self.kept, self.receive()


def sum_over_dp(values):
    hop = 1
    while hop < lax.axis_size("dp"):
        values = values + over_dp(values, hop)
        hop *= 2
    return values


def body(
    residual_in,
    norm_gain,
    w_zx,
    w_bc,
    w_dt,
    conv_x,
    conv_bc,
    dt_bias,
    a_log,
    d_skip,
    gate_gain,
    w_out,
    lengths,
    cotangent,
):
    shards = lax.axis_size("tensor")
    dp_count = lax.axis_size("dp")
    rows, depth = residual_in.shape
    inner = gate_gain.shape[1]
    heads = dt_bias.shape[1]
    width = inner // heads
    wide = w_bc.shape[2]
    total_rows = rows * shards
    inner_all = inner * shards
    slab = norm_gain.shape[1]
    index = lax.axis_index("tensor").reshape(1).astype(jnp.int32)
    place = lax.axis_index("dp").reshape(1).astype(jnp.int32)
    message = (rows, depth + LANES)

    order = range(LAYERS)
    columns = [w_zx[0, :, 1, :], w_zx[0, :, 0, :], w_out[0].T]
    packed = jnp.concatenate(columns, axis=1)
    packed, w_dt = lax.optimization_barrier((packed, w_dt))
    w_first = lax.all_gather(packed, "dp", axis=0, tiled=True)
    x_half = [w_zx[1, :, 1, :], over_dp(w_zx[1, :, 1, :], dp_count // 2)]
    few = jnp.concatenate(
        [
            w_dt.transpose(0, 2, 1).reshape(LAYERS * heads, slab),
            norm_gain,
            jnp.pad(conv_bc.reshape(LAYERS * 5, -1), ((0, 0), (0, slab - wide // dp_count))),
        ],
        axis=0,
    )
    few = jnp.pad(few, ((0, -few.shape[0] % 16), (0, 0)))
    few, x_half[1] = lax.optimization_barrier((few, x_half[1]))
    few = gather_dp({0: few})
    x_blocks = gather_dp({0: x_half[0], dp_count // 2: x_half[1]})
    residual_blocks = spread_out(residual_in, "tensor")
    late_blocks = spread_out(cotangent, "tensor")
    w_last = lax.all_gather(
        jnp.concatenate([w_zx[1, :, 0, :], w_out[1].T], axis=1), "dp", axis=0, tiled=True
    )
    w_x = [Far(w_first, inner, 0)]
    w_gates = [Far(w_first, inner, 1), Far(w_last, inner, 0)]
    w_outs = [Far(w_first, inner, 2), Far(w_last, inner, 1)]
    piece = wide // shards
    maps = lax.dynamic_slice_in_dim(w_bc, index[0] * piece, piece, 2)
    (maps,) = call(
        pack_kernel,
        "pack_maps",
        [place],
        gather_dp({0: jnp.concatenate([maps[layer] for layer in order], axis=1)}),
        [((depth, LAYERS * piece), BF16)],
    )
    w_bcs = call(
        unpack_maps_kernel,
        "unpack_maps",
        [index],
        spread_out(maps, "tensor"),
        [far((depth, wide), BF16)] * LAYERS,
    )
    params = []
    for layer in order:
        ends = jnp.stack([dt_bias[layer], a_log[layer]])
        params.append(
            jnp.concatenate(
                [
                    conv_x[layer],
                    jnp.repeat(d_skip[layer], width)[None],
                    gate_gain[layer][None],
                    jnp.pad(ends, ((0, 7), (0, inner - heads))),
                ],
                axis=0,
            )
        )
    few[1], params[0], params[1] = lax.optimization_barrier((few[1], params[0], params[1]))
    few = call(
        functools.partial(unpack_kernel, heads),
        "unpack",
        [place],
        few,
        [far((LANES, depth), BF16)] * LAYERS + [far((1, depth), F32)] * LAYERS + [far((5, wide), F32)] * LAYERS,
    )
    w_steps, gains, taps_bc = few[:LAYERS], few[LAYERS : 2 * LAYERS], few[2 * LAYERS :]
    params = [Far(part) for part in params]
    w_steps, gains, taps_bc, w_bcs = (
        [Far(part) for part in parts] for parts in (w_steps, gains, taps_bc, w_bcs)
    )

    flops = 2 * total_rows * depth * inner
    kept = []
    blocks = residual_blocks
    current = residual_in
    for layer in order:
        last = layer == LAYERS - 1
        long = near if last else far
        hold = near if last else Far
        outs = [
            long((total_rows, depth), BF16),
            far((total_rows, inner), F32),
            far((total_rows, wide), F32),
            far((total_rows, LANES), F32),
            long((total_rows, inner), F32),
        ]
        if layer:
            outs += [far((depth, inner), BF16), far((total_rows, LANES), F32)]
        normed, u_rows, bc_rows, q_rows, y_rows, *more = call(
            functools.partial(first_kernel, layer, shards, dp_count, width),
            f"mix_{layer}",
            [index, place],
            [
                *blocks,
                *(x_blocks if layer else w_x),
                w_bcs[layer],
                gains[layer],
                w_steps[layer],
                taps_bc[layer],
                params[layer],
            ],
            outs,
            flops * 3,
            [pltpu.VMEM((LANES, total_rows), F32)],
        )
        if layer:
            w_x.append(Far(more[0]))
            scales = more[1]
        arrays = [hold(normed), w_gates[layer], w_outs[layer], hold(y_rows), params[layer]]
        if last:
            gate, last_hidden, grad_all, grad_hidden, sums = call(
                functools.partial(last_second_kernel, shards),
                f"gate_{layer}",
                [index, lengths],
                [*late_blocks, *arrays],
                [
                    ((total_rows, inner), F32),
                    ((total_rows, inner), BF16),
                    ((total_rows, depth), BF16),
                    ((total_rows, inner), F32),
                    ((8, total_rows), F32),
                ],
                flops * 2,
            )
            sums = spread_out(sums, "tensor")
        else:
            gate, *sent = call(
                functools.partial(second_kernel, shards),
                f"gate_{layer}",
                [index, lengths],
                arrays,
                [far((total_rows, inner), F32)] + [(message, BF16)] * shards,
                flops * 2,
                [pltpu.VMEM((total_rows, depth + LANES), BF16)],
            )
            sent = exchange(sent, "tensor")
        kept.append([normed, u_rows, bc_rows, q_rows, y_rows, gate, current])
        if not last:
            current, branch, packed = call(
                functools.partial(residual_kernel, shards, inner_all),
                f"residual_{layer}",
                [],
                [*sent, Far(current), gains[layer + 1]],
                [far((rows, depth), F32), far((rows, depth), F32), (message, BF16)],
            )
            blocks = spread_out(packed, "tensor")

    grad_now = cotangent
    few_x, few_bc, few_gain = {}, {}, {}
    for layer in reversed(order):
        last = layer == LAYERS - 1
        normed, u_rows, bc_rows, q_rows, y_rows, gate, rows_in = kept[layer]
        hold = near if last else Far
        outs = [
            ((total_rows, inner), F32),
            ((total_rows, inner), BF16),
            ((8, inner), F32),
        ]
        slots = depth // 512
        if last:
            grad_y, grad_gate, gain_sum, grads, out_scales = call(
                functools.partial(last_gate_kernel, shards, inner_all),
                f"gate_back_{layer}",
                [lengths],
                [*sums, y_rows, gate, grad_hidden, params[layer], normed, grad_all],
                outs
                + [((depth, 2 * inner), BF16, "raw"), far((total_rows, LANES), F32)],
                flops * 2,
                [pltpu.VMEM((slots, 512, 2 * inner), BF16), pltpu.SemaphoreType.DMA((slots,))],
            )
            grads, grad_y = lax.optimization_barrier((grads, grad_y))
            last_early = lax.psum_scatter(grads, "dp", scatter_dimension=0, tiled=True)
        else:
            grad_y, grad_gate, gain_sum, hidden, grad_all = call(
                functools.partial(gate_kernel, shards, inner_all),
                f"gate_back_{layer}",
                [index, lengths],
                [*blocks, Far(scales), w_outs[layer], Far(y_rows), Far(gate), params[layer], Far(normed)],
                outs + [((total_rows, inner), BF16), ((total_rows, depth), BF16)],
                flops * 3,
                [pltpu.VMEM((total_rows, LANES), F32)],
            )
        du, dbc, dq, few_x[layer], few_bc[layer], *pieces_bc = call(
            functools.partial(scan_back_kernel, width),
            f"mix_back_{layer}",
            [index],
            [
                Far(u_rows),
                Far(bc_rows),
                Far(q_rows),
                hold(y_rows),
                grad_y,
                gain_sum,
                taps_bc[layer],
                params[layer],
            ],
            [
                ((total_rows, inner), BF16),
                ((total_rows, wide), BF16),
                ((total_rows, LANES), BF16),
                far((8, inner), F32),
                far((8, wide), F32),
            ]
            + [((total_rows, LANES), BF16)] * shards,
            flops * 2,
            [
                pltpu.VMEM((LANES, total_rows), F32),
                pltpu.VMEM((total_rows, total_rows), F32),
                pltpu.VMEM((total_rows, LANES), F32),
                pltpu.VMEM((total_rows, LANES), F32),
                pltpu.VMEM((8, LANES), F32),
            ],
        )
        if not last:
            if last_halves.more():
                last_halves.step()
            du, last_halves.sent = lax.optimization_barrier((du, last_halves.sent))
            (grads,) = call(
                grads_kernel,
                f"grads_{layer}",
                [],
                [Far(normed), grad_gate, grad_all, hidden, du],
                [((depth, 3 * inner), BF16, "raw")],
                flops * 3,
                [pltpu.VMEM((slots, 512, 3 * inner), BF16), pltpu.SemaphoreType.DMA((slots,))],
            )
            grads, du, dq = lax.optimization_barrier((grads, du, dq))
            first_early = lax.psum_scatter(grads, "dp", scatter_dimension=0, tiled=True)
        pieces = call(
            functools.partial(input_grad_kernel, shards),
            f"input_grad_{layer}",
            [index],
            [
                grad_gate,
                du,
                dbc,
                dq,
                w_x[layer],
                w_gates[layer],
                w_bcs[layer],
                w_steps[layer],
            ],
            [((rows, depth), BF16)] * shards,
            flops * 2,
            [pltpu.VMEM((total_rows, depth), BF16)],
        )
        if last:
            pieces = list(pieces)
            pieces[0], dq = lax.optimization_barrier((pieces[0], dq))
        pieces = exchange(pieces, "tensor")
        pieces_bc = exchange(pieces_bc, "tensor")
        if last:
            tall = (depth // 2, inner + LANES)
            mine, theirs = call(
                functools.partial(late_grads_kernel, shards, dp_count),
                f"late_{layer}",
                [place],
                [normed, du, dq, *pieces_bc],
                [far(tall, BF16), (tall, BF16)],
                flops * 2,
                [pltpu.VMEM((depth, inner + LANES), BF16)],
            )
            last_halves = Halves(f"fold_{layer}", mine, theirs)
            last_halves.step()
            pieces[-1], last_halves.sent = lax.optimization_barrier((pieces[-1], last_halves.sent))
        else:
            tall = (depth // 2, LANES)
            mine, theirs = call(
                functools.partial(late_tail_kernel, shards, dp_count),
                f"late_{layer}",
                [place],
                [Far(normed), dq, *pieces_bc],
                [far(tall, BF16), (tall, BF16)],
                flops * 2,
                [pltpu.VMEM((depth, LANES), BF16)],
            )
            halves = Halves(f"fold_{layer}", mine, theirs)
            halves.step()
            first_kept, first_part = halves.last()
            last_kept, last_part = last_halves.last()
            pieces[1], last_part = lax.optimization_barrier((pieces[1], last_part))
        arrays = [*pieces, Far(rows_in), gains[layer], Far(grad_now)]
        outs = [far((rows, depth), F32), far((8, depth), F32)]
        if layer:
            arrays.append(Far(branch))
            outs.append((message, BF16))
        back = call(
            functools.partial(norm_back_kernel, shards, bool(layer)),
            f"norm_back_{layer}",
            [],
            arrays,
            outs,
        )
        grad_now, few_gain[layer] = back[:2]
        if not last:
            last_hidden, few_gain[0] = lax.optimization_barrier((last_hidden, few_gain[0]))
            messages = call(
                functools.partial(branch_kernel, shards),
                "branch",
                [index],
                [last_hidden, w_outs[-1], Far(out_scales)],
                [((rows, depth), BF16)] * shards,
                flops,
                [pltpu.VMEM((total_rows, depth), BF16)],
            )
            (output,) = call(
                functools.partial(output_kernel, shards),
                "output",
                [],
                [*exchange(messages, "tensor"), Far(current)],
                [far((rows, depth), F32)],
            )
        if layer:
            blocks = spread_out(back[2], "tensor")

    shared = jnp.stack(
        [
            jnp.concatenate([few_gain[layer][0], few_bc[layer][:5].reshape(-1)])
            for layer in order
        ]
    )
    shared = functools.reduce(jnp.add, spread_out(shared, "tensor"))
    own = jnp.stack([few_x[layer] for layer in order]).reshape(-1, LANES)
    few = jnp.concatenate([own, shared.reshape(-1, LANES)], axis=0)
    few = sum_over_dp(few)
    own = few[: own.shape[0]].reshape(LAYERS, 8, inner)
    shared = few[own.size // LANES :].reshape(LAYERS, -1)
    grad_gain = lax.dynamic_slice_in_dim(shared[:, :depth], place[0] * slab, slab, 1)
    grad_conv_bc = lax.dynamic_slice_in_dim(
        shared[:, depth:].reshape(LAYERS, 5, wide), place[0] * (wide // dp_count), wide // dp_count, 2
    )
    grad_tail, low = call(
        tails_kernel,
        "tails",
        [],
        [Far(first_kept), first_part, Far(last_kept), last_part],
        [far((slab, LAYERS * LANES), F32), ((slab, LAYERS * LANES), BF16)],
    )
    grad_bc = call(
        widen_kernel,
        "widen",
        [index],
        spread_out(low, "tensor"),
        [far((slab, wide), F32)] * LAYERS,
    )
    outs = [((LAYERS, slab, 2, inner), F32, "raw"), ((LAYERS, slab, inner), F32, "raw")]
    staged = [
        pltpu.VMEM((slab, 2, inner), F32),
        pltpu.VMEM((slab, inner), F32),
        pltpu.SemaphoreType.DMA((2,)),
    ]
    grads = call(
        functools.partial(finish_kernel, 1),
        "finish_1",
        [],
        [Far(last_early), Far(last_kept), last_part],
        outs,
        0,
        staged,
    )
    grad_zx, grad_out = call(
        functools.partial(finish_kernel, 0),
        "finish_0",
        [],
        [Far(first_early), *(Raw(part) for part in grads)],
        outs,
        0,
        staged,
        aliases={1: 0, 2: 1},
    )
    grad_out = grad_out.transpose(0, 2, 1)
    grad_bc = jnp.stack([grad_bc[layer] for layer in order])
    grad_dt = jnp.stack(
        [grad_tail[:, layer * LANES + HALF : layer * LANES + HALF + heads] for layer in order]
    )
    return (
        output,
        grad_now,
        grad_gain,
        grad_zx,
        grad_bc,
        grad_dt,
        own[:, :5],
        grad_conv_bc,
        own[:, 6, :heads],
        own[:, 6, LANES : LANES + heads],
        own[:, 6, 2 * LANES : 2 * LANES + heads],
        own[:, 5],
        grad_out,
    )


def solution(mesh):
    return jax.shard_map(
        body,
        mesh=mesh,
        in_specs=(
            P(("dp", "tensor"), None),
            P(None, "dp"),
            P(None, "dp", None, "tensor"),
            P(None, "dp", None),
            P(None, "dp", "tensor"),
            P(None, None, "tensor"),
            P(None, None, "dp"),
            P(None, "tensor"),
            P(None, "tensor"),
            P(None, "tensor"),
            P(None, "tensor"),
            P(None, "tensor", "dp"),
            P("dp"),
            P(("dp", "tensor"), None),
        ),
        out_specs=(
            P(("dp", "tensor"), None),
            P(("dp", "tensor"), None),
            P(None, "dp"),
            P(None, "dp", None, "tensor"),
            P(None, "dp", None),
            P(None, "dp", "tensor"),
            P(None, None, "tensor"),
            P(None, None, "dp"),
            P(None, "tensor"),
            P(None, "tensor"),
            P(None, "tensor"),
            P(None, "tensor"),
            P(None, "tensor", "dp"),
        ),
        check_vma=False,
    )
```

```python
import functools
import math

import jax
import jax.numpy as jnp
from jax import lax
from jax.experimental import pallas as pl
from jax.experimental.pallas import tpu as pltpu
from jax.sharding import PartitionSpec as P

LAYERS = 2
EPSILON = 1e-05
LANES = 128
HALF = 64
F32 = jnp.float32
BF16 = jnp.bfloat16
EXACT = lax.Precision.HIGHEST


class Far:
    def __init__(self, array, columns=None, place=0):
        self.array, self.place = array, place
        self.columns = array.shape[1] if columns is None else columns
        self.shape, self.dtype = (array.shape[0], self.columns), array.dtype


class Raw:
    def __init__(self, array):
        self.array, self.shape, self.dtype = array, array.shape, array.dtype


class Arrival:
    def __init__(self, copy, ref):
        self.copy, self.ref, self.waiting = copy, ref, True
        self.shape = ref.shape
        copy.start()

    def wait(self):
        if self.waiting:
            self.copy.wait()
            self.waiting = False

    def __getitem__(self, at):
        self.wait()
        return self.ref[at]


class Departure:
    def __init__(self, copy, ref):
        self.copy, self.ref, self.started = copy, ref, False
        self.shape = ref.shape

    def send(self):
        if not self.started:
            self.copy.start()
            self.started = True

    def __getitem__(self, at):
        return self.ref[at]

    def __setitem__(self, at, values):
        self.ref[at] = values
        if at is Ellipsis:
            self.send()


def dot(left, right, left_dim=1, right_dim=0, precision=None):
    return lax.dot_general(
        left,
        right,
        (((left_dim,), (right_dim,)), ((), ())),
        precision=precision,
        preferred_element_type=F32,
    )


def iota(shape, dim):
    return lax.broadcasted_iota(jnp.int32, shape, dim)


def sigmoid(values):
    return 1.0 / (1.0 + jnp.exp(-values))


def softplus(values):
    return jnp.maximum(values, 0.0) + jnp.log1p(jnp.exp(-jnp.abs(values)))


def rows_later(values, steps):
    return jnp.where(iota(values.shape, 0) >= steps, pltpu.roll(values, steps, 0), 0.0)


def rows_earlier(values, steps):
    total = values.shape[0]
    return jnp.where(
        iota(values.shape, 0) < total - steps, pltpu.roll(values, total - steps, 0), 0.0
    )


def conv(values, taps):
    result = taps[4:5, :] + taps[3:4, :] * values
    for offset in range(3):
        result = result + taps[offset : offset + 1, :] * rows_later(values, 3 - offset)
    return result


def conv_back(values, taps, grad):
    back = taps[3:4, :] * grad
    for offset in range(3):
        back = back + taps[offset : offset + 1, :] * rows_earlier(grad, 3 - offset)
    sums = [
        jnp.sum(grad * rows_later(values, 3 - offset), axis=0, keepdims=True)
        for offset in range(3)
    ]
    sums.append(jnp.sum(grad * values, axis=0, keepdims=True))
    sums.append(jnp.sum(grad, axis=0, keepdims=True))
    return back, sums


def pair_of_parts(column):
    high = column.astype(BF16).astype(F32)
    wide = jnp.broadcast_to(high, (column.shape[0], LANES))
    rest = jnp.broadcast_to(column - high, (column.shape[0], LANES))
    return jnp.where(iota(wide.shape, 1) < HALF, wide, rest).astype(BF16)


def joined_parts(message, width):
    return message[:, width : width + 1].astype(F32) + message[
        :, width + HALF : width + HALF + 1
    ].astype(F32)


def three_parts(values):
    high = values.astype(BF16)
    rest = values - high.astype(F32)
    middle = rest.astype(BF16)
    return high, middle, (rest - middle.astype(F32)).astype(BF16)


def spread_sum(parts, spread):
    spread = spread.astype(BF16)
    return dot(parts[0], spread) + dot(parts[1], spread) + dot(parts[2], spread)


def send(output):
    if isinstance(output, Departure):
        output.send()


def ready(operand):
    if isinstance(operand, Arrival):
        operand.wait()
    return operand.ref if isinstance(operand, (Arrival, Departure)) else operand


def step_state(q_rows, dt_bias, a_log):
    rows = q_rows.shape[0]
    shifted = q_rows + dt_bias
    steps = softplus(shifted)
    rates = -jnp.exp(a_log)
    below = (iota((rows, rows), 0) >= iota((rows, rows), 1)).astype(F32)
    running = dot(below, steps * rates, precision=EXACT)
    return shifted, steps, rates, running


SKIP_ROW, GAIN_ROW, BIAS_ROW, RATE_ROW = 5, 6, 7, 8


def mixer_forward(u_ref, y_ref, params, turned, bc_rows, q_rows, conv_bc, width):
    rows, inner = u_ref.shape
    states = bc_rows.shape[1] // 2
    maps = conv(bc_rows, conv_bc)
    maps = maps * sigmoid(maps)
    _, steps, _, running = step_state(
        q_rows, params[BIAS_ROW : BIAS_ROW + 1, :LANES], params[RATE_ROW : RATE_ROW + 1, :LANES]
    )
    turned[...] = running.T
    scores = dot(maps[:, states:], maps[:, :states], 1, 1, EXACT)
    steps = three_parts(steps)
    causal = iota((rows, rows), 0) >= iota((rows, rows), 1)
    lane = iota((rows, LANES), 1)
    per_block = LANES // width

    def block_step(block):
        at = pl.ds(block * LANES, LANES)
        mixed_in = conv(u_ref[:, at], params[:5, at])
        mixed_in = mixed_in * sigmoid(mixed_in)
        shape = (LANES, LANES)
        heads = block * per_block + iota(shape, 1) // width
        scaled = (mixed_in * spread_sum(steps, heads == iota(shape, 0))).astype(BF16)
        total = None
        for slot in range(per_block):
            head = block * per_block + slot
            gap = running[:, head : head + 1] - turned[head : head + 1, :]
            decay = jnp.exp(jnp.where(causal, gap, -1e30))
            part = dot((decay * scores).astype(BF16), scaled)
            total = part if slot == 0 else jnp.where(lane < slot * width, total, part)
        y_ref[:, at] = total + params[SKIP_ROW : SKIP_ROW + 1, at] * mixed_in

    for block in range(inner // LANES):
        block_step(block)


def gather_rows(target, index, blocks, width):
    rows = blocks[0].shape[0]
    for order, block in enumerate(blocks):
        place = pl.multiple_of((index ^ order) * rows, rows)
        target[pl.ds(place, rows), :] = block[:, :width]


def unpack_kernel(heads, *refs):
    index = refs[0][0]
    outs = refs[-3 * LAYERS :]
    blocks = refs[1 : -3 * LAYERS]
    slab = blocks[0].shape[1]
    depth, wide = outs[LAYERS].shape[1], outs[2 * LAYERS].shape[1]
    piece = wide // len(blocks)

    def placed(start, stop, held, total):
        result = None
        for order, block in enumerate(blocks):
            shape = (held, total)
            ones = iota(shape, 1) - (index ^ order) * held == iota(shape, 0)
            part = dot(block[...][start:stop, :held], ones.astype(BF16))
            result = part if result is None else result + part
        return result

    norm_at = LAYERS * heads
    taps_at = norm_at + LAYERS
    rows = placed(0, taps_at, slab, depth)
    taps = placed(taps_at, taps_at + 5 * LAYERS, piece, wide)
    for layer in range(LAYERS):
        steps = rows[layer * heads : (layer + 1) * heads, :]
        padding = jnp.zeros((LANES - heads, depth), F32)
        outs[layer][...] = jnp.concatenate([steps, padding], axis=0).astype(BF16)
        outs[LAYERS + layer][...] = rows[norm_at + layer : norm_at + layer + 1, :]
        outs[2 * LAYERS + layer][...] = taps[5 * layer : 5 * layer + 5, :]


def pack_kernel(index, *refs):
    blocks, (out,) = refs[:-1], refs[-1:]
    gather_rows(out, index[0], blocks, out.shape[1])


def unpack_maps_kernel(index, *refs):
    blocks, outs = refs[:-LAYERS], refs[-LAYERS:]
    piece = blocks[0].shape[1] // LAYERS
    for layer, out in enumerate(outs):
        total = None
        for order, block in enumerate(blocks):
            shape = (LAYERS * piece, out.shape[1])
            row = iota(shape, 0) - layer * piece
            ones = (row == iota(shape, 1) - (index[0] ^ order) * piece) & (row >= 0) & (row < piece)
            part = dot(block[...], ones.astype(BF16))
            total = part if total is None else total + part
        out[...] = total.astype(BF16)


def first_kernel(layer, shards, slabs, width, *refs):
    index, place = refs[0][0], refs[1][0]
    blocks, refs = refs[2 : 2 + shards], refs[2 + shards :]
    if layer:
        weights, refs = refs[:slabs], refs[slabs:]
        w_in, scales_out = refs[-3:-1]
        refs = refs[:-3] + refs[-1:]
    else:
        w_in, refs = refs[0], refs[1:]
    w_bc, gain, w_dt, conv_bc, params, normed, u_out, bc_out, q_out, y_out, turned = refs
    depth = normed.shape[1]
    inner = u_out.shape[1]
    rows = blocks[0].shape[0]
    if layer == 0:
        for order, block in enumerate(blocks):
            values = block[...].astype(F32)
            scale = lax.rsqrt(jnp.mean(values * values, axis=1, keepdims=True) + EPSILON)
            start = pl.multiple_of((index ^ order) * rows, rows)
            normed[pl.ds(start, rows), :] = (values * scale * gain[...]).astype(BF16)
    else:
        gather_rows(normed, index, blocks, depth)
        for order, block in enumerate(blocks):
            start = pl.multiple_of((index ^ order) * rows, rows)
            scales_out[pl.ds(start, rows), :] = jnp.broadcast_to(
                joined_parts(block, depth), (rows, LANES)
            )
        gather_rows(w_in, place, weights, inner)
        send(scales_out)
        send(w_in)
    send(normed)
    rows_in = normed[...]
    bc_rows = dot(rows_in, w_bc[...])
    q_rows = dot(rows_in, w_dt[...], 1, 1)
    u_rows = dot(rows_in, w_in[...])
    u_out[...] = u_rows
    bc_out[...] = bc_rows
    q_out[...] = q_rows
    mixer_forward(
        ready(u_out), ready(y_out), ready(params), turned, bc_rows, q_rows, conv_bc[...], width
    )


def live_column(length, rows):
    return (iota((rows, 1), 0) < length).astype(F32)


def second_kernel(shards, *refs):
    index = refs[0][0]
    length = refs[1][0]
    normed, w_gate, w_out, y_rows, params, z_out = refs[2:8]
    messages, scratch = refs[8 : 8 + shards], refs[8 + shards]
    depth = normed.shape[1]
    part = messages[0].shape[0]
    gate = dot(normed[...], w_gate[...])
    z_out[...] = gate
    gated = y_rows[...] * (gate * sigmoid(gate))
    live = live_column(length, y_rows.shape[0])
    hidden = (gated * params[GAIN_ROW : GAIN_ROW + 1, :] * live).astype(BF16)
    scratch[:, :depth] = dot(hidden, w_out[...], 1, 1).astype(BF16)
    scratch[:, depth:] = pair_of_parts(jnp.sum(gated * gated, axis=1, keepdims=True))
    for order, message in enumerate(messages):
        place = pl.multiple_of((index ^ order) * part, part)
        message[...] = scratch[pl.ds(place, part), :]


def last_second_kernel(shards, *refs):
    index = refs[0][0]
    length = refs[1][0]
    blocks, refs = refs[2 : 2 + shards], refs[2 + shards :]
    normed, w_gate, w_out, y_rows, params = refs[:5]
    z_out, hidden_out, grad_all, grad_hidden_out, sums_out = refs[5:]
    rows = y_rows.shape[0]
    gather_rows(grad_all, index, blocks, normed.shape[1])
    send(grad_all)
    grad_hidden = dot(grad_all[...], w_out[...])
    grad_hidden_out[...] = grad_hidden
    gate = dot(normed[...], w_gate[...])
    z_out[...] = gate
    gated = y_rows[...] * (gate * sigmoid(gate))
    squares = jnp.sum(gated * gated, axis=1, keepdims=True)
    weighted = gated * params[GAIN_ROW : GAIN_ROW + 1, :] * live_column(length, rows)
    hidden_out[...] = weighted.astype(BF16)
    products = jnp.sum(grad_hidden * weighted, axis=1, keepdims=True)
    lane = iota((rows, LANES), 1)
    table = jnp.where(lane == 0, squares, jnp.where(lane == 1, products, 0.0))
    sums_out[...] = table.T[:8, :]


def branch_kernel(shards, *refs):
    index = refs[0][0]
    hidden, w_out, scales = refs[1:4]
    messages, scratch = refs[4 : 4 + shards], refs[4 + shards]
    part = messages[0].shape[0]
    scratch[...] = (scales[:, 0:1] * dot(hidden[...], w_out[...], 1, 1)).astype(BF16)
    for order, message in enumerate(messages):
        place = pl.multiple_of((index ^ order) * part, part)
        message[...] = scratch[pl.ds(place, part), :]


def gate_back(length, scale, product, inner_all, y_rows, gate, grad_hidden, gate_gain):
    live = live_column(length, y_rows.shape[0])
    turn = sigmoid(gate)
    opened = gate * turn
    gated = y_rows * opened
    grad_live = grad_hidden * live
    grad_gain = jnp.sum(grad_live * gated * scale, axis=0, keepdims=True)
    grad_gated = scale * grad_live * gate_gain - gated * (
        scale * scale * scale * (product / inner_all)
    )
    hidden = (gated * scale * gate_gain * live).astype(BF16)
    grad_y = grad_gated * opened
    grad_gate = grad_gated * y_rows * (turn * (1.0 + gate * (1.0 - turn)))
    return hidden, grad_y, grad_gate.astype(BF16), grad_gain


def weight_grads(pairs, out, staged, sems):
    slots, part = staged.shape[:2]
    copies = []
    for slot in range(slots):
        cut = slice(slot * part, (slot + 1) * part)
        at = 0
        for left, right in pairs:
            columns = right.shape[1]
            staged[slot, :, at : at + columns] = dot(left[:, cut], right[...], 0, 0).astype(BF16)
            at += columns
        copies.append(
            pltpu.make_async_copy(staged.at[slot], out.at[pl.ds(slot * part, part), :], sems.at[slot])
        )
        copies[-1].start()
    for copy in copies:
        copy.wait()


def last_gate_kernel(shards, inner_all, *refs):
    length = refs[0][0]
    sums, refs = refs[1 : 1 + shards], refs[1 + shards :]
    y_rows, gate, grad_hidden, params, normed, grad_all = refs[:6]
    grad_y_out, grad_gate_out, gain_out, grads_out, scale_out, staged, sems = refs[6:]
    rows = y_rows.shape[0]
    total = sums[0][...]
    for other in sums[1:]:
        total = total + other[...]
    table = jnp.concatenate([total, jnp.zeros((LANES - 8, rows), F32)], axis=0).T
    scale = lax.rsqrt(table[:, 0:1] / inner_all + EPSILON)
    scale_out[...] = jnp.broadcast_to(scale, scale_out.shape)
    hidden, grad_y, grad_gate, grad_gain = gate_back(
        length,
        scale,
        table[:, 1:2],
        inner_all,
        y_rows[...],
        gate[...],
        grad_hidden[...],
        params[GAIN_ROW : GAIN_ROW + 1, :],
    )
    grad_y_out[...] = grad_y
    grad_gate_out[...] = grad_gate
    gain_out[...] = jnp.broadcast_to(grad_gain, gain_out.shape)
    weight_grads(((normed, grad_gate), (grad_all, hidden)), grads_out, staged, sems)


def gate_kernel(shards, inner_all, *refs):
    index = refs[0][0]
    length = refs[1][0]
    blocks, refs = refs[2 : 2 + shards], refs[2 + shards :]
    scales, w_out, y_rows, gate, params, normed = refs[:6]
    grad_y_out, grad_gate_out, gain_out, hidden_out, grad_all, products = refs[6:]
    depth = grad_all.shape[1]
    part = blocks[0].shape[0]
    gather_rows(grad_all, index, blocks, depth)
    for order, block in enumerate(blocks):
        place = pl.multiple_of((index ^ order) * part, part)
        products[pl.ds(place, part), :] = jnp.broadcast_to(
            joined_parts(block, depth), (part, LANES)
        )
    hidden, grad_y, grad_gate, grad_gain = gate_back(
        length,
        scales[:, 0:1],
        products[:, 0:1],
        inner_all,
        y_rows[...],
        gate[...],
        dot(grad_all[...], w_out[...]),
        params[GAIN_ROW : GAIN_ROW + 1, :],
    )
    grad_y_out[...] = grad_y
    grad_gate_out[...] = grad_gate
    hidden_out[...] = hidden
    gain_out[...] = jnp.broadcast_to(grad_gain, gain_out.shape)


def grads_kernel(normed, grad_gate, grad_all, hidden, du, out, staged, sems):
    weight_grads(((normed, grad_gate), (grad_all, hidden), (normed, du)), out, staged, sems)


def scan_back_kernel(width, index, *refs):
    u_ref, bc_ref, q_ref, y_ref, grad_ref, gain_sum, conv_bc, params_ref = refs[:8]
    du_out, dbc_out, dq_out, sums_out, sums_bc = refs[8:13]
    pieces = refs[13:-5]
    turned, grad_scores, grad_running, grad_steps, skip_sum = refs[-5:]
    params, u_ref, y_ref, grad_ref = ready(params_ref), ready(u_ref), ready(y_ref), ready(grad_ref)
    sums_x, du_ref = ready(sums_out), ready(du_out)
    bc_rows, q_rows = bc_ref[...], q_ref[...]
    rows, inner = u_ref.shape
    states = bc_rows.shape[1] // 2
    taps_bc = conv_bc[...]
    pre_bc = conv(bc_rows, taps_bc)
    turn_bc = sigmoid(pre_bc)
    maps = pre_bc * turn_bc
    shifted, steps, rates, running = step_state(
        q_rows, params[BIAS_ROW : BIAS_ROW + 1, :LANES], params[RATE_ROW : RATE_ROW + 1, :LANES]
    )
    turned[...] = running.T
    b_rows, c_rows = maps[:, :states], maps[:, states:]
    scores = dot(b_rows, c_rows, 1, 1, EXACT)
    steps_parts = three_parts(steps)
    causal = iota((rows, rows), 0) <= iota((rows, rows), 1)
    lane = iota((rows, LANES), 1)
    per_block = LANES // width
    for total in (grad_scores, grad_running, grad_steps, skip_sum):
        total[...] = jnp.zeros(total.shape, F32)

    def block_step(block):
        at = pl.ds(block * LANES, LANES)
        u_rows, grad_y = u_ref[:, at], grad_ref[:, at]
        taps_x, skips = params[:5, at], params[SKIP_ROW : SKIP_ROW + 1, at]
        pre_x = conv(u_rows, taps_x)
        turn_x = sigmoid(pre_x)
        mixed_in = pre_x * turn_x
        shape = (LANES, LANES)
        heads = block * per_block + iota(shape, 1) // width
        steps_wide = spread_sum(steps_parts, heads == iota(shape, 0))
        scaled = (mixed_in * steps_wide).astype(BF16)
        grad_low = grad_y.astype(BF16)
        grad_scaled = None
        for slot in range(per_block):
            head = block * per_block + slot
            gap = turned[head : head + 1, :] - running[:, head : head + 1]
            decay = jnp.exp(jnp.where(causal, gap, -1e30))
            part = dot((decay * scores).astype(BF16), grad_low)
            grad_scaled = part if slot == 0 else jnp.where(lane < slot * width, grad_scaled, part)
            own = jnp.where(
                (lane >= slot * width) & (lane < (slot + 1) * width), scaled, jnp.zeros_like(scaled)
            )
            grad_scores[...] += dot(own, grad_low, 1, 1) * decay
        gather = block * per_block + iota(shape, 0) // width == iota(shape, 1)
        within = y_ref[:, at] - skips * mixed_in
        moved = grad_low.astype(F32) * within - scaled.astype(F32) * grad_scaled
        grad_running[...] += spread_sum(three_parts(moved), gather)
        grad_steps[...] += spread_sum(three_parts(mixed_in * grad_scaled), gather)
        skip_row = jnp.sum(grad_y * mixed_in, axis=0, keepdims=True)
        skip_sum[...] += spread_sum(three_parts(jnp.broadcast_to(skip_row, (8, LANES))), gather)
        grad_x = steps_wide * grad_scaled + skips * grad_y
        grad_x = grad_x * (turn_x * (1.0 + pre_x * (1.0 - turn_x)))
        du, tap_sums = conv_back(u_rows, taps_x, grad_x)
        du_ref[:, at] = du.astype(BF16)
        tap_sums.append(gain_sum[0:1, at])
        tap_sums.append(jnp.zeros((2, LANES), F32))
        sums_x[:, at] = jnp.concatenate(tap_sums, axis=0)

    for block in range(inner // LANES):
        block_step(block)
    grad_b = dot(grad_scores[...], c_rows, precision=EXACT)
    grad_c = dot(grad_scores[...], b_rows, 0, 0, EXACT)
    above = (iota((rows, rows), 0) <= iota((rows, rows), 1)).astype(F32)
    grad_decay = dot(above, grad_running[...], precision=EXACT)
    grad_q = (grad_steps[...] + grad_decay * rates) * sigmoid(shifted)
    dq_out[...] = grad_q.astype(BF16)
    sums_x[6:7, :LANES] = jnp.sum(grad_q, axis=0, keepdims=True)
    sums_x[6:7, LANES : 2 * LANES] = jnp.sum(grad_decay * steps, axis=0, keepdims=True) * rates
    sums_x[6:7, 2 * LANES : 3 * LANES] = skip_sum[0:1, :]
    grad_bc = jnp.concatenate([grad_b, grad_c], axis=1)
    grad_bc = grad_bc * (turn_bc * (1.0 + pre_bc * (1.0 - turn_bc)))
    dbc, tap_sums = conv_back(bc_rows, taps_bc, grad_bc)
    low = dbc.astype(BF16)
    dbc_out[...] = low
    piece = low.shape[1] // len(pieces)
    for order, out in enumerate(pieces):
        shape = (low.shape[1], LANES)
        ones = iota(shape, 0) - (index[0] ^ order) * piece == iota(shape, 1)
        ones = ones & (iota(shape, 1) < piece)
        out[...] = dot(low, ones.astype(BF16)).astype(BF16)
    tap_sums.append(jnp.zeros((3, low.shape[1]), F32))
    sums_bc[...] = jnp.concatenate(tap_sums, axis=0)


def halving_order(count):
    order = [0]
    step = count // 2
    while step > 1:
        order = order + [place + step for place in order]
        step //= 2
    return order


def late_tail(parts, dq):
    total = parts[0][...].astype(F32)
    for other in parts[1:]:
        total = total + other[...].astype(F32)
    shape = (LANES, LANES)
    moved = (iota(shape, 1) - HALF == iota(shape, 0)).astype(BF16)
    tail = (total + dot(dq[...], moved)).astype(BF16)
    return tail


def split_slabs(place, slabs, scratch, mine, theirs):
    slab = scratch.shape[0] // slabs
    for slot, order in enumerate(halving_order(slabs)):
        cut = slice(slot * slab, (slot + 1) * slab)
        for out, flip in ((mine, 0), (theirs, 1)):
            start = pl.multiple_of((place[0] ^ (order + flip)) * slab, slab)
            out[cut, :] = scratch[pl.ds(start, slab), :]


def late_tail_kernel(shards, slabs, place, *refs):
    mine, theirs, scratch = refs[-3:]
    for layer in range(LAYERS):
        normed, dq, *parts = refs[layer * (2 + shards) : (layer + 1) * (2 + shards)]
        grads = dot(normed[...], late_tail(parts, dq), 0, 0)
        scratch[:, layer * LANES : (layer + 1) * LANES] = grads.astype(BF16)
    split_slabs(place, slabs, scratch, mine, theirs)


def late_x_kernel(slabs, place, normed, du, mine, theirs, scratch):
    scratch[...] = dot(normed[...], du[...], 0, 0).astype(BF16)
    split_slabs(place, slabs, scratch, mine, theirs)


def fold_kernel(mine, other, kept, sent):
    half = kept.shape[0]
    kept[...] = mine[:half, :].astype(F32) + other[:half, :].astype(F32)
    sent[...] = (mine[half:, :].astype(F32) + other[half:, :].astype(F32)).astype(BF16)


def tails_kernel(kept, part, tail_out, low_out):
    tail = kept[...] + part[...].astype(F32)
    low_out[...] = tail.astype(BF16)
    tail_out[...] = tail


def finish_kernel(layer, early, *refs):
    zx_out, out_out, zx_rows, out_rows, sems = refs[-5:]
    inner = out_rows.shape[1]
    zx_rows[:, 0, :] = early[:, :inner].astype(F32)
    if layer:
        kept, part = refs[:2]
        zx_rows[:, 1, :] = kept[:, :inner] + part[:, :inner].astype(F32)
    else:
        zx_rows[:, 1, :] = early[:, 2 * inner :].astype(F32)
    first = pltpu.make_async_copy(zx_rows, zx_out.at[layer], sems.at[0])
    first.start()
    out_rows[...] = early[:, inner : 2 * inner].astype(F32)
    second = pltpu.make_async_copy(out_rows, out_out.at[layer], sems.at[1])
    second.start()
    first.wait()
    second.wait()


def widen_kernel(index, *refs):
    blocks, outs = refs[:-LAYERS], refs[-LAYERS:]
    wide = outs[0].shape[1]
    piece = wide // len(blocks)
    for layer, out in enumerate(outs):
        total = None
        for order, block in enumerate(blocks):
            shape = (LANES, wide)
            lane = iota(shape, 1) - (index[0] ^ order) * piece
            ones = (lane == iota(shape, 0)) & (iota(shape, 0) < piece)
            part = dot(block[:, layer * LANES : (layer + 1) * LANES], ones.astype(BF16))
            total = part if total is None else total + part
        out[...] = total


def input_grad_kernel(shards, *refs):
    index = refs[0][0]
    grad_gate, du, dbc, dq, w_in, w_gate, w_bc, w_dt = refs[1:9]
    outs, scratch = refs[9 : 9 + shards], refs[9 + shards]
    part = outs[0].shape[0]
    total = dot(dbc[...], w_bc[...], 1, 1) + dot(dq[...], w_dt[...])
    total = total + dot(du[...], w_in[...], 1, 1)
    scratch[...] = (total + dot(grad_gate[...], w_gate[...], 1, 1)).astype(BF16)
    for order, out in enumerate(outs):
        place = pl.multiple_of((index ^ order) * part, part)
        out[...] = scratch[pl.ds(place, part), :]


def branch_total(messages, depth, inner_all):
    total = messages[0][:, :depth].astype(F32)
    squares = joined_parts(messages[0], depth)
    for other in messages[1:]:
        total = total + other[:, :depth].astype(F32)
        squares = squares + joined_parts(other, depth)
    return total, lax.rsqrt(squares / inner_all + EPSILON)


def residual_kernel(shards, inner_all, *refs):
    messages = refs[:shards]
    start, gain, current_out, branch_out, message_out = refs[shards:]
    depth = start.shape[1]
    branch, scale = branch_total(messages, depth, inner_all)
    current = start[...].astype(F32) + scale * branch
    current_out[...] = current
    branch_out[...] = branch
    norm = lax.rsqrt(jnp.mean(current * current, axis=1, keepdims=True) + EPSILON)
    message_out[:, :depth] = (current * norm * gain[...]).astype(BF16)
    message_out[:, depth:] = pair_of_parts(scale)


def output_kernel(shards, *refs):
    messages = refs[:shards]
    start, out = refs[shards:]
    total = start[...]
    for message in messages:
        total = total + message[...].astype(F32)
    out[...] = total


def norm_back_kernel(shards, last, *refs):
    blocks = refs[:shards]
    refs = refs[shards:]
    rows_in, gain, grad_in = refs[:3]
    current = rows_in[...].astype(F32)
    depth = current.shape[1]
    grad_normed = blocks[0][...].astype(F32)
    for other in blocks[1:]:
        grad_normed = grad_normed + other[...].astype(F32)
    norm = lax.rsqrt(jnp.mean(current * current, axis=1, keepdims=True) + EPSILON)
    weighted = grad_normed * gain[...]
    inner_product = jnp.mean(weighted * current, axis=1, keepdims=True)
    grad = grad_in[...].astype(F32) + norm * weighted - current * (norm * norm * norm * inner_product)
    gain_row = jnp.sum(grad_normed * current * norm, axis=0, keepdims=True)
    if last:
        branch, grad_out, gain_out, message_out = refs[3:]
        low = grad.astype(BF16)
        message_out[:, :depth] = low
        message_out[:, depth:] = pair_of_parts(
            jnp.sum(low.astype(F32) * branch[...], axis=1, keepdims=True)
        )
    else:
        grad_out, gain_out = refs[3:]
    grad_out[...] = grad
    gain_out[...] = jnp.broadcast_to(gain_row, gain_out.shape)


def call(kernel, name, scalars, arrays, outs, flops=0, scratch=(), vmem=24, aliases=None):
    far_in = [item for item in arrays if isinstance(item, Far)]
    far_out = [out for out in outs if out[2:] == ("far",)]
    specs, given, out_specs, shapes, held = [], [], [], [], 0
    for item in arrays:
        if isinstance(item, (Far, Raw)):
            specs.append(pl.BlockSpec(memory_space=pl.ANY))
            given.append(pltpu.with_memory_space_constraint(item.array, pltpu.HBM))
        else:
            specs.append(pl.BlockSpec(memory_space=pltpu.VMEM))
            given.append(item)
        held += math.prod(item.shape) * item.dtype.itemsize
    for shape, dtype, *kind in outs:
        out_specs.append(pl.BlockSpec(memory_space=pl.ANY if kind else pltpu.VMEM))
        shapes.append(pltpu.HBM(shape, dtype) if kind else jax.ShapeDtypeStruct(shape, dtype))
        held += math.prod(shape) * jnp.dtype(dtype).itemsize
    extra = [pltpu.VMEM(item.shape, item.dtype) for item in far_in]
    extra += [pltpu.VMEM(out[0], out[1]) for out in far_out]
    extra += [pltpu.SemaphoreType.DMA((max(1, len(far_in) + len(far_out)),))]

    def whole(*refs):
        refs = list(refs)
        own = len(refs) - len(extra)
        places, sems = refs[own:-1], refs[-1]
        refs = refs[:own]
        moved, slot = [], 0
        for order, item in enumerate(arrays):
            if isinstance(item, Far):
                at = len(scalars) + order
                source = refs[at]
                if item.columns != item.array.shape[1]:
                    source = source.at[:, pl.ds(item.place * item.columns, item.columns)]
                copy = pltpu.make_async_copy(source, places[slot], sems.at[slot])
                refs[at] = Arrival(copy, places[slot])
                moved.append(refs[at])
                slot += 1
        leaving = []
        for order, out in enumerate(outs):
            if out[2:] == ("far",):
                at = len(scalars) + len(arrays) + order
                copy = pltpu.make_async_copy(places[slot], refs[at], sems.at[slot])
                refs[at] = Departure(copy, places[slot])
                leaving.append(refs[at])
                slot += 1
        kernel(*refs)
        for item in moved:
            item.wait()
        for item in leaving:
            item.send()
        for item in leaving:
            item.copy.wait()

    return pl.pallas_call(
        whole,
        out_shape=tuple(shapes),
        in_specs=[pl.BlockSpec(memory_space=pltpu.SMEM)] * len(scalars) + specs,
        out_specs=tuple(out_specs),
        scratch_shapes=list(scratch) + extra,
        input_output_aliases=aliases or {},
        compiler_params=pltpu.CompilerParams(vmem_limit_bytes=vmem * 1024 * 1024),
        cost_estimate=pl.CostEstimate(flops=1, bytes_accessed=1, transcendentals=0),
        name=name,
    )(*scalars, *given)


def near(*parts):
    return parts if len(parts) > 1 else parts[0]


def far(shape, dtype):
    return (shape, dtype, "far")


def exchange(blocks, axis):
    count = lax.axis_size(axis)
    return [blocks[0]] + [
        lax.ppermute(blocks[k], axis, [(i, i ^ k) for i in range(count)]) for k in range(1, count)
    ]


def spread_out(block, axis):
    return exchange([block] * lax.axis_size(axis), axis)


def gather_dp(blocks):
    count = lax.axis_size("dp")
    hop = count // 2 // len(blocks)
    while hop:
        for k in list(blocks):
            blocks[k ^ hop] = lax.ppermute(blocks[k], "dp", [(i, i ^ hop) for i in range(count)])
        hop //= 2
    return [blocks[k] for k in range(count)]


def over_dp(block, hop):
    count = lax.axis_size("dp")
    return lax.ppermute(block, "dp", [(i, i ^ hop) for i in range(count)])


class Halves:
    def __init__(self, name, mine, theirs):
        self.name, self.kept, self.sent, self.hop = name, mine, theirs, 1

    def receive(self):
        other = over_dp(self.sent, self.hop)
        self.hop *= 2
        return other

    def step(self, other=None):
        half = (self.kept.shape[0] // 2, self.kept.shape[1])
        self.kept, self.sent = call(
            fold_kernel,
            self.name,
            [],
            [Far(self.kept), self.receive() if other is None else other],
            [far(half, F32), (half, BF16)],
        )

    def more(self):
        return self.hop * 2 < lax.axis_size("dp")

    def last(self):
        while self.more():
            self.step()
        return self.kept, self.receive()


def sum_over_dp(values):
    hop = 1
    while hop < lax.axis_size("dp"):
        values = values + over_dp(values, hop)
        hop *= 2
    return values


def body(
    residual_in,
    norm_gain,
    w_zx,
    w_bc,
    w_dt,
    conv_x,
    conv_bc,
    dt_bias,
    a_log,
    d_skip,
    gate_gain,
    w_out,
    lengths,
    cotangent,
):
    shards = lax.axis_size("tensor")
    dp_count = lax.axis_size("dp")
    rows, depth = residual_in.shape
    inner = gate_gain.shape[1]
    heads = dt_bias.shape[1]
    width = inner // heads
    wide = w_bc.shape[2]
    total_rows = rows * shards
    inner_all = inner * shards
    slab = norm_gain.shape[1]
    index = lax.axis_index("tensor").reshape(1).astype(jnp.int32)
    place = lax.axis_index("dp").reshape(1).astype(jnp.int32)
    message = (rows, depth + LANES)

    order = range(LAYERS)
    columns = [w_zx[0, :, 1, :], w_zx[0, :, 0, :], w_out[0].T]
    packed = jnp.concatenate(columns, axis=1)
    packed, w_dt = lax.optimization_barrier((packed, w_dt))
    w_first = lax.all_gather(packed, "dp", axis=0, tiled=True)
    x_half = [w_zx[1, :, 1, :], over_dp(w_zx[1, :, 1, :], dp_count // 2)]
    few = jnp.concatenate(
        [
            w_dt.transpose(0, 2, 1).reshape(LAYERS * heads, slab),
            norm_gain,
            jnp.pad(conv_bc.reshape(LAYERS * 5, -1), ((0, 0), (0, slab - wide // dp_count))),
        ],
        axis=0,
    )
    few = jnp.pad(few, ((0, -few.shape[0] % 16), (0, 0)))
    few, x_half[1] = lax.optimization_barrier((few, x_half[1]))
    few = gather_dp({0: few})
    x_blocks = gather_dp({0: x_half[0], dp_count // 2: x_half[1]})
    residual_blocks = spread_out(residual_in, "tensor")
    late_blocks = spread_out(cotangent, "tensor")
    w_last = lax.all_gather(
        jnp.concatenate([w_zx[1, :, 0, :], w_out[1].T], axis=1), "dp", axis=0, tiled=True
    )
    w_x = [Far(w_first, inner, 0)]
    w_gates = [Far(w_first, inner, 1), Far(w_last, inner, 0)]
    w_outs = [Far(w_first, inner, 2), Far(w_last, inner, 1)]
    piece = wide // shards
    maps = lax.dynamic_slice_in_dim(w_bc, index[0] * piece, piece, 2)
    (maps,) = call(
        pack_kernel,
        "pack_maps",
        [place],
        gather_dp({0: jnp.concatenate([maps[layer] for layer in order], axis=1)}),
        [((depth, LAYERS * piece), BF16)],
    )
    w_bcs = call(
        unpack_maps_kernel,
        "unpack_maps",
        [index],
        spread_out(maps, "tensor"),
        [far((depth, wide), BF16)] * LAYERS,
    )
    params = []
    for layer in order:
        ends = jnp.stack([dt_bias[layer], a_log[layer]])
        params.append(
            jnp.concatenate(
                [
                    conv_x[layer],
                    jnp.repeat(d_skip[layer], width)[None],
                    gate_gain[layer][None],
                    jnp.pad(ends, ((0, 7), (0, inner - heads))),
                ],
                axis=0,
            )
        )
    few[1], params[0], params[1] = lax.optimization_barrier((few[1], params[0], params[1]))
    few = call(
        functools.partial(unpack_kernel, heads),
        "unpack",
        [place],
        few,
        [far((LANES, depth), BF16)] * LAYERS + [far((1, depth), F32)] * LAYERS + [far((5, wide), F32)] * LAYERS,
    )
    w_steps, gains, taps_bc = few[:LAYERS], few[LAYERS : 2 * LAYERS], few[2 * LAYERS :]
    params = [Far(part) for part in params]
    w_steps, gains, taps_bc, w_bcs = (
        [Far(part) for part in parts] for parts in (w_steps, gains, taps_bc, w_bcs)
    )

    flops = 2 * total_rows * depth * inner
    kept = []
    blocks = residual_blocks
    current = residual_in
    for layer in order:
        last = layer == LAYERS - 1
        long = near if last else far
        hold = near if last else Far
        outs = [
            long((total_rows, depth), BF16),
            far((total_rows, inner), F32),
            far((total_rows, wide), F32),
            far((total_rows, LANES), F32),
            long((total_rows, inner), F32),
        ]
        if layer:
            outs += [far((depth, inner), BF16), far((total_rows, LANES), F32)]
        normed, u_rows, bc_rows, q_rows, y_rows, *more = call(
            functools.partial(first_kernel, layer, shards, dp_count, width),
            f"mix_{layer}",
            [index, place],
            [
                *blocks,
                *(x_blocks if layer else w_x),
                w_bcs[layer],
                gains[layer],
                w_steps[layer],
                taps_bc[layer],
                params[layer],
            ],
            outs,
            flops * 3,
            [pltpu.VMEM((LANES, total_rows), F32)],
        )
        if layer:
            w_x.append(Far(more[0]))
            scales = more[1]
        arrays = [hold(normed), w_gates[layer], w_outs[layer], hold(y_rows), params[layer]]
        if last:
            gate, last_hidden, grad_all, grad_hidden, sums = call(
                functools.partial(last_second_kernel, shards),
                f"gate_{layer}",
                [index, lengths],
                [*late_blocks, *arrays],
                [
                    ((total_rows, inner), F32),
                    ((total_rows, inner), BF16),
                    ((total_rows, depth), BF16),
                    ((total_rows, inner), F32),
                    ((8, total_rows), F32),
                ],
                flops * 2,
            )
            sums = spread_out(sums, "tensor")
        else:
            gate, *sent = call(
                functools.partial(second_kernel, shards),
                f"gate_{layer}",
                [index, lengths],
                arrays,
                [far((total_rows, inner), F32)] + [(message, BF16)] * shards,
                flops * 2,
                [pltpu.VMEM((total_rows, depth + LANES), BF16)],
            )
            sent = exchange(sent, "tensor")
        kept.append([normed, u_rows, bc_rows, q_rows, y_rows, gate, current])
        if not last:
            current, branch, packed = call(
                functools.partial(residual_kernel, shards, inner_all),
                f"residual_{layer}",
                [],
                [*sent, Far(current), gains[layer + 1]],
                [far((rows, depth), F32), far((rows, depth), F32), (message, BF16)],
            )
            blocks = spread_out(packed, "tensor")

    grad_now = cotangent
    few_x, few_bc, few_gain = {}, {}, {}
    for layer in reversed(order):
        last = layer == LAYERS - 1
        normed, u_rows, bc_rows, q_rows, y_rows, gate, rows_in = kept[layer]
        hold = near if last else Far
        outs = [
            ((total_rows, inner), F32),
            ((total_rows, inner), BF16),
            ((8, inner), F32),
        ]
        slots = depth // 512
        if last:
            grad_y, grad_gate, gain_sum, grads, out_scales = call(
                functools.partial(last_gate_kernel, shards, inner_all),
                f"gate_back_{layer}",
                [lengths],
                [*sums, y_rows, gate, grad_hidden, params[layer], normed, grad_all],
                outs
                + [((depth, 2 * inner), BF16, "raw"), far((total_rows, LANES), F32)],
                flops * 2,
                [pltpu.VMEM((slots, 512, 2 * inner), BF16), pltpu.SemaphoreType.DMA((slots,))],
            )
            grads, grad_y = lax.optimization_barrier((grads, grad_y))
            last_early = lax.psum_scatter(grads, "dp", scatter_dimension=0, tiled=True)
        else:
            grad_y, grad_gate, gain_sum, hidden, grad_all = call(
                functools.partial(gate_kernel, shards, inner_all),
                f"gate_back_{layer}",
                [index, lengths],
                [*blocks, Far(scales), w_outs[layer], Far(y_rows), Far(gate), params[layer], Far(normed)],
                outs + [((total_rows, inner), BF16), ((total_rows, depth), BF16)],
                flops * 3,
                [pltpu.VMEM((total_rows, LANES), F32)],
            )
        du, dbc, dq, few_x[layer], few_bc[layer], *pieces_bc = call(
            functools.partial(scan_back_kernel, width),
            f"mix_back_{layer}",
            [index],
            [
                Far(u_rows),
                Far(bc_rows),
                Far(q_rows),
                hold(y_rows),
                grad_y,
                gain_sum,
                taps_bc[layer],
                params[layer],
            ],
            [
                ((total_rows, inner), BF16),
                ((total_rows, wide), BF16),
                ((total_rows, LANES), BF16),
                far((8, inner), F32),
                far((8, wide), F32),
            ]
            + [((total_rows, LANES), BF16)] * shards,
            flops * 2,
            [
                pltpu.VMEM((LANES, total_rows), F32),
                pltpu.VMEM((total_rows, total_rows), F32),
                pltpu.VMEM((total_rows, LANES), F32),
                pltpu.VMEM((total_rows, LANES), F32),
                pltpu.VMEM((8, LANES), F32),
            ],
        )
        if not last:
            if last_halves.more():
                last_halves.step()
            du, last_halves.sent = lax.optimization_barrier((du, last_halves.sent))
            (grads,) = call(
                grads_kernel,
                f"grads_{layer}",
                [],
                [Far(normed), grad_gate, grad_all, hidden, du],
                [((depth, 3 * inner), BF16, "raw")],
                flops * 3,
                [pltpu.VMEM((slots, 512, 3 * inner), BF16), pltpu.SemaphoreType.DMA((slots,))],
            )
            grads, du, dq, *last_tail[1:] = lax.optimization_barrier((grads, du, dq, *last_tail[1:]))
            first_early = lax.psum_scatter(grads, "dp", scatter_dimension=0, tiled=True)
        pieces = call(
            functools.partial(input_grad_kernel, shards),
            f"input_grad_{layer}",
            [index],
            [
                grad_gate,
                du,
                dbc,
                dq,
                w_x[layer],
                w_gates[layer],
                w_bcs[layer],
                w_steps[layer],
            ],
            [((rows, depth), BF16)] * shards,
            flops * 2,
            [pltpu.VMEM((total_rows, depth), BF16)],
        )
        if last:
            pieces = list(pieces)
            pieces[0], du = lax.optimization_barrier((pieces[0], du))
        pieces = exchange(pieces, "tensor")
        if last:
            tall = (depth // 2, inner)
            mine, theirs = call(
                functools.partial(late_x_kernel, dp_count),
                f"late_{layer}",
                [place],
                [normed, du],
                [far(tall, BF16), (tall, BF16)],
                flops * 2,
                [pltpu.VMEM((depth, inner), BF16)],
            )
            last_tail = [normed, dq, *pieces_bc]
            last_halves = Halves(f"fold_{layer}", mine, theirs)
            last_halves.step()
            pieces[-1], last_halves.sent = lax.optimization_barrier((pieces[-1], last_halves.sent))
        else:
            tall = (depth // 2, LAYERS * LANES)
            mine, theirs = call(
                functools.partial(late_tail_kernel, shards, dp_count),
                f"late_{layer}",
                [place],
                [
                    Far(normed),
                    dq,
                    *exchange(pieces_bc, "tensor"),
                    *last_tail[:2],
                    *exchange(last_tail[2:], "tensor"),
                ],
                [far(tall, BF16), (tall, BF16)],
                flops * 2,
                [pltpu.VMEM((depth, LAYERS * LANES), BF16)],
            )
            halves = Halves(f"fold_{layer}", mine, theirs)
            halves.step()
            first_kept, first_part = halves.last()
            last_kept, last_part = last_halves.last()
            pieces[1], last_part = lax.optimization_barrier((pieces[1], last_part))
        arrays = [*pieces, Far(rows_in), gains[layer], Far(grad_now)]
        outs = [far((rows, depth), F32), far((8, depth), F32)]
        if layer:
            arrays.append(Far(branch))
            outs.append((message, BF16))
        back = call(
            functools.partial(norm_back_kernel, shards, bool(layer)),
            f"norm_back_{layer}",
            [],
            arrays,
            outs,
        )
        grad_now, few_gain[layer] = back[:2]
        if not last:
            last_hidden, few_gain[0] = lax.optimization_barrier((last_hidden, few_gain[0]))
            messages = call(
                functools.partial(branch_kernel, shards),
                "branch",
                [index],
                [last_hidden, w_outs[-1], Far(out_scales)],
                [((rows, depth), BF16)] * shards,
                flops,
                [pltpu.VMEM((total_rows, depth), BF16)],
            )
            (output,) = call(
                functools.partial(output_kernel, shards),
                "output",
                [],
                [*exchange(messages, "tensor"), Far(current)],
                [far((rows, depth), F32)],
            )
        if layer:
            blocks = spread_out(back[2], "tensor")

    shared = jnp.stack(
        [
            jnp.concatenate([few_gain[layer][0], few_bc[layer][:5].reshape(-1)])
            for layer in order
        ]
    )
    shared = functools.reduce(jnp.add, spread_out(shared, "tensor"))
    own = jnp.stack([few_x[layer] for layer in order]).reshape(-1, LANES)
    few = jnp.concatenate([own, shared.reshape(-1, LANES)], axis=0)
    few = sum_over_dp(few)
    own = few[: own.shape[0]].reshape(LAYERS, 8, inner)
    shared = few[own.size // LANES :].reshape(LAYERS, -1)
    grad_gain = lax.dynamic_slice_in_dim(shared[:, :depth], place[0] * slab, slab, 1)
    grad_conv_bc = lax.dynamic_slice_in_dim(
        shared[:, depth:].reshape(LAYERS, 5, wide), place[0] * (wide // dp_count), wide // dp_count, 2
    )
    grad_tail, low = call(
        tails_kernel,
        "tails",
        [],
        [Far(first_kept), first_part],
        [far((slab, LAYERS * LANES), F32), ((slab, LAYERS * LANES), BF16)],
    )
    grad_bc = call(
        widen_kernel,
        "widen",
        [index],
        spread_out(low, "tensor"),
        [far((slab, wide), F32)] * LAYERS,
    )
    outs = [((LAYERS, slab, 2, inner), F32, "raw"), ((LAYERS, slab, inner), F32, "raw")]
    staged = [
        pltpu.VMEM((slab, 2, inner), F32),
        pltpu.VMEM((slab, inner), F32),
        pltpu.SemaphoreType.DMA((2,)),
    ]
    grads = call(
        functools.partial(finish_kernel, 1),
        "finish_1",
        [],
        [Far(last_early), Far(last_kept), last_part],
        outs,
        0,
        staged,
    )
    grad_zx, grad_out = call(
        functools.partial(finish_kernel, 0),
        "finish_0",
        [],
        [Far(first_early), *(Raw(part) for part in grads)],
        outs,
        0,
        staged,
        aliases={1: 0, 2: 1},
    )
    grad_out = grad_out.transpose(0, 2, 1)
    grad_bc = jnp.stack([grad_bc[layer] for layer in order])
    grad_dt = jnp.stack(
        [grad_tail[:, layer * LANES + HALF : layer * LANES + HALF + heads] for layer in order]
    )
    return (
        output,
        grad_now,
        grad_gain,
        grad_zx,
        grad_bc,
        grad_dt,
        own[:, :5],
        grad_conv_bc,
        own[:, 6, :heads],
        own[:, 6, LANES : LANES + heads],
        own[:, 6, 2 * LANES : 2 * LANES + heads],
        own[:, 5],
        grad_out,
    )


def solution(mesh):
    return jax.shard_map(
        body,
        mesh=mesh,
        in_specs=(
            P(("dp", "tensor"), None),
            P(None, "dp"),
            P(None, "dp", None, "tensor"),
            P(None, "dp", None),
            P(None, "dp", "tensor"),
            P(None, None, "tensor"),
            P(None, None, "dp"),
            P(None, "tensor"),
            P(None, "tensor"),
            P(None, "tensor"),
            P(None, "tensor"),
            P(None, "tensor", "dp"),
            P("dp"),
            P(("dp", "tensor"), None),
        ),
        out_specs=(
            P(("dp", "tensor"), None),
            P(("dp", "tensor"), None),
            P(None, "dp"),
            P(None, "dp", None, "tensor"),
            P(None, "dp", None),
            P(None, "dp", "tensor"),
            P(None, None, "tensor"),
            P(None, None, "dp"),
            P(None, "tensor"),
            P(None, "tensor"),
            P(None, "tensor"),
            P(None, "tensor"),
            P(None, "tensor", "dp"),
        ),
        check_vma=False,
    )
```

```python
import functools
import math

import jax
import jax.numpy as jnp
from jax import lax
from jax.experimental import pallas as pl
from jax.experimental.pallas import tpu as pltpu
from jax.sharding import PartitionSpec as P

LAYERS = 2
EPSILON = 1e-05
LANES = 128
HALF = 64
F32 = jnp.float32
BF16 = jnp.bfloat16
EXACT = lax.Precision.HIGHEST


class Far:
    def __init__(self, array, columns=None, place=0):
        self.array, self.place = array, place
        self.columns = array.shape[1] if columns is None else columns
        self.shape, self.dtype = (array.shape[0], self.columns), array.dtype


class Raw:
    def __init__(self, array):
        self.array, self.shape, self.dtype = array, array.shape, array.dtype


class Arrival:
    def __init__(self, copy, ref):
        self.copy, self.ref, self.waiting = copy, ref, True
        self.shape = ref.shape
        copy.start()

    def wait(self):
        if self.waiting:
            self.copy.wait()
            self.waiting = False

    def __getitem__(self, at):
        self.wait()
        return self.ref[at]


class Departure:
    def __init__(self, copy, ref):
        self.copy, self.ref, self.started = copy, ref, False
        self.shape = ref.shape

    def send(self):
        if not self.started:
            self.copy.start()
            self.started = True

    def __getitem__(self, at):
        return self.ref[at]

    def __setitem__(self, at, values):
        self.ref[at] = values
        if at is Ellipsis:
            self.send()


def dot(left, right, left_dim=1, right_dim=0, precision=None):
    return lax.dot_general(
        left,
        right,
        (((left_dim,), (right_dim,)), ((), ())),
        precision=precision,
        preferred_element_type=F32,
    )


def iota(shape, dim):
    return lax.broadcasted_iota(jnp.int32, shape, dim)


def sigmoid(values):
    return 1.0 / (1.0 + jnp.exp(-values))


def softplus(values):
    return jnp.maximum(values, 0.0) + jnp.log1p(jnp.exp(-jnp.abs(values)))


def rows_later(values, steps):
    return jnp.where(iota(values.shape, 0) >= steps, pltpu.roll(values, steps, 0), 0.0)


def rows_earlier(values, steps):
    total = values.shape[0]
    return jnp.where(
        iota(values.shape, 0) < total - steps, pltpu.roll(values, total - steps, 0), 0.0
    )


def conv(values, taps):
    result = taps[4:5, :] + taps[3:4, :] * values
    for offset in range(3):
        result = result + taps[offset : offset + 1, :] * rows_later(values, 3 - offset)
    return result


def conv_back(values, taps, grad):
    back = taps[3:4, :] * grad
    for offset in range(3):
        back = back + taps[offset : offset + 1, :] * rows_earlier(grad, 3 - offset)
    sums = [
        jnp.sum(grad * rows_later(values, 3 - offset), axis=0, keepdims=True)
        for offset in range(3)
    ]
    sums.append(jnp.sum(grad * values, axis=0, keepdims=True))
    sums.append(jnp.sum(grad, axis=0, keepdims=True))
    return back, sums


def pair_of_parts(column):
    high = column.astype(BF16).astype(F32)
    wide = jnp.broadcast_to(high, (column.shape[0], LANES))
    rest = jnp.broadcast_to(column - high, (column.shape[0], LANES))
    return jnp.where(iota(wide.shape, 1) < HALF, wide, rest).astype(BF16)


def joined_parts(message, width):
    return message[:, width : width + 1].astype(F32) + message[
        :, width + HALF : width + HALF + 1
    ].astype(F32)


def three_parts(values):
    high = values.astype(BF16)
    rest = values - high.astype(F32)
    middle = rest.astype(BF16)
    return high, middle, (rest - middle.astype(F32)).astype(BF16)


def spread_sum(parts, spread):
    spread = spread.astype(BF16)
    return dot(parts[0], spread) + dot(parts[1], spread) + dot(parts[2], spread)


def send(output):
    if isinstance(output, Departure):
        output.send()


def ready(operand):
    if isinstance(operand, Arrival):
        operand.wait()
    return operand.ref if isinstance(operand, (Arrival, Departure)) else operand


def step_state(q_rows, dt_bias, a_log):
    rows = q_rows.shape[0]
    shifted = q_rows + dt_bias
    steps = softplus(shifted)
    rates = -jnp.exp(a_log)
    below = (iota((rows, rows), 0) >= iota((rows, rows), 1)).astype(F32)
    running = dot(below, steps * rates, precision=EXACT)
    return shifted, steps, rates, running


SKIP_ROW, GAIN_ROW, BIAS_ROW, RATE_ROW = 5, 6, 7, 8


def mixer_forward(u_ref, y_ref, params, turned, bc_rows, q_rows, conv_bc, width):
    rows, inner = u_ref.shape
    states = bc_rows.shape[1] // 2
    maps = conv(bc_rows, conv_bc)
    maps = maps * sigmoid(maps)
    _, steps, _, running = step_state(
        q_rows, params[BIAS_ROW : BIAS_ROW + 1, :LANES], params[RATE_ROW : RATE_ROW + 1, :LANES]
    )
    turned[...] = running.T
    scores = dot(maps[:, states:], maps[:, :states], 1, 1, EXACT)
    steps = three_parts(steps)
    causal = iota((rows, rows), 0) >= iota((rows, rows), 1)
    lane = iota((rows, LANES), 1)
    per_block = LANES // width

    def block_step(block):
        at = pl.ds(block * LANES, LANES)
        mixed_in = conv(u_ref[:, at], params[:5, at])
        mixed_in = mixed_in * sigmoid(mixed_in)
        shape = (LANES, LANES)
        heads = block * per_block + iota(shape, 1) // width
        scaled = (mixed_in * spread_sum(steps, heads == iota(shape, 0))).astype(BF16)
        total = None
        for slot in range(per_block):
            head = block * per_block + slot
            gap = running[:, head : head + 1] - turned[head : head + 1, :]
            decay = jnp.exp(jnp.where(causal, gap, -1e30))
            part = dot((decay * scores).astype(BF16), scaled)
            total = part if slot == 0 else jnp.where(lane < slot * width, total, part)
        y_ref[:, at] = total + params[SKIP_ROW : SKIP_ROW + 1, at] * mixed_in

    for block in range(inner // LANES):
        block_step(block)


def gather_rows(target, index, blocks, width):
    rows = blocks[0].shape[0]
    for order, block in enumerate(blocks):
        place = pl.multiple_of((index ^ order) * rows, rows)
        target[pl.ds(place, rows), :] = block[:, :width]


def unpack_kernel(heads, *refs):
    index = refs[0][0]
    outs = refs[-3 * LAYERS :]
    blocks = refs[1 : -3 * LAYERS]
    slab = blocks[0].shape[1]
    depth, wide = outs[LAYERS].shape[1], outs[2 * LAYERS].shape[1]
    piece = wide // len(blocks)

    def placed(start, stop, held, total):
        result = None
        for order, block in enumerate(blocks):
            shape = (held, total)
            ones = iota(shape, 1) - (index ^ order) * held == iota(shape, 0)
            part = dot(block[...][start:stop, :held], ones.astype(BF16))
            result = part if result is None else result + part
        return result

    norm_at = LAYERS * heads
    taps_at = norm_at + LAYERS
    rows = placed(0, taps_at, slab, depth)
    taps = placed(taps_at, taps_at + 5 * LAYERS, piece, wide)
    for layer in range(LAYERS):
        steps = rows[layer * heads : (layer + 1) * heads, :]
        padding = jnp.zeros((LANES - heads, depth), F32)
        outs[layer][...] = jnp.concatenate([steps, padding], axis=0).astype(BF16)
        outs[LAYERS + layer][...] = rows[norm_at + layer : norm_at + layer + 1, :]
        outs[2 * LAYERS + layer][...] = taps[5 * layer : 5 * layer + 5, :]


def pack_kernel(index, *refs):
    blocks, (out,) = refs[:-1], refs[-1:]
    gather_rows(out, index[0], blocks, out.shape[1])


def unpack_maps_kernel(index, *refs):
    blocks, outs = refs[:-LAYERS], refs[-LAYERS:]
    piece = blocks[0].shape[1] // LAYERS
    for layer, out in enumerate(outs):
        total = None
        for order, block in enumerate(blocks):
            shape = (LAYERS * piece, out.shape[1])
            row = iota(shape, 0) - layer * piece
            ones = (row == iota(shape, 1) - (index[0] ^ order) * piece) & (row >= 0) & (row < piece)
            part = dot(block[...], ones.astype(BF16))
            total = part if total is None else total + part
        out[...] = total.astype(BF16)


def first_kernel(layer, shards, slabs, width, *refs):
    index, place = refs[0][0], refs[1][0]
    blocks, refs = refs[2 : 2 + shards], refs[2 + shards :]
    if layer:
        weights, refs = refs[:slabs], refs[slabs:]
        w_in, scales_out = refs[-3:-1]
        refs = refs[:-3] + refs[-1:]
    else:
        w_in, refs = refs[0], refs[1:]
    w_bc, gain, w_dt, conv_bc, params, normed, u_out, bc_out, q_out, y_out, turned = refs
    depth = normed.shape[1]
    inner = u_out.shape[1]
    rows = blocks[0].shape[0]
    if layer == 0:
        for order, block in enumerate(blocks):
            values = block[...].astype(F32)
            scale = lax.rsqrt(jnp.mean(values * values, axis=1, keepdims=True) + EPSILON)
            start = pl.multiple_of((index ^ order) * rows, rows)
            normed[pl.ds(start, rows), :] = (values * scale * gain[...]).astype(BF16)
    else:
        gather_rows(normed, index, blocks, depth)
        for order, block in enumerate(blocks):
            start = pl.multiple_of((index ^ order) * rows, rows)
            scales_out[pl.ds(start, rows), :] = jnp.broadcast_to(
                joined_parts(block, depth), (rows, LANES)
            )
        gather_rows(w_in, place, weights, inner)
        send(scales_out)
        send(w_in)
    send(normed)
    rows_in = normed[...]
    bc_rows = dot(rows_in, w_bc[...])
    q_rows = dot(rows_in, w_dt[...], 1, 1)
    u_rows = dot(rows_in, w_in[...])
    u_out[...] = u_rows
    bc_out[...] = bc_rows
    q_out[...] = q_rows
    mixer_forward(
        ready(u_out), ready(y_out), ready(params), turned, bc_rows, q_rows, conv_bc[...], width
    )


def live_column(length, rows):
    return (iota((rows, 1), 0) < length).astype(F32)


def second_kernel(shards, *refs):
    index = refs[0][0]
    length = refs[1][0]
    normed, w_gate, w_out, y_rows, params, z_out = refs[2:8]
    messages, scratch = refs[8 : 8 + shards], refs[8 + shards]
    depth = normed.shape[1]
    part = messages[0].shape[0]
    gate = dot(normed[...], w_gate[...])
    z_out[...] = gate
    gated = y_rows[...] * (gate * sigmoid(gate))
    live = live_column(length, y_rows.shape[0])
    hidden = (gated * params[GAIN_ROW : GAIN_ROW + 1, :] * live).astype(BF16)
    scratch[:, :depth] = dot(hidden, w_out[...], 1, 1).astype(BF16)
    scratch[:, depth:] = pair_of_parts(jnp.sum(gated * gated, axis=1, keepdims=True))
    for order, message in enumerate(messages):
        place = pl.multiple_of((index ^ order) * part, part)
        message[...] = scratch[pl.ds(place, part), :]


def last_second_kernel(shards, *refs):
    index = refs[0][0]
    length = refs[1][0]
    blocks, refs = refs[2 : 2 + shards], refs[2 + shards :]
    normed, w_gate, w_out, y_rows, params = refs[:5]
    z_out, hidden_out, grad_all, grad_hidden_out, sums_out = refs[5:]
    rows = y_rows.shape[0]
    gather_rows(grad_all, index, blocks, normed.shape[1])
    send(grad_all)
    grad_hidden = dot(grad_all[...], w_out[...])
    grad_hidden_out[...] = grad_hidden
    gate = dot(normed[...], w_gate[...])
    z_out[...] = gate
    gated = y_rows[...] * (gate * sigmoid(gate))
    squares = jnp.sum(gated * gated, axis=1, keepdims=True)
    weighted = gated * params[GAIN_ROW : GAIN_ROW + 1, :] * live_column(length, rows)
    hidden_out[...] = weighted.astype(BF16)
    products = jnp.sum(grad_hidden * weighted, axis=1, keepdims=True)
    lane = iota((rows, LANES), 1)
    table = jnp.where(lane == 0, squares, jnp.where(lane == 1, products, 0.0))
    sums_out[...] = table.T[:8, :]


def branch_kernel(shards, *refs):
    index = refs[0][0]
    hidden, w_out, scales = refs[1:4]
    messages, scratch = refs[4 : 4 + shards], refs[4 + shards]
    part = messages[0].shape[0]
    scratch[...] = (scales[:, 0:1] * dot(hidden[...], w_out[...], 1, 1)).astype(BF16)
    for order, message in enumerate(messages):
        place = pl.multiple_of((index ^ order) * part, part)
        message[...] = scratch[pl.ds(place, part), :]


def gate_back(length, scale, product, inner_all, y_rows, gate, grad_hidden, gate_gain):
    live = live_column(length, y_rows.shape[0])
    turn = sigmoid(gate)
    opened = gate * turn
    gated = y_rows * opened
    grad_live = grad_hidden * live
    grad_gain = jnp.sum(grad_live * gated * scale, axis=0, keepdims=True)
    grad_gated = scale * grad_live * gate_gain - gated * (
        scale * scale * scale * (product / inner_all)
    )
    hidden = (gated * scale * gate_gain * live).astype(BF16)
    grad_y = grad_gated * opened
    grad_gate = grad_gated * y_rows * (turn * (1.0 + gate * (1.0 - turn)))
    return hidden, grad_y, grad_gate.astype(BF16), grad_gain


def weight_grads(pairs, out, staged, sems):
    slots, part = staged.shape[:2]
    copies = []
    for slot in range(slots):
        cut = slice(slot * part, (slot + 1) * part)
        at = 0
        for left, right in pairs:
            columns = right.shape[1]
            staged[slot, :, at : at + columns] = dot(left[:, cut], right[...], 0, 0).astype(BF16)
            at += columns
        copies.append(
            pltpu.make_async_copy(staged.at[slot], out.at[pl.ds(slot * part, part), :], sems.at[slot])
        )
        copies[-1].start()
    for copy in copies:
        copy.wait()


def last_gate_kernel(shards, inner_all, *refs):
    length = refs[0][0]
    sums, refs = refs[1 : 1 + shards], refs[1 + shards :]
    y_rows, gate, grad_hidden, params, normed, grad_all = refs[:6]
    grad_y_out, grad_gate_out, gain_out, grads_out, scale_out, staged, sems = refs[6:]
    rows = y_rows.shape[0]
    total = sums[0][...]
    for other in sums[1:]:
        total = total + other[...]
    table = jnp.concatenate([total, jnp.zeros((LANES - 8, rows), F32)], axis=0).T
    scale = lax.rsqrt(table[:, 0:1] / inner_all + EPSILON)
    scale_out[...] = jnp.broadcast_to(scale, scale_out.shape)
    hidden, grad_y, grad_gate, grad_gain = gate_back(
        length,
        scale,
        table[:, 1:2],
        inner_all,
        y_rows[...],
        gate[...],
        grad_hidden[...],
        params[GAIN_ROW : GAIN_ROW + 1, :],
    )
    grad_y_out[...] = grad_y
    grad_gate_out[...] = grad_gate
    gain_out[...] = jnp.broadcast_to(grad_gain, gain_out.shape)
    weight_grads(((normed, grad_gate), (grad_all, hidden)), grads_out, staged, sems)


def gate_kernel(shards, inner_all, *refs):
    index = refs[0][0]
    length = refs[1][0]
    blocks, refs = refs[2 : 2 + shards], refs[2 + shards :]
    scales, w_out, y_rows, gate, params, normed = refs[:6]
    grad_y_out, grad_gate_out, gain_out, hidden_out, grad_all, products = refs[6:]
    depth = grad_all.shape[1]
    part = blocks[0].shape[0]
    gather_rows(grad_all, index, blocks, depth)
    for order, block in enumerate(blocks):
        place = pl.multiple_of((index ^ order) * part, part)
        products[pl.ds(place, part), :] = jnp.broadcast_to(
            joined_parts(block, depth), (part, LANES)
        )
    hidden, grad_y, grad_gate, grad_gain = gate_back(
        length,
        scales[:, 0:1],
        products[:, 0:1],
        inner_all,
        y_rows[...],
        gate[...],
        dot(grad_all[...], w_out[...]),
        params[GAIN_ROW : GAIN_ROW + 1, :],
    )
    grad_y_out[...] = grad_y
    grad_gate_out[...] = grad_gate
    hidden_out[...] = hidden
    gain_out[...] = jnp.broadcast_to(grad_gain, gain_out.shape)


def grads_kernel(normed, grad_gate, grad_all, hidden, du, out, staged, sems):
    weight_grads(((normed, grad_gate), (grad_all, hidden), (normed, du)), out, staged, sems)


def scan_back_kernel(width, index, *refs):
    u_ref, bc_ref, q_ref, y_ref, grad_ref, gain_sum, conv_bc, params_ref = refs[:8]
    du_out, dbc_out, dq_out, sums_out, sums_bc = refs[8:13]
    pieces = refs[13:-5]
    turned, grad_scores, grad_running, grad_steps, skip_sum = refs[-5:]
    params, u_ref, y_ref, grad_ref = ready(params_ref), ready(u_ref), ready(y_ref), ready(grad_ref)
    sums_x, du_ref = ready(sums_out), ready(du_out)
    bc_rows, q_rows = bc_ref[...], q_ref[...]
    rows, inner = u_ref.shape
    states = bc_rows.shape[1] // 2
    taps_bc = conv_bc[...]
    pre_bc = conv(bc_rows, taps_bc)
    turn_bc = sigmoid(pre_bc)
    maps = pre_bc * turn_bc
    shifted, steps, rates, running = step_state(
        q_rows, params[BIAS_ROW : BIAS_ROW + 1, :LANES], params[RATE_ROW : RATE_ROW + 1, :LANES]
    )
    turned[...] = running.T
    b_rows, c_rows = maps[:, :states], maps[:, states:]
    scores = dot(b_rows, c_rows, 1, 1, EXACT)
    steps_parts = three_parts(steps)
    causal = iota((rows, rows), 0) <= iota((rows, rows), 1)
    lane = iota((rows, LANES), 1)
    per_block = LANES // width
    for total in (grad_scores, grad_running, grad_steps, skip_sum):
        total[...] = jnp.zeros(total.shape, F32)

    def block_step(block):
        at = pl.ds(block * LANES, LANES)
        u_rows, grad_y = u_ref[:, at], grad_ref[:, at]
        taps_x, skips = params[:5, at], params[SKIP_ROW : SKIP_ROW + 1, at]
        pre_x = conv(u_rows, taps_x)
        turn_x = sigmoid(pre_x)
        mixed_in = pre_x * turn_x
        shape = (LANES, LANES)
        heads = block * per_block + iota(shape, 1) // width
        steps_wide = spread_sum(steps_parts, heads == iota(shape, 0))
        scaled = (mixed_in * steps_wide).astype(BF16)
        grad_low = grad_y.astype(BF16)
        grad_scaled = None
        for slot in range(per_block):
            head = block * per_block + slot
            gap = turned[head : head + 1, :] - running[:, head : head + 1]
            decay = jnp.exp(jnp.where(causal, gap, -1e30))
            part = dot((decay * scores).astype(BF16), grad_low)
            grad_scaled = part if slot == 0 else jnp.where(lane < slot * width, grad_scaled, part)
            own = jnp.where(
                (lane >= slot * width) & (lane < (slot + 1) * width), scaled, jnp.zeros_like(scaled)
            )
            grad_scores[...] += dot(own, grad_low, 1, 1) * decay
        gather = block * per_block + iota(shape, 0) // width == iota(shape, 1)
        within = y_ref[:, at] - skips * mixed_in
        moved = grad_low.astype(F32) * within - scaled.astype(F32) * grad_scaled
        grad_running[...] += spread_sum(three_parts(moved), gather)
        grad_steps[...] += spread_sum(three_parts(mixed_in * grad_scaled), gather)
        skip_row = jnp.sum(grad_y * mixed_in, axis=0, keepdims=True)
        skip_sum[...] += spread_sum(three_parts(jnp.broadcast_to(skip_row, (8, LANES))), gather)
        grad_x = steps_wide * grad_scaled + skips * grad_y
        grad_x = grad_x * (turn_x * (1.0 + pre_x * (1.0 - turn_x)))
        du, tap_sums = conv_back(u_rows, taps_x, grad_x)
        du_ref[:, at] = du.astype(BF16)
        tap_sums.append(gain_sum[0:1, at])
        tap_sums.append(jnp.zeros((2, LANES), F32))
        sums_x[:, at] = jnp.concatenate(tap_sums, axis=0)

    for block in range(inner // LANES):
        block_step(block)
    grad_b = dot(grad_scores[...], c_rows, precision=EXACT)
    grad_c = dot(grad_scores[...], b_rows, 0, 0, EXACT)
    above = (iota((rows, rows), 0) <= iota((rows, rows), 1)).astype(F32)
    grad_decay = dot(above, grad_running[...], precision=EXACT)
    grad_q = (grad_steps[...] + grad_decay * rates) * sigmoid(shifted)
    dq_out[...] = grad_q.astype(BF16)
    sums_x[6:7, :LANES] = jnp.sum(grad_q, axis=0, keepdims=True)
    sums_x[6:7, LANES : 2 * LANES] = jnp.sum(grad_decay * steps, axis=0, keepdims=True) * rates
    sums_x[6:7, 2 * LANES : 3 * LANES] = skip_sum[0:1, :]
    grad_bc = jnp.concatenate([grad_b, grad_c], axis=1)
    grad_bc = grad_bc * (turn_bc * (1.0 + pre_bc * (1.0 - turn_bc)))
    dbc, tap_sums = conv_back(bc_rows, taps_bc, grad_bc)
    low = dbc.astype(BF16)
    dbc_out[...] = low
    piece = low.shape[1] // len(pieces)
    for order, out in enumerate(pieces):
        shape = (low.shape[1], LANES)
        ones = iota(shape, 0) - (index[0] ^ order) * piece == iota(shape, 1)
        ones = ones & (iota(shape, 1) < piece)
        out[...] = dot(low, ones.astype(BF16)).astype(BF16)
    tap_sums.append(jnp.zeros((3, low.shape[1]), F32))
    sums_bc[...] = jnp.concatenate(tap_sums, axis=0)


def halving_order(count):
    order = [0]
    step = count // 2
    while step > 1:
        order = order + [place + step for place in order]
        step //= 2
    return order


def late_tail(parts, dq):
    total = parts[0][...].astype(F32)
    for other in parts[1:]:
        total = total + other[...].astype(F32)
    shape = (LANES, LANES)
    moved = (iota(shape, 1) - HALF == iota(shape, 0)).astype(BF16)
    tail = (total + dot(dq[...], moved)).astype(BF16)
    return tail


def split_slabs(place, slabs, scratch, mine, theirs):
    slab = scratch.shape[0] // slabs
    for slot, order in enumerate(halving_order(slabs)):
        cut = slice(slot * slab, (slot + 1) * slab)
        for out, flip in ((mine, 0), (theirs, 1)):
            start = pl.multiple_of((place[0] ^ (order + flip)) * slab, slab)
            out[cut, :] = scratch[pl.ds(start, slab), :]


def late_tail_kernel(shards, slabs, place, *refs):
    mine, theirs, scratch = refs[-3:]
    for layer in range(LAYERS):
        normed, dq, *parts = refs[layer * (2 + shards) : (layer + 1) * (2 + shards)]
        grads = dot(normed[...], late_tail(parts, dq), 0, 0)
        scratch[:, layer * LANES : (layer + 1) * LANES] = grads.astype(BF16)
    split_slabs(place, slabs, scratch, mine, theirs)


def late_x_kernel(slabs, place, normed, du, mine, theirs, scratch):
    scratch[...] = dot(normed[...], du[...], 0, 0).astype(BF16)
    split_slabs(place, slabs, scratch, mine, theirs)


def fold_kernel(mine, other, kept, sent):
    half = kept.shape[0]
    kept[...] = mine[:half, :].astype(F32) + other[:half, :].astype(F32)
    sent[...] = (mine[half:, :].astype(F32) + other[half:, :].astype(F32)).astype(BF16)


def tails_kernel(kept, part, tail_out, low_out):
    tail = kept[...] + part[...].astype(F32)
    low_out[...] = tail.astype(BF16)
    tail_out[...] = tail


def finish_kernel(layer, early, *refs):
    zx_out, out_out, zx_rows, out_rows, sems = refs[-5:]
    rows, inner = out_rows.shape
    slots = sems.shape[0] // 2
    part = rows // slots
    copies = []
    for slot in range(slots):
        cut = pl.ds(slot * part, part)
        zx_rows[cut, 0, :] = early[cut, :inner].astype(F32)
        if layer:
            kept, other = refs[:2]
            zx_rows[cut, 1, :] = kept[cut, :inner] + other[cut, :inner].astype(F32)
        else:
            zx_rows[cut, 1, :] = early[cut, 2 * inner :].astype(F32)
        out_rows[cut, :] = early[cut, inner : 2 * inner].astype(F32)
        copies += [
            pltpu.make_async_copy(zx_rows.at[cut], zx_out.at[layer, cut], sems.at[2 * slot]),
            pltpu.make_async_copy(out_rows.at[cut], out_out.at[layer, cut], sems.at[2 * slot + 1]),
        ]
        copies[-2].start()
        copies[-1].start()
    for copy in copies:
        copy.wait()


def widen_kernel(index, *refs):
    blocks, (out,) = refs[:-1], refs[-1:]
    wide = out.shape[2]
    piece = wide // len(blocks)
    for layer in range(LAYERS):
        total = None
        for order, block in enumerate(blocks):
            shape = (LANES, wide)
            lane = iota(shape, 1) - (index[0] ^ order) * piece
            ones = (lane == iota(shape, 0)) & (iota(shape, 0) < piece)
            part = dot(block[:, layer * LANES : (layer + 1) * LANES], ones.astype(BF16))
            total = part if total is None else total + part
        out[layer, :, :] = total


def input_grad_kernel(shards, *refs):
    index = refs[0][0]
    grad_gate, du, dbc, dq, w_in, w_gate, w_bc, w_dt = refs[1:9]
    outs, scratch = refs[9 : 9 + shards], refs[9 + shards]
    part = outs[0].shape[0]
    total = dot(dbc[...], w_bc[...], 1, 1) + dot(dq[...], w_dt[...])
    total = total + dot(du[...], w_in[...], 1, 1)
    scratch[...] = (total + dot(grad_gate[...], w_gate[...], 1, 1)).astype(BF16)
    for order, out in enumerate(outs):
        place = pl.multiple_of((index ^ order) * part, part)
        out[...] = scratch[pl.ds(place, part), :]


def branch_total(messages, depth, inner_all):
    total = messages[0][:, :depth].astype(F32)
    squares = joined_parts(messages[0], depth)
    for other in messages[1:]:
        total = total + other[:, :depth].astype(F32)
        squares = squares + joined_parts(other, depth)
    return total, lax.rsqrt(squares / inner_all + EPSILON)


def residual_kernel(shards, inner_all, *refs):
    messages = refs[:shards]
    start, gain, current_out, branch_out, message_out = refs[shards:]
    depth = start.shape[1]
    branch, scale = branch_total(messages, depth, inner_all)
    current = start[...].astype(F32) + scale * branch
    current_out[...] = current
    branch_out[...] = branch
    norm = lax.rsqrt(jnp.mean(current * current, axis=1, keepdims=True) + EPSILON)
    message_out[:, :depth] = (current * norm * gain[...]).astype(BF16)
    message_out[:, depth:] = pair_of_parts(scale)


def output_kernel(shards, *refs):
    messages = refs[:shards]
    start, out = refs[shards:]
    total = start[...]
    for message in messages:
        total = total + message[...].astype(F32)
    out[...] = total


def norm_back_kernel(shards, last, *refs):
    blocks = refs[:shards]
    refs = refs[shards:]
    rows_in, gain, grad_in = refs[:3]
    current = rows_in[...].astype(F32)
    depth = current.shape[1]
    grad_normed = blocks[0][...].astype(F32)
    for other in blocks[1:]:
        grad_normed = grad_normed + other[...].astype(F32)
    norm = lax.rsqrt(jnp.mean(current * current, axis=1, keepdims=True) + EPSILON)
    weighted = grad_normed * gain[...]
    inner_product = jnp.mean(weighted * current, axis=1, keepdims=True)
    grad = grad_in[...].astype(F32) + norm * weighted - current * (norm * norm * norm * inner_product)
    gain_row = jnp.sum(grad_normed * current * norm, axis=0, keepdims=True)
    if last:
        branch, grad_out, gain_out, message_out = refs[3:]
        low = grad.astype(BF16)
        message_out[:, :depth] = low
        message_out[:, depth:] = pair_of_parts(
            jnp.sum(low.astype(F32) * branch[...], axis=1, keepdims=True)
        )
    else:
        grad_out, gain_out = refs[3:]
    grad_out[...] = grad
    gain_out[...] = jnp.broadcast_to(gain_row, gain_out.shape)


def call(kernel, name, scalars, arrays, outs, flops=0, scratch=(), vmem=24, aliases=None):
    far_in = [item for item in arrays if isinstance(item, Far)]
    far_out = [out for out in outs if out[2:] == ("far",)]
    specs, given, out_specs, shapes, held = [], [], [], [], 0
    for item in arrays:
        if isinstance(item, (Far, Raw)):
            specs.append(pl.BlockSpec(memory_space=pl.ANY))
            given.append(pltpu.with_memory_space_constraint(item.array, pltpu.HBM))
        else:
            specs.append(pl.BlockSpec(memory_space=pltpu.VMEM))
            given.append(item)
        held += math.prod(item.shape) * item.dtype.itemsize
    for shape, dtype, *kind in outs:
        out_specs.append(pl.BlockSpec(memory_space=pl.ANY if kind else pltpu.VMEM))
        shapes.append(pltpu.HBM(shape, dtype) if kind else jax.ShapeDtypeStruct(shape, dtype))
        held += math.prod(shape) * jnp.dtype(dtype).itemsize
    extra = [pltpu.VMEM(item.shape, item.dtype) for item in far_in]
    extra += [pltpu.VMEM(out[0], out[1]) for out in far_out]
    extra += [pltpu.SemaphoreType.DMA((max(1, len(far_in) + len(far_out)),))]

    def whole(*refs):
        refs = list(refs)
        own = len(refs) - len(extra)
        places, sems = refs[own:-1], refs[-1]
        refs = refs[:own]
        moved, slot = [], 0
        for order, item in enumerate(arrays):
            if isinstance(item, Far):
                at = len(scalars) + order
                source = refs[at]
                if item.columns != item.array.shape[1]:
                    source = source.at[:, pl.ds(item.place * item.columns, item.columns)]
                copy = pltpu.make_async_copy(source, places[slot], sems.at[slot])
                refs[at] = Arrival(copy, places[slot])
                moved.append(refs[at])
                slot += 1
        leaving = []
        for order, out in enumerate(outs):
            if out[2:] == ("far",):
                at = len(scalars) + len(arrays) + order
                copy = pltpu.make_async_copy(places[slot], refs[at], sems.at[slot])
                refs[at] = Departure(copy, places[slot])
                leaving.append(refs[at])
                slot += 1
        kernel(*refs)
        for item in moved:
            item.wait()
        for item in leaving:
            item.send()
        for item in leaving:
            item.copy.wait()

    return pl.pallas_call(
        whole,
        out_shape=tuple(shapes),
        in_specs=[pl.BlockSpec(memory_space=pltpu.SMEM)] * len(scalars) + specs,
        out_specs=tuple(out_specs),
        scratch_shapes=list(scratch) + extra,
        input_output_aliases=aliases or {},
        compiler_params=pltpu.CompilerParams(vmem_limit_bytes=vmem * 1024 * 1024),
        cost_estimate=pl.CostEstimate(flops=1, bytes_accessed=1, transcendentals=0),
        name=name,
    )(*scalars, *given)


def near(*parts):
    return parts if len(parts) > 1 else parts[0]


def far(shape, dtype):
    return (shape, dtype, "far")


def exchange(blocks, axis):
    count = lax.axis_size(axis)
    return [blocks[0]] + [
        lax.ppermute(blocks[k], axis, [(i, i ^ k) for i in range(count)]) for k in range(1, count)
    ]


def spread_out(block, axis):
    return exchange([block] * lax.axis_size(axis), axis)


def gather_dp(blocks):
    count = lax.axis_size("dp")
    hop = count // 2 // len(blocks)
    while hop:
        for k in list(blocks):
            blocks[k ^ hop] = lax.ppermute(blocks[k], "dp", [(i, i ^ hop) for i in range(count)])
        hop //= 2
    return [blocks[k] for k in range(count)]


def over_dp(block, hop):
    count = lax.axis_size("dp")
    return lax.ppermute(block, "dp", [(i, i ^ hop) for i in range(count)])


class Halves:
    def __init__(self, name, mine, theirs):
        self.name, self.kept, self.sent, self.hop = name, mine, theirs, 1

    def receive(self):
        other = over_dp(self.sent, self.hop)
        self.hop *= 2
        return other

    def step(self, other=None):
        half = (self.kept.shape[0] // 2, self.kept.shape[1])
        self.kept, self.sent = call(
            fold_kernel,
            self.name,
            [],
            [Far(self.kept), self.receive() if other is None else other],
            [far(half, F32), (half, BF16)],
        )

    def more(self):
        return self.hop * 2 < lax.axis_size("dp")

    def last(self):
        while self.more():
            self.step()
        return self.kept, self.receive()


def sum_over_dp(values):
    hop = 1
    while hop < lax.axis_size("dp"):
        values = values + over_dp(values, hop)
        hop *= 2
    return values


def body(
    residual_in,
    norm_gain,
    w_zx,
    w_bc,
    w_dt,
    conv_x,
    conv_bc,
    dt_bias,
    a_log,
    d_skip,
    gate_gain,
    w_out,
    lengths,
    cotangent,
):
    shards = lax.axis_size("tensor")
    dp_count = lax.axis_size("dp")
    rows, depth = residual_in.shape
    inner = gate_gain.shape[1]
    heads = dt_bias.shape[1]
    width = inner // heads
    wide = w_bc.shape[2]
    total_rows = rows * shards
    inner_all = inner * shards
    slab = norm_gain.shape[1]
    index = lax.axis_index("tensor").reshape(1).astype(jnp.int32)
    place = lax.axis_index("dp").reshape(1).astype(jnp.int32)
    message = (rows, depth + LANES)

    order = range(LAYERS)
    columns = [w_zx[0, :, 1, :], w_zx[0, :, 0, :], w_out[0].T]
    packed = jnp.concatenate(columns, axis=1)
    packed, w_dt, w_zx, w_out = lax.optimization_barrier((packed, w_dt, w_zx, w_out))
    w_first = lax.all_gather(packed, "dp", axis=0, tiled=True)
    x_half = [w_zx[1, :, 1, :], over_dp(w_zx[1, :, 1, :], dp_count // 2)]
    few = jnp.concatenate(
        [
            w_dt.transpose(0, 2, 1).reshape(LAYERS * heads, slab),
            norm_gain,
            jnp.pad(conv_bc.reshape(LAYERS * 5, -1), ((0, 0), (0, slab - wide // dp_count))),
        ],
        axis=0,
    )
    few = jnp.pad(few, ((0, -few.shape[0] % 16), (0, 0)))
    few, x_half[1] = lax.optimization_barrier((few, x_half[1]))
    few = gather_dp({0: few})
    x_blocks = gather_dp({0: x_half[0], dp_count // 2: x_half[1]})
    residual_blocks = spread_out(residual_in, "tensor")
    late_blocks = spread_out(cotangent, "tensor")
    w_last = lax.all_gather(
        jnp.concatenate([w_zx[1, :, 0, :], w_out[1].T], axis=1), "dp", axis=0, tiled=True
    )
    w_x = [Far(w_first, inner, 0)]
    w_gates = [Far(w_first, inner, 1), Far(w_last, inner, 0)]
    w_outs = [Far(w_first, inner, 2), Far(w_last, inner, 1)]
    piece = wide // shards
    maps = lax.dynamic_slice_in_dim(w_bc, index[0] * piece, piece, 2)
    (maps,) = call(
        pack_kernel,
        "pack_maps",
        [place],
        gather_dp({0: jnp.concatenate([maps[layer] for layer in order], axis=1)}),
        [((depth, LAYERS * piece), BF16)],
    )
    w_bcs = call(
        unpack_maps_kernel,
        "unpack_maps",
        [index],
        spread_out(maps, "tensor"),
        [far((depth, wide), BF16)] * LAYERS,
    )
    params = []
    for layer in order:
        ends = jnp.stack([dt_bias[layer], a_log[layer]])
        params.append(
            jnp.concatenate(
                [
                    conv_x[layer],
                    jnp.repeat(d_skip[layer], width)[None],
                    gate_gain[layer][None],
                    jnp.pad(ends, ((0, 7), (0, inner - heads))),
                ],
                axis=0,
            )
        )
    few[1], params[0], params[1] = lax.optimization_barrier((few[1], params[0], params[1]))
    few = call(
        functools.partial(unpack_kernel, heads),
        "unpack",
        [place],
        few,
        [far((LANES, depth), BF16)] * LAYERS + [far((1, depth), F32)] * LAYERS + [far((5, wide), F32)] * LAYERS,
    )
    w_steps, gains, taps_bc = few[:LAYERS], few[LAYERS : 2 * LAYERS], few[2 * LAYERS :]
    params = [Far(part) for part in params]
    w_steps, gains, taps_bc, w_bcs = (
        [Far(part) for part in parts] for parts in (w_steps, gains, taps_bc, w_bcs)
    )

    flops = 2 * total_rows * depth * inner
    kept = []
    blocks = residual_blocks
    current = residual_in
    for layer in order:
        last = layer == LAYERS - 1
        long = near if last else far
        hold = near if last else Far
        outs = [
            long((total_rows, depth), BF16),
            far((total_rows, inner), F32),
            far((total_rows, wide), F32),
            far((total_rows, LANES), F32),
            long((total_rows, inner), F32),
        ]
        if layer:
            outs += [far((depth, inner), BF16), far((total_rows, LANES), F32)]
        normed, u_rows, bc_rows, q_rows, y_rows, *more = call(
            functools.partial(first_kernel, layer, shards, dp_count, width),
            f"mix_{layer}",
            [index, place],
            [
                *blocks,
                *(x_blocks if layer else w_x),
                w_bcs[layer],
                gains[layer],
                w_steps[layer],
                taps_bc[layer],
                params[layer],
            ],
            outs,
            flops * 3,
            [pltpu.VMEM((LANES, total_rows), F32)],
        )
        if layer:
            w_x.append(Far(more[0]))
            scales = more[1]
        arrays = [hold(normed), w_gates[layer], w_outs[layer], hold(y_rows), params[layer]]
        if last:
            gate, last_hidden, grad_all, grad_hidden, sums = call(
                functools.partial(last_second_kernel, shards),
                f"gate_{layer}",
                [index, lengths],
                [*late_blocks, *arrays],
                [
                    ((total_rows, inner), F32),
                    ((total_rows, inner), BF16),
                    ((total_rows, depth), BF16),
                    ((total_rows, inner), F32),
                    ((8, total_rows), F32),
                ],
                flops * 2,
            )
            sums = spread_out(sums, "tensor")
        else:
            gate, *sent = call(
                functools.partial(second_kernel, shards),
                f"gate_{layer}",
                [index, lengths],
                arrays,
                [far((total_rows, inner), F32)] + [(message, BF16)] * shards,
                flops * 2,
                [pltpu.VMEM((total_rows, depth + LANES), BF16)],
            )
            sent = exchange(sent, "tensor")
        kept.append([normed, u_rows, bc_rows, q_rows, y_rows, gate, current])
        if not last:
            current, branch, packed = call(
                functools.partial(residual_kernel, shards, inner_all),
                f"residual_{layer}",
                [],
                [*sent, Far(current), gains[layer + 1]],
                [far((rows, depth), F32), far((rows, depth), F32), (message, BF16)],
            )
            blocks = spread_out(packed, "tensor")

    grad_now = cotangent
    few_x, few_bc, few_gain = {}, {}, {}
    for layer in reversed(order):
        last = layer == LAYERS - 1
        normed, u_rows, bc_rows, q_rows, y_rows, gate, rows_in = kept[layer]
        hold = near if last else Far
        outs = [
            ((total_rows, inner), F32),
            ((total_rows, inner), BF16),
            ((8, inner), F32),
        ]
        slots = depth // 512
        if last:
            grad_y, grad_gate, gain_sum, grads, out_scales = call(
                functools.partial(last_gate_kernel, shards, inner_all),
                f"gate_back_{layer}",
                [lengths],
                [*sums, y_rows, gate, grad_hidden, params[layer], normed, grad_all],
                outs
                + [((depth, 2 * inner), BF16, "raw"), far((total_rows, LANES), F32)],
                flops * 2,
                [pltpu.VMEM((slots, 512, 2 * inner), BF16), pltpu.SemaphoreType.DMA((slots,))],
            )
            grads, grad_y = lax.optimization_barrier((grads, grad_y))
            last_early = lax.psum_scatter(grads, "dp", scatter_dimension=0, tiled=True)
        else:
            grad_y, grad_gate, gain_sum, hidden, grad_all = call(
                functools.partial(gate_kernel, shards, inner_all),
                f"gate_back_{layer}",
                [index, lengths],
                [*blocks, Far(scales), w_outs[layer], Far(y_rows), Far(gate), params[layer], Far(normed)],
                outs + [((total_rows, inner), BF16), ((total_rows, depth), BF16)],
                flops * 3,
                [pltpu.VMEM((total_rows, LANES), F32)],
            )
        du, dbc, dq, few_x[layer], few_bc[layer], *pieces_bc = call(
            functools.partial(scan_back_kernel, width),
            f"mix_back_{layer}",
            [index],
            [
                Far(u_rows),
                Far(bc_rows),
                Far(q_rows),
                hold(y_rows),
                grad_y,
                gain_sum,
                taps_bc[layer],
                params[layer],
            ],
            [
                ((total_rows, inner), BF16),
                ((total_rows, wide), BF16),
                ((total_rows, LANES), BF16),
                far((8, inner), F32),
                far((8, wide), F32),
            ]
            + [((total_rows, LANES), BF16)] * shards,
            flops * 2,
            [
                pltpu.VMEM((LANES, total_rows), F32),
                pltpu.VMEM((total_rows, total_rows), F32),
                pltpu.VMEM((total_rows, LANES), F32),
                pltpu.VMEM((total_rows, LANES), F32),
                pltpu.VMEM((8, LANES), F32),
            ],
        )
        if not last:
            if last_halves.more():
                last_halves.step()
            du, last_halves.sent = lax.optimization_barrier((du, last_halves.sent))
            (grads,) = call(
                grads_kernel,
                f"grads_{layer}",
                [],
                [Far(normed), grad_gate, grad_all, hidden, du],
                [((depth, 3 * inner), BF16, "raw")],
                flops * 3,
                [pltpu.VMEM((slots, 512, 3 * inner), BF16), pltpu.SemaphoreType.DMA((slots,))],
            )
            grads, du, dq, *last_tail[1:] = lax.optimization_barrier((grads, du, dq, *last_tail[1:]))
            last_kept, last_part = last_halves.last()
            last_tail[1], last_part = lax.optimization_barrier((last_tail[1], last_part))
            first_early = lax.psum_scatter(grads, "dp", scatter_dimension=0, tiled=True)
        pieces = call(
            functools.partial(input_grad_kernel, shards),
            f"input_grad_{layer}",
            [index],
            [
                grad_gate,
                du,
                dbc,
                dq,
                w_x[layer],
                w_gates[layer],
                w_bcs[layer],
                w_steps[layer],
            ],
            [((rows, depth), BF16)] * shards,
            flops * 2,
            [pltpu.VMEM((total_rows, depth), BF16)],
        )
        if last:
            pieces = list(pieces)
            pieces[0], du = lax.optimization_barrier((pieces[0], du))
        pieces = exchange(pieces, "tensor")
        if last:
            tall = (depth // 2, inner)
            mine, theirs = call(
                functools.partial(late_x_kernel, dp_count),
                f"late_{layer}",
                [place],
                [normed, du],
                [far(tall, BF16), (tall, BF16)],
                flops * 2,
                [pltpu.VMEM((depth, inner), BF16)],
            )
            last_tail = [normed, dq, *pieces_bc]
            last_halves = Halves(f"fold_{layer}", mine, theirs)
            last_halves.step()
            pieces[-1], last_halves.sent = lax.optimization_barrier((pieces[-1], last_halves.sent))
        else:
            tall = (depth // 2, LAYERS * LANES)
            mine, theirs = call(
                functools.partial(late_tail_kernel, shards, dp_count),
                f"late_{layer}",
                [place],
                [
                    Far(normed),
                    dq,
                    *exchange(pieces_bc, "tensor"),
                    *last_tail[:2],
                    *exchange(last_tail[2:], "tensor"),
                ],
                [far(tall, BF16), (tall, BF16)],
                flops * 2,
                [pltpu.VMEM((depth, LAYERS * LANES), BF16)],
            )
            halves = Halves(f"fold_{layer}", mine, theirs)
            halves.step()
        arrays = [*pieces, Far(rows_in), gains[layer], Far(grad_now)]
        outs = [far((rows, depth), F32), far((8, depth), F32)]
        if layer:
            arrays.append(Far(branch))
            outs.append((message, BF16))
        back = call(
            functools.partial(norm_back_kernel, shards, bool(layer)),
            f"norm_back_{layer}",
            [],
            arrays,
            outs,
        )
        grad_now, few_gain[layer] = back[:2]
        if not last:
            final = [((LAYERS, slab, 2, inner), F32, "raw"), ((LAYERS, slab, inner), F32, "raw")]
            staged = [
                pltpu.VMEM((slab, 2, inner), F32),
                pltpu.VMEM((slab, inner), F32),
                pltpu.SemaphoreType.DMA((6,)),
            ]
            grads = call(
                functools.partial(finish_kernel, 1),
                "finish_1",
                [],
                [Far(last_early), Far(last_kept), last_part],
                final,
                0,
                staged,
            )
            grads = list(grads)
            last_hidden, few_gain[0], grads[0] = lax.optimization_barrier((last_hidden, few_gain[0], grads[0]))
            messages = call(
                functools.partial(branch_kernel, shards),
                "branch",
                [index],
                [last_hidden, w_outs[-1], Far(out_scales)],
                [((rows, depth), BF16)] * shards,
                flops,
                [pltpu.VMEM((total_rows, depth), BF16)],
            )
            messages = list(messages)
            messages[0], halves.kept = lax.optimization_barrier((messages[0], halves.kept))
            (output,) = call(
                functools.partial(output_kernel, shards),
                "output",
                [],
                [*exchange(messages, "tensor"), Far(current)],
                [far((rows, depth), F32)],
            )
            first_kept, first_part = halves.last()
            first_kept, output = lax.optimization_barrier((first_kept, output))
        if layer:
            blocks = spread_out(back[2], "tensor")

    shared = jnp.stack(
        [
            jnp.concatenate([few_gain[layer][0], few_bc[layer][:5].reshape(-1)])
            for layer in order
        ]
    )
    shared = functools.reduce(jnp.add, spread_out(shared, "tensor"))
    own = jnp.stack([few_x[layer] for layer in order]).reshape(-1, LANES)
    few = jnp.concatenate([own, shared.reshape(-1, LANES)], axis=0)
    few = sum_over_dp(few)
    own = few[: own.shape[0]].reshape(LAYERS, 8, inner)
    shared = few[own.size // LANES :].reshape(LAYERS, -1)
    grad_gain = lax.dynamic_slice_in_dim(shared[:, :depth], place[0] * slab, slab, 1)
    grad_conv_bc = lax.dynamic_slice_in_dim(
        shared[:, depth:].reshape(LAYERS, 5, wide), place[0] * (wide // dp_count), wide // dp_count, 2
    )
    grad_tail, low = call(
        tails_kernel,
        "tails",
        [],
        [Far(first_kept), first_part],
        [far((slab, LAYERS * LANES), F32), ((slab, LAYERS * LANES), BF16)],
    )
    (grad_bc,) = call(
        widen_kernel,
        "widen",
        [index],
        spread_out(low, "tensor"),
        [far((LAYERS, slab, wide), F32)],
    )
    grad_zx, grad_out = call(
        functools.partial(finish_kernel, 0),
        "finish_0",
        [],
        [Far(first_early), *(Raw(part) for part in grads)],
        final,
        0,
        staged,
        aliases={1: 0, 2: 1},
    )
    grad_out = grad_out.transpose(0, 2, 1)
    grad_dt = jnp.stack(
        [grad_tail[:, layer * LANES + HALF : layer * LANES + HALF + heads] for layer in order]
    )
    return (
        output,
        grad_now,
        grad_gain,
        grad_zx,
        grad_bc,
        grad_dt,
        own[:, :5],
        grad_conv_bc,
        own[:, 6, :heads],
        own[:, 6, LANES : LANES + heads],
        own[:, 6, 2 * LANES : 2 * LANES + heads],
        own[:, 5],
        grad_out,
    )


def solution(mesh):
    return jax.shard_map(
        body,
        mesh=mesh,
        in_specs=(
            P(("dp", "tensor"), None),
            P(None, "dp"),
            P(None, "dp", None, "tensor"),
            P(None, "dp", None),
            P(None, "dp", "tensor"),
            P(None, None, "tensor"),
            P(None, None, "dp"),
            P(None, "tensor"),
            P(None, "tensor"),
            P(None, "tensor"),
            P(None, "tensor"),
            P(None, "tensor", "dp"),
            P("dp"),
            P(("dp", "tensor"), None),
        ),
        out_specs=(
            P(("dp", "tensor"), None),
            P(("dp", "tensor"), None),
            P(None, "dp"),
            P(None, "dp", None, "tensor"),
            P(None, "dp", None),
            P(None, "dp", "tensor"),
            P(None, None, "tensor"),
            P(None, None, "dp"),
            P(None, "tensor"),
            P(None, "tensor"),
            P(None, "tensor"),
            P(None, "tensor"),
            P(None, "tensor", "dp"),
        ),
        check_vma=False,
    )
```

```python
import functools
import math

import jax
import jax.numpy as jnp
from jax import lax
from jax.experimental import pallas as pl
from jax.experimental.pallas import tpu as pltpu
from jax.sharding import PartitionSpec as P

LAYERS = 2
EPSILON = 1e-05
LANES = 128
HALF = 64
F32 = jnp.float32
BF16 = jnp.bfloat16
EXACT = lax.Precision.HIGHEST


class Far:
    def __init__(self, array, columns=None, place=0):
        self.array, self.place = array, place
        self.columns = array.shape[1] if columns is None else columns
        self.shape, self.dtype = (array.shape[0], self.columns), array.dtype


class Raw:
    def __init__(self, array):
        self.array, self.shape, self.dtype = array, array.shape, array.dtype


class Arrival:
    def __init__(self, copy, ref):
        self.copy, self.ref, self.waiting = copy, ref, True
        self.shape = ref.shape
        copy.start()

    def wait(self):
        if self.waiting:
            self.copy.wait()
            self.waiting = False

    def __getitem__(self, at):
        self.wait()
        return self.ref[at]


class Departure:
    def __init__(self, copy, ref):
        self.copy, self.ref, self.started = copy, ref, False
        self.shape = ref.shape

    def send(self):
        if not self.started:
            self.copy.start()
            self.started = True

    def __getitem__(self, at):
        return self.ref[at]

    def __setitem__(self, at, values):
        self.ref[at] = values
        if at is Ellipsis:
            self.send()


def dot(left, right, left_dim=1, right_dim=0, precision=None):
    return lax.dot_general(
        left,
        right,
        (((left_dim,), (right_dim,)), ((), ())),
        precision=precision,
        preferred_element_type=F32,
    )


def iota(shape, dim):
    return lax.broadcasted_iota(jnp.int32, shape, dim)


def sigmoid(values):
    return 1.0 / (1.0 + jnp.exp(-values))


def softplus(values):
    return jnp.maximum(values, 0.0) + jnp.log1p(jnp.exp(-jnp.abs(values)))


def rows_later(values, steps):
    return jnp.where(iota(values.shape, 0) >= steps, pltpu.roll(values, steps, 0), 0.0)


def rows_earlier(values, steps):
    total = values.shape[0]
    return jnp.where(
        iota(values.shape, 0) < total - steps, pltpu.roll(values, total - steps, 0), 0.0
    )


def conv(values, taps):
    result = taps[4:5, :] + taps[3:4, :] * values
    for offset in range(3):
        result = result + taps[offset : offset + 1, :] * rows_later(values, 3 - offset)
    return result


def conv_back(values, taps, grad):
    back = taps[3:4, :] * grad
    for offset in range(3):
        back = back + taps[offset : offset + 1, :] * rows_earlier(grad, 3 - offset)
    sums = [
        jnp.sum(grad * rows_later(values, 3 - offset), axis=0, keepdims=True)
        for offset in range(3)
    ]
    sums.append(jnp.sum(grad * values, axis=0, keepdims=True))
    sums.append(jnp.sum(grad, axis=0, keepdims=True))
    return back, sums


def pair_of_parts(column):
    high = column.astype(BF16).astype(F32)
    wide = jnp.broadcast_to(high, (column.shape[0], LANES))
    rest = jnp.broadcast_to(column - high, (column.shape[0], LANES))
    return jnp.where(iota(wide.shape, 1) < HALF, wide, rest).astype(BF16)


def joined_parts(message, width):
    return message[:, width : width + 1].astype(F32) + message[
        :, width + HALF : width + HALF + 1
    ].astype(F32)


def three_parts(values):
    high = values.astype(BF16)
    rest = values - high.astype(F32)
    middle = rest.astype(BF16)
    return high, middle, (rest - middle.astype(F32)).astype(BF16)


def spread_sum(parts, spread):
    spread = spread.astype(BF16)
    return dot(parts[0], spread) + dot(parts[1], spread) + dot(parts[2], spread)


def send(output):
    if isinstance(output, Departure):
        output.send()


def ready(operand):
    if isinstance(operand, Arrival):
        operand.wait()
    return operand.ref if isinstance(operand, (Arrival, Departure)) else operand


def step_state(q_rows, dt_bias, a_log):
    rows = q_rows.shape[0]
    shifted = q_rows + dt_bias
    steps = softplus(shifted)
    rates = -jnp.exp(a_log)
    below = (iota((rows, rows), 0) >= iota((rows, rows), 1)).astype(F32)
    running = dot(below, steps * rates, precision=EXACT)
    return shifted, steps, rates, running


SKIP_ROW, GAIN_ROW, BIAS_ROW, RATE_ROW = 5, 6, 7, 8


def mixer_forward(u_ref, y_ref, params, turned, bc_rows, q_rows, conv_bc, width):
    rows, inner = u_ref.shape
    states = bc_rows.shape[1] // 2
    maps = conv(bc_rows, conv_bc)
    maps = maps * sigmoid(maps)
    _, steps, _, running = step_state(
        q_rows, params[BIAS_ROW : BIAS_ROW + 1, :LANES], params[RATE_ROW : RATE_ROW + 1, :LANES]
    )
    turned[...] = running.T
    scores = dot(maps[:, states:], maps[:, :states], 1, 1, EXACT)
    steps = three_parts(steps)
    causal = iota((rows, rows), 0) >= iota((rows, rows), 1)
    lane = iota((rows, LANES), 1)
    per_block = LANES // width

    def block_step(block):
        at = pl.ds(block * LANES, LANES)
        mixed_in = conv(u_ref[:, at], params[:5, at])
        mixed_in = mixed_in * sigmoid(mixed_in)
        shape = (LANES, LANES)
        heads = block * per_block + iota(shape, 1) // width
        scaled = (mixed_in * spread_sum(steps, heads == iota(shape, 0))).astype(BF16)
        total = None
        for slot in range(per_block):
            head = block * per_block + slot
            gap = running[:, head : head + 1] - turned[head : head + 1, :]
            decay = jnp.exp(jnp.where(causal, gap, -1e30))
            part = dot((decay * scores).astype(BF16), scaled)
            total = part if slot == 0 else jnp.where(lane < slot * width, total, part)
        y_ref[:, at] = total + params[SKIP_ROW : SKIP_ROW + 1, at] * mixed_in

    for block in range(inner // LANES):
        block_step(block)


def gather_rows(target, index, blocks, width):
    rows = blocks[0].shape[0]
    for order, block in enumerate(blocks):
        place = pl.multiple_of((index ^ order) * rows, rows)
        target[pl.ds(place, rows), :] = block[:, :width]


def unpack_kernel(heads, *refs):
    index = refs[0][0]
    outs = refs[-3 * LAYERS :]
    blocks = refs[1 : -3 * LAYERS]
    slab = blocks[0].shape[1]
    depth, wide = outs[LAYERS].shape[1], outs[2 * LAYERS].shape[1]
    piece = wide // len(blocks)

    def placed(start, stop, held, total):
        result = None
        for order, block in enumerate(blocks):
            shape = (held, total)
            ones = iota(shape, 1) - (index ^ order) * held == iota(shape, 0)
            part = dot(block[...][start:stop, :held], ones.astype(BF16))
            result = part if result is None else result + part
        return result

    norm_at = LAYERS * heads
    taps_at = norm_at + LAYERS
    rows = placed(0, taps_at, slab, depth)
    taps = placed(taps_at, taps_at + 5 * LAYERS, piece, wide)
    for layer in range(LAYERS):
        steps = rows[layer * heads : (layer + 1) * heads, :]
        padding = jnp.zeros((LANES - heads, depth), F32)
        outs[layer][...] = jnp.concatenate([steps, padding], axis=0).astype(BF16)
        outs[LAYERS + layer][...] = rows[norm_at + layer : norm_at + layer + 1, :]
        outs[2 * LAYERS + layer][...] = taps[5 * layer : 5 * layer + 5, :]


def pack_kernel(index, *refs):
    blocks, (out,) = refs[:-1], refs[-1:]
    gather_rows(out, index[0], blocks, out.shape[1])


def unpack_maps_kernel(index, *refs):
    blocks, outs = refs[:-LAYERS], refs[-LAYERS:]
    piece = blocks[0].shape[1] // LAYERS
    for layer, out in enumerate(outs):
        total = None
        for order, block in enumerate(blocks):
            shape = (LAYERS * piece, out.shape[1])
            row = iota(shape, 0) - layer * piece
            ones = (row == iota(shape, 1) - (index[0] ^ order) * piece) & (row >= 0) & (row < piece)
            part = dot(block[...], ones.astype(BF16))
            total = part if total is None else total + part
        out[...] = total.astype(BF16)


def first_kernel(layer, shards, slabs, width, *refs):
    index, place = refs[0][0], refs[1][0]
    blocks, refs = refs[2 : 2 + shards], refs[2 + shards :]
    if layer:
        weights, refs = refs[:slabs], refs[slabs:]
        w_in, scales_out = refs[-3:-1]
        refs = refs[:-3] + refs[-1:]
    else:
        w_in, refs = refs[0], refs[1:]
    w_bc, gain, w_dt, conv_bc, params, normed, u_out, bc_out, q_out, y_out, turned = refs
    depth = normed.shape[1]
    inner = u_out.shape[1]
    rows = blocks[0].shape[0]
    if layer == 0:
        for order, block in enumerate(blocks):
            values = block[...].astype(F32)
            scale = lax.rsqrt(jnp.mean(values * values, axis=1, keepdims=True) + EPSILON)
            start = pl.multiple_of((index ^ order) * rows, rows)
            normed[pl.ds(start, rows), :] = (values * scale * gain[...]).astype(BF16)
    else:
        gather_rows(normed, index, blocks, depth)
        for order, block in enumerate(blocks):
            start = pl.multiple_of((index ^ order) * rows, rows)
            scales_out[pl.ds(start, rows), :] = jnp.broadcast_to(
                joined_parts(block, depth), (rows, LANES)
            )
        gather_rows(w_in, place, weights, inner)
        send(scales_out)
        send(w_in)
    send(normed)
    rows_in = normed[...]
    bc_rows = dot(rows_in, w_bc[...])
    q_rows = dot(rows_in, w_dt[...], 1, 1)
    u_rows = dot(rows_in, w_in[...])
    u_out[...] = u_rows
    bc_out[...] = bc_rows
    q_out[...] = q_rows
    mixer_forward(
        ready(u_out), ready(y_out), ready(params), turned, bc_rows, q_rows, conv_bc[...], width
    )


def live_column(length, rows):
    return (iota((rows, 1), 0) < length).astype(F32)


def second_kernel(shards, *refs):
    index = refs[0][0]
    length = refs[1][0]
    normed, w_gate, w_out, y_rows, params, z_out = refs[2:8]
    messages, scratch = refs[8 : 8 + shards], refs[8 + shards]
    depth = normed.shape[1]
    part = messages[0].shape[0]
    gate = dot(normed[...], w_gate[...])
    z_out[...] = gate
    gated = y_rows[...] * (gate * sigmoid(gate))
    live = live_column(length, y_rows.shape[0])
    hidden = (gated * params[GAIN_ROW : GAIN_ROW + 1, :] * live).astype(BF16)
    scratch[:, :depth] = dot(hidden, w_out[...], 1, 1).astype(BF16)
    scratch[:, depth:] = pair_of_parts(jnp.sum(gated * gated, axis=1, keepdims=True))
    for order, message in enumerate(messages):
        place = pl.multiple_of((index ^ order) * part, part)
        message[...] = scratch[pl.ds(place, part), :]


def last_second_kernel(shards, *refs):
    index = refs[0][0]
    length = refs[1][0]
    blocks, refs = refs[2 : 2 + shards], refs[2 + shards :]
    normed, w_gate, w_out, y_rows, params = refs[:5]
    z_out, hidden_out, grad_all, grad_hidden_out, sums_out = refs[5:]
    rows = y_rows.shape[0]
    gather_rows(grad_all, index, blocks, normed.shape[1])
    send(grad_all)
    gate = dot(normed[...], w_gate[...])
    z_out[...] = gate
    gated = y_rows[...] * (gate * sigmoid(gate))
    squares = jnp.sum(gated * gated, axis=1, keepdims=True)
    weighted = gated * params[GAIN_ROW : GAIN_ROW + 1, :] * live_column(length, rows)
    hidden_out[...] = weighted.astype(BF16)
    grad_hidden = dot(grad_all[...], w_out[...])
    grad_hidden_out[...] = grad_hidden
    products = jnp.sum(grad_hidden * weighted, axis=1, keepdims=True)
    lane = iota((rows, LANES), 1)
    table = jnp.where(lane == 0, squares, jnp.where(lane == 1, products, 0.0))
    sums_out[...] = table.T[:8, :]


def branch_kernel(shards, *refs):
    index = refs[0][0]
    hidden, w_out, scales = refs[1:4]
    messages, scratch = refs[4 : 4 + shards], refs[4 + shards]
    part = messages[0].shape[0]
    scratch[...] = (scales[:, 0:1] * dot(hidden[...], w_out[...], 1, 1)).astype(BF16)
    for order, message in enumerate(messages):
        place = pl.multiple_of((index ^ order) * part, part)
        message[...] = scratch[pl.ds(place, part), :]


def gate_back(length, scale, product, inner_all, y_rows, gate, grad_hidden, gate_gain):
    live = live_column(length, y_rows.shape[0])
    turn = sigmoid(gate)
    opened = gate * turn
    gated = y_rows * opened
    grad_live = grad_hidden * live
    grad_gain = jnp.sum(grad_live * gated * scale, axis=0, keepdims=True)
    grad_gated = scale * grad_live * gate_gain - gated * (
        scale * scale * scale * (product / inner_all)
    )
    hidden = (gated * scale * gate_gain * live).astype(BF16)
    grad_y = grad_gated * opened
    grad_gate = grad_gated * y_rows * (turn * (1.0 + gate * (1.0 - turn)))
    return hidden, grad_y, grad_gate.astype(BF16), grad_gain


def weight_grads(pairs, out, staged, sems):
    slots, part = staged.shape[:2]
    copies = []
    for slot in range(slots):
        cut = slice(slot * part, (slot + 1) * part)
        at = 0
        for left, right in pairs:
            columns = right.shape[1]
            staged[slot, :, at : at + columns] = dot(left[:, cut], right[...], 0, 0).astype(BF16)
            at += columns
        copies.append(
            pltpu.make_async_copy(staged.at[slot], out.at[pl.ds(slot * part, part), :], sems.at[slot])
        )
        copies[-1].start()
    for copy in copies:
        copy.wait()


def last_gate_kernel(shards, inner_all, *refs):
    length = refs[0][0]
    sums, refs = refs[1 : 1 + shards], refs[1 + shards :]
    y_rows, gate, grad_hidden, params, normed, grad_all = refs[:6]
    grad_y_out, grad_gate_out, gain_out, grads_out, scale_out, staged, sems = refs[6:]
    rows = y_rows.shape[0]
    total = sums[0][...]
    for other in sums[1:]:
        total = total + other[...]
    table = jnp.concatenate([total, jnp.zeros((LANES - 8, rows), F32)], axis=0).T
    scale = lax.rsqrt(table[:, 0:1] / inner_all + EPSILON)
    scale_out[...] = jnp.broadcast_to(scale, scale_out.shape)
    hidden, grad_y, grad_gate, grad_gain = gate_back(
        length,
        scale,
        table[:, 1:2],
        inner_all,
        y_rows[...],
        gate[...],
        grad_hidden[...],
        params[GAIN_ROW : GAIN_ROW + 1, :],
    )
    grad_y_out[...] = grad_y
    grad_gate_out[...] = grad_gate
    gain_out[...] = jnp.broadcast_to(grad_gain, gain_out.shape)
    weight_grads(((normed, grad_gate), (grad_all, hidden)), grads_out, staged, sems)


def gate_kernel(shards, inner_all, *refs):
    index = refs[0][0]
    length = refs[1][0]
    blocks, refs = refs[2 : 2 + shards], refs[2 + shards :]
    scales, w_out, y_rows, gate, params, normed = refs[:6]
    grad_y_out, grad_gate_out, gain_out, hidden_out, grad_all, products = refs[6:]
    depth = grad_all.shape[1]
    part = blocks[0].shape[0]
    gather_rows(grad_all, index, blocks, depth)
    for order, block in enumerate(blocks):
        place = pl.multiple_of((index ^ order) * part, part)
        products[pl.ds(place, part), :] = jnp.broadcast_to(
            joined_parts(block, depth), (part, LANES)
        )
    hidden, grad_y, grad_gate, grad_gain = gate_back(
        length,
        scales[:, 0:1],
        products[:, 0:1],
        inner_all,
        y_rows[...],
        gate[...],
        dot(grad_all[...], w_out[...]),
        params[GAIN_ROW : GAIN_ROW + 1, :],
    )
    grad_y_out[...] = grad_y
    grad_gate_out[...] = grad_gate
    hidden_out[...] = hidden
    gain_out[...] = jnp.broadcast_to(grad_gain, gain_out.shape)


def grads_kernel(normed, grad_gate, grad_all, hidden, du, out, staged, sems):
    weight_grads(((normed, grad_gate), (grad_all, hidden), (normed, du)), out, staged, sems)


def scan_back_kernel(width, index, *refs):
    u_ref, bc_ref, q_ref, y_ref, grad_ref, gain_sum, conv_bc, params_ref = refs[:8]
    du_out, dbc_out, dq_out, sums_out, sums_bc = refs[8:13]
    pieces = refs[13:-5]
    turned, grad_scores, grad_running, grad_steps, skip_sum = refs[-5:]
    params, u_ref, y_ref, grad_ref = ready(params_ref), ready(u_ref), ready(y_ref), ready(grad_ref)
    sums_x, du_ref = ready(sums_out), ready(du_out)
    bc_rows, q_rows = bc_ref[...], q_ref[...]
    rows, inner = u_ref.shape
    states = bc_rows.shape[1] // 2
    taps_bc = conv_bc[...]
    pre_bc = conv(bc_rows, taps_bc)
    turn_bc = sigmoid(pre_bc)
    maps = pre_bc * turn_bc
    shifted, steps, rates, running = step_state(
        q_rows, params[BIAS_ROW : BIAS_ROW + 1, :LANES], params[RATE_ROW : RATE_ROW + 1, :LANES]
    )
    turned[...] = running.T
    b_rows, c_rows = maps[:, :states], maps[:, states:]
    scores = dot(b_rows, c_rows, 1, 1, EXACT)
    steps_parts = three_parts(steps)
    causal = iota((rows, rows), 0) <= iota((rows, rows), 1)
    lane = iota((rows, LANES), 1)
    per_block = LANES // width
    for total in (grad_scores, grad_running, grad_steps, skip_sum):
        total[...] = jnp.zeros(total.shape, F32)

    def block_step(block):
        at = pl.ds(block * LANES, LANES)
        u_rows, grad_y = u_ref[:, at], grad_ref[:, at]
        taps_x, skips = params[:5, at], params[SKIP_ROW : SKIP_ROW + 1, at]
        pre_x = conv(u_rows, taps_x)
        turn_x = sigmoid(pre_x)
        mixed_in = pre_x * turn_x
        shape = (LANES, LANES)
        heads = block * per_block + iota(shape, 1) // width
        steps_wide = spread_sum(steps_parts, heads == iota(shape, 0))
        scaled = (mixed_in * steps_wide).astype(BF16)
        grad_low = grad_y.astype(BF16)
        grad_scaled = None
        for slot in range(per_block):
            head = block * per_block + slot
            gap = turned[head : head + 1, :] - running[:, head : head + 1]
            decay = jnp.exp(jnp.where(causal, gap, -1e30))
            part = dot((decay * scores).astype(BF16), grad_low)
            grad_scaled = part if slot == 0 else jnp.where(lane < slot * width, grad_scaled, part)
            own = jnp.where(
                (lane >= slot * width) & (lane < (slot + 1) * width), scaled, jnp.zeros_like(scaled)
            )
            grad_scores[...] += dot(own, grad_low, 1, 1) * decay
        gather = block * per_block + iota(shape, 0) // width == iota(shape, 1)
        within = y_ref[:, at] - skips * mixed_in
        moved = grad_low.astype(F32) * within - scaled.astype(F32) * grad_scaled
        grad_running[...] += spread_sum(three_parts(moved), gather)
        grad_steps[...] += spread_sum(three_parts(mixed_in * grad_scaled), gather)
        skip_row = jnp.sum(grad_y * mixed_in, axis=0, keepdims=True)
        skip_sum[...] += spread_sum(three_parts(jnp.broadcast_to(skip_row, (8, LANES))), gather)
        grad_x = steps_wide * grad_scaled + skips * grad_y
        grad_x = grad_x * (turn_x * (1.0 + pre_x * (1.0 - turn_x)))
        du, tap_sums = conv_back(u_rows, taps_x, grad_x)
        du_ref[:, at] = du.astype(BF16)
        tap_sums.append(gain_sum[0:1, at])
        tap_sums.append(jnp.zeros((2, LANES), F32))
        sums_x[:, at] = jnp.concatenate(tap_sums, axis=0)

    for block in range(inner // LANES):
        block_step(block)
    grad_b = dot(grad_scores[...], c_rows, precision=EXACT)
    grad_c = dot(grad_scores[...], b_rows, 0, 0, EXACT)
    above = (iota((rows, rows), 0) <= iota((rows, rows), 1)).astype(F32)
    grad_decay = dot(above, grad_running[...], precision=EXACT)
    grad_q = (grad_steps[...] + grad_decay * rates) * sigmoid(shifted)
    dq_out[...] = grad_q.astype(BF16)
    sums_x[6:7, :LANES] = jnp.sum(grad_q, axis=0, keepdims=True)
    sums_x[6:7, LANES : 2 * LANES] = jnp.sum(grad_decay * steps, axis=0, keepdims=True) * rates
    sums_x[6:7, 2 * LANES : 3 * LANES] = skip_sum[0:1, :]
    grad_bc = jnp.concatenate([grad_b, grad_c], axis=1)
    grad_bc = grad_bc * (turn_bc * (1.0 + pre_bc * (1.0 - turn_bc)))
    dbc, tap_sums = conv_back(bc_rows, taps_bc, grad_bc)
    low = dbc.astype(BF16)
    dbc_out[...] = low
    piece = low.shape[1] // len(pieces)
    for order, out in enumerate(pieces):
        shape = (low.shape[1], LANES)
        ones = iota(shape, 0) - (index[0] ^ order) * piece == iota(shape, 1)
        ones = ones & (iota(shape, 1) < piece)
        out[...] = dot(low, ones.astype(BF16)).astype(BF16)
    tap_sums.append(jnp.zeros((3, low.shape[1]), F32))
    sums_bc[...] = jnp.concatenate(tap_sums, axis=0)


def halving_order(count):
    order = [0]
    step = count // 2
    while step > 1:
        order = order + [place + step for place in order]
        step //= 2
    return order


def late_tail(parts, dq):
    total = parts[0][...].astype(F32)
    for other in parts[1:]:
        total = total + other[...].astype(F32)
    shape = (LANES, LANES)
    moved = (iota(shape, 1) - HALF == iota(shape, 0)).astype(BF16)
    tail = (total + dot(dq[...], moved)).astype(BF16)
    return tail


def split_slabs(place, slabs, scratch, mine, theirs):
    slab = scratch.shape[0] // slabs
    for slot, order in enumerate(halving_order(slabs)):
        cut = slice(slot * slab, (slot + 1) * slab)
        for out, flip in ((mine, 0), (theirs, 1)):
            start = pl.multiple_of((place[0] ^ (order + flip)) * slab, slab)
            out[cut, :] = scratch[pl.ds(start, slab), :]


def late_tail_kernel(shards, slabs, place, *refs):
    mine, theirs, scratch = refs[-3:]
    for layer in range(LAYERS):
        normed, dq, *parts = refs[layer * (2 + shards) : (layer + 1) * (2 + shards)]
        grads = dot(normed[...], late_tail(parts, dq), 0, 0)
        scratch[:, layer * LANES : (layer + 1) * LANES] = grads.astype(BF16)
    split_slabs(place, slabs, scratch, mine, theirs)


def late_x_kernel(slabs, place, normed, du, mine, theirs, scratch):
    scratch[...] = dot(normed[...], du[...], 0, 0).astype(BF16)
    split_slabs(place, slabs, scratch, mine, theirs)


def fold_kernel(mine, other, kept, sent):
    half = kept.shape[0]
    kept[...] = mine[:half, :].astype(F32) + other[:half, :].astype(F32)
    sent[...] = (mine[half:, :].astype(F32) + other[half:, :].astype(F32)).astype(BF16)


def tails_kernel(kept, part, tail_out, low_out):
    tail = kept[...] + part[...].astype(F32)
    low_out[...] = tail.astype(BF16)
    tail_out[...] = tail


def finish_kernel(layer, early, *refs):
    zx_out, out_out, zx_rows, out_rows, sems = refs[-5:]
    rows, inner = out_rows.shape
    slots = sems.shape[0] // 2
    part = rows // slots
    copies = []
    for slot in range(slots):
        cut = pl.ds(slot * part, part)
        zx_rows[cut, 0, :] = early[cut, :inner].astype(F32)
        if layer:
            kept, other = refs[:2]
            zx_rows[cut, 1, :] = kept[cut, :inner] + other[cut, :inner].astype(F32)
        else:
            zx_rows[cut, 1, :] = early[cut, 2 * inner :].astype(F32)
        out_rows[cut, :] = early[cut, inner : 2 * inner].astype(F32)
        copies += [
            pltpu.make_async_copy(zx_rows.at[cut], zx_out.at[layer, cut], sems.at[2 * slot]),
            pltpu.make_async_copy(out_rows.at[cut], out_out.at[layer, cut], sems.at[2 * slot + 1]),
        ]
        copies[-2].start()
        copies[-1].start()
    for copy in copies:
        copy.wait()


def widen_kernel(index, *refs):
    blocks, (out,) = refs[:-1], refs[-1:]
    wide = out.shape[2]
    piece = wide // len(blocks)
    for layer in range(LAYERS):
        total = None
        for order, block in enumerate(blocks):
            shape = (LANES, wide)
            lane = iota(shape, 1) - (index[0] ^ order) * piece
            ones = (lane == iota(shape, 0)) & (iota(shape, 0) < piece)
            part = dot(block[:, layer * LANES : (layer + 1) * LANES], ones.astype(BF16))
            total = part if total is None else total + part
        out[layer, :, :] = total


def input_grad_kernel(shards, *refs):
    index = refs[0][0]
    grad_gate, du, dbc, dq, w_in, w_gate, w_bc, w_dt = refs[1:9]
    outs, scratch = refs[9 : 9 + shards], refs[9 + shards]
    part = outs[0].shape[0]
    total = dot(dbc[...], w_bc[...], 1, 1) + dot(dq[...], w_dt[...])
    total = total + dot(du[...], w_in[...], 1, 1)
    scratch[...] = (total + dot(grad_gate[...], w_gate[...], 1, 1)).astype(BF16)
    for order, out in enumerate(outs):
        place = pl.multiple_of((index ^ order) * part, part)
        out[...] = scratch[pl.ds(place, part), :]


def branch_total(messages, depth, inner_all):
    total = messages[0][:, :depth].astype(F32)
    squares = joined_parts(messages[0], depth)
    for other in messages[1:]:
        total = total + other[:, :depth].astype(F32)
        squares = squares + joined_parts(other, depth)
    return total, lax.rsqrt(squares / inner_all + EPSILON)


def residual_kernel(shards, inner_all, *refs):
    messages = refs[:shards]
    start, gain, current_out, branch_out, message_out = refs[shards:]
    depth = start.shape[1]
    branch, scale = branch_total(messages, depth, inner_all)
    current = start[...].astype(F32) + scale * branch
    current_out[...] = current
    branch_out[...] = branch
    norm = lax.rsqrt(jnp.mean(current * current, axis=1, keepdims=True) + EPSILON)
    message_out[:, :depth] = (current * norm * gain[...]).astype(BF16)
    message_out[:, depth:] = pair_of_parts(scale)


def output_kernel(shards, *refs):
    messages = refs[:shards]
    start, out = refs[shards:]
    total = start[...]
    for message in messages:
        total = total + message[...].astype(F32)
    out[...] = total


def norm_back_kernel(shards, last, *refs):
    blocks = refs[:shards]
    refs = refs[shards:]
    rows_in, gain, grad_in = refs[:3]
    current = rows_in[...].astype(F32)
    depth = current.shape[1]
    grad_normed = blocks[0][...].astype(F32)
    for other in blocks[1:]:
        grad_normed = grad_normed + other[...].astype(F32)
    norm = lax.rsqrt(jnp.mean(current * current, axis=1, keepdims=True) + EPSILON)
    weighted = grad_normed * gain[...]
    inner_product = jnp.mean(weighted * current, axis=1, keepdims=True)
    grad = grad_in[...].astype(F32) + norm * weighted - current * (norm * norm * norm * inner_product)
    gain_row = jnp.sum(grad_normed * current * norm, axis=0, keepdims=True)
    if last:
        branch, grad_out, gain_out, message_out = refs[3:]
        low = grad.astype(BF16)
        message_out[:, :depth] = low
        message_out[:, depth:] = pair_of_parts(
            jnp.sum(low.astype(F32) * branch[...], axis=1, keepdims=True)
        )
    else:
        grad_out, gain_out = refs[3:]
    grad_out[...] = grad
    gain_out[...] = jnp.broadcast_to(gain_row, gain_out.shape)


def call(kernel, name, scalars, arrays, outs, flops=0, scratch=(), vmem=24, aliases=None):
    far_in = [item for item in arrays if isinstance(item, Far)]
    far_out = [out for out in outs if out[2:] == ("far",)]
    specs, given, out_specs, shapes, held = [], [], [], [], 0
    for item in arrays:
        if isinstance(item, (Far, Raw)):
            specs.append(pl.BlockSpec(memory_space=pl.ANY))
            given.append(pltpu.with_memory_space_constraint(item.array, pltpu.HBM))
        else:
            specs.append(pl.BlockSpec(memory_space=pltpu.VMEM))
            given.append(item)
        held += math.prod(item.shape) * item.dtype.itemsize
    for shape, dtype, *kind in outs:
        out_specs.append(pl.BlockSpec(memory_space=pl.ANY if kind else pltpu.VMEM))
        shapes.append(pltpu.HBM(shape, dtype) if kind else jax.ShapeDtypeStruct(shape, dtype))
        held += math.prod(shape) * jnp.dtype(dtype).itemsize
    extra = [pltpu.VMEM(item.shape, item.dtype) for item in far_in]
    extra += [pltpu.VMEM(out[0], out[1]) for out in far_out]
    extra += [pltpu.SemaphoreType.DMA((max(1, len(far_in) + len(far_out)),))]

    def whole(*refs):
        refs = list(refs)
        own = len(refs) - len(extra)
        places, sems = refs[own:-1], refs[-1]
        refs = refs[:own]
        moved, slot = [], 0
        for order, item in enumerate(arrays):
            if isinstance(item, Far):
                at = len(scalars) + order
                source = refs[at]
                if item.columns != item.array.shape[1]:
                    source = source.at[:, pl.ds(item.place * item.columns, item.columns)]
                copy = pltpu.make_async_copy(source, places[slot], sems.at[slot])
                refs[at] = Arrival(copy, places[slot])
                moved.append(refs[at])
                slot += 1
        leaving = []
        for order, out in enumerate(outs):
            if out[2:] == ("far",):
                at = len(scalars) + len(arrays) + order
                copy = pltpu.make_async_copy(places[slot], refs[at], sems.at[slot])
                refs[at] = Departure(copy, places[slot])
                leaving.append(refs[at])
                slot += 1
        kernel(*refs)
        for item in moved:
            item.wait()
        for item in leaving:
            item.send()
        for item in leaving:
            item.copy.wait()

    return pl.pallas_call(
        whole,
        out_shape=tuple(shapes),
        in_specs=[pl.BlockSpec(memory_space=pltpu.SMEM)] * len(scalars) + specs,
        out_specs=tuple(out_specs),
        scratch_shapes=list(scratch) + extra,
        input_output_aliases=aliases or {},
        compiler_params=pltpu.CompilerParams(vmem_limit_bytes=vmem * 1024 * 1024),
        cost_estimate=pl.CostEstimate(flops=1, bytes_accessed=1, transcendentals=0),
        name=name,
    )(*scalars, *given)


def near(*parts):
    return parts if len(parts) > 1 else parts[0]


def far(shape, dtype):
    return (shape, dtype, "far")


def exchange(blocks, axis):
    count = lax.axis_size(axis)
    return [blocks[0]] + [
        lax.ppermute(blocks[k], axis, [(i, i ^ k) for i in range(count)]) for k in range(1, count)
    ]


def spread_out(block, axis):
    return exchange([block] * lax.axis_size(axis), axis)


def gather_dp(blocks):
    count = lax.axis_size("dp")
    hop = count // 2 // len(blocks)
    while hop:
        for k in list(blocks):
            blocks[k ^ hop] = lax.ppermute(blocks[k], "dp", [(i, i ^ hop) for i in range(count)])
        hop //= 2
    return [blocks[k] for k in range(count)]


def over_dp(block, hop):
    count = lax.axis_size("dp")
    return lax.ppermute(block, "dp", [(i, i ^ hop) for i in range(count)])


class Halves:
    def __init__(self, name, mine, theirs):
        self.name, self.kept, self.sent, self.hop = name, mine, theirs, 1

    def receive(self):
        other = over_dp(self.sent, self.hop)
        self.hop *= 2
        return other

    def step(self, other=None):
        half = (self.kept.shape[0] // 2, self.kept.shape[1])
        self.kept, self.sent = call(
            fold_kernel,
            self.name,
            [],
            [Far(self.kept), self.receive() if other is None else other],
            [far(half, F32), (half, BF16)],
        )

    def more(self):
        return self.hop * 2 < lax.axis_size("dp")

    def last(self):
        while self.more():
            self.step()
        return self.kept, self.receive()


def sum_over_dp(values):
    hop = 1
    while hop < lax.axis_size("dp"):
        values = values + over_dp(values, hop)
        hop *= 2
    return values


def body(
    residual_in,
    norm_gain,
    w_zx,
    w_bc,
    w_dt,
    conv_x,
    conv_bc,
    dt_bias,
    a_log,
    d_skip,
    gate_gain,
    w_out,
    lengths,
    cotangent,
):
    shards = lax.axis_size("tensor")
    dp_count = lax.axis_size("dp")
    rows, depth = residual_in.shape
    inner = gate_gain.shape[1]
    heads = dt_bias.shape[1]
    width = inner // heads
    wide = w_bc.shape[2]
    total_rows = rows * shards
    inner_all = inner * shards
    slab = norm_gain.shape[1]
    index = lax.axis_index("tensor").reshape(1).astype(jnp.int32)
    place = lax.axis_index("dp").reshape(1).astype(jnp.int32)
    message = (rows, depth + LANES)

    order = range(LAYERS)
    columns = [w_zx[0, :, 1, :], w_zx[0, :, 0, :], w_out[0].T]
    packed = jnp.concatenate(columns, axis=1)
    packed, w_dt, w_zx, w_out = lax.optimization_barrier((packed, w_dt, w_zx, w_out))
    w_first = lax.all_gather(packed, "dp", axis=0, tiled=True)
    x_half = [w_zx[1, :, 1, :], over_dp(w_zx[1, :, 1, :], dp_count // 2)]
    few = jnp.concatenate(
        [
            w_dt.transpose(0, 2, 1).reshape(LAYERS * heads, slab),
            norm_gain,
            jnp.pad(conv_bc.reshape(LAYERS * 5, -1), ((0, 0), (0, slab - wide // dp_count))),
        ],
        axis=0,
    )
    few = jnp.pad(few, ((0, -few.shape[0] % 16), (0, 0)))
    few, x_half[1] = lax.optimization_barrier((few, x_half[1]))
    few = gather_dp({0: few})
    x_blocks = gather_dp({0: x_half[0], dp_count // 2: x_half[1]})
    residual_blocks = spread_out(residual_in, "tensor")
    late_blocks = spread_out(cotangent, "tensor")
    w_last = lax.all_gather(
        jnp.concatenate([w_zx[1, :, 0, :], w_out[1].T], axis=1), "dp", axis=0, tiled=True
    )
    w_x = [Far(w_first, inner, 0)]
    w_gates = [Far(w_first, inner, 1), Far(w_last, inner, 0)]
    w_outs = [Far(w_first, inner, 2), Far(w_last, inner, 1)]
    piece = wide // shards
    maps = lax.dynamic_slice_in_dim(w_bc, index[0] * piece, piece, 2)
    (maps,) = call(
        pack_kernel,
        "pack_maps",
        [place],
        gather_dp({0: jnp.concatenate([maps[layer] for layer in order], axis=1)}),
        [((depth, LAYERS * piece), BF16)],
    )
    w_bcs = call(
        unpack_maps_kernel,
        "unpack_maps",
        [index],
        spread_out(maps, "tensor"),
        [far((depth, wide), BF16)] * LAYERS,
    )
    params = []
    for layer in order:
        ends = jnp.stack([dt_bias[layer], a_log[layer]])
        params.append(
            jnp.concatenate(
                [
                    conv_x[layer],
                    jnp.repeat(d_skip[layer], width)[None],
                    gate_gain[layer][None],
                    jnp.pad(ends, ((0, 7), (0, inner - heads))),
                ],
                axis=0,
            )
        )
    few[1], params[0], params[1] = lax.optimization_barrier((few[1], params[0], params[1]))
    few = call(
        functools.partial(unpack_kernel, heads),
        "unpack",
        [place],
        few,
        [far((LANES, depth), BF16)] * LAYERS + [far((1, depth), F32)] * LAYERS + [far((5, wide), F32)] * LAYERS,
    )
    w_steps, gains, taps_bc = few[:LAYERS], few[LAYERS : 2 * LAYERS], few[2 * LAYERS :]
    params = [Far(part) for part in params]
    w_steps, gains, taps_bc, w_bcs = (
        [Far(part) for part in parts] for parts in (w_steps, gains, taps_bc, w_bcs)
    )

    flops = 2 * total_rows * depth * inner
    kept = []
    blocks = residual_blocks
    current = residual_in
    for layer in order:
        last = layer == LAYERS - 1
        long = near if last else far
        hold = near if last else Far
        outs = [
            long((total_rows, depth), BF16),
            far((total_rows, inner), F32),
            far((total_rows, wide), F32),
            far((total_rows, LANES), F32),
            long((total_rows, inner), F32),
        ]
        if layer:
            outs += [far((depth, inner), BF16), far((total_rows, LANES), F32)]
        normed, u_rows, bc_rows, q_rows, y_rows, *more = call(
            functools.partial(first_kernel, layer, shards, dp_count, width),
            f"mix_{layer}",
            [index, place],
            [
                *blocks,
                *(x_blocks if layer else w_x),
                w_bcs[layer],
                gains[layer],
                w_steps[layer],
                taps_bc[layer],
                params[layer],
            ],
            outs,
            flops * 3,
            [pltpu.VMEM((LANES, total_rows), F32)],
        )
        if layer:
            w_x.append(Far(more[0]))
            scales = more[1]
        arrays = [hold(normed), w_gates[layer], w_outs[layer], hold(y_rows), params[layer]]
        if last:
            gate, last_hidden, grad_all, grad_hidden, sums = call(
                functools.partial(last_second_kernel, shards),
                f"gate_{layer}",
                [index, lengths],
                [*late_blocks, *arrays],
                [
                    ((total_rows, inner), F32),
                    ((total_rows, inner), BF16),
                    ((total_rows, depth), BF16),
                    ((total_rows, inner), F32),
                    ((8, total_rows), F32),
                ],
                flops * 2,
            )
            sums = spread_out(sums, "tensor")
        else:
            gate, *sent = call(
                functools.partial(second_kernel, shards),
                f"gate_{layer}",
                [index, lengths],
                arrays,
                [far((total_rows, inner), F32)] + [(message, BF16)] * shards,
                flops * 2,
                [pltpu.VMEM((total_rows, depth + LANES), BF16)],
            )
            sent = exchange(sent, "tensor")
        kept.append([normed, u_rows, bc_rows, q_rows, y_rows, gate, current])
        if not last:
            current, branch, packed = call(
                functools.partial(residual_kernel, shards, inner_all),
                f"residual_{layer}",
                [],
                [*sent, Far(current), gains[layer + 1]],
                [far((rows, depth), F32), far((rows, depth), F32), (message, BF16)],
            )
            blocks = spread_out(packed, "tensor")

    grad_now = cotangent
    few_x, few_bc, few_gain = {}, {}, {}
    for layer in reversed(order):
        last = layer == LAYERS - 1
        normed, u_rows, bc_rows, q_rows, y_rows, gate, rows_in = kept[layer]
        hold = near if last else Far
        outs = [
            ((total_rows, inner), F32),
            ((total_rows, inner), BF16),
            ((8, inner), F32),
        ]
        slots = depth // 512
        if last:
            grad_y, grad_gate, gain_sum, grads, out_scales = call(
                functools.partial(last_gate_kernel, shards, inner_all),
                f"gate_back_{layer}",
                [lengths],
                [*sums, y_rows, gate, grad_hidden, params[layer], normed, grad_all],
                outs
                + [((depth, 2 * inner), BF16, "raw"), far((total_rows, LANES), F32)],
                flops * 2,
                [pltpu.VMEM((slots, 512, 2 * inner), BF16), pltpu.SemaphoreType.DMA((slots,))],
            )
            grads, grad_y = lax.optimization_barrier((grads, grad_y))
            last_early = lax.psum_scatter(grads, "dp", scatter_dimension=0, tiled=True)
        else:
            grad_y, grad_gate, gain_sum, hidden, grad_all = call(
                functools.partial(gate_kernel, shards, inner_all),
                f"gate_back_{layer}",
                [index, lengths],
                [*blocks, Far(scales), w_outs[layer], Far(y_rows), Far(gate), params[layer], Far(normed)],
                outs + [((total_rows, inner), BF16), ((total_rows, depth), BF16)],
                flops * 3,
                [pltpu.VMEM((total_rows, LANES), F32)],
            )
        du, dbc, dq, few_x[layer], few_bc[layer], *pieces_bc = call(
            functools.partial(scan_back_kernel, width),
            f"mix_back_{layer}",
            [index],
            [
                Far(u_rows),
                Far(bc_rows),
                Far(q_rows),
                hold(y_rows),
                grad_y,
                gain_sum,
                taps_bc[layer],
                params[layer],
            ],
            [
                ((total_rows, inner), BF16),
                ((total_rows, wide), BF16),
                ((total_rows, LANES), BF16),
                far((8, inner), F32),
                far((8, wide), F32),
            ]
            + [((total_rows, LANES), BF16)] * shards,
            flops * 2,
            [
                pltpu.VMEM((LANES, total_rows), F32),
                pltpu.VMEM((total_rows, total_rows), F32),
                pltpu.VMEM((total_rows, LANES), F32),
                pltpu.VMEM((total_rows, LANES), F32),
                pltpu.VMEM((8, LANES), F32),
            ],
        )
        if not last:
            if last_halves.more():
                last_halves.step()
            du, last_halves.sent = lax.optimization_barrier((du, last_halves.sent))
            (grads,) = call(
                grads_kernel,
                f"grads_{layer}",
                [],
                [Far(normed), grad_gate, grad_all, hidden, du],
                [((depth, 3 * inner), BF16, "raw")],
                flops * 3,
                [pltpu.VMEM((slots, 512, 3 * inner), BF16), pltpu.SemaphoreType.DMA((slots,))],
            )
            grads, du, dq, *last_tail[1:] = lax.optimization_barrier((grads, du, dq, *last_tail[1:]))
            last_kept, last_part = last_halves.last()
            last_tail[1], last_part = lax.optimization_barrier((last_tail[1], last_part))
            first_early = lax.psum_scatter(grads, "dp", scatter_dimension=0, tiled=True)
        pieces = call(
            functools.partial(input_grad_kernel, shards),
            f"input_grad_{layer}",
            [index],
            [
                grad_gate,
                du,
                dbc,
                dq,
                w_x[layer],
                w_gates[layer],
                w_bcs[layer],
                w_steps[layer],
            ],
            [((rows, depth), BF16)] * shards,
            flops * 2,
            [pltpu.VMEM((total_rows, depth), BF16)],
        )
        if last:
            pieces = list(pieces)
            pieces[0], du = lax.optimization_barrier((pieces[0], du))
        pieces = exchange(pieces, "tensor")
        if last:
            tall = (depth // 2, inner)
            mine, theirs = call(
                functools.partial(late_x_kernel, dp_count),
                f"late_{layer}",
                [place],
                [normed, du],
                [far(tall, BF16), (tall, BF16)],
                flops * 2,
                [pltpu.VMEM((depth, inner), BF16)],
            )
            last_tail = [normed, dq, *pieces_bc]
            last_halves = Halves(f"fold_{layer}", mine, theirs)
            last_halves.step()
            pieces[-1], last_halves.sent = lax.optimization_barrier((pieces[-1], last_halves.sent))
        else:
            tall = (depth // 2, LAYERS * LANES)
            mine, theirs = call(
                functools.partial(late_tail_kernel, shards, dp_count),
                f"late_{layer}",
                [place],
                [
                    Far(normed),
                    dq,
                    *exchange(pieces_bc, "tensor"),
                    *last_tail[:2],
                    *exchange(last_tail[2:], "tensor"),
                ],
                [far(tall, BF16), (tall, BF16)],
                flops * 2,
                [pltpu.VMEM((depth, LAYERS * LANES), BF16)],
            )
            halves = Halves(f"fold_{layer}", mine, theirs)
            halves.step()
        arrays = [*pieces, Far(rows_in), gains[layer], Far(grad_now)]
        outs = [far((rows, depth), F32), far((8, depth), F32)]
        if layer:
            arrays.append(Far(branch))
            outs.append((message, BF16))
        back = call(
            functools.partial(norm_back_kernel, shards, bool(layer)),
            f"norm_back_{layer}",
            [],
            arrays,
            outs,
        )
        grad_now, few_gain[layer] = back[:2]
        if not last:
            final = [((LAYERS, slab, 2, inner), F32, "raw"), ((LAYERS, slab, inner), F32, "raw")]
            staged = [
                pltpu.VMEM((slab, 2, inner), F32),
                pltpu.VMEM((slab, inner), F32),
                pltpu.SemaphoreType.DMA((6,)),
            ]
            grads = call(
                functools.partial(finish_kernel, 1),
                "finish_1",
                [],
                [Far(last_early), Far(last_kept), last_part],
                final,
                0,
                staged,
            )
            grads = list(grads)
            last_hidden, few_gain[0], grads[0] = lax.optimization_barrier((last_hidden, few_gain[0], grads[0]))
            messages = call(
                functools.partial(branch_kernel, shards),
                "branch",
                [index],
                [last_hidden, w_outs[-1], Far(out_scales)],
                [((rows, depth), BF16)] * shards,
                flops,
                [pltpu.VMEM((total_rows, depth), BF16)],
            )
            messages = list(messages)
            messages[0], halves.kept = lax.optimization_barrier((messages[0], halves.kept))
            (output,) = call(
                functools.partial(output_kernel, shards),
                "output",
                [],
                [*exchange(messages, "tensor"), Far(current)],
                [far((rows, depth), F32)],
            )
            first_kept, first_part = halves.last()
            first_kept, output = lax.optimization_barrier((first_kept, output))
        if layer:
            blocks = spread_out(back[2], "tensor")

    shared = jnp.stack(
        [
            jnp.concatenate([few_gain[layer][0], few_bc[layer][:5].reshape(-1)])
            for layer in order
        ]
    )
    shared = functools.reduce(jnp.add, spread_out(shared, "tensor"))
    own = jnp.stack([few_x[layer] for layer in order]).reshape(-1, LANES)
    few = jnp.concatenate([own, shared.reshape(-1, LANES)], axis=0)
    few = sum_over_dp(few)
    own = few[: own.shape[0]].reshape(LAYERS, 8, inner)
    shared = few[own.size // LANES :].reshape(LAYERS, -1)
    grad_gain = lax.dynamic_slice_in_dim(shared[:, :depth], place[0] * slab, slab, 1)
    grad_conv_bc = lax.dynamic_slice_in_dim(
        shared[:, depth:].reshape(LAYERS, 5, wide), place[0] * (wide // dp_count), wide // dp_count, 2
    )
    grad_tail, low = call(
        tails_kernel,
        "tails",
        [],
        [Far(first_kept), first_part],
        [far((slab, LAYERS * LANES), F32), ((slab, LAYERS * LANES), BF16)],
    )
    (grad_bc,) = call(
        widen_kernel,
        "widen",
        [index],
        spread_out(low, "tensor"),
        [far((LAYERS, slab, wide), F32)],
    )
    grad_zx, grad_out = call(
        functools.partial(finish_kernel, 0),
        "finish_0",
        [],
        [Far(first_early), *(Raw(part) for part in grads)],
        final,
        0,
        staged,
        aliases={1: 0, 2: 1},
    )
    grad_out = grad_out.transpose(0, 2, 1)
    grad_dt = jnp.stack(
        [grad_tail[:, layer * LANES + HALF : layer * LANES + HALF + heads] for layer in order]
    )
    return (
        output,
        grad_now,
        grad_gain,
        grad_zx,
        grad_bc,
        grad_dt,
        own[:, :5],
        grad_conv_bc,
        own[:, 6, :heads],
        own[:, 6, LANES : LANES + heads],
        own[:, 6, 2 * LANES : 2 * LANES + heads],
        own[:, 5],
        grad_out,
    )


def solution(mesh):
    return jax.shard_map(
        body,
        mesh=mesh,
        in_specs=(
            P(("dp", "tensor"), None),
            P(None, "dp"),
            P(None, "dp", None, "tensor"),
            P(None, "dp", None),
            P(None, "dp", "tensor"),
            P(None, None, "tensor"),
            P(None, None, "dp"),
            P(None, "tensor"),
            P(None, "tensor"),
            P(None, "tensor"),
            P(None, "tensor"),
            P(None, "tensor", "dp"),
            P("dp"),
            P(("dp", "tensor"), None),
        ),
        out_specs=(
            P(("dp", "tensor"), None),
            P(("dp", "tensor"), None),
            P(None, "dp"),
            P(None, "dp", None, "tensor"),
            P(None, "dp", None),
            P(None, "dp", "tensor"),
            P(None, None, "tensor"),
            P(None, None, "dp"),
            P(None, "tensor"),
            P(None, "tensor"),
            P(None, "tensor"),
            P(None, "tensor"),
            P(None, "tensor", "dp"),
        ),
        check_vma=False,
    )
```
